32 devices in a mesh: row: 8 (over z, y), col: 4 (over x, core).
Axes of the slice: x: 2, y: 2, z: 4, core: 2. Of those that a mesh axis runs over, the one named last changes fastest.
Arguments:
- object_field: float32 [2, 2048, 1024], P(None, 'row', 'col'), may hold values from -5 to 5
- probe: float32 [2, 256, 256], replicated, may hold values from -6 to 6
- amplitudes: float32 [8, 4, 4, 256, 256], P('row', 'col'), may hold values from 0 to 11, as said below
- positions: int32 [8, 4, 4, 2], P('row', 'col'), may hold values from 0 to 64
Outputs:
- object_next: float32 [2, 2048, 1024], P(None, 'row', 'col')
- probe_next: float32 [2, 256, 256], replicated
The draws below stay inside these ranges and needn't reach their ends.
Inputs may be any that keep to these rules, and one draw needn't show every extreme that they name: Positive amplitudes.
All inputs are finite; a program needn't handle non-finite values.
Results may differ from the reference program's by a relative error of at most 0.0003.
Values sent between devices are 32-bit elements; how exact they have to be, the bound alone decides.
No kernel may reach another device: no remote copies, remote signals or barrier semaphores. Data moves between devices by JAX's collectives and lax.ppermute only.
A program may use at most 64 MiB of HBM per device.

```python
import math
import jax
import jax.numpy as jnp
from jax import lax

W = 256
TILE = 256
MARGIN = 32
FRAMES = 4
TILES_R = 8
TILES_C = 4


def draw_amplitudes(key, part):
    first = jax.random.fold_in(key, 0)
    row_frac = jnp.arange(TILES_R, dtype=jnp.float32) / max(TILES_R - 1, 1)
    col_frac = jnp.arange(TILES_C, dtype=jnp.float32) / max(TILES_C - 1, 1)
    spread = 0.5 * (row_frac[:, None] + col_frac[None, :])
    scaling = jnp.sqrt(1.0 + 2.0 * spread)[:, :, None, None, None]
    normal_draw = jax.random.normal(first, (TILES_R, TILES_C, FRAMES, W, W), jnp.float32)
    base = jnp.exp(0.5 * jnp.clip(normal_draw, -3.0, 3.0))
    factor = jnp.ones((TILES_R, TILES_C, FRAMES, 1, 1), jnp.float32)
    return (scaling * factor * base).astype(jnp.float32)


def place_ends(array, rng, smallest, top_value):
    longest = array.shape.index(max(array.shape))
    spots = []
    for shift in (0, 1):
        where = [jax.random.randint(jax.random.fold_in(rng, axis), (), 0, length) for axis, length in enumerate(array.shape)]
        where[longest] = (where[longest] + shift) % array.shape[longest]
        spots.append(tuple(where))
    return array.at[spots[0]].set(smallest).at[spots[1]].set(top_value)


def level_of(stream_key, extent, shards, smallest, largest):
    factor_of = 1.0
    for axis_at, blocks in shards:
        draws = jax.random.uniform(jax.random.fold_in(jax.random.fold_in(stream_key, 6), axis_at), (blocks,), jnp.float32, smallest / len(shards), largest / len(shards))
        factor_of = factor_of * jnp.repeat(jnp.exp(draws), extent[axis_at] // blocks).reshape((-1,) + (1,) * (len(extent) - 1 - axis_at))
    return factor_of


def scatter_about(own_key, shape, width, limit, cuts=(), held_as=jnp.bfloat16):
    values = width * jax.random.normal(own_key, shape, jnp.float32)
    if cuts:
        values = values * level_of(own_key, shape, cuts, -0.22, 0.18)
    return jnp.clip(values, -limit, limit).astype(held_as)


def setup_inputs(seed: int = 0) -> dict:
    streams_of = jax.random.split(jax.random.key(seed), 5)
    object_field = scatter_about(streams_of[0], (2, TILES_R * TILE, TILES_C * TILE), 0.7, 5.0, ((1, 8), (2, 4)), jnp.float32)
    probe = scatter_about(streams_of[1], (2, W, W), 1.0, 6.0, (), jnp.float32)
    amplitudes = draw_amplitudes(jax.random.fold_in(streams_of[4], 71), 0)
    positions = place_ends(jax.random.randint(streams_of[3], (TILES_R, TILES_C, FRAMES, 2), 0, TILE + 2 * MARGIN - W + 1), jax.random.fold_in(streams_of[3], 1), 0, TILE + 2 * MARGIN - W).astype(jnp.int32)
    return {"object_field": object_field, "probe": probe, "amplitudes": amplitudes, "positions": positions}


smoothing = 0.1
regular = 1.0
epsilon = 1e-06

def tables(length):
    indices = jnp.arange(length, dtype=jnp.int32)
    phases = (indices[:, None] * indices[None, :] % length).astype(jnp.float32) * (2.0 * math.pi / length)
    scaling = 1.0 / math.sqrt(length)
    cosine = jnp.cos(phases) * scaling
    sines = jnp.sin(phases) * scaling
    forward = jnp.concatenate([jnp.concatenate([cosine, sines], 1), jnp.concatenate([-sines, cosine], 1)], 0)
    inverse = jnp.concatenate([jnp.concatenate([cosine, -sines], 1), jnp.concatenate([sines, cosine], 1)], 0)
    return (forward, inverse)

def transform(wavefield, left_matrix, right_matrix):
    length = wavefield.shape[1]
    stacked = wavefield.reshape(2 * length, length)
    mixed = jnp.dot(left_matrix, stacked, precision=lax.Precision.HIGHEST)
    paired = jnp.concatenate([mixed[:length], mixed[length:]], axis=1)
    result = jnp.dot(paired, right_matrix, precision=lax.Precision.HIGHEST)
    return jnp.stack([result[:, :length], result[:, length:]])

def frame_terms(probe, window, amplitude, forward, inverse):
    exit_real = probe[0] * window[0] - probe[1] * window[1]
    exit_imag = probe[0] * window[1] + probe[1] * window[0]
    wave = jnp.stack([exit_real, exit_imag])
    far_field = transform(wave, forward, inverse)
    factor = amplitude / jnp.sqrt(far_field[0] * far_field[0] + far_field[1] * far_field[1] + smoothing)
    near_field = transform(far_field * factor[None], inverse, forward)
    difference = near_field - wave
    object_real = probe[0] * difference[0] + probe[1] * difference[1]
    object_imag = probe[0] * difference[1] - probe[1] * difference[0]
    probe_real = window[0] * difference[0] + window[1] * difference[1]
    probe_imag = window[0] * difference[1] - window[1] * difference[0]
    window_power = window[0] * window[0] + window[1] * window[1]
    return (jnp.stack([object_real, object_imag]), jnp.stack([probe_real, probe_imag, window_power]))

def reference(object_field, probe, amplitudes, positions):
    forward, inverse = tables(W)
    height = TILES_R * TILE
    breadth = TILES_C * TILE
    padded = jnp.pad(object_field, ((0, 0), (MARGIN, MARGIN), (MARGIN, MARGIN)))
    power_map = probe[0] * probe[0] + probe[1] * probe[1]
    frame_count = TILES_R * TILES_C * FRAMES
    measured = amplitudes.reshape(frame_count, W, W)
    offsets = positions.reshape(frame_count, 2).astype(jnp.int32)
    tile_flat = jnp.arange(frame_count, dtype=jnp.int32) // FRAMES
    tile_rows = tile_flat // TILES_C
    tile_cols = tile_flat % TILES_C

    def visit(carried, inputs):
        canvas, probe_acc = carried
        amplitude, offset, tile_row, tile_col = inputs
        row_start = (tile_row * TILE + offset[0]).astype(jnp.int32)
        col_start = (tile_col * TILE + offset[1]).astype(jnp.int32)
        anchor = jnp.zeros((), jnp.int32)
        window = lax.dynamic_slice(padded, (anchor, row_start, col_start), (2, W, W))
        object_term, probe_term = frame_terms(probe, window, amplitude, forward, inverse)
        update = jnp.concatenate([object_term, power_map[None]], 0)
        current = lax.dynamic_slice(canvas, (anchor, row_start, col_start), (3, W, W))
        canvas = lax.dynamic_update_slice(canvas, current + update, (anchor, row_start, col_start))
        return ((canvas, probe_acc + probe_term), None)
    canvas_start = jnp.zeros((3, height + 2 * MARGIN, breadth + 2 * MARGIN), jnp.float32)
    probe_start = jnp.zeros((3, W, W), jnp.float32)
    (canvas, probe_acc), _ = lax.scan(visit, (canvas_start, probe_start), (measured, offsets, tile_rows, tile_cols))
    interior = canvas[:, MARGIN:MARGIN + height, MARGIN:MARGIN + breadth]
    object_next = object_field + interior[0:2] / (interior[2] + regular)
    stepped = probe + probe_acc[0:2] / (probe_acc[2] + regular)
    target = jnp.sum(amplitudes * amplitudes) / frame_count
    probe_power = jnp.sum(stepped * stepped)
    probe_next = stepped * jnp.sqrt(target / (probe_power + epsilon))
    return (object_next, probe_next)
```

```python
import functools
import math

import jax
import jax.numpy as jnp
import numpy as np
from jax import lax
from jax.experimental import pallas as pl
from jax.experimental.pallas import tpu as pltpu
from jax.sharding import PartitionSpec as P

MARGIN = 32
LANES = 128
SUBLANES = 8
HALVINGS = 3

smoothing = 0.1
regular = 1.0
epsilon = 1e-06

f32 = jnp.float32
bf16 = jnp.bfloat16


def tables(length):
    half = length // 2
    scaling = 1.0 / math.sqrt(length)
    k = np.arange(half)
    phases = (k[:, None] * k[None, :] % half) * (2.0 * math.pi / half)
    cosine, sine = np.cos(phases) * scaling, np.sin(phases) * scaling
    right = np.block([[cosine, -sine], [sine, cosine]])
    left = np.block([[cosine, sine], [-sine, cosine]])
    both = np.stack([left, right]).astype(np.float32)
    high = both.astype(bf16)
    low = (both - high.astype(np.float32)).astype(bf16)
    matrices = np.stack([high, low], 1)
    angle = k * (2.0 * math.pi / length)
    turn = np.stack([np.cos(angle), np.sin(angle)]).astype(np.float32)
    rows = np.broadcast_to(turn[:, :, None], (2, half, LANES)).copy()
    columns = np.broadcast_to(turn[:, None, :], (2, SUBLANES, half)).copy()
    return matrices, rows, columns


def split(x):
    high = x.astype(bf16)
    return high, (x - high.astype(f32)).astype(bf16)


def dot(a, b):
    return jnp.dot(a, b, preferred_element_type=f32)


def times_matrix(data, high, low):
    data_high, data_low = split(data)
    return dot(data_high, high) + (dot(data_low, high) + dot(data_high, low))


def matrix_times(high, low, data):
    data_high, data_low = split(data)
    return dot(high, data_high) + (dot(high, data_low) + dot(low, data_high))


def turned(real, imag, cosine, sine):
    return real * cosine - imag * sine, real * sine + imag * cosine


def pack(chunks, lane, width):
    place = lax.broadcasted_iota(jnp.int32, chunks[0].shape, 1) // width
    out = jnp.zeros_like(chunks[0])
    for q, chunk in enumerate(chunks):
        shift = (q * width - lane) % LANES
        moved = pltpu.roll(chunk, shift, 1) if shift else chunk
        out = jnp.where(place == q, moved, out)
    return out


def unpack(packed, q, lane, width):
    shift = (lane - q * width) % LANES
    moved = pltpu.roll(packed, shift, 1) if shift else packed
    place = lax.broadcasted_iota(jnp.int32, packed.shape, 1)
    return jnp.where((place >= lane) & (place < lane + width), moved, 0.0)


def prepare_kernel(amplitude, sorted_out, total_out, held):
    frames, length, _ = amplitude.shape
    half = length // 2
    row = lax.broadcasted_iota(jnp.int32, (length, length), 0)
    column = lax.broadcasted_iota(jnp.int32, (length, length), 1)
    source = jnp.where(column < half, 2 * column, 2 * (column - half) + 1)
    order = jnp.where(row == source, 1.0, 0.0).astype(bf16)
    total = jnp.zeros((SUBLANES, length), f32)
    for f in range(frames):
        values = amplitude[f]
        total += jnp.sum((values * values).reshape(length // SUBLANES, SUBLANES, length), 0)
        high = values.astype(bf16)
        rest = values - high.astype(f32)
        middle = rest.astype(bf16)
        low = (rest - middle.astype(f32)).astype(bf16)
        placed = dot(high, order) + (dot(middle, order) + dot(low, order))
        for parity in range(2):
            held[f, parity] = placed[:, parity * half : (parity + 1) * half]
            for start in range(2):
                at = 2 * parity + start
                sorted_out[f, at * half : (at + 1) * half, :] = held[
                    f, parity, pl.ds(start, half, stride=2), :
                ]
    total_out[...] = total


def edge_kernel(field, above, below, left_out, right_out):
    planes, side, _ = field.shape
    margin = above.shape[1]
    per = LANES // margin
    rows = (side + 2 * margin) // per
    for plane in range(planes):
        for out, tile, lane in (
            (left_out, 0, 0),
            (right_out, side // LANES - 1, LANES - margin),
        ):
            at = pl.ds(tile * LANES, LANES)
            whole = jnp.concatenate(
                [above[plane, :, at], field[plane, :, at], below[plane, :, at]], 0
            )
            chunks = [whole[q * rows : (q + 1) * rows] for q in range(per)]
            out[plane] = pack(chunks, lane, margin)


def frames_kernel(
    blocks,
    place,
    offsets,
    field,
    above,
    below,
    from_left,
    from_right,
    probe,
    amplitude,
    total,
    matrices,
    row_turn,
    column_turn,
    canvas_low,
    canvas,
    canvas_high,
    kept,
    sent,
    padded,
    work,
    sums,
):
    frames = amplitude.shape[0]
    length = probe.shape[1]
    half = length // 2
    side = field.shape[1]
    margin = above.shape[1]
    reach = side + 2 * margin
    wide = side + LANES
    taller = length + SUBLANES
    per = LANES // margin
    chunk = reach // per

    for plane in range(2):
        padded[plane, :margin, :side] = above[plane]
        padded[plane, margin : margin + side, :side] = field[plane]
        padded[plane, margin + side : reach, :side] = below[plane]
        for q in range(per):
            padded[plane, q * chunk : (q + 1) * chunk, side:] = unpack(
                from_right[plane], q, 0, margin
            ) + unpack(from_left[plane], q, LANES - margin, margin)
        padded[plane, reach:, :] = jnp.zeros((SUBLANES, wide), f32)
        work[plane] = jnp.zeros((reach + SUBLANES, wide), f32)
        work[plane, margin : margin + side, :side] = field[plane]
    work[2] = jnp.zeros((reach + SUBLANES, wide), f32)
    work[2, margin : margin + side, :side] = jnp.full((side, side), regular, f32)
    first = jnp.where(place[1] == 0, 1.0, 0.0).astype(f32)
    sums[0] = probe[0] * first
    sums[1] = probe[1] * first
    sums[2] = jnp.full((length, length), regular, f32) * first

    left_high, left_low = matrices[0, 0], matrices[0, 1]
    right_high, right_low = matrices[1, 0], matrices[1, 1]
    row_cos = jnp.concatenate([row_turn[0]] * (length // LANES), 1)
    row_sin = jnp.concatenate([row_turn[1]] * (length // LANES), 1)
    column_cos = column_turn[0, 0:1, :]
    column_sin = column_turn[1, 0:1, :]

    def visit(f, carry):
        a = offsets[f, 0]
        b = offsets[f, 1]
        shift = lax.rem(a, SUBLANES)
        at = pl.ds(pl.multiple_of(a - shift, SUBLANES), taller)
        back = lax.rem(wide + margin - b, wide)
        ahead = lax.rem(wide - margin + b, wide)
        probe_real, probe_imag = probe[0], probe[1]
        window_real, window_imag = (
            pltpu.roll(
                pltpu.roll(padded[plane, at, :], back, 1)[:, :length],
                lax.rem(taller - shift, taller),
                0,
            )[:length]
            for plane in range(2)
        )
        wave_real = probe_real * window_real - probe_imag * window_imag
        wave_imag = probe_real * window_imag + probe_imag * window_real

        even_real = wave_real[:half] + wave_real[half:]
        even_imag = wave_imag[:half] + wave_imag[half:]
        odd_real, odd_imag = turned(
            wave_real[:half] - wave_real[half:],
            wave_imag[:half] - wave_imag[half:],
            row_cos,
            -row_sin,
        )
        stacked = jnp.concatenate(
            [
                jnp.concatenate([even_real, even_imag], 0),
                jnp.concatenate([odd_real, odd_imag], 0),
            ],
            1,
        )
        mixed = matrix_times(left_high, left_low, stacked)
        evens, odds = [], []
        for parity in range(2):
            part = mixed[:, parity * length : (parity + 1) * length]
            real, imag = part[:half], part[half:]
            evens.append(
                jnp.concatenate([real[:, :half] + real[:, half:], imag[:, :half] + imag[:, half:]], 1)
            )
            odds.append(
                jnp.concatenate(
                    turned(
                        real[:, :half] - real[:, half:],
                        imag[:, :half] - imag[:, half:],
                        column_cos,
                        -column_sin,
                    ),
                    1,
                )
            )
        far = times_matrix(jnp.concatenate(evens + odds, 0), right_high, right_low)
        far_real, far_imag = far[:, :half], far[:, half:]
        factor = amplitude[f] * lax.rsqrt(far_real * far_real + far_imag * far_imag + smoothing)
        corrected = jnp.concatenate([far_real * factor, far_imag * factor], 1)

        back_far = times_matrix(corrected, left_high, left_low)
        even, odd = back_far[:length], back_far[length:]
        odd_real, odd_imag = turned(odd[:, :half], odd[:, half:], column_cos, column_sin)
        even_real, even_imag = even[:, :half], even[:, half:]
        real = jnp.concatenate([even_real + odd_real, even_real - odd_real], 1)
        imag = jnp.concatenate([even_imag + odd_imag, even_imag - odd_imag], 1)
        stacked = jnp.concatenate(
            [
                jnp.concatenate([real[:half], imag[:half]], 0),
                jnp.concatenate([real[half:], imag[half:]], 0),
            ],
            1,
        )
        near = matrix_times(right_high, right_low, stacked)
        even, odd = near[:, :length], near[:, length:]
        odd_real, odd_imag = turned(odd[:half], odd[half:], row_cos, row_sin)
        near_real = jnp.concatenate([even[:half] + odd_real, even[:half] - odd_real], 0)
        near_imag = jnp.concatenate([even[half:] + odd_imag, even[half:] - odd_imag], 0)

        sums[0] += window_real * near_real + window_imag * near_imag
        sums[1] += window_real * near_imag - window_imag * near_real
        sums[2] += window_real * window_real + window_imag * window_imag
        under = jnp.zeros((SUBLANES, length), f32)
        beside = jnp.zeros((taller, wide - length), f32)
        terms = (
            probe_real * near_real + probe_imag * near_imag,
            probe_real * near_imag - probe_imag * near_real,
            probe_real * probe_real + probe_imag * probe_imag,
        )
        for plane, term in enumerate(terms):
            lowered = pltpu.roll(jnp.concatenate([term, under], 0), shift, 0)
            work[plane, at, :] += pltpu.roll(jnp.concatenate([lowered, beside], 1), ahead, 1)
        return carry

    lax.fori_loop(0, frames, visit, 0)

    canvas_low[...] = work[:, :margin, :]
    canvas[...] = work[:, margin : margin + side, :]
    canvas_high[...] = work[:, margin + side : reach, :]

    kept[:SUBLANES] = total[...]
    sent[:SUBLANES] = total[...]
    rows = length // blocks
    for p in range(blocks):
        source = pl.multiple_of((place[0] ^ p) * rows, rows)
        out, q = (kept, p) if p < blocks // 2 else (sent, p - blocks // 2)
        for plane in range(3):
            start = SUBLANES + (3 * q + plane) * rows
            out[start : start + rows] = sums[plane, pl.ds(source, rows), :]


def fold_rows_kernel(canvas, above, below, left_out, right_out):
    planes, side, _ = canvas.shape
    margin = above.shape[1]
    per = LANES // margin
    rows = side // per
    at = pl.ds(side, LANES)
    for plane in range(planes):
        whole = jnp.concatenate(
            [
                canvas[plane, :margin, at] + above[plane, :, at],
                canvas[plane, margin : side - margin, at],
                canvas[plane, side - margin :, at] + below[plane, :, at],
            ],
            0,
        )
        chunks = [whole[q * rows : (q + 1) * rows] for q in range(per)]
        left_out[plane] = pack(chunks, LANES - margin, margin)
        right_out[plane] = pack(chunks, 0, margin)


def object_kernel(canvas, above, below, from_left, from_right, out):
    planes, side, _ = canvas.shape
    margin = above.shape[1]
    per = LANES // margin
    rows = side // per
    total = []
    for plane in range(planes):
        whole = jnp.concatenate(
            [
                canvas[plane, :margin, :side] + above[plane, :, :side],
                canvas[plane, margin : side - margin, :side],
                canvas[plane, side - margin :, :side] + below[plane, :, :side],
            ],
            0,
        )
        low = jnp.concatenate([unpack(from_left[plane], q, 0, margin) for q in range(per)], 0)
        high = jnp.concatenate(
            [unpack(from_right[plane], q, LANES - margin, margin) for q in range(per)], 0
        )
        middle = [whole[:, LANES : side - LANES]] if side > 2 * LANES else []
        total.append(
            jnp.concatenate(
                [whole[:, :LANES] + low] + middle + [whole[:, side - LANES :] + high], 1
            )
        )
    weight = 1.0 / total[2]
    out[0] = total[0] * weight
    out[1] = total[1] * weight


def probe_kernel(frame_count, blocks, place, stepped, total, out):
    planes, length, _ = out.shape
    rows = length // blocks
    values = stepped[...]
    power = jnp.sum(values * values)
    target = jnp.sum(total[...]) / frame_count
    scale = jnp.sqrt(jnp.full((rows, length), target / (power + epsilon), f32))
    for p in range(blocks):
        home = pl.multiple_of((place[0] ^ p) * rows, rows)
        for plane in range(planes):
            start = (planes * p + plane) * rows
            out[plane, pl.ds(home, rows), :] = values[start : start + rows] * scale


def shape(*dims):
    return jax.ShapeDtypeStruct(dims, f32)


def call(kernel, outputs, scalars=0, operands=0, scratch=(), cost=None):
    vmem = pl.BlockSpec(memory_space=pltpu.VMEM)
    smem = pl.BlockSpec(memory_space=pltpu.SMEM)
    return pl.pallas_call(
        kernel,
        out_shape=outputs,
        in_specs=[smem] * scalars + [vmem] * operands,
        out_specs=jax.tree.map(lambda _: vmem, outputs),
        scratch_shapes=list(scratch),
        cost_estimate=cost,
        compiler_params=pltpu.CompilerParams(vmem_limit_bytes=40 * 1024 * 1024),
    )


def moved(block, axis, distance):
    devices = range(lax.axis_size(axis))
    return lax.ppermute(
        block, axis, [(i - distance, i) for i in devices if i - distance in devices]
    )


def swapped(block, axis, bit):
    return lax.ppermute(block, axis, [(i, i ^ bit) for i in range(lax.axis_size(axis))])


def per_device(object_field, probe, amplitudes, positions):
    planes, side, _ = object_field.shape
    length = probe.shape[1]
    margin = MARGIN
    reach = side + 2 * margin
    wide = side + LANES
    per = LANES // margin
    measured = amplitudes[0, 0]
    frames = measured.shape[0]
    steps = [(axis, 1 << k) for axis in ("col", "row") for k in range((lax.axis_size(axis) - 1).bit_length())]
    halvings = min(HALVINGS, len(steps), (length // SUBLANES - 1).bit_length())
    blocks = 1 << halvings
    rows = length // blocks
    row, col = lax.axis_index("row"), lax.axis_index("col")
    index = {"row": row, "col": col}
    block = jnp.zeros((), jnp.int32)
    for k, (axis, bit) in enumerate(steps[:halvings]):
        block += jnp.where(index[axis] & bit != 0, blocks >> (k + 1), 0).astype(jnp.int32)
    place = jnp.stack([block, (row * lax.axis_size("col") + col).astype(jnp.int32)])

    above = moved(object_field[:, side - margin :, :], "row", 1)
    below = moved(object_field[:, :margin, :], "row", -1)
    ordered, total = call(
        prepare_kernel,
        (shape(frames, 2 * length, length // 2), shape(SUBLANES, length)),
        operands=1,
        scratch=(pltpu.VMEM((frames, 2, length, length // 2), f32),),
        cost=pl.CostEstimate(flops=10**9, bytes_accessed=2 * measured.size * 4, transcendentals=0),
    )(measured)
    packed = shape(planes, reach // per, LANES)
    left, right = call(edge_kernel, (packed, packed), operands=3)(object_field, above, below)
    from_left = moved(right, "col", 1)
    from_right = moved(left, "col", -1)

    matrices, row_turn, column_turn = tables(length)
    half_rows = SUBLANES + 3 * length // 2
    low, canvas, high, kept, sent = call(
        functools.partial(frames_kernel, blocks),
        (
            shape(3, margin, wide),
            shape(3, side, wide),
            shape(3, margin, wide),
            shape(half_rows, length),
            shape(half_rows, length),
        ),
        scalars=2,
        operands=11,
        scratch=(
            pltpu.VMEM((2, reach + SUBLANES, wide), f32),
            pltpu.VMEM((3, reach + SUBLANES, wide), f32),
            pltpu.VMEM((3, length, length), f32),
        ),
    )(
        place,
        positions[0, 0],
        object_field,
        above,
        below,
        from_left,
        from_right,
        probe,
        ordered,
        total,
        jnp.asarray(matrices),
        jnp.asarray(row_turn),
        jnp.asarray(column_turn),
    )

    current = None
    for k, (axis, bit) in enumerate(steps):
        if k:
            if k < halvings:
                half = (current.shape[0] - SUBLANES) // 2
                kept = current[: SUBLANES + half]
                sent = jnp.concatenate([current[:SUBLANES], current[SUBLANES + half :]], 0)
            else:
                kept = sent = current
        current = kept + swapped(sent, axis, bit)
    total = current[:SUBLANES]
    weight = current[SUBLANES + 2 * rows :]
    stepped = current[SUBLANES : SUBLANES + 2 * rows] / jnp.concatenate([weight, weight], 0)
    for axis, bit in steps[:halvings][::-1]:
        stepped = jnp.concatenate([stepped, swapped(stepped, axis, bit)], 0)
    frame_count = frames * lax.axis_size("row") * lax.axis_size("col")
    probe_next = call(
        functools.partial(probe_kernel, frame_count, blocks),
        shape(*probe.shape),
        scalars=1,
        operands=2,
    )(place, stepped, total)

    above = moved(high, "row", 1)
    below = moved(low, "row", -1)
    packed = shape(3, side // per, LANES)
    left, right = call(fold_rows_kernel, (packed, packed), operands=3)(canvas, above, below)
    from_left = moved(right, "col", 1)
    from_right = moved(left, "col", -1)
    object_next = call(object_kernel, shape(*object_field.shape), operands=5)(
        canvas, above, below, from_left, from_right
    )
    return (object_next, probe_next)


def solution(mesh):
    return jax.shard_map(
        per_device,
        mesh=mesh,
        in_specs=(
            P(None, "row", "col"),
            P(),
            P("row", "col", None, None, None),
            P("row", "col", None, None),
        ),
        out_specs=(P(None, "row", "col"), P()),
        check_vma=False,
    )
```

```python
import functools
import math

import jax
import jax.numpy as jnp
import numpy as np
from jax import lax
from jax.experimental import pallas as pl
from jax.experimental.pallas import tpu as pltpu
from jax.sharding import PartitionSpec as P

MARGIN = 32
LANES = 128
SUBLANES = 8
HALVINGS = 3

smoothing = 0.1
regular = 1.0
epsilon = 1e-06

f32 = jnp.float32
bf16 = jnp.bfloat16


def tables(length):
    half = length // 2
    scaling = 1.0 / math.sqrt(length)
    k = np.arange(half)
    phases = (k[:, None] * k[None, :] % half) * (2.0 * math.pi / half)
    cosine, sine = np.cos(phases) * scaling, np.sin(phases) * scaling
    right = np.block([[cosine, -sine], [sine, cosine]])
    left = np.block([[cosine, sine], [-sine, cosine]])
    both = np.stack([left, right]).astype(np.float32)
    high = both.astype(bf16)
    low = (both - high.astype(np.float32)).astype(bf16)
    matrices = np.stack([high, low], 1)
    angle = k * (2.0 * math.pi / length)
    turn = np.stack([np.cos(angle), np.sin(angle)]).astype(np.float32)
    rows = np.broadcast_to(turn[:, :, None], (2, half, LANES)).copy()
    columns = np.broadcast_to(turn[:, None, :], (2, SUBLANES, half)).copy()
    return matrices, rows, columns


def split(x):
    high = x.astype(bf16)
    return high, (x - high.astype(f32)).astype(bf16)


def dot(a, b):
    return jnp.dot(a, b, preferred_element_type=f32)


def times_matrix(data, high, low):
    data_high, data_low = split(data)
    return dot(data_high, high) + (dot(data_low, high) + dot(data_high, low))


def matrix_times(high, low, data):
    data_high, data_low = split(data)
    return dot(high, data_high) + (dot(high, data_low) + dot(low, data_high))


def turned(real, imag, cosine, sine):
    return real * cosine - imag * sine, real * sine + imag * cosine


def pack(chunks, lane, width):
    place = lax.broadcasted_iota(jnp.int32, chunks[0].shape, 1) // width
    out = jnp.zeros_like(chunks[0])
    for q, chunk in enumerate(chunks):
        shift = (q * width - lane) % LANES
        moved = pltpu.roll(chunk, shift, 1) if shift else chunk
        out = jnp.where(place == q, moved, out)
    return out


def unpack(packed, q, lane, width):
    shift = (lane - q * width) % LANES
    moved = pltpu.roll(packed, shift, 1) if shift else packed
    place = lax.broadcasted_iota(jnp.int32, packed.shape, 1)
    return jnp.where((place >= lane) & (place < lane + width), moved, 0.0)


def prepare_kernel(amplitude, sorted_out, total_out, held):
    frames, length, _ = amplitude.shape
    half = length // 2
    row = lax.broadcasted_iota(jnp.int32, (length, length), 0)
    column = lax.broadcasted_iota(jnp.int32, (length, length), 1)
    source = jnp.where(column < half, 2 * column, 2 * (column - half) + 1)
    order = jnp.where(row == source, 1.0, 0.0).astype(bf16)
    total = jnp.zeros((SUBLANES, length), f32)
    for f in range(frames):
        values = amplitude[f]
        total += jnp.sum((values * values).reshape(length // SUBLANES, SUBLANES, length), 0)
        high = values.astype(bf16)
        rest = values - high.astype(f32)
        middle = rest.astype(bf16)
        low = (rest - middle.astype(f32)).astype(bf16)
        placed = dot(high, order) + (dot(middle, order) + dot(low, order))
        for parity in range(2):
            held[f, parity] = placed[:, parity * half : (parity + 1) * half]
            for start in range(2):
                at = 2 * parity + start
                sorted_out[f, at * half : (at + 1) * half, :] = held[
                    f, parity, pl.ds(start, half, stride=2), :
                ]
    total_out[...] = total


def edge_kernel(field, above, below, left_out, right_out):
    planes, side, _ = field.shape
    margin = above.shape[1]
    per = LANES // margin
    rows = (side + 2 * margin) // per
    for plane in range(planes):
        for out, tile, lane in (
            (left_out, 0, 0),
            (right_out, side // LANES - 1, LANES - margin),
        ):
            at = pl.ds(tile * LANES, LANES)
            whole = jnp.concatenate(
                [above[plane, :, at], field[plane, :, at], below[plane, :, at]], 0
            )
            chunks = [whole[q * rows : (q + 1) * rows] for q in range(per)]
            out[plane] = pack(chunks, lane, margin)


def frames_kernel(
    blocks,
    place,
    offsets,
    field,
    above,
    below,
    from_left,
    from_right,
    probe,
    amplitude,
    total,
    matrices,
    row_turn,
    column_turn,
    canvas_low,
    canvas,
    canvas_high,
    kept,
    sent,
    padded,
    work,
    sums,
):
    frames = amplitude.shape[0]
    length = probe.shape[1]
    half = length // 2
    side = field.shape[1]
    margin = above.shape[1]
    reach = side + 2 * margin
    wide = side + LANES
    taller = length + SUBLANES
    per = LANES // margin
    chunk = reach // per

    for plane in range(2):
        padded[plane, :margin, :side] = above[plane]
        padded[plane, margin : margin + side, :side] = field[plane]
        padded[plane, margin + side : reach, :side] = below[plane]
        for q in range(per):
            padded[plane, q * chunk : (q + 1) * chunk, side:] = unpack(
                from_right[plane], q, 0, margin
            ) + unpack(from_left[plane], q, LANES - margin, margin)
        padded[plane, reach:, :] = jnp.zeros((SUBLANES, wide), f32)
        work[plane] = jnp.zeros((reach + SUBLANES, wide), f32)
        work[plane, margin : margin + side, :side] = field[plane]
    work[2] = jnp.zeros((reach + SUBLANES, wide), f32)
    work[2, margin : margin + side, :side] = jnp.full((side, side), regular, f32)
    first = jnp.where(place[1] == 0, 1.0, 0.0).astype(f32)
    sums[0] = probe[0] * first
    sums[1] = probe[1] * first
    sums[2] = jnp.full((length, length), regular, f32) * first

    left_high, left_low = matrices[0, 0], matrices[0, 1]
    right_high, right_low = matrices[1, 0], matrices[1, 1]
    row_cos = jnp.concatenate([row_turn[0]] * (length // LANES), 1)
    row_sin = jnp.concatenate([row_turn[1]] * (length // LANES), 1)
    column_cos = column_turn[0, 0:1, :]
    column_sin = column_turn[1, 0:1, :]

    def visit(f, carry):
        a = offsets[f, 0]
        b = offsets[f, 1]
        shift = lax.rem(a, SUBLANES)
        at = pl.ds(pl.multiple_of(a - shift, SUBLANES), taller)
        back = lax.rem(wide + margin - b, wide)
        ahead = lax.rem(wide - margin + b, wide)
        probe_real, probe_imag = probe[0], probe[1]
        window_real, window_imag = (
            pltpu.roll(
                pltpu.roll(padded[plane, at, :], back, 1)[:, :length],
                lax.rem(taller - shift, taller),
                0,
            )[:length]
            for plane in range(2)
        )
        wave_real = probe_real * window_real - probe_imag * window_imag
        wave_imag = probe_real * window_imag + probe_imag * window_real

        even_real = wave_real[:half] + wave_real[half:]
        even_imag = wave_imag[:half] + wave_imag[half:]
        odd_real, odd_imag = turned(
            wave_real[:half] - wave_real[half:],
            wave_imag[:half] - wave_imag[half:],
            row_cos,
            -row_sin,
        )
        stacked = jnp.concatenate(
            [
                jnp.concatenate([even_real, even_imag], 0),
                jnp.concatenate([odd_real, odd_imag], 0),
            ],
            1,
        )
        mixed = matrix_times(left_high, left_low, stacked)
        evens, odds = [], []
        for parity in range(2):
            part = mixed[:, parity * length : (parity + 1) * length]
            real, imag = part[:half], part[half:]
            evens.append(
                jnp.concatenate([real[:, :half] + real[:, half:], imag[:, :half] + imag[:, half:]], 1)
            )
            odds.append(
                jnp.concatenate(
                    turned(
                        real[:, :half] - real[:, half:],
                        imag[:, :half] - imag[:, half:],
                        column_cos,
                        -column_sin,
                    ),
                    1,
                )
            )
        far = times_matrix(jnp.concatenate(evens + odds, 0), right_high, right_low)
        far_real, far_imag = far[:, :half], far[:, half:]
        factor = amplitude[f] * lax.rsqrt(far_real * far_real + far_imag * far_imag + smoothing)
        corrected = jnp.concatenate([far_real * factor, far_imag * factor], 1)

        back_far = times_matrix(corrected, left_high, left_low)
        even, odd = back_far[:length], back_far[length:]
        odd_real, odd_imag = turned(odd[:, :half], odd[:, half:], column_cos, column_sin)
        even_real, even_imag = even[:, :half], even[:, half:]
        real = jnp.concatenate([even_real + odd_real, even_real - odd_real], 1)
        imag = jnp.concatenate([even_imag + odd_imag, even_imag - odd_imag], 1)
        stacked = jnp.concatenate(
            [
                jnp.concatenate([real[:half], imag[:half]], 0),
                jnp.concatenate([real[half:], imag[half:]], 0),
            ],
            1,
        )
        near = matrix_times(right_high, right_low, stacked)
        even, odd = near[:, :length], near[:, length:]
        odd_real, odd_imag = turned(odd[:half], odd[half:], row_cos, row_sin)
        near_real = jnp.concatenate([even[:half] + odd_real, even[:half] - odd_real], 0)
        near_imag = jnp.concatenate([even[half:] + odd_imag, even[half:] - odd_imag], 0)

        sums[0] += window_real * near_real + window_imag * near_imag
        sums[1] += window_real * near_imag - window_imag * near_real
        sums[2] += window_real * window_real + window_imag * window_imag
        under = jnp.zeros((SUBLANES, length), f32)
        beside = jnp.zeros((taller, wide - length), f32)
        terms = (
            probe_real * near_real + probe_imag * near_imag,
            probe_real * near_imag - probe_imag * near_real,
            probe_real * probe_real + probe_imag * probe_imag,
        )
        for plane, term in enumerate(terms):
            lowered = pltpu.roll(jnp.concatenate([term, under], 0), shift, 0)
            work[plane, at, :] += pltpu.roll(jnp.concatenate([lowered, beside], 1), ahead, 1)
        return carry

    lax.fori_loop(0, frames, visit, 0)

    canvas_low[...] = work[:, :margin, :]
    canvas[...] = work[:, margin : margin + side, :]
    canvas_high[...] = work[:, margin + side : reach, :]

    kept[:SUBLANES] = total[...]
    sent[:SUBLANES] = total[...]
    rows = length // blocks
    for p in range(blocks):
        source = pl.multiple_of((place[0] ^ p) * rows, rows)
        out, q = (kept, p) if p < blocks // 2 else (sent, p - blocks // 2)
        for plane in range(3):
            start = SUBLANES + (3 * q + plane) * rows
            out[start : start + rows] = sums[plane, pl.ds(source, rows), :]


def fold_rows_kernel(canvas, above, below, left_out, right_out):
    planes, side, _ = canvas.shape
    margin = above.shape[1]
    per = LANES // margin
    rows = side // per
    at = pl.ds(side, LANES)
    for plane in range(planes):
        whole = jnp.concatenate(
            [
                canvas[plane, :margin, at] + above[plane, :, at],
                canvas[plane, margin : side - margin, at],
                canvas[plane, side - margin :, at] + below[plane, :, at],
            ],
            0,
        )
        chunks = [whole[q * rows : (q + 1) * rows] for q in range(per)]
        left_out[plane] = pack(chunks, LANES - margin, margin)
        right_out[plane] = pack(chunks, 0, margin)


def object_kernel(canvas, above, below, from_left, from_right, out):
    planes, side, _ = canvas.shape
    margin = above.shape[1]
    per = LANES // margin
    rows = side // per
    total = []
    for plane in range(planes):
        whole = jnp.concatenate(
            [
                canvas[plane, :margin, :side] + above[plane, :, :side],
                canvas[plane, margin : side - margin, :side],
                canvas[plane, side - margin :, :side] + below[plane, :, :side],
            ],
            0,
        )
        low = jnp.concatenate([unpack(from_left[plane], q, 0, margin) for q in range(per)], 0)
        high = jnp.concatenate(
            [unpack(from_right[plane], q, LANES - margin, margin) for q in range(per)], 0
        )
        middle = [whole[:, LANES : side - LANES]] if side > 2 * LANES else []
        total.append(
            jnp.concatenate(
                [whole[:, :LANES] + low] + middle + [whole[:, side - LANES :] + high], 1
            )
        )
    weight = 1.0 / total[2]
    out[0] = total[0] * weight
    out[1] = total[1] * weight


def probe_kernel(frame_count, blocks, place, stepped, total, out):
    planes, length, _ = out.shape
    rows = length // blocks
    values = stepped[...]
    power = jnp.sum(values * values)
    target = jnp.sum(total[...]) / frame_count
    scale = jnp.sqrt(jnp.full((rows, length), target / (power + epsilon), f32))
    for p in range(blocks):
        home = pl.multiple_of((place[0] ^ p) * rows, rows)
        for plane in range(planes):
            start = (planes * p + plane) * rows
            out[plane, pl.ds(home, rows), :] = values[start : start + rows] * scale


def shape(*dims):
    return jax.ShapeDtypeStruct(dims, f32)


def call(kernel, outputs, scalars=0, operands=0, scratch=(), cost=None):
    vmem = pl.BlockSpec(memory_space=pltpu.VMEM)
    smem = pl.BlockSpec(memory_space=pltpu.SMEM)
    return pl.pallas_call(
        kernel,
        out_shape=outputs,
        in_specs=[smem] * scalars + [vmem] * operands,
        out_specs=jax.tree.map(lambda _: vmem, outputs),
        scratch_shapes=list(scratch),
        cost_estimate=cost,
        compiler_params=pltpu.CompilerParams(vmem_limit_bytes=40 * 1024 * 1024),
    )


def moved(block, axis, distance):
    devices = range(lax.axis_size(axis))
    return lax.ppermute(
        block, axis, [(i - distance, i) for i in devices if i - distance in devices]
    )


def swapped(block, axis, bit):
    return lax.ppermute(block, axis, [(i, i ^ bit) for i in range(lax.axis_size(axis))])


def per_device(object_field, probe, amplitudes, positions):
    planes, side, _ = object_field.shape
    length = probe.shape[1]
    margin = MARGIN
    reach = side + 2 * margin
    wide = side + LANES
    per = LANES // margin
    measured = amplitudes[0, 0]
    frames = measured.shape[0]
    steps = [(axis, 1 << k) for axis in ("col", "row") for k in range((lax.axis_size(axis) - 1).bit_length())]
    halvings = min(HALVINGS, len(steps), (length // SUBLANES - 1).bit_length())
    blocks = 1 << halvings
    rows = length // blocks
    row, col = lax.axis_index("row"), lax.axis_index("col")
    index = {"row": row, "col": col}
    block = jnp.zeros((), jnp.int32)
    for k, (axis, bit) in enumerate(steps[:halvings]):
        block += jnp.where(index[axis] & bit != 0, blocks >> (k + 1), 0).astype(jnp.int32)
    place = jnp.stack([block, (row * lax.axis_size("col") + col).astype(jnp.int32)])

    above = moved(object_field[:, side - margin :, :], "row", 1)
    below = moved(object_field[:, :margin, :], "row", -1)
    ordered, total = call(
        prepare_kernel,
        (shape(frames, 2 * length, length // 2), shape(SUBLANES, length)),
        operands=1,
        scratch=(pltpu.VMEM((frames, 2, length, length // 2), f32),),
        cost=pl.CostEstimate(flops=10**9, bytes_accessed=2 * measured.size * 4, transcendentals=0),
    )(measured)
    packed = shape(planes, reach // per, LANES)
    left, right = call(edge_kernel, (packed, packed), operands=3)(object_field, above, below)
    from_left = moved(right, "col", 1)
    from_right = moved(left, "col", -1)

    matrices, row_turn, column_turn = tables(length)
    half_rows = SUBLANES + 3 * length // 2
    low, canvas, high, kept, sent = call(
        functools.partial(frames_kernel, blocks),
        (
            shape(3, margin, wide),
            shape(3, side, wide),
            shape(3, margin, wide),
            shape(half_rows, length),
            shape(half_rows, length),
        ),
        scalars=2,
        operands=11,
        scratch=(
            pltpu.VMEM((2, reach + SUBLANES, wide), f32),
            pltpu.VMEM((3, reach + SUBLANES, wide), f32),
            pltpu.VMEM((3, length, length), f32),
        ),
    )(
        place,
        positions[0, 0],
        object_field,
        above,
        below,
        from_left,
        from_right,
        probe,
        ordered,
        total,
        jnp.asarray(matrices),
        jnp.asarray(row_turn),
        jnp.asarray(column_turn),
    )

    above = moved(high, "row", 1)
    below = moved(low, "row", -1)
    current = None
    for k, (axis, bit) in enumerate(steps):
        if k:
            if k < halvings:
                half = (current.shape[0] - SUBLANES) // 2
                kept = current[: SUBLANES + half]
                sent = jnp.concatenate([current[:SUBLANES], current[SUBLANES + half :]], 0)
            else:
                kept = sent = current
        if k == 2:
            sent, above, below = lax.optimization_barrier((sent, above, below))
            packed = shape(3, side // per, LANES)
            left, right = call(fold_rows_kernel, (packed, packed), operands=3)(canvas, above, below)
            from_left = moved(right, "col", 1)
            from_right = moved(left, "col", -1)
        if k == 4:
            sent, from_left, from_right = lax.optimization_barrier((sent, from_left, from_right))
        current = kept + swapped(sent, axis, bit)
    object_next = call(object_kernel, shape(*object_field.shape), operands=5)(
        canvas, above, below, from_left, from_right
    )
    total = current[:SUBLANES]
    weight = current[SUBLANES + 2 * rows :]
    stepped = current[SUBLANES : SUBLANES + 2 * rows] / jnp.concatenate([weight, weight], 0)
    for axis, bit in steps[:halvings][::-1]:
        stepped = jnp.concatenate([stepped, swapped(stepped, axis, bit)], 0)
    frame_count = frames * lax.axis_size("row") * lax.axis_size("col")
    probe_next = call(
        functools.partial(probe_kernel, frame_count, blocks),
        shape(*probe.shape),
        scalars=1,
        operands=2,
    )(place, stepped, total)
    return (object_next, probe_next)


def solution(mesh):
    return jax.shard_map(
        per_device,
        mesh=mesh,
        in_specs=(
            P(None, "row", "col"),
            P(),
            P("row", "col", None, None, None),
            P("row", "col", None, None),
        ),
        out_specs=(P(None, "row", "col"), P()),
        check_vma=False,
    )
```

```python
import functools
import math

import jax
import jax.numpy as jnp
import numpy as np
from jax import lax
from jax.experimental import pallas as pl
from jax.experimental.pallas import tpu as pltpu
from jax.sharding import PartitionSpec as P

MARGIN = 32
LANES = 128
SUBLANES = 8

smoothing = 0.1
regular = 1.0
epsilon = 1e-06

f32 = jnp.float32
bf16 = jnp.bfloat16


def tables(length):
    half = length // 2
    scaling = 1.0 / math.sqrt(length)
    k = np.arange(half)
    phases = (k[:, None] * k[None, :] % half) * (2.0 * math.pi / half)
    cosine, sine = np.cos(phases) * scaling, np.sin(phases) * scaling
    right = np.block([[cosine, -sine], [sine, cosine]])
    left = np.block([[cosine, sine], [-sine, cosine]])
    both = np.stack([left, right]).astype(np.float32)
    high = both.astype(bf16)
    low = (both - high.astype(np.float32)).astype(bf16)
    matrices = np.stack([high, low], 1)
    angle = k * (2.0 * math.pi / length)
    turn = np.stack([np.cos(angle), np.sin(angle)]).astype(np.float32)
    rows = np.broadcast_to(turn[:, :, None], (2, half, LANES)).copy()
    columns = np.broadcast_to(turn[:, None, :], (2, SUBLANES, half)).copy()
    return matrices, rows, columns


def split(x):
    high = x.astype(bf16)
    return high, (x - high.astype(f32)).astype(bf16)


def dot(a, b):
    return jnp.dot(a, b, preferred_element_type=f32)


def times_matrix(data, high, low):
    data_high, data_low = split(data)
    return dot(data_high, high) + (dot(data_low, high) + dot(data_high, low))


def matrix_times(high, low, data):
    data_high, data_low = split(data)
    return dot(high, data_high) + (dot(high, data_low) + dot(low, data_high))


def turned(real, imag, cosine, sine):
    return real * cosine - imag * sine, real * sine + imag * cosine


def pack(chunks, lane, width):
    place = lax.broadcasted_iota(jnp.int32, chunks[0].shape, 1) // width
    out = jnp.zeros_like(chunks[0])
    for q, chunk in enumerate(chunks):
        shift = (q * width - lane) % LANES
        moved = pltpu.roll(chunk, shift, 1) if shift else chunk
        out = jnp.where(place == q, moved, out)
    return out


def unpack(packed, q, lane, width):
    shift = (lane - q * width) % LANES
    moved = pltpu.roll(packed, shift, 1) if shift else packed
    place = lax.broadcasted_iota(jnp.int32, packed.shape, 1)
    return jnp.where((place >= lane) & (place < lane + width), moved, 0.0)


def prepare_kernel(amplitude, sorted_out, total_out, held):
    frames, length, _ = amplitude.shape
    half = length // 2
    row = lax.broadcasted_iota(jnp.int32, (length, length), 0)
    column = lax.broadcasted_iota(jnp.int32, (length, length), 1)
    source = jnp.where(column < half, 2 * column, 2 * (column - half) + 1)
    order = jnp.where(row == source, 1.0, 0.0).astype(bf16)
    total = jnp.zeros((SUBLANES, length), f32)
    for f in range(frames):
        values = amplitude[f]
        total += jnp.sum((values * values).reshape(length // SUBLANES, SUBLANES, length), 0)
        high = values.astype(bf16)
        rest = values - high.astype(f32)
        middle = rest.astype(bf16)
        low = (rest - middle.astype(f32)).astype(bf16)
        placed = dot(high, order) + (dot(middle, order) + dot(low, order))
        for parity in range(2):
            held[f, parity] = placed[:, parity * half : (parity + 1) * half]
            for start in range(2):
                at = 2 * parity + start
                sorted_out[f, at * half : (at + 1) * half, :] = held[
                    f, parity, pl.ds(start, half, stride=2), :
                ]
    total_out[...] = sum(total[:, t * LANES : (t + 1) * LANES] for t in range(length // LANES))


def edge_kernel(field, above, below, left_out, right_out):
    planes, side, _ = field.shape
    margin = above.shape[1]
    per = LANES // margin
    rows = (side + 2 * margin) // per
    for plane in range(planes):
        for out, tile, lane in (
            (left_out, 0, 0),
            (right_out, side // LANES - 1, LANES - margin),
        ):
            at = pl.ds(tile * LANES, LANES)
            whole = jnp.concatenate(
                [above[plane, :, at], field[plane, :, at], below[plane, :, at]], 0
            )
            chunks = [whole[q * rows : (q + 1) * rows] for q in range(per)]
            out[plane] = pack(chunks, lane, margin)


def frames_kernel(
    groups,
    pieces,
    place,
    offsets,
    field,
    above,
    below,
    from_left,
    from_right,
    probe,
    amplitude,
    total,
    matrices,
    row_turn,
    column_turn,
    canvas_low,
    canvas,
    canvas_high,
    kept,
    sent,
    padded,
    work,
    sums,
):
    frames = amplitude.shape[0]
    length = probe.shape[1]
    half = length // 2
    side = field.shape[1]
    margin = above.shape[1]
    reach = side + 2 * margin
    wide = side + LANES
    taller = length + SUBLANES
    per = LANES // margin
    chunk = reach // per

    for plane in range(2):
        padded[plane, :margin, :side] = above[plane]
        padded[plane, margin : margin + side, :side] = field[plane]
        padded[plane, margin + side : reach, :side] = below[plane]
        for q in range(per):
            padded[plane, q * chunk : (q + 1) * chunk, side:] = unpack(
                from_right[plane], q, 0, margin
            ) + unpack(from_left[plane], q, LANES - margin, margin)
        padded[plane, reach:, :] = jnp.zeros((SUBLANES, wide), f32)
        work[plane] = jnp.zeros((reach + SUBLANES, wide), f32)
        work[plane, margin : margin + side, :side] = field[plane]
    work[2] = jnp.zeros((reach + SUBLANES, wide), f32)
    work[2, margin : margin + side, :side] = jnp.full((side, side), regular, f32)
    first = jnp.where(place[1] == 0, 1.0, 0.0).astype(f32)
    sums[0] = probe[0] * first
    sums[1] = probe[1] * first
    sums[2] = jnp.full((length, length), regular, f32) * first

    left_high, left_low = matrices[0, 0], matrices[0, 1]
    right_high, right_low = matrices[1, 0], matrices[1, 1]
    row_cos = jnp.concatenate([row_turn[0]] * (length // LANES), 1)
    row_sin = jnp.concatenate([row_turn[1]] * (length // LANES), 1)
    column_cos = column_turn[0, 0:1, :]
    column_sin = column_turn[1, 0:1, :]

    def visit(f, carry):
        a = offsets[f, 0]
        b = offsets[f, 1]
        shift = lax.rem(a, SUBLANES)
        at = pl.ds(pl.multiple_of(a - shift, SUBLANES), taller)
        back = lax.rem(wide + margin - b, wide)
        ahead = lax.rem(wide - margin + b, wide)
        probe_real, probe_imag = probe[0], probe[1]
        window_real, window_imag = (
            pltpu.roll(
                pltpu.roll(padded[plane, at, :], back, 1)[:, :length],
                lax.rem(taller - shift, taller),
                0,
            )[:length]
            for plane in range(2)
        )
        wave_real = probe_real * window_real - probe_imag * window_imag
        wave_imag = probe_real * window_imag + probe_imag * window_real

        even_real = wave_real[:half] + wave_real[half:]
        even_imag = wave_imag[:half] + wave_imag[half:]
        odd_real, odd_imag = turned(
            wave_real[:half] - wave_real[half:],
            wave_imag[:half] - wave_imag[half:],
            row_cos,
            -row_sin,
        )
        stacked = jnp.concatenate(
            [
                jnp.concatenate([even_real, even_imag], 0),
                jnp.concatenate([odd_real, odd_imag], 0),
            ],
            1,
        )
        mixed = matrix_times(left_high, left_low, stacked)
        evens, odds = [], []
        for parity in range(2):
            part = mixed[:, parity * length : (parity + 1) * length]
            real, imag = part[:half], part[half:]
            evens.append(
                jnp.concatenate([real[:, :half] + real[:, half:], imag[:, :half] + imag[:, half:]], 1)
            )
            odds.append(
                jnp.concatenate(
                    turned(
                        real[:, :half] - real[:, half:],
                        imag[:, :half] - imag[:, half:],
                        column_cos,
                        -column_sin,
                    ),
                    1,
                )
            )
        far = times_matrix(jnp.concatenate(evens + odds, 0), right_high, right_low)
        far_real, far_imag = far[:, :half], far[:, half:]
        factor = amplitude[f] * lax.rsqrt(far_real * far_real + far_imag * far_imag + smoothing)
        corrected = jnp.concatenate([far_real * factor, far_imag * factor], 1)

        back_far = times_matrix(corrected, left_high, left_low)
        even, odd = back_far[:length], back_far[length:]
        odd_real, odd_imag = turned(odd[:, :half], odd[:, half:], column_cos, column_sin)
        even_real, even_imag = even[:, :half], even[:, half:]
        real = jnp.concatenate([even_real + odd_real, even_real - odd_real], 1)
        imag = jnp.concatenate([even_imag + odd_imag, even_imag - odd_imag], 1)
        stacked = jnp.concatenate(
            [
                jnp.concatenate([real[:half], imag[:half]], 0),
                jnp.concatenate([real[half:], imag[half:]], 0),
            ],
            1,
        )
        near = matrix_times(right_high, right_low, stacked)
        even, odd = near[:, :length], near[:, length:]
        odd_real, odd_imag = turned(odd[:half], odd[half:], row_cos, row_sin)
        near_real = jnp.concatenate([even[:half] + odd_real, even[:half] - odd_real], 0)
        near_imag = jnp.concatenate([even[half:] + odd_imag, even[half:] - odd_imag], 0)

        sums[0] += window_real * near_real + window_imag * near_imag
        sums[1] += window_real * near_imag - window_imag * near_real
        sums[2] += window_real * window_real + window_imag * window_imag
        under = jnp.zeros((SUBLANES, length), f32)
        beside = jnp.zeros((taller, wide - length), f32)
        terms = (
            probe_real * near_real + probe_imag * near_imag,
            probe_real * near_imag - probe_imag * near_real,
            probe_real * probe_real + probe_imag * probe_imag,
        )
        for plane, term in enumerate(terms):
            lowered = pltpu.roll(jnp.concatenate([term, under], 0), shift, 0)
            work[plane, at, :] += pltpu.roll(jnp.concatenate([lowered, beside], 1), ahead, 1)
        return carry

    lax.fori_loop(0, frames, visit, 0)

    canvas_low[...] = work[:, :margin, :]
    canvas[...] = work[:, margin : margin + side, :]
    canvas_high[...] = work[:, margin + side : reach, :]

    tiles = length // LANES
    rows = length // (groups * pieces)
    for p in range(groups):
        out, at = (kept, p) if p < groups // 2 else (sent, p - groups // 2)
        for piece in range(pieces):
            q = at * pieces + piece
            source = pl.multiple_of(((place[0] ^ p) * pieces + piece) * rows, rows)
            out[q, 3 * tiles * rows :, :] = total[...]
            for plane in range(3):
                for tile in range(tiles):
                    start = (plane * tiles + tile) * rows
                    out[q, start : start + rows, :] = sums[
                        plane, pl.ds(source, rows), pl.ds(tile * LANES, LANES)
                    ]


def fold_rows_kernel(canvas, above, below, left_out, right_out):
    planes, side, _ = canvas.shape
    margin = above.shape[1]
    per = LANES // margin
    rows = side // per
    at = pl.ds(side, LANES)
    for plane in range(planes):
        whole = jnp.concatenate(
            [
                canvas[plane, :margin, at] + above[plane, :, at],
                canvas[plane, margin : side - margin, at],
                canvas[plane, side - margin :, at] + below[plane, :, at],
            ],
            0,
        )
        chunks = [whole[q * rows : (q + 1) * rows] for q in range(per)]
        left_out[plane] = pack(chunks, LANES - margin, margin)
        right_out[plane] = pack(chunks, 0, margin)


def object_kernel(canvas, above, below, from_left, from_right, out):
    planes, side, _ = canvas.shape
    margin = above.shape[1]
    per = LANES // margin
    rows = side // per
    total = []
    for plane in range(planes):
        whole = jnp.concatenate(
            [
                canvas[plane, :margin, :side] + above[plane, :, :side],
                canvas[plane, margin : side - margin, :side],
                canvas[plane, side - margin :, :side] + below[plane, :, :side],
            ],
            0,
        )
        low = jnp.concatenate([unpack(from_left[plane], q, 0, margin) for q in range(per)], 0)
        high = jnp.concatenate(
            [unpack(from_right[plane], q, LANES - margin, margin) for q in range(per)], 0
        )
        middle = [whole[:, LANES : side - LANES]] if side > 2 * LANES else []
        total.append(
            jnp.concatenate(
                [whole[:, :LANES] + low] + middle + [whole[:, side - LANES :] + high], 1
            )
        )
    weight = 1.0 / total[2]
    out[0] = total[0] * weight
    out[1] = total[1] * weight


def probe_kernel(frame_count, place, stepped, total, out):
    planes, length, _ = out.shape
    groups, pieces, depth, _ = stepped.shape
    tiles = length // LANES
    rows = depth // (planes * tiles)
    values = stepped[...]
    power = jnp.sum(values * values)
    target = jnp.sum(total[...]) / frame_count
    scale = jnp.sqrt(jnp.full((rows, LANES), target / (power + epsilon), f32))
    for p in range(groups):
        for piece in range(pieces):
            home = pl.multiple_of(((place[0] ^ p) * pieces + piece) * rows, rows)
            for plane in range(planes):
                for tile in range(tiles):
                    start = (plane * tiles + tile) * rows
                    out[plane, pl.ds(home, rows), pl.ds(tile * LANES, LANES)] = (
                        values[p, piece, start : start + rows] * scale
                    )


def shape(*dims):
    return jax.ShapeDtypeStruct(dims, f32)


def call(kernel, outputs, scalars=0, operands=0, scratch=(), cost=None):
    vmem = pl.BlockSpec(memory_space=pltpu.VMEM)
    smem = pl.BlockSpec(memory_space=pltpu.SMEM)
    return pl.pallas_call(
        kernel,
        out_shape=outputs,
        in_specs=[smem] * scalars + [vmem] * operands,
        out_specs=jax.tree.map(lambda _: vmem, outputs),
        scratch_shapes=list(scratch),
        cost_estimate=cost,
        compiler_params=pltpu.CompilerParams(vmem_limit_bytes=40 * 1024 * 1024),
    )


def moved(block, axis, distance):
    devices = range(lax.axis_size(axis))
    return lax.ppermute(
        block, axis, [(i - distance, i) for i in devices if i - distance in devices]
    )


def swapped(block, axis, bit):
    return lax.ppermute(block, axis, [(i, i ^ bit) for i in range(lax.axis_size(axis))])


def per_device(object_field, probe, amplitudes, positions):
    planes, side, _ = object_field.shape
    length = probe.shape[1]
    margin = MARGIN
    reach = side + 2 * margin
    wide = side + LANES
    per = LANES // margin
    measured = amplitudes[0, 0]
    frames = measured.shape[0]
    pieces = lax.axis_size("row")
    steps = [1 << k for k in range((lax.axis_size("col") - 1).bit_length())]
    halvings = min(len(steps), (length // (SUBLANES * pieces)).bit_length() - 1)
    groups = 1 << halvings
    rows = length // (groups * pieces)
    row, col = lax.axis_index("row"), lax.axis_index("col")
    group = jnp.zeros((), jnp.int32)
    for k, bit in enumerate(steps[:halvings]):
        group += jnp.where(col & bit != 0, groups >> (k + 1), 0).astype(jnp.int32)
    place = jnp.stack([group, (row * lax.axis_size("col") + col).astype(jnp.int32)])

    above = moved(object_field[:, side - margin :, :], "row", 1)
    below = moved(object_field[:, :margin, :], "row", -1)
    ordered, total = call(
        prepare_kernel,
        (shape(frames, 2 * length, length // 2), shape(SUBLANES, LANES)),
        operands=1,
        scratch=(pltpu.VMEM((frames, 2, length, length // 2), f32),),
        cost=pl.CostEstimate(flops=10**9, bytes_accessed=2 * measured.size * 4, transcendentals=0),
    )(measured)
    packed = shape(planes, reach // per, LANES)
    left, right = call(edge_kernel, (packed, packed), operands=3)(object_field, above, below)
    from_left = moved(right, "col", 1)
    from_right = moved(left, "col", -1)

    matrices, row_turn, column_turn = tables(length)
    tiles = length // LANES
    half_shape = shape(groups // 2 * pieces, 3 * tiles * rows + SUBLANES, LANES)
    low, canvas, high, kept, sent = call(
        functools.partial(frames_kernel, groups, pieces),
        (
            shape(3, margin, wide),
            shape(3, side, wide),
            shape(3, margin, wide),
            half_shape,
            half_shape,
        ),
        scalars=2,
        operands=11,
        scratch=(
            pltpu.VMEM((2, reach + SUBLANES, wide), f32),
            pltpu.VMEM((3, reach + SUBLANES, wide), f32),
            pltpu.VMEM((3, length, length), f32),
        ),
    )(
        place,
        positions[0, 0],
        object_field,
        above,
        below,
        from_left,
        from_right,
        probe,
        ordered,
        total,
        jnp.asarray(matrices),
        jnp.asarray(row_turn),
        jnp.asarray(column_turn),
    )

    above = moved(high, "row", 1)
    below = moved(low, "row", -1)
    current = kept + swapped(sent, "col", steps[0])
    for k, bit in enumerate(steps[1:], 1):
        if k < halvings:
            half = current.shape[0] // 2
            kept, sent = current[:half], current[half:]
        else:
            kept = sent = current
        current = kept + swapped(sent, "col", bit)
    current, above, below = lax.optimization_barrier((current, above, below))
    packed = shape(3, side // per, LANES)
    left, right = call(fold_rows_kernel, (packed, packed), operands=3)(canvas, above, below)
    from_left = moved(right, "col", 1)
    from_right = moved(left, "col", -1)
    current = jnp.sum(lax.all_to_all(current, "row", 0, 0), 0)
    total = current[3 * tiles * rows :]
    weight = current[2 * tiles * rows : 3 * tiles * rows]
    stepped = current[: 2 * tiles * rows] / jnp.concatenate([weight, weight], 0)
    stepped = lax.all_to_all(jnp.broadcast_to(stepped[None], (pieces, *stepped.shape)), "row", 0, 0)
    stepped, from_left, from_right = lax.optimization_barrier((stepped, from_left, from_right))
    object_next = call(object_kernel, shape(*object_field.shape), operands=5)(
        canvas, above, below, from_left, from_right
    )
    stepped = stepped[None]
    for bit in steps[:halvings][::-1]:
        stepped = jnp.concatenate([stepped, swapped(stepped, "col", bit)], 0)
    frame_count = frames * lax.axis_size("row") * lax.axis_size("col")
    probe_next = call(
        functools.partial(probe_kernel, frame_count),
        shape(*probe.shape),
        scalars=1,
        operands=2,
    )(place, stepped, total)
    return (object_next, probe_next)


def solution(mesh):
    return jax.shard_map(
        per_device,
        mesh=mesh,
        in_specs=(
            P(None, "row", "col"),
            P(),
            P("row", "col", None, None, None),
            P("row", "col", None, None),
        ),
        out_specs=(P(None, "row", "col"), P()),
        check_vma=False,
    )
```

```python
import functools
import math

import jax
import jax.numpy as jnp
import numpy as np
from jax import lax
from jax.experimental import pallas as pl
from jax.experimental.pallas import tpu as pltpu
from jax.sharding import PartitionSpec as P

MARGIN = 32
LANES = 128
SUBLANES = 8

smoothing = 0.1
regular = 1.0
epsilon = 1e-06

f32 = jnp.float32
bf16 = jnp.bfloat16


def tables(length):
    half = length // 2
    scaling = 1.0 / math.sqrt(length)
    k = np.arange(half)
    phases = (k[:, None] * k[None, :] % half) * (2.0 * math.pi / half)
    cosine, sine = np.cos(phases) * scaling, np.sin(phases) * scaling
    right = np.block([[cosine, -sine], [sine, cosine]])
    left = np.block([[cosine, sine], [-sine, cosine]])
    both = np.stack([left, right]).astype(np.float32)
    high = both.astype(bf16)
    low = (both - high.astype(np.float32)).astype(bf16)
    matrices = np.stack([high, low], 1)
    angle = k * (2.0 * math.pi / length)
    turn = np.stack([np.cos(angle), np.sin(angle)]).astype(np.float32)
    rows = np.broadcast_to(turn[:, :, None], (2, half, LANES)).copy()
    columns = np.broadcast_to(turn[:, None, :], (2, SUBLANES, half)).copy()
    return matrices, rows, columns


def split(x):
    high = x.astype(bf16)
    return high, (x - high.astype(f32)).astype(bf16)


def dot(a, b):
    return jnp.dot(a, b, preferred_element_type=f32)


def times_matrix(data, high, low):
    data_high, data_low = split(data)
    return dot(data_high, high) + (dot(data_low, high) + dot(data_high, low))


def matrix_times(high, low, data):
    data_high, data_low = split(data)
    return dot(high, data_high) + (dot(high, data_low) + dot(low, data_high))


def turned(real, imag, cosine, sine):
    return real * cosine - imag * sine, real * sine + imag * cosine


def pack(chunks, lane, width):
    place = lax.broadcasted_iota(jnp.int32, chunks[0].shape, 1) // width
    out = jnp.zeros_like(chunks[0])
    for q, chunk in enumerate(chunks):
        shift = (q * width - lane) % LANES
        moved = pltpu.roll(chunk, shift, 1) if shift else chunk
        out = jnp.where(place == q, moved, out)
    return out


def pack_rows(rows, lane, width):
    count = rows.shape[0] * width // LANES
    return pack([rows[q : q + count] for q in range(0, rows.shape[0], count)], lane, width)


def unpack(packed, q, lane, width):
    shift = (lane - q * width) % LANES
    moved = pltpu.roll(packed, shift, 1) if shift else packed
    place = lax.broadcasted_iota(jnp.int32, packed.shape, 1)
    return jnp.where((place >= lane) & (place < lane + width), moved, 0.0)


def unpack_rows(packed, lane, width):
    return jnp.concatenate([unpack(packed, q, lane, width) for q in range(LANES // width)], 0)


def prepare_kernel(amplitude, field, sorted_out, total_out, left_out, right_out, held):
    frames, length, _ = amplitude.shape
    half = length // 2
    planes, side, _ = field.shape
    margin = MARGIN
    for out, tile, lane in ((left_out, 0, 0), (right_out, side // LANES - 1, LANES - margin)):
        for plane in range(planes):
            out[plane] = pack_rows(field[plane, :, pl.ds(tile * LANES, LANES)], lane, margin)
    row = lax.broadcasted_iota(jnp.int32, (length, length), 0)
    column = lax.broadcasted_iota(jnp.int32, (length, length), 1)
    source = jnp.where(column < half, 2 * column, 2 * (column - half) + 1)
    order = jnp.where(row == source, 1.0, 0.0).astype(bf16)
    total = jnp.zeros((SUBLANES, length), f32)
    for f in range(frames):
        values = amplitude[f]
        total += jnp.sum((values * values).reshape(length // SUBLANES, SUBLANES, length), 0)
        high = values.astype(bf16)
        rest = values - high.astype(f32)
        middle = rest.astype(bf16)
        low = (rest - middle.astype(f32)).astype(bf16)
        placed = dot(high, order) + (dot(middle, order) + dot(low, order))
        for parity in range(2):
            held[f, parity] = placed[:, parity * half : (parity + 1) * half]
            for start in range(2):
                at = 2 * parity + start
                sorted_out[f, at * half : (at + 1) * half, :] = held[
                    f, parity, pl.ds(start, half, stride=2), :
                ]
    total_out[...] = sum(total[:, t * LANES : (t + 1) * LANES] for t in range(length // LANES))


def corner_kernel(above, below, left_inner, right_inner, left_out, right_out):
    planes, margin, side = above.shape
    inner = left_inner.shape[1]
    for plane in range(planes):
        for out, source, tile, lane in (
            (left_out, left_inner, 0, 0),
            (right_out, right_inner, side // LANES - 1, LANES - margin),
        ):
            at = pl.ds(tile * LANES, LANES)
            both = jnp.concatenate([above[plane, :, at], below[plane, :, at]], 0)
            out[plane, :inner] = source[plane]
            out[plane, inner:] = pack_rows(both, lane, margin)


def frames_kernel(
    blocks,
    place,
    offsets,
    field,
    above,
    below,
    from_left,
    from_right,
    probe,
    amplitude,
    total,
    matrices,
    row_turn,
    column_turn,
    canvas_low,
    canvas,
    canvas_high,
    kept,
    sent,
    later,
    padded,
    work,
    sums,
):
    frames = amplitude.shape[0]
    length = probe.shape[1]
    half = length // 2
    side = field.shape[1]
    margin = above.shape[1]
    reach = side + 2 * margin
    wide = side + LANES
    taller = length + SUBLANES
    per = LANES // margin

    for plane in range(2):
        padded[plane, :margin, :side] = above[plane]
        padded[plane, margin : margin + side, :side] = field[plane]
        padded[plane, margin + side : reach, :side] = below[plane]
        inner = side // per
        sides = [
            unpack_rows(from_right[plane, :inner], 0, margin)
            + unpack_rows(from_left[plane, :inner], LANES - margin, margin),
            unpack_rows(from_right[plane, inner:], 0, margin)
            + unpack_rows(from_left[plane, inner:], LANES - margin, margin),
        ]
        padded[plane, :margin, side:] = sides[1][:margin]
        padded[plane, margin : margin + side, side:] = sides[0]
        padded[plane, margin + side : reach, side:] = sides[1][margin:]
        padded[plane, reach:, :] = jnp.zeros((SUBLANES, wide), f32)
        work[plane] = jnp.zeros((reach + SUBLANES, wide), f32)
        work[plane, margin : margin + side, :side] = field[plane]
    work[2] = jnp.zeros((reach + SUBLANES, wide), f32)
    work[2, margin : margin + side, :side] = jnp.full((side, side), regular, f32)
    first = jnp.where(place[1] + place[2] == 0, 1.0, 0.0).astype(f32)
    sums[0] = probe[0] * first
    sums[1] = probe[1] * first
    sums[2] = jnp.full((length, length), regular, f32) * first

    left_high, left_low = matrices[0, 0], matrices[0, 1]
    right_high, right_low = matrices[1, 0], matrices[1, 1]
    row_cos = jnp.concatenate([row_turn[0]] * (length // LANES), 1)
    row_sin = jnp.concatenate([row_turn[1]] * (length // LANES), 1)
    column_cos = column_turn[0, 0:1, :]
    column_sin = column_turn[1, 0:1, :]

    def visit(f, carry):
        a = offsets[f, 0]
        b = offsets[f, 1]
        shift = lax.rem(a, SUBLANES)
        at = pl.ds(pl.multiple_of(a - shift, SUBLANES), taller)
        back = lax.rem(wide + margin - b, wide)
        ahead = lax.rem(wide - margin + b, wide)
        probe_real, probe_imag = probe[0], probe[1]
        window_real, window_imag = (
            pltpu.roll(
                pltpu.roll(padded[plane, at, :], back, 1)[:, :length],
                lax.rem(taller - shift, taller),
                0,
            )[:length]
            for plane in range(2)
        )
        wave_real = probe_real * window_real - probe_imag * window_imag
        wave_imag = probe_real * window_imag + probe_imag * window_real

        even_real = wave_real[:half] + wave_real[half:]
        even_imag = wave_imag[:half] + wave_imag[half:]
        odd_real, odd_imag = turned(
            wave_real[:half] - wave_real[half:],
            wave_imag[:half] - wave_imag[half:],
            row_cos,
            -row_sin,
        )
        stacked = jnp.concatenate(
            [
                jnp.concatenate([even_real, even_imag], 0),
                jnp.concatenate([odd_real, odd_imag], 0),
            ],
            1,
        )
        mixed = matrix_times(left_high, left_low, stacked)
        evens, odds = [], []
        for parity in range(2):
            part = mixed[:, parity * length : (parity + 1) * length]
            real, imag = part[:half], part[half:]
            evens.append(
                jnp.concatenate([real[:, :half] + real[:, half:], imag[:, :half] + imag[:, half:]], 1)
            )
            odds.append(
                jnp.concatenate(
                    turned(
                        real[:, :half] - real[:, half:],
                        imag[:, :half] - imag[:, half:],
                        column_cos,
                        -column_sin,
                    ),
                    1,
                )
            )
        far = times_matrix(jnp.concatenate(evens + odds, 0), right_high, right_low)
        far_real, far_imag = far[:, :half], far[:, half:]
        factor = amplitude[f] * lax.rsqrt(far_real * far_real + far_imag * far_imag + smoothing)
        corrected = jnp.concatenate([far_real * factor, far_imag * factor], 1)

        back_far = times_matrix(corrected, left_high, left_low)
        even, odd = back_far[:length], back_far[length:]
        odd_real, odd_imag = turned(odd[:, :half], odd[:, half:], column_cos, column_sin)
        even_real, even_imag = even[:, :half], even[:, half:]
        real = jnp.concatenate([even_real + odd_real, even_real - odd_real], 1)
        imag = jnp.concatenate([even_imag + odd_imag, even_imag - odd_imag], 1)
        stacked = jnp.concatenate(
            [
                jnp.concatenate([real[:half], imag[:half]], 0),
                jnp.concatenate([real[half:], imag[half:]], 0),
            ],
            1,
        )
        near = matrix_times(right_high, right_low, stacked)
        even, odd = near[:, :length], near[:, length:]
        odd_real, odd_imag = turned(odd[:half], odd[half:], row_cos, row_sin)
        near_real = jnp.concatenate([even[:half] + odd_real, even[:half] - odd_real], 0)
        near_imag = jnp.concatenate([even[half:] + odd_imag, even[half:] - odd_imag], 0)

        sums[0] += window_real * near_real + window_imag * near_imag
        sums[1] += window_real * near_imag - window_imag * near_real
        sums[2] += window_real * window_real + window_imag * window_imag
        under = jnp.zeros((SUBLANES, length), f32)
        beside = jnp.zeros((taller, wide - length), f32)
        terms = (
            probe_real * near_real + probe_imag * near_imag,
            probe_real * near_imag - probe_imag * near_real,
            probe_real * probe_real + probe_imag * probe_imag,
        )
        for plane, term in enumerate(terms):
            lowered = pltpu.roll(jnp.concatenate([term, under], 0), shift, 0)
            work[plane, at, :] += pltpu.roll(jnp.concatenate([lowered, beside], 1), ahead, 1)
        return carry

    lax.fori_loop(0, frames, visit, 0)

    canvas_low[...] = work[:, :margin, :side]
    canvas[...] = work[:, margin : margin + side, :side]
    canvas_high[...] = work[:, margin + side : reach, :side]

    tiles = length // LANES
    rows = length // blocks
    half_rows = blocks // 2 * 3 * tiles * rows
    for p in range(blocks):
        source = pl.multiple_of((place[0] ^ p) * rows, rows)
        out, q = (kept, p) if p < blocks // 2 else (sent, p - blocks // 2)
        for plane in range(3):
            for tile in range(tiles):
                start = ((3 * q + plane) * tiles + tile) * rows
                out[start : start + rows, :] = sums[
                    plane, pl.ds(source, rows), pl.ds(tile * LANES, LANES)
                ]
    kept[half_rows:, :] = total[...]
    sent[half_rows : half_rows + SUBLANES, :] = total[...]
    even = place[2] % 2 == 0
    start = half_rows + SUBLANES
    depth = reach // per
    for plane in range(3):
        edge = work[plane, :reach, side:]
        right = pack_rows(edge, 0, margin)
        left = pack_rows(edge, LANES - margin, margin)
        at = start + plane * depth
        sent[at : at + depth, :] = jnp.where(even, right, left)
        later[plane * depth : (plane + 1) * depth, :] = jnp.where(even, left, right)


def neighbours(first, second, index, count):
    even = index % 2 == 0
    before = jnp.where(even, second, first)
    after = jnp.where(even, first, second)
    return jnp.where(index > 0, before, 0.0), jnp.where(index < count - 1, after, 0.0)


def row_edge_kernel(counts, place, low, high, first, second, first_out, second_out):
    planes, margin, side = low.shape
    tiles = side // LANES
    depth = first.shape[0] // planes
    even = place[1] % 2 == 0
    for plane in range(planes):
        at = pl.ds(plane * depth, depth)
        before, after = neighbours(first[at, :], second[at, :], place[2], counts[1])
        lows = low[plane], unpack(before, 0, 0, margin), unpack(after, 0, LANES - margin, margin)
        last = LANES // margin - 1
        highs = (
            high[plane],
            unpack(before, last, 0, margin),
            unpack(after, last, LANES - margin, margin),
        )
        edges = []
        for (edge, left, right), cut in (
            (lows, slice(None, margin)),
            (highs, slice(depth - margin, None)),
        ):
            parts = [edge[:, t * LANES : (t + 1) * LANES] for t in range(tiles)]
            parts[0] += left[cut]
            parts[-1] += right[cut]
            edges.append(parts)
        for tile in range(tiles):
            at = pl.ds((plane * tiles + tile) * margin, margin)
            first_out[at, :] = jnp.where(even, edges[1][tile], edges[0][tile])
            second_out[at, :] = jnp.where(even, edges[0][tile], edges[1][tile])


def object_kernel(counts, place, canvas, first, second, row_first, row_second, out):
    planes, side, _ = canvas.shape
    margin = MARGIN
    tiles = side // LANES
    depth = first.shape[0] // planes
    for tile in range(tiles):
        total = []
        for plane in range(planes):
            at = pl.ds((plane * tiles + tile) * margin, margin)
            above, below = neighbours(row_first[at, :], row_second[at, :], place[1], counts[0])
            part = canvas[plane, :, pl.ds(tile * LANES, LANES)]
            at = pl.ds(plane * depth, depth)
            before, after = neighbours(first[at, :], second[at, :], place[2], counts[1])
            if tile == 0:
                part += unpack_rows(before, 0, margin)[margin : margin + side]
            if tile == tiles - 1:
                part += unpack_rows(after, LANES - margin, margin)[margin : margin + side]
            part = jnp.concatenate(
                [
                    part[:margin] + above,
                    part[margin : side - margin],
                    part[side - margin :] + below,
                ],
                0,
            )
            total.append(part)
        weight = 1.0 / total[2]
        out[0, :, pl.ds(tile * LANES, LANES)] = total[0] * weight
        out[1, :, pl.ds(tile * LANES, LANES)] = total[1] * weight


def probe_kernel(frame_count, blocks, place, stepped, total, out):
    planes, length, _ = out.shape
    tiles = length // LANES
    rows = length // blocks
    values = stepped[...]
    power = jnp.sum(values * values)
    target = jnp.sum(total[...]) / frame_count
    scale = jnp.sqrt(jnp.full((rows, LANES), target / (power + epsilon), f32))
    for p in range(blocks):
        home = pl.multiple_of((place[0] ^ p) * rows, rows)
        for plane in range(planes):
            for tile in range(tiles):
                start = ((planes * p + plane) * tiles + tile) * rows
                out[plane, pl.ds(home, rows), pl.ds(tile * LANES, LANES)] = (
                    values[start : start + rows] * scale
                )


def shape(*dims):
    return jax.ShapeDtypeStruct(dims, f32)


def call(kernel, outputs, scalars=0, operands=0, scratch=(), cost=None):
    vmem = pl.BlockSpec(memory_space=pltpu.VMEM)
    smem = pl.BlockSpec(memory_space=pltpu.SMEM)
    return pl.pallas_call(
        kernel,
        out_shape=outputs,
        in_specs=[smem] * scalars + [vmem] * operands,
        out_specs=jax.tree.map(lambda _: vmem, outputs),
        scratch_shapes=list(scratch),
        cost_estimate=cost,
        compiler_params=pltpu.CompilerParams(vmem_limit_bytes=40 * 1024 * 1024),
    )


def moved(block, axis, distance):
    devices = range(lax.axis_size(axis))
    return lax.ppermute(
        block, axis, [(i - distance, i) for i in devices if i - distance in devices]
    )


def partner(i, step, count):
    if step == 0:
        return i ^ 1
    if step == 1:
        return (i + 1 if i % 2 else i - 1) % count
    return i ^ (1 << step)


def swapped(block, axis, step):
    count = lax.axis_size(axis)
    return lax.ppermute(block, axis, [(i, partner(i, step, count)) for i in range(count)])


def per_device(object_field, probe, amplitudes, positions):
    planes, side, _ = object_field.shape
    length = probe.shape[1]
    margin = MARGIN
    reach = side + 2 * margin
    wide = side + LANES
    per = LANES // margin
    tiles = length // LANES
    measured = amplitudes[0, 0]
    frames = measured.shape[0]
    counts = lax.axis_size("row"), lax.axis_size("col")
    steps = [
        (axis, k) for axis in ("col", "row") for k in range((lax.axis_size(axis) - 1).bit_length())
    ]
    halved = [("col", 0), ("col", 1), ("row", 0)]
    blocks = 1 << len(halved)
    rows = length // blocks
    row = lax.axis_index("row").astype(jnp.int32)
    col = lax.axis_index("col").astype(jnp.int32)
    bits = [(col ^ (col >> 1)) & 1, (col >> 1) & 1, (row ^ (row >> 1)) & 1]
    place = jnp.stack([bits[0] * 4 + bits[1] * 2 + bits[2], row, col])

    above = moved(object_field[:, side - margin :, :], "row", 1)
    below = moved(object_field[:, :margin, :], "row", -1)
    inner = shape(planes, side // per, LANES)
    ordered, total, left, right = call(
        prepare_kernel,
        (shape(frames, 2 * length, length // 2), shape(SUBLANES, LANES), inner, inner),
        operands=2,
        scratch=(pltpu.VMEM((frames, 2, length, length // 2), f32),),
        cost=pl.CostEstimate(flops=10**9, bytes_accessed=2 * measured.size * 4, transcendentals=0),
    )(measured, object_field)
    packed = shape(planes, reach // per, LANES)
    left, right = call(corner_kernel, (packed, packed), operands=4)(above, below, left, right)
    from_left = moved(right, "col", 1)
    from_right = moved(left, "col", -1)

    matrices, row_turn, column_turn = tables(length)
    half_rows = blocks // 2 * 3 * tiles * rows
    depth = 3 * reach // per
    low, canvas, high, kept, sent, edge = call(
        functools.partial(frames_kernel, blocks),
        (
            shape(3, margin, side),
            shape(3, side, side),
            shape(3, margin, side),
            shape(half_rows + SUBLANES, LANES),
            shape(half_rows + SUBLANES + depth, LANES),
            shape(depth, LANES),
        ),
        scalars=2,
        operands=11,
        scratch=(
            pltpu.VMEM((2, reach + SUBLANES, wide), f32),
            pltpu.VMEM((3, reach + SUBLANES, wide), f32),
            pltpu.VMEM((3, length, length), f32),
        ),
    )(
        place,
        positions[0, 0],
        object_field,
        above,
        below,
        from_left,
        from_right,
        probe,
        ordered,
        total,
        jnp.asarray(matrices),
        jnp.asarray(row_turn),
        jnp.asarray(column_turn),
    )

    edges = {("col", 0): None, ("col", 1): edge}
    received = {}
    current = None
    for axis, step in steps:
        if axis == "row" and step == 0:
            out = shape(3 * tiles * margin, LANES)
            edges["row", 0], edges["row", 1] = call(
                functools.partial(row_edge_kernel, counts), (out, out), scalars=1, operands=4
            )(place, low, high, received["col", 0], received["col", 1])
        if current is not None:
            count = current.shape[0] - SUBLANES
            keep = count // 2 if (axis, step) in halved else count
            sent = [current[count - keep : count], current[count:]]
            if (axis, step) in edges:
                sent.append(edges[axis, step])
            sent = jnp.concatenate(sent, 0)
            kept = jnp.concatenate([current[:keep], current[count:]], 0)
        arrived = swapped(sent, axis, step)
        current = kept + arrived[: kept.shape[0]]
        received[axis, step] = arrived[kept.shape[0] :]
    object_next = call(
        functools.partial(object_kernel, counts),
        shape(*object_field.shape),
        scalars=1,
        operands=5,
    )(
        place,
        canvas,
        received["col", 0],
        received["col", 1],
        received["row", 0],
        received["row", 1],
    )
    size = tiles * rows
    weight = current[2 * size : 3 * size]
    stepped = current[: 2 * size] / jnp.concatenate([weight, weight], 0)
    for axis, step in halved[::-1]:
        stepped = jnp.concatenate([stepped, swapped(stepped, axis, step)], 0)
    frame_count = frames * counts[0] * counts[1]
    probe_next = call(
        functools.partial(probe_kernel, frame_count, blocks),
        shape(*probe.shape),
        scalars=1,
        operands=2,
    )(place, stepped, current[3 * size :])
    return (object_next, probe_next)


def solution(mesh):
    return jax.shard_map(
        per_device,
        mesh=mesh,
        in_specs=(
            P(None, "row", "col"),
            P(),
            P("row", "col", None, None, None),
            P("row", "col", None, None),
        ),
        out_specs=(P(None, "row", "col"), P()),
        check_vma=False,
    )
```

```python
import functools
import math

import jax
import jax.numpy as jnp
import numpy as np
from jax import lax
from jax.experimental import pallas as pl
from jax.experimental.pallas import tpu as pltpu
from jax.sharding import PartitionSpec as P

MARGIN = 32
LANES = 128
SUBLANES = 8

smoothing = 0.1
regular = 1.0
epsilon = 1e-06

f32 = jnp.float32
bf16 = jnp.bfloat16


def tables(length):
    half = length // 2
    scaling = 1.0 / math.sqrt(length)
    k = np.arange(half)
    phases = (k[:, None] * k[None, :] % half) * (2.0 * math.pi / half)
    cosine, sine = np.cos(phases) * scaling, np.sin(phases) * scaling
    right = np.block([[cosine, -sine], [sine, cosine]])
    left = np.block([[cosine, sine], [-sine, cosine]])
    both = np.stack([left, right]).astype(np.float32)
    high = both.astype(bf16)
    low = (both - high.astype(np.float32)).astype(bf16)
    matrices = np.stack([high, low], 1)
    angle = k * (2.0 * math.pi / length)
    turn = np.stack([np.cos(angle), np.sin(angle)]).astype(np.float32)
    rows = np.broadcast_to(turn[:, :, None], (2, half, LANES)).copy()
    columns = np.broadcast_to(turn[:, None, :], (2, SUBLANES, half)).copy()
    return matrices, rows, columns


def split(x):
    high = x.astype(bf16)
    return high, (x - high.astype(f32)).astype(bf16)


def dot(a, b):
    return jnp.dot(a, b, preferred_element_type=f32)


def times_matrix(data, high, low):
    data_high, data_low = split(data)
    return dot(data_high, high) + (dot(data_low, high) + dot(data_high, low))


def matrix_times(high, low, data):
    data_high, data_low = split(data)
    return dot(high, data_high) + (dot(high, data_low) + dot(low, data_high))


def turned(real, imag, cosine, sine):
    return real * cosine - imag * sine, real * sine + imag * cosine


def pack(chunks, lane, width):
    place = lax.broadcasted_iota(jnp.int32, chunks[0].shape, 1) // width
    out = jnp.zeros_like(chunks[0])
    for q, chunk in enumerate(chunks):
        shift = (q * width - lane) % LANES
        moved = pltpu.roll(chunk, shift, 1) if shift else chunk
        out = jnp.where(place == q, moved, out)
    return out


def pack_rows(rows, lane, width):
    count = rows.shape[0] * width // LANES
    return pack([rows[q : q + count] for q in range(0, rows.shape[0], count)], lane, width)


def unpack(packed, q, lane, width):
    shift = (lane - q * width) % LANES
    moved = pltpu.roll(packed, shift, 1) if shift else packed
    place = lax.broadcasted_iota(jnp.int32, packed.shape, 1)
    return jnp.where((place >= lane) & (place < lane + width), moved, 0.0)


def unpack_rows(packed, lane, width):
    return jnp.concatenate([unpack(packed, q, lane, width) for q in range(LANES // width)], 0)


def prepare_kernel(amplitude, field, sorted_out, total_out, left_out, right_out, held):
    frames, length, _ = amplitude.shape
    half = length // 2
    planes, side, _ = field.shape
    margin = MARGIN
    for out, tile, lane in ((left_out, 0, 0), (right_out, side // LANES - 1, LANES - margin)):
        for plane in range(planes):
            out[plane] = pack_rows(field[plane, :, pl.ds(tile * LANES, LANES)], lane, margin)
    row = lax.broadcasted_iota(jnp.int32, (length, length), 0)
    column = lax.broadcasted_iota(jnp.int32, (length, length), 1)
    source = jnp.where(column < half, 2 * column, 2 * (column - half) + 1)
    order = jnp.where(row == source, 1.0, 0.0).astype(bf16)
    total = jnp.zeros((SUBLANES, length), f32)
    for f in range(frames):
        values = amplitude[f]
        total += jnp.sum((values * values).reshape(length // SUBLANES, SUBLANES, length), 0)
        high = values.astype(bf16)
        rest = values - high.astype(f32)
        middle = rest.astype(bf16)
        low = (rest - middle.astype(f32)).astype(bf16)
        placed = dot(high, order) + (dot(middle, order) + dot(low, order))
        for parity in range(2):
            held[f, parity] = placed[:, parity * half : (parity + 1) * half]
            for start in range(2):
                at = 2 * parity + start
                sorted_out[f, at * half : (at + 1) * half, :] = held[
                    f, parity, pl.ds(start, half, stride=2), :
                ]
    total_out[...] = sum(total[:, t * LANES : (t + 1) * LANES] for t in range(length // LANES))


def corner_kernel(above, below, left_inner, right_inner, left_out, right_out):
    planes, margin, side = above.shape
    inner = left_inner.shape[1]
    for plane in range(planes):
        for out, source, tile, lane in (
            (left_out, left_inner, 0, 0),
            (right_out, right_inner, side // LANES - 1, LANES - margin),
        ):
            at = pl.ds(tile * LANES, LANES)
            both = jnp.concatenate([above[plane, :, at], below[plane, :, at]], 0)
            out[plane, :inner] = source[plane]
            out[plane, inner:] = pack_rows(both, lane, margin)


def frames_kernel(
    groups,
    pieces,
    place,
    offsets,
    field,
    above,
    below,
    from_left,
    from_right,
    probe,
    amplitude,
    total,
    matrices,
    row_turn,
    column_turn,
    canvas_low,
    canvas,
    canvas_high,
    kept,
    sent,
    later,
    padded,
    work,
    sums,
):
    frames = amplitude.shape[0]
    length = probe.shape[1]
    half = length // 2
    side = field.shape[1]
    margin = above.shape[1]
    reach = side + 2 * margin
    wide = side + LANES
    taller = length + SUBLANES
    per = LANES // margin

    for plane in range(2):
        padded[plane, :margin, :side] = above[plane]
        padded[plane, margin : margin + side, :side] = field[plane]
        padded[plane, margin + side : reach, :side] = below[plane]
        inner = side // per
        sides = [
            unpack_rows(from_right[plane, :inner], 0, margin)
            + unpack_rows(from_left[plane, :inner], LANES - margin, margin),
            unpack_rows(from_right[plane, inner:], 0, margin)
            + unpack_rows(from_left[plane, inner:], LANES - margin, margin),
        ]
        padded[plane, :margin, side:] = sides[1][:margin]
        padded[plane, margin : margin + side, side:] = sides[0]
        padded[plane, margin + side : reach, side:] = sides[1][margin:]
        padded[plane, reach:, :] = jnp.zeros((SUBLANES, wide), f32)
        work[plane] = jnp.zeros((reach + SUBLANES, wide), f32)
        work[plane, margin : margin + side, :side] = field[plane]
    work[2] = jnp.zeros((reach + SUBLANES, wide), f32)
    work[2, margin : margin + side, :side] = jnp.full((side, side), regular, f32)
    first = jnp.where(place[1] + place[2] == 0, 1.0, 0.0).astype(f32)
    sums[0] = probe[0] * first
    sums[1] = probe[1] * first
    sums[2] = jnp.full((length, length), regular, f32) * first

    left_high, left_low = matrices[0, 0], matrices[0, 1]
    right_high, right_low = matrices[1, 0], matrices[1, 1]
    row_cos = jnp.concatenate([row_turn[0]] * (length // LANES), 1)
    row_sin = jnp.concatenate([row_turn[1]] * (length // LANES), 1)
    column_cos = column_turn[0, 0:1, :]
    column_sin = column_turn[1, 0:1, :]

    def visit(f, carry):
        a = offsets[f, 0]
        b = offsets[f, 1]
        shift = lax.rem(a, SUBLANES)
        at = pl.ds(pl.multiple_of(a - shift, SUBLANES), taller)
        back = lax.rem(wide + margin - b, wide)
        ahead = lax.rem(wide - margin + b, wide)
        probe_real, probe_imag = probe[0], probe[1]
        window_real, window_imag = (
            pltpu.roll(
                pltpu.roll(padded[plane, at, :], back, 1)[:, :length],
                lax.rem(taller - shift, taller),
                0,
            )[:length]
            for plane in range(2)
        )
        wave_real = probe_real * window_real - probe_imag * window_imag
        wave_imag = probe_real * window_imag + probe_imag * window_real

        even_real = wave_real[:half] + wave_real[half:]
        even_imag = wave_imag[:half] + wave_imag[half:]
        odd_real, odd_imag = turned(
            wave_real[:half] - wave_real[half:],
            wave_imag[:half] - wave_imag[half:],
            row_cos,
            -row_sin,
        )
        stacked = jnp.concatenate(
            [
                jnp.concatenate([even_real, even_imag], 0),
                jnp.concatenate([odd_real, odd_imag], 0),
            ],
            1,
        )
        mixed = matrix_times(left_high, left_low, stacked)
        evens, odds = [], []
        for parity in range(2):
            part = mixed[:, parity * length : (parity + 1) * length]
            real, imag = part[:half], part[half:]
            evens.append(
                jnp.concatenate([real[:, :half] + real[:, half:], imag[:, :half] + imag[:, half:]], 1)
            )
            odds.append(
                jnp.concatenate(
                    turned(
                        real[:, :half] - real[:, half:],
                        imag[:, :half] - imag[:, half:],
                        column_cos,
                        -column_sin,
                    ),
                    1,
                )
            )
        far = times_matrix(jnp.concatenate(evens + odds, 0), right_high, right_low)
        far_real, far_imag = far[:, :half], far[:, half:]
        factor = amplitude[f] * lax.rsqrt(far_real * far_real + far_imag * far_imag + smoothing)
        corrected = jnp.concatenate([far_real * factor, far_imag * factor], 1)

        back_far = times_matrix(corrected, left_high, left_low)
        even, odd = back_far[:length], back_far[length:]
        odd_real, odd_imag = turned(odd[:, :half], odd[:, half:], column_cos, column_sin)
        even_real, even_imag = even[:, :half], even[:, half:]
        real = jnp.concatenate([even_real + odd_real, even_real - odd_real], 1)
        imag = jnp.concatenate([even_imag + odd_imag, even_imag - odd_imag], 1)
        stacked = jnp.concatenate(
            [
                jnp.concatenate([real[:half], imag[:half]], 0),
                jnp.concatenate([real[half:], imag[half:]], 0),
            ],
            1,
        )
        near = matrix_times(right_high, right_low, stacked)
        even, odd = near[:, :length], near[:, length:]
        odd_real, odd_imag = turned(odd[:half], odd[half:], row_cos, row_sin)
        near_real = jnp.concatenate([even[:half] + odd_real, even[:half] - odd_real], 0)
        near_imag = jnp.concatenate([even[half:] + odd_imag, even[half:] - odd_imag], 0)

        sums[0] += window_real * near_real + window_imag * near_imag
        sums[1] += window_real * near_imag - window_imag * near_real
        sums[2] += window_real * window_real + window_imag * window_imag
        under = jnp.zeros((SUBLANES, length), f32)
        beside = jnp.zeros((taller, wide - length), f32)
        terms = (
            probe_real * near_real + probe_imag * near_imag,
            probe_real * near_imag - probe_imag * near_real,
            probe_real * probe_real + probe_imag * probe_imag,
        )
        for plane, term in enumerate(terms):
            lowered = pltpu.roll(jnp.concatenate([term, under], 0), shift, 0)
            work[plane, at, :] += pltpu.roll(jnp.concatenate([lowered, beside], 1), ahead, 1)
        return carry

    lax.fori_loop(0, frames, visit, 0)

    canvas_low[...] = work[:, :margin, :side]
    canvas[...] = work[:, margin : margin + side, :side]
    canvas_high[...] = work[:, margin + side : reach, :side]

    tiles = length // LANES
    rows = length // (groups * pieces)
    half_rows = groups // 2 * pieces * 3 * tiles * rows
    for p in range(groups):
        out, at = (kept, p) if p < groups // 2 else (sent, p - groups // 2)
        for piece in range(pieces):
            source = pl.multiple_of(((place[0] ^ p) * pieces + piece) * rows, rows)
            for plane in range(3):
                for tile in range(tiles):
                    start = (((at * pieces + piece) * 3 + plane) * tiles + tile) * rows
                    out[start : start + rows, :] = sums[
                        plane, pl.ds(source, rows), pl.ds(tile * LANES, LANES)
                    ]
    kept[half_rows:, :] = total[...]
    sent[half_rows : half_rows + SUBLANES, :] = total[...]
    even = place[2] % 2 == 0
    start = half_rows + SUBLANES
    depth = reach // per
    for plane in range(3):
        edge = work[plane, :reach, side:]
        right = pack_rows(edge, 0, margin)
        left = pack_rows(edge, LANES - margin, margin)
        at = start + plane * depth
        sent[at : at + depth, :] = jnp.where(even, right, left)
        later[plane * depth : (plane + 1) * depth, :] = jnp.where(even, left, right)


def neighbours(first, second, index, count):
    even = index % 2 == 0
    before = jnp.where(even, second, first)
    after = jnp.where(even, first, second)
    return jnp.where(index > 0, before, 0.0), jnp.where(index < count - 1, after, 0.0)


def row_edge_kernel(columns, place, low, high, first, second, low_out, high_out):
    planes, margin, side = low.shape
    tiles = side // LANES
    depth = first.shape[0] // planes
    last = LANES // margin - 1
    for plane in range(planes):
        at = pl.ds(plane * depth, depth)
        before, after = neighbours(first[at, :], second[at, :], place[2], columns)
        for edge, out, chunk, cut in (
            (low, low_out, 0, slice(None, margin)),
            (high, high_out, last, slice(depth - margin, None)),
        ):
            parts = [edge[plane, :, t * LANES : (t + 1) * LANES] for t in range(tiles)]
            parts[0] += unpack(before, chunk, 0, margin)[cut]
            parts[-1] += unpack(after, chunk, LANES - margin, margin)[cut]
            for tile in range(tiles):
                out[plane, :, pl.ds(tile * LANES, LANES)] = parts[tile]


def object_kernel(columns, place, canvas, first, second, above, below, out):
    planes, side, _ = canvas.shape
    margin = MARGIN
    tiles = side // LANES
    depth = first.shape[0] // planes
    for tile in range(tiles):
        total = []
        for plane in range(planes):
            lanes = pl.ds(tile * LANES, LANES)
            part = canvas[plane, :, lanes]
            at = pl.ds(plane * depth, depth)
            before, after = neighbours(first[at, :], second[at, :], place[2], columns)
            if tile == 0:
                part += unpack_rows(before, 0, margin)[margin : margin + side]
            if tile == tiles - 1:
                part += unpack_rows(after, LANES - margin, margin)[margin : margin + side]
            part = jnp.concatenate(
                [
                    part[:margin] + above[plane, :, lanes],
                    part[margin : side - margin],
                    part[side - margin :] + below[plane, :, lanes],
                ],
                0,
            )
            total.append(part)
        weight = 1.0 / total[2]
        out[0, :, pl.ds(tile * LANES, LANES)] = total[0] * weight
        out[1, :, pl.ds(tile * LANES, LANES)] = total[1] * weight


def probe_kernel(frame_count, place, stepped, total, out):
    planes, length, _ = out.shape
    groups, pieces, depth, _ = stepped.shape
    tiles = length // LANES
    rows = depth // (planes * tiles)
    values = stepped[...]
    power = jnp.sum(values * values)
    target = jnp.sum(total[...]) / frame_count
    scale = jnp.sqrt(jnp.full((rows, LANES), target / (power + epsilon), f32))
    for p in range(groups):
        for piece in range(pieces):
            home = pl.multiple_of(((place[0] ^ p) * pieces + piece) * rows, rows)
            for plane in range(planes):
                for tile in range(tiles):
                    start = (plane * tiles + tile) * rows
                    out[plane, pl.ds(home, rows), pl.ds(tile * LANES, LANES)] = (
                        values[p, piece, start : start + rows] * scale
                    )


def shape(*dims):
    return jax.ShapeDtypeStruct(dims, f32)


def call(kernel, outputs, scalars=0, operands=0, scratch=(), cost=None):
    vmem = pl.BlockSpec(memory_space=pltpu.VMEM)
    smem = pl.BlockSpec(memory_space=pltpu.SMEM)
    return pl.pallas_call(
        kernel,
        out_shape=outputs,
        in_specs=[smem] * scalars + [vmem] * operands,
        out_specs=jax.tree.map(lambda _: vmem, outputs),
        scratch_shapes=list(scratch),
        cost_estimate=cost,
        compiler_params=pltpu.CompilerParams(vmem_limit_bytes=40 * 1024 * 1024),
    )


def moved(block, axis, distance):
    devices = range(lax.axis_size(axis))
    return lax.ppermute(
        block, axis, [(i - distance, i) for i in devices if i - distance in devices]
    )


def partner(i, step, count):
    if step == 0:
        return i ^ 1
    if step == 1:
        return (i + 1 if i % 2 else i - 1) % count
    return i ^ (1 << step)


def swapped(block, axis, step):
    count = lax.axis_size(axis)
    return lax.ppermute(block, axis, [(i, partner(i, step, count)) for i in range(count)])


def per_device(object_field, probe, amplitudes, positions):
    planes, side, _ = object_field.shape
    length = probe.shape[1]
    margin = MARGIN
    reach = side + 2 * margin
    wide = side + LANES
    per = LANES // margin
    tiles = length // LANES
    measured = amplitudes[0, 0]
    frames = measured.shape[0]
    counts = lax.axis_size("row"), lax.axis_size("col")
    steps = (counts[1] - 1).bit_length()
    halvings = min(2, (length // (SUBLANES * counts[0])).bit_length() - 1)
    groups, pieces = 1 << halvings, counts[0]
    rows = length // (groups * pieces)
    row = lax.axis_index("row").astype(jnp.int32)
    col = lax.axis_index("col").astype(jnp.int32)
    bits = [(col ^ (col >> 1)) & 1, (col >> 1) & 1]
    group = sum(bits[k] << (halvings - 1 - k) for k in range(halvings))
    place = jnp.stack([group, row, col])

    above = moved(object_field[:, side - margin :, :], "row", 1)
    below = moved(object_field[:, :margin, :], "row", -1)
    inner = shape(planes, side // per, LANES)
    ordered, total, left, right = call(
        prepare_kernel,
        (shape(frames, 2 * length, length // 2), shape(SUBLANES, LANES), inner, inner),
        operands=2,
        scratch=(pltpu.VMEM((frames, 2, length, length // 2), f32),),
        cost=pl.CostEstimate(flops=10**9, bytes_accessed=2 * measured.size * 4, transcendentals=0),
    )(measured, object_field)
    packed = shape(planes, reach // per, LANES)
    left, right = call(corner_kernel, (packed, packed), operands=4)(above, below, left, right)
    from_left = moved(right, "col", 1)
    from_right = moved(left, "col", -1)

    matrices, row_turn, column_turn = tables(length)
    half_rows = groups // 2 * pieces * 3 * tiles * rows
    depth = 3 * reach // per
    low, canvas, high, kept, sent, edge = call(
        functools.partial(frames_kernel, groups, pieces),
        (
            shape(3, margin, side),
            shape(3, side, side),
            shape(3, margin, side),
            shape(half_rows + SUBLANES, LANES),
            shape(half_rows + SUBLANES + depth, LANES),
            shape(depth, LANES),
        ),
        scalars=2,
        operands=11,
        scratch=(
            pltpu.VMEM((2, reach + SUBLANES, wide), f32),
            pltpu.VMEM((3, reach + SUBLANES, wide), f32),
            pltpu.VMEM((3, length, length), f32),
        ),
    )(
        place,
        positions[0, 0],
        object_field,
        above,
        below,
        from_left,
        from_right,
        probe,
        ordered,
        total,
        jnp.asarray(matrices),
        jnp.asarray(row_turn),
        jnp.asarray(column_turn),
    )

    arrived = swapped(sent, "col", 0)
    current = kept + arrived[: half_rows + SUBLANES]
    first = arrived[half_rows + SUBLANES :]
    for step in range(1, steps):
        count = current.shape[0] - SUBLANES
        keep = count // 2 if step < halvings else count
        sent = [current[count - keep : count], current[count:]]
        if step == 1:
            sent.append(edge)
        arrived = swapped(jnp.concatenate(sent, 0), "col", step)
        current = jnp.concatenate([current[:keep], current[count:]], 0) + arrived[: keep + SUBLANES]
        if step == 1:
            second = arrived[keep + SUBLANES :]
    size = tiles * rows
    values = current[: pieces * 3 * size].reshape(pieces, 3 * size, LANES)
    total = jnp.broadcast_to(current[None, pieces * 3 * size :], (pieces, SUBLANES, LANES))
    values = lax.all_to_all(jnp.concatenate([values, total], 1), "row", 0, 0)

    out = shape(3, margin, side)
    low, high = call(
        functools.partial(row_edge_kernel, counts[1]), (out, out), scalars=1, operands=4
    )(place, low, high, first, second)
    above = moved(high, "row", 1)
    below = moved(low, "row", -1)
    values, above, below = lax.optimization_barrier((values, above, below))
    current = jnp.sum(values, 0)
    weight = current[2 * size : 3 * size]
    stepped = current[: 2 * size] / jnp.concatenate([weight, weight], 0)
    stepped = lax.all_to_all(jnp.broadcast_to(stepped[None], (pieces, *stepped.shape)), "row", 0, 0)
    object_next = call(
        functools.partial(object_kernel, counts[1]),
        shape(*object_field.shape),
        scalars=1,
        operands=5,
    )(place, canvas, first, second, above, below)
    stepped, object_next = lax.optimization_barrier((stepped, object_next))
    stepped = stepped[None]
    for step in reversed(range(halvings)):
        stepped = jnp.concatenate([stepped, swapped(stepped, "col", step)], 0)
    frame_count = frames * counts[0] * counts[1]
    probe_next = call(
        functools.partial(probe_kernel, frame_count),
        shape(*probe.shape),
        scalars=1,
        operands=2,
    )(place, stepped, current[3 * size :])
    return (object_next, probe_next)


def solution(mesh):
    return jax.shard_map(
        per_device,
        mesh=mesh,
        in_specs=(
            P(None, "row", "col"),
            P(),
            P("row", "col", None, None, None),
            P("row", "col", None, None),
        ),
        out_specs=(P(None, "row", "col"), P()),
        check_vma=False,
    )
```

```python
import functools
import math

import jax
import jax.numpy as jnp
import numpy as np
from jax import lax
from jax.experimental import pallas as pl
from jax.experimental.pallas import tpu as pltpu
from jax.sharding import PartitionSpec as P

MARGIN = 32
LANES = 128
SUBLANES = 8

smoothing = 0.1
regular = 1.0
epsilon = 1e-06

f32 = jnp.float32
bf16 = jnp.bfloat16


def tables(length):
    half = length // 2
    scaling = 1.0 / math.sqrt(length)
    k = np.arange(half)
    phases = (k[:, None] * k[None, :] % half) * (2.0 * math.pi / half)
    cosine, sine = np.cos(phases) * scaling, np.sin(phases) * scaling
    right = np.block([[cosine, -sine], [sine, cosine]])
    left = np.block([[cosine, sine], [-sine, cosine]])
    both = np.stack([left, right]).astype(np.float32)
    high = both.astype(bf16)
    low = (both - high.astype(np.float32)).astype(bf16)
    matrices = np.stack([high, low], 1)
    angle = k * (2.0 * math.pi / length)
    turn = np.stack([np.cos(angle), np.sin(angle)]).astype(np.float32)
    rows = np.broadcast_to(turn[:, :, None], (2, half, LANES)).copy()
    columns = np.broadcast_to(turn[:, None, :], (2, SUBLANES, half)).copy()
    return matrices, rows, columns


def split(x):
    high = x.astype(bf16)
    return high, (x - high.astype(f32)).astype(bf16)


def dot(a, b):
    return jnp.dot(a, b, preferred_element_type=f32)


def times_matrix(data, high, low):
    data_high, data_low = split(data)
    return dot(data_high, high) + (dot(data_low, high) + dot(data_high, low))


def matrix_times(high, low, data):
    data_high, data_low = split(data)
    return dot(high, data_high) + (dot(high, data_low) + dot(low, data_high))


def turned(real, imag, cosine, sine):
    return real * cosine - imag * sine, real * sine + imag * cosine


def pack(chunks, lane, width):
    place = lax.broadcasted_iota(jnp.int32, chunks[0].shape, 1) // width
    out = jnp.zeros_like(chunks[0])
    for q, chunk in enumerate(chunks):
        shift = (q * width - lane) % LANES
        moved = pltpu.roll(chunk, shift, 1) if shift else chunk
        out = jnp.where(place == q, moved, out)
    return out


def pack_rows(rows, lane, width):
    count = rows.shape[0] * width // LANES
    return pack([rows[q : q + count] for q in range(0, rows.shape[0], count)], lane, width)


def unpack(packed, q, lane, width):
    shift = (lane - q * width) % LANES
    moved = pltpu.roll(packed, shift, 1) if shift else packed
    place = lax.broadcasted_iota(jnp.int32, packed.shape, 1)
    return jnp.where((place >= lane) & (place < lane + width), moved, 0.0)


def unpack_rows(packed, lane, width):
    return jnp.concatenate([unpack(packed, q, lane, width) for q in range(LANES // width)], 0)


def prepare_kernel(amplitude, field, sorted_out, total_out, left_out, right_out, held):
    frames, length, _ = amplitude.shape
    half = length // 2
    planes, side, _ = field.shape
    margin = MARGIN
    for out, tile, lane in ((left_out, 0, 0), (right_out, side // LANES - 1, LANES - margin)):
        for plane in range(planes):
            out[plane] = pack_rows(field[plane, :, pl.ds(tile * LANES, LANES)], lane, margin)
    row = lax.broadcasted_iota(jnp.int32, (length, length), 0)
    column = lax.broadcasted_iota(jnp.int32, (length, length), 1)
    source = jnp.where(column < half, 2 * column, 2 * (column - half) + 1)
    order = jnp.where(row == source, 1.0, 0.0).astype(bf16)
    total = jnp.zeros((SUBLANES, length), f32)
    for f in range(frames):
        values = amplitude[f]
        total += jnp.sum((values * values).reshape(length // SUBLANES, SUBLANES, length), 0)
        high = values.astype(bf16)
        rest = values - high.astype(f32)
        middle = rest.astype(bf16)
        low = (rest - middle.astype(f32)).astype(bf16)
        placed = dot(high, order) + (dot(middle, order) + dot(low, order))
        for parity in range(2):
            held[f, parity] = placed[:, parity * half : (parity + 1) * half]
            for start in range(2):
                at = 2 * parity + start
                sorted_out[f, at * half : (at + 1) * half, :] = held[
                    f, parity, pl.ds(start, half, stride=2), :
                ]
    total_out[...] = sum(total[:, t * LANES : (t + 1) * LANES] for t in range(length // LANES))


def corner_kernel(above, below, left_inner, right_inner, left_out, right_out):
    planes, margin, side = above.shape
    inner = left_inner.shape[1]
    for plane in range(planes):
        for out, source, tile, lane in (
            (left_out, left_inner, 0, 0),
            (right_out, right_inner, side // LANES - 1, LANES - margin),
        ):
            at = pl.ds(tile * LANES, LANES)
            both = jnp.concatenate([above[plane, :, at], below[plane, :, at]], 0)
            out[plane, :inner] = source[plane]
            out[plane, inner:] = pack_rows(both, lane, margin)


def frames_kernel(
    blocks,
    place,
    offsets,
    field,
    above,
    below,
    from_left,
    from_right,
    probe,
    amplitude,
    total,
    matrices,
    row_turn,
    column_turn,
    canvas_low,
    canvas,
    canvas_high,
    kept,
    sent,
    later,
    padded,
    work,
    sums,
):
    frames = amplitude.shape[0]
    length = probe.shape[1]
    half = length // 2
    side = field.shape[1]
    margin = above.shape[1]
    reach = side + 2 * margin
    wide = side + LANES
    taller = length + SUBLANES
    per = LANES // margin

    for plane in range(2):
        padded[plane, :margin, :side] = above[plane]
        padded[plane, margin : margin + side, :side] = field[plane]
        padded[plane, margin + side : reach, :side] = below[plane]
        inner = side // per
        sides = [
            unpack_rows(from_right[plane, :inner], 0, margin)
            + unpack_rows(from_left[plane, :inner], LANES - margin, margin),
            unpack_rows(from_right[plane, inner:], 0, margin)
            + unpack_rows(from_left[plane, inner:], LANES - margin, margin),
        ]
        padded[plane, :margin, side:] = sides[1][:margin]
        padded[plane, margin : margin + side, side:] = sides[0]
        padded[plane, margin + side : reach, side:] = sides[1][margin:]
        padded[plane, reach:, :] = jnp.zeros((SUBLANES, wide), f32)
        work[plane] = jnp.zeros((reach + SUBLANES, wide), f32)
        work[plane, margin : margin + side, :side] = field[plane]
    work[2] = jnp.zeros((reach + SUBLANES, wide), f32)
    work[2, margin : margin + side, :side] = jnp.full((side, side), regular, f32)
    first = jnp.where(place[1] + place[2] == 0, 1.0, 0.0).astype(f32)
    sums[0] = probe[0] * first
    sums[1] = probe[1] * first
    sums[2] = jnp.full((length, length), regular, f32) * first

    left_high, left_low = matrices[0, 0], matrices[0, 1]
    right_high, right_low = matrices[1, 0], matrices[1, 1]
    row_cos = jnp.concatenate([row_turn[0]] * (length // LANES), 1)
    row_sin = jnp.concatenate([row_turn[1]] * (length // LANES), 1)
    column_cos = column_turn[0, 0:1, :]
    column_sin = column_turn[1, 0:1, :]

    def visit(f, carry):
        a = offsets[f, 0]
        b = offsets[f, 1]
        shift = lax.rem(a, SUBLANES)
        at = pl.ds(pl.multiple_of(a - shift, SUBLANES), taller)
        back = lax.rem(wide + margin - b, wide)
        ahead = lax.rem(wide - margin + b, wide)
        probe_real, probe_imag = probe[0], probe[1]
        window_real, window_imag = (
            pltpu.roll(
                pltpu.roll(padded[plane, at, :], back, 1)[:, :length],
                lax.rem(taller - shift, taller),
                0,
            )[:length]
            for plane in range(2)
        )
        wave_real = probe_real * window_real - probe_imag * window_imag
        wave_imag = probe_real * window_imag + probe_imag * window_real

        even_real = wave_real[:half] + wave_real[half:]
        even_imag = wave_imag[:half] + wave_imag[half:]
        odd_real, odd_imag = turned(
            wave_real[:half] - wave_real[half:],
            wave_imag[:half] - wave_imag[half:],
            row_cos,
            -row_sin,
        )
        stacked = jnp.concatenate(
            [
                jnp.concatenate([even_real, even_imag], 0),
                jnp.concatenate([odd_real, odd_imag], 0),
            ],
            1,
        )
        mixed = matrix_times(left_high, left_low, stacked)
        evens, odds = [], []
        for parity in range(2):
            part = mixed[:, parity * length : (parity + 1) * length]
            real, imag = part[:half], part[half:]
            evens.append(
                jnp.concatenate([real[:, :half] + real[:, half:], imag[:, :half] + imag[:, half:]], 1)
            )
            odds.append(
                jnp.concatenate(
                    turned(
                        real[:, :half] - real[:, half:],
                        imag[:, :half] - imag[:, half:],
                        column_cos,
                        -column_sin,
                    ),
                    1,
                )
            )
        far = times_matrix(jnp.concatenate(evens + odds, 0), right_high, right_low)
        far_real, far_imag = far[:, :half], far[:, half:]
        factor = amplitude[f] * lax.rsqrt(far_real * far_real + far_imag * far_imag + smoothing)
        corrected = jnp.concatenate([far_real * factor, far_imag * factor], 1)

        back_far = times_matrix(corrected, left_high, left_low)
        even, odd = back_far[:length], back_far[length:]
        odd_real, odd_imag = turned(odd[:, :half], odd[:, half:], column_cos, column_sin)
        even_real, even_imag = even[:, :half], even[:, half:]
        real = jnp.concatenate([even_real + odd_real, even_real - odd_real], 1)
        imag = jnp.concatenate([even_imag + odd_imag, even_imag - odd_imag], 1)
        stacked = jnp.concatenate(
            [
                jnp.concatenate([real[:half], imag[:half]], 0),
                jnp.concatenate([real[half:], imag[half:]], 0),
            ],
            1,
        )
        near = matrix_times(right_high, right_low, stacked)
        even, odd = near[:, :length], near[:, length:]
        odd_real, odd_imag = turned(odd[:half], odd[half:], row_cos, row_sin)
        near_real = jnp.concatenate([even[:half] + odd_real, even[:half] - odd_real], 0)
        near_imag = jnp.concatenate([even[half:] + odd_imag, even[half:] - odd_imag], 0)

        sums[0] += window_real * near_real + window_imag * near_imag
        sums[1] += window_real * near_imag - window_imag * near_real
        sums[2] += window_real * window_real + window_imag * window_imag
        under = jnp.zeros((SUBLANES, length), f32)
        beside = jnp.zeros((taller, wide - length), f32)
        terms = (
            probe_real * near_real + probe_imag * near_imag,
            probe_real * near_imag - probe_imag * near_real,
            probe_real * probe_real + probe_imag * probe_imag,
        )
        for plane, term in enumerate(terms):
            lowered = pltpu.roll(jnp.concatenate([term, under], 0), shift, 0)
            work[plane, at, :] += pltpu.roll(jnp.concatenate([lowered, beside], 1), ahead, 1)
        return carry

    lax.fori_loop(0, frames, visit, 0)

    canvas_low[...] = work[:, :margin, :side]
    canvas[...] = work[:, margin : margin + side, :side]
    canvas_high[...] = work[:, margin + side : reach, :side]

    tiles = length // LANES
    rows = length // blocks
    half_rows = blocks // 2 * 3 * tiles * rows
    for p in range(blocks):
        out, q, base = (
            (kept, p, place[0]) if p < blocks // 2 else (sent, p - blocks // 2, place[3])
        )
        source = pl.multiple_of((base ^ q) * rows, rows)
        for plane in range(3):
            for tile in range(tiles):
                start = ((3 * q + plane) * tiles + tile) * rows
                out[start : start + rows, :] = sums[
                    plane, pl.ds(source, rows), pl.ds(tile * LANES, LANES)
                ]
    kept[half_rows:, :] = total[...]
    sent[half_rows : half_rows + SUBLANES, :] = total[...]
    even = place[2] % 2 == 0
    start = half_rows + SUBLANES
    depth = reach // per
    for plane in range(3):
        edge = work[plane, :reach, side:]
        right = pack_rows(edge, 0, margin)
        left = pack_rows(edge, LANES - margin, margin)
        at = start + plane * depth
        sent[at : at + depth, :] = jnp.where(even, right, left)
        later[plane * depth : (plane + 1) * depth, :] = jnp.where(even, left, right)


def neighbours(first, second, index):
    even = index % 2 == 0
    return jnp.where(even, second, first), jnp.where(even, first, second)


def row_edge_kernel(place, low, high, first, second, first_out, second_out):
    planes, margin, side = low.shape
    tiles = side // LANES
    depth = first.shape[0] // planes
    even = place[1] % 2 == 0
    for plane in range(planes):
        at = pl.ds(plane * depth, depth)
        before, after = neighbours(first[at, :], second[at, :], place[2])
        lows = low[plane], unpack(before, 0, 0, margin), unpack(after, 0, LANES - margin, margin)
        last = LANES // margin - 1
        highs = (
            high[plane],
            unpack(before, last, 0, margin),
            unpack(after, last, LANES - margin, margin),
        )
        edges = []
        for (edge, left, right), cut in (
            (lows, slice(None, margin)),
            (highs, slice(depth - margin, None)),
        ):
            parts = [edge[:, t * LANES : (t + 1) * LANES] for t in range(tiles)]
            parts[0] += left[cut]
            parts[-1] += right[cut]
            edges.append(parts)
        for tile in range(tiles):
            at = pl.ds((plane * tiles + tile) * margin, margin)
            first_out[at, :] = jnp.where(even, edges[1][tile], edges[0][tile])
            second_out[at, :] = jnp.where(even, edges[0][tile], edges[1][tile])


def object_kernel(place, canvas, first, second, row_first, row_second, out):
    planes, side, _ = canvas.shape
    margin = MARGIN
    tiles = side // LANES
    depth = first.shape[0] // planes
    for tile in range(tiles):
        total = []
        for plane in range(planes):
            at = pl.ds((plane * tiles + tile) * margin, margin)
            above, below = neighbours(row_first[at, :], row_second[at, :], place[1])
            part = canvas[plane, :, pl.ds(tile * LANES, LANES)]
            at = pl.ds(plane * depth, depth)
            before, after = neighbours(first[at, :], second[at, :], place[2])
            if tile == 0:
                part += unpack_rows(before, 0, margin)[margin : margin + side]
            if tile == tiles - 1:
                part += unpack_rows(after, LANES - margin, margin)[margin : margin + side]
            part = jnp.concatenate(
                [
                    part[:margin] + above,
                    part[margin : side - margin],
                    part[side - margin :] + below,
                ],
                0,
            )
            total.append(part)
        weight = 1.0 / total[2]
        out[0, :, pl.ds(tile * LANES, LANES)] = total[0] * weight
        out[1, :, pl.ds(tile * LANES, LANES)] = total[1] * weight


def probe_kernel(frame_count, blocks, place, stepped, total, out):
    planes, length, _ = out.shape
    tiles = length // LANES
    rows = length // blocks
    values = stepped[...]
    power = jnp.sum(values * values)
    target = jnp.sum(total[...]) / frame_count
    scale = jnp.sqrt(jnp.full((rows, LANES), target / (power + epsilon), f32))
    for p in range(blocks):
        base, q = (place[0], p) if p < blocks // 2 else (place[3], p - blocks // 2)
        home = pl.multiple_of((base ^ q) * rows, rows)
        for plane in range(planes):
            for tile in range(tiles):
                start = ((planes * p + plane) * tiles + tile) * rows
                out[plane, pl.ds(home, rows), pl.ds(tile * LANES, LANES)] = (
                    values[start : start + rows] * scale
                )


def shape(*dims):
    return jax.ShapeDtypeStruct(dims, f32)


def call(kernel, outputs, scalars=0, operands=0, scratch=(), cost=None):
    vmem = pl.BlockSpec(memory_space=pltpu.VMEM)
    smem = pl.BlockSpec(memory_space=pltpu.SMEM)
    return pl.pallas_call(
        kernel,
        out_shape=outputs,
        in_specs=[smem] * scalars + [vmem] * operands,
        out_specs=jax.tree.map(lambda _: vmem, outputs),
        scratch_shapes=list(scratch),
        cost_estimate=cost,
        compiler_params=pltpu.CompilerParams(vmem_limit_bytes=40 * 1024 * 1024),
    )


def moved(block, axis, distance):
    devices = range(lax.axis_size(axis))
    return lax.ppermute(
        block, axis, [(i - distance, i) for i in devices if i - distance in devices]
    )


def paired(block, axis, first):
    pairs = [(i, i + 1) for i in range(first, lax.axis_size(axis) - 1, 2)]
    return lax.ppermute(block, axis, pairs + [(target, source) for source, target in pairs])


def exchanged(block, orders, step):
    count = lax.axis_size("row") * lax.axis_size("col")
    pairs = [(i, i ^ (1 << orders[i % 2][step])) for i in range(count)]
    return lax.ppermute(block, ("row", "col"), pairs)


def per_device(object_field, probe, amplitudes, positions):
    planes, side, _ = object_field.shape
    length = probe.shape[1]
    margin = MARGIN
    reach = side + 2 * margin
    wide = side + LANES
    per = LANES // margin
    tiles = length // LANES
    measured = amplitudes[0, 0]
    frames = measured.shape[0]
    counts = lax.axis_size("row"), lax.axis_size("col")
    row = lax.axis_index("row").astype(jnp.int32)
    col = lax.axis_index("col").astype(jnp.int32)
    index = row * counts[1] + col
    col_bits = (counts[1] - 1).bit_length()
    across = list(range(1, col_bits))
    along = list(range(col_bits, col_bits + (counts[0] - 1).bit_length()))
    orders = (across + along, along + across)
    halvings = 2
    blocks = 2 << halvings
    rows = length // blocks
    homes = [
        sum(((index >> order[k]) & 1) << (halvings - 1 - k) for k in range(halvings))
        for order in orders
    ]
    core = index & 1
    homes[1] += blocks // 2
    place = jnp.stack(
        [
            jnp.where(core == 0, homes[0], homes[1]),
            row,
            col,
            jnp.where(core == 0, homes[1], homes[0]),
        ]
    )

    above = moved(object_field[:, side - margin :, :], "row", 1)
    below = moved(object_field[:, :margin, :], "row", -1)
    inner = shape(planes, side // per, LANES)
    ordered, total, left, right = call(
        prepare_kernel,
        (shape(frames, 2 * length, length // 2), shape(SUBLANES, LANES), inner, inner),
        operands=2,
        scratch=(pltpu.VMEM((frames, 2, length, length // 2), f32),),
        cost=pl.CostEstimate(flops=10**9, bytes_accessed=2 * measured.size * 4, transcendentals=0),
    )(measured, object_field)
    packed = shape(planes, reach // per, LANES)
    left, right = call(corner_kernel, (packed, packed), operands=4)(above, below, left, right)
    from_left = moved(right, "col", 1)
    from_right = moved(left, "col", -1)

    matrices, row_turn, column_turn = tables(length)
    half_rows = blocks // 2 * 3 * tiles * rows
    depth = 3 * reach // per
    low, canvas, high, kept, sent, edge = call(
        functools.partial(frames_kernel, blocks),
        (
            shape(3, margin, side),
            shape(3, side, side),
            shape(3, margin, side),
            shape(half_rows + SUBLANES, LANES),
            shape(half_rows + SUBLANES + depth, LANES),
            shape(depth, LANES),
        ),
        scalars=2,
        operands=11,
        scratch=(
            pltpu.VMEM((2, reach + SUBLANES, wide), f32),
            pltpu.VMEM((3, reach + SUBLANES, wide), f32),
            pltpu.VMEM((3, length, length), f32),
        ),
    )(
        place,
        positions[0, 0],
        object_field,
        above,
        below,
        from_left,
        from_right,
        probe,
        ordered,
        total,
        jnp.asarray(matrices),
        jnp.asarray(row_turn),
        jnp.asarray(column_turn),
    )

    arrived = paired(sent, "col", 0)
    current = kept + arrived[: half_rows + SUBLANES]
    first = arrived[half_rows + SUBLANES :]
    second = paired(edge, "col", 1)
    for step in range(len(orders[0])):
        if step == 1:
            current, second = lax.optimization_barrier((current, second))
            out = shape(3 * tiles * margin, LANES)
            row_first, row_second = call(row_edge_kernel, (out, out), scalars=1, operands=4)(
                place, low, high, first, second
            )
            row_first = paired(row_first, "row", 0)
            row_second = paired(row_second, "row", 1)
        if step == 3:
            current, row_first, row_second = lax.optimization_barrier(
                (current, row_first, row_second)
            )
        count = current.shape[0] - SUBLANES
        if step < halvings:
            sent = jnp.concatenate([current[count // 2 : count], current[count:]], 0)
            kept = jnp.concatenate([current[: count // 2], current[count:]], 0)
        else:
            kept = sent = current
        current = kept + exchanged(sent, orders, step)
    size = tiles * rows
    weight = current[2 * size : 3 * size]
    stepped = current[: 2 * size] / jnp.concatenate([weight, weight], 0)
    object_next = call(object_kernel, shape(*object_field.shape), scalars=1, operands=5)(
        place, canvas, first, second, row_first, row_second
    )
    for step in reversed(range(halvings)):
        stepped = jnp.concatenate([stepped, exchanged(stepped, orders, step)], 0)
    stepped = jnp.concatenate([stepped, paired(stepped, "col", 0)], 0)
    frame_count = frames * counts[0] * counts[1]
    probe_next = call(
        functools.partial(probe_kernel, frame_count, blocks),
        shape(*probe.shape),
        scalars=1,
        operands=2,
    )(place, stepped, current[3 * size :])
    return (object_next, probe_next)


def solution(mesh):
    return jax.shard_map(
        per_device,
        mesh=mesh,
        in_specs=(
            P(None, "row", "col"),
            P(),
            P("row", "col", None, None, None),
            P("row", "col", None, None),
        ),
        out_specs=(P(None, "row", "col"), P()),
        check_vma=False,
    )
```

```python
import functools
import math

import jax
import jax.numpy as jnp
import numpy as np
from jax import lax
from jax.experimental import pallas as pl
from jax.experimental.pallas import tpu as pltpu
from jax.sharding import PartitionSpec as P

MARGIN = 32
LANES = 128
SUBLANES = 8

smoothing = 0.1
regular = 1.0
epsilon = 1e-06

f32 = jnp.float32
bf16 = jnp.bfloat16


def tables(length):
    half = length // 2
    scaling = 1.0 / math.sqrt(length)
    k = np.arange(half)
    phases = (k[:, None] * k[None, :] % half) * (2.0 * math.pi / half)
    cosine, sine = np.cos(phases) * scaling, np.sin(phases) * scaling
    right = np.block([[cosine, -sine], [sine, cosine]])
    left = np.block([[cosine, sine], [-sine, cosine]])
    both = np.stack([left, right]).astype(np.float32)
    high = both.astype(bf16)
    low = (both - high.astype(np.float32)).astype(bf16)
    matrices = np.stack([high, low], 1)
    angle = k * (2.0 * math.pi / length)
    turn = np.stack([np.cos(angle), np.sin(angle)]).astype(np.float32)
    rows = np.broadcast_to(turn[:, :, None], (2, half, LANES)).copy()
    columns = np.broadcast_to(turn[:, None, :], (2, SUBLANES, half)).copy()
    return matrices, rows, columns


def split(x):
    high = x.astype(bf16)
    return high, (x - high.astype(f32)).astype(bf16)


def dot(a, b):
    return jnp.dot(a, b, preferred_element_type=f32)


def times_matrix(data, high, low):
    data_high, data_low = split(data)
    return dot(data_high, high) + (dot(data_low, high) + dot(data_high, low))


def matrix_times(high, low, data):
    data_high, data_low = split(data)
    return dot(high, data_high) + (dot(high, data_low) + dot(low, data_high))


def turned(real, imag, cosine, sine):
    return real * cosine - imag * sine, real * sine + imag * cosine


def pack(chunks, lane, width):
    place = lax.broadcasted_iota(jnp.int32, chunks[0].shape, 1) // width
    out = jnp.zeros_like(chunks[0])
    for q, chunk in enumerate(chunks):
        shift = (q * width - lane) % LANES
        moved = pltpu.roll(chunk, shift, 1) if shift else chunk
        out = jnp.where(place == q, moved, out)
    return out


def pack_rows(rows, lane, width):
    count = rows.shape[0] * width // LANES
    return pack([rows[q : q + count] for q in range(0, rows.shape[0], count)], lane, width)


def unpack(packed, q, lane, width):
    shift = (lane - q * width) % LANES
    moved = pltpu.roll(packed, shift, 1) if shift else packed
    place = lax.broadcasted_iota(jnp.int32, packed.shape, 1)
    return jnp.where((place >= lane) & (place < lane + width), moved, 0.0)


def unpack_rows(packed, lane, width):
    return jnp.concatenate([unpack(packed, q, lane, width) for q in range(LANES // width)], 0)


def neighbours(first, second, index, count):
    even = index % 2 == 0
    before = jnp.where(even, second, first)
    after = jnp.where(even, first, second)
    return jnp.where(index > 0, before, 0.0), jnp.where(index < count - 1, after, 0.0)


def begin_kernel(place, source, field, rows_first, rows_second, columns_first, columns_second, sem):
    copy = pltpu.make_async_copy(source, field, sem)
    copy.start()
    copy.wait()
    planes, side, _ = field.shape
    margin = rows_first.shape[1]
    even_row = place[1] % 2 == 0
    even_column = place[2] % 2 == 0
    for plane in range(planes):
        top, bottom = field[plane, :margin], field[plane, side - margin :]
        rows_first[plane] = jnp.where(even_row, bottom, top)
        rows_second[plane] = jnp.where(even_row, top, bottom)
        left = pack_rows(field[plane, :, :LANES], 0, margin)
        right = pack_rows(field[plane, :, side - LANES :], LANES - margin, margin)
        columns_first[plane] = jnp.where(even_column, right, left)
        columns_second[plane] = jnp.where(even_column, left, right)


def amplitude_kernel(amplitude, sorted_out, total_out, held):
    frames, length, _ = amplitude.shape
    half = length // 2
    row = lax.broadcasted_iota(jnp.int32, (length, length), 0)
    column = lax.broadcasted_iota(jnp.int32, (length, length), 1)
    source = jnp.where(column < half, 2 * column, 2 * (column - half) + 1)
    order = jnp.where(row == source, 1.0, 0.0).astype(bf16)
    total = jnp.zeros((SUBLANES, length), f32)
    for f in range(frames):
        values = amplitude[f]
        total += jnp.sum((values * values).reshape(length // SUBLANES, SUBLANES, length), 0)
        high = values.astype(bf16)
        rest = values - high.astype(f32)
        middle = rest.astype(bf16)
        low = (rest - middle.astype(f32)).astype(bf16)
        placed = dot(high, order) + (dot(middle, order) + dot(low, order))
        for parity in range(2):
            held[f, parity] = placed[:, parity * half : (parity + 1) * half]
            for start in range(2):
                at = 2 * parity + start
                sorted_out[f, at * half : (at + 1) * half, :] = held[
                    f, parity, pl.ds(start, half, stride=2), :
                ]
    total_out[...] = sum(total[:, t * LANES : (t + 1) * LANES] for t in range(length // LANES))


def corner_kernel(
    counts, place, first, second, inner_first, inner_second, above, below, first_out, second_out
):
    planes, margin, side = first.shape
    inner = inner_first.shape[1]
    even = place[2] % 2 == 0
    for plane in range(planes):
        before, after = neighbours(first[plane], second[plane], place[1], counts[0])
        above[plane] = before
        below[plane] = after
        both = jnp.concatenate([before, after], 0)
        left = pack_rows(both[:, :LANES], 0, margin)
        right = pack_rows(both[:, side - LANES :], LANES - margin, margin)
        first_out[plane, :inner] = inner_first[plane]
        first_out[plane, inner:] = jnp.where(even, right, left)
        second_out[plane, :inner] = inner_second[plane]
        second_out[plane, inner:] = jnp.where(even, left, right)


def frames_kernel(
    counts,
    blocks,
    place,
    offsets,
    field,
    above,
    below,
    columns_first,
    columns_second,
    probe,
    amplitude,
    total,
    matrices,
    row_turn,
    column_turn,
    canvas_low,
    canvas,
    canvas_high,
    kept,
    sent,
    later,
    padded,
    work,
    sums,
):
    frames = amplitude.shape[0]
    length = probe.shape[1]
    half = length // 2
    side = field.shape[1]
    margin = above.shape[1]
    reach = side + 2 * margin
    wide = side + LANES
    taller = length + SUBLANES
    per = LANES // margin

    for plane in range(2):
        padded[plane, :margin, :side] = above[plane]
        padded[plane, margin : margin + side, :side] = field[plane]
        padded[plane, margin + side : reach, :side] = below[plane]
        inner = side // per
        before, after = neighbours(
            columns_first[plane], columns_second[plane], place[2], counts[1]
        )
        sides = [
            unpack_rows(after[part], 0, margin) + unpack_rows(before[part], LANES - margin, margin)
            for part in (slice(None, inner), slice(inner, None))
        ]
        padded[plane, :margin, side:] = sides[1][:margin]
        padded[plane, margin : margin + side, side:] = sides[0]
        padded[plane, margin + side : reach, side:] = sides[1][margin:]
        padded[plane, reach:, :] = jnp.zeros((SUBLANES, wide), f32)
        work[plane] = jnp.zeros((reach + SUBLANES, wide), f32)
        work[plane, margin : margin + side, :side] = field[plane]
    work[2] = jnp.zeros((reach + SUBLANES, wide), f32)
    work[2, margin : margin + side, :side] = jnp.full((side, side), regular, f32)
    first = jnp.where(place[1] + place[2] == 0, 1.0, 0.0).astype(f32)
    sums[0] = probe[0] * first
    sums[1] = probe[1] * first
    sums[2] = jnp.full((length, length), regular, f32) * first

    left_high, left_low = matrices[0, 0], matrices[0, 1]
    right_high, right_low = matrices[1, 0], matrices[1, 1]
    row_cos = jnp.concatenate([row_turn[0]] * (length // LANES), 1)
    row_sin = jnp.concatenate([row_turn[1]] * (length // LANES), 1)
    column_cos = column_turn[0, 0:1, :]
    column_sin = column_turn[1, 0:1, :]

    def visit(f, carry):
        a = offsets[f, 0]
        b = offsets[f, 1]
        shift = lax.rem(a, SUBLANES)
        at = pl.ds(pl.multiple_of(a - shift, SUBLANES), taller)
        back = lax.rem(wide + margin - b, wide)
        ahead = lax.rem(wide - margin + b, wide)
        probe_real, probe_imag = probe[0], probe[1]
        window_real, window_imag = (
            pltpu.roll(
                pltpu.roll(padded[plane, at, :], back, 1)[:, :length],
                lax.rem(taller - shift, taller),
                0,
            )[:length]
            for plane in range(2)
        )
        wave_real = probe_real * window_real - probe_imag * window_imag
        wave_imag = probe_real * window_imag + probe_imag * window_real

        even_real = wave_real[:half] + wave_real[half:]
        even_imag = wave_imag[:half] + wave_imag[half:]
        odd_real, odd_imag = turned(
            wave_real[:half] - wave_real[half:],
            wave_imag[:half] - wave_imag[half:],
            row_cos,
            -row_sin,
        )
        stacked = jnp.concatenate(
            [
                jnp.concatenate([even_real, even_imag], 0),
                jnp.concatenate([odd_real, odd_imag], 0),
            ],
            1,
        )
        mixed = matrix_times(left_high, left_low, stacked)
        evens, odds = [], []
        for parity in range(2):
            part = mixed[:, parity * length : (parity + 1) * length]
            real, imag = part[:half], part[half:]
            evens.append(
                jnp.concatenate([real[:, :half] + real[:, half:], imag[:, :half] + imag[:, half:]], 1)
            )
            odds.append(
                jnp.concatenate(
                    turned(
                        real[:, :half] - real[:, half:],
                        imag[:, :half] - imag[:, half:],
                        column_cos,
                        -column_sin,
                    ),
                    1,
                )
            )
        far = times_matrix(jnp.concatenate(evens + odds, 0), right_high, right_low)
        far_real, far_imag = far[:, :half], far[:, half:]
        factor = amplitude[f] * lax.rsqrt(far_real * far_real + far_imag * far_imag + smoothing)
        corrected = jnp.concatenate([far_real * factor, far_imag * factor], 1)

        back_far = times_matrix(corrected, left_high, left_low)
        even, odd = back_far[:length], back_far[length:]
        odd_real, odd_imag = turned(odd[:, :half], odd[:, half:], column_cos, column_sin)
        even_real, even_imag = even[:, :half], even[:, half:]
        real = jnp.concatenate([even_real + odd_real, even_real - odd_real], 1)
        imag = jnp.concatenate([even_imag + odd_imag, even_imag - odd_imag], 1)
        stacked = jnp.concatenate(
            [
                jnp.concatenate([real[:half], imag[:half]], 0),
                jnp.concatenate([real[half:], imag[half:]], 0),
            ],
            1,
        )
        near = matrix_times(right_high, right_low, stacked)
        even, odd = near[:, :length], near[:, length:]
        odd_real, odd_imag = turned(odd[:half], odd[half:], row_cos, row_sin)
        near_real = jnp.concatenate([even[:half] + odd_real, even[:half] - odd_real], 0)
        near_imag = jnp.concatenate([even[half:] + odd_imag, even[half:] - odd_imag], 0)

        sums[0] += window_real * near_real + window_imag * near_imag
        sums[1] += window_real * near_imag - window_imag * near_real
        sums[2] += window_real * window_real + window_imag * window_imag
        under = jnp.zeros((SUBLANES, length), f32)
        beside = jnp.zeros((taller, wide - length), f32)
        terms = (
            probe_real * near_real + probe_imag * near_imag,
            probe_real * near_imag - probe_imag * near_real,
            probe_real * probe_real + probe_imag * probe_imag,
        )
        for plane, term in enumerate(terms):
            lowered = pltpu.roll(jnp.concatenate([term, under], 0), shift, 0)
            work[plane, at, :] += pltpu.roll(jnp.concatenate([lowered, beside], 1), ahead, 1)
        return carry

    lax.fori_loop(0, frames, visit, 0)

    canvas_low[...] = work[:, :margin, :side]
    canvas[...] = work[:, margin : margin + side, :side]
    canvas_high[...] = work[:, margin + side : reach, :side]

    tiles = length // LANES
    rows = length // blocks
    half_rows = blocks // 2 * 3 * tiles * rows
    for p in range(blocks):
        out, q, base = (
            (kept, p, place[0]) if p < blocks // 2 else (sent, p - blocks // 2, place[3])
        )
        source = pl.multiple_of((base ^ q) * rows, rows)
        for plane in range(3):
            for tile in range(tiles):
                start = ((3 * q + plane) * tiles + tile) * rows
                out[start : start + rows, :] = sums[
                    plane, pl.ds(source, rows), pl.ds(tile * LANES, LANES)
                ]
    kept[half_rows:, :] = total[...]
    sent[half_rows : half_rows + SUBLANES, :] = total[...]
    even = place[2] % 2 == 0
    start = half_rows + SUBLANES
    depth = reach // per
    for plane in range(3):
        edge = work[plane, :reach, side:]
        right = pack_rows(edge, 0, margin)
        left = pack_rows(edge, LANES - margin, margin)
        at = start + plane * depth
        sent[at : at + depth, :] = jnp.where(even, right, left)
        later[plane * depth : (plane + 1) * depth, :] = jnp.where(even, left, right)


def row_edge_kernel(counts, place, low, high, first, second, first_out, second_out):
    planes, margin, side = low.shape
    tiles = side // LANES
    depth = first.shape[0] // planes
    even = place[1] % 2 == 0
    for plane in range(planes):
        at = pl.ds(plane * depth, depth)
        before, after = neighbours(first[at, :], second[at, :], place[2], counts[1])
        lows = low[plane], unpack(before, 0, 0, margin), unpack(after, 0, LANES - margin, margin)
        last = LANES // margin - 1
        highs = (
            high[plane],
            unpack(before, last, 0, margin),
            unpack(after, last, LANES - margin, margin),
        )
        edges = []
        for (edge, left, right), cut in (
            (lows, slice(None, margin)),
            (highs, slice(depth - margin, None)),
        ):
            parts = [edge[:, t * LANES : (t + 1) * LANES] for t in range(tiles)]
            parts[0] += left[cut]
            parts[-1] += right[cut]
            edges.append(parts)
        for tile in range(tiles):
            at = pl.ds((plane * tiles + tile) * margin, margin)
            first_out[at, :] = jnp.where(even, edges[1][tile], edges[0][tile])
            second_out[at, :] = jnp.where(even, edges[0][tile], edges[1][tile])


def object_kernel(counts, place, canvas, first, second, row_first, row_second, out):
    planes, side, _ = canvas.shape
    margin = MARGIN
    tiles = side // LANES
    depth = first.shape[0] // planes
    for tile in range(tiles):
        total = []
        for plane in range(planes):
            at = pl.ds((plane * tiles + tile) * margin, margin)
            above, below = neighbours(row_first[at, :], row_second[at, :], place[1], counts[0])
            part = canvas[plane, :, pl.ds(tile * LANES, LANES)]
            at = pl.ds(plane * depth, depth)
            before, after = neighbours(first[at, :], second[at, :], place[2], counts[1])
            if tile == 0:
                part += unpack_rows(before, 0, margin)[margin : margin + side]
            if tile == tiles - 1:
                part += unpack_rows(after, LANES - margin, margin)[margin : margin + side]
            part = jnp.concatenate(
                [
                    part[:margin] + above,
                    part[margin : side - margin],
                    part[side - margin :] + below,
                ],
                0,
            )
            total.append(part)
        weight = 1.0 / total[2]
        out[0, :, pl.ds(tile * LANES, LANES)] = total[0] * weight
        out[1, :, pl.ds(tile * LANES, LANES)] = total[1] * weight


def probe_kernel(frame_count, blocks, place, stepped, total, out):
    planes, length, _ = out.shape
    tiles = length // LANES
    rows = length // blocks
    values = stepped[...]
    power = jnp.sum(values * values)
    target = jnp.sum(total[...]) / frame_count
    scale = jnp.sqrt(jnp.full((rows, LANES), target / (power + epsilon), f32))
    for p in range(blocks):
        base, q = (place[0], p) if p < blocks // 2 else (place[3], p - blocks // 2)
        home = pl.multiple_of((base ^ q) * rows, rows)
        for plane in range(planes):
            for tile in range(tiles):
                start = ((planes * p + plane) * tiles + tile) * rows
                out[plane, pl.ds(home, rows), pl.ds(tile * LANES, LANES)] = (
                    values[start : start + rows] * scale
                )


def shape(*dims):
    return jax.ShapeDtypeStruct(dims, f32)


def call(kernel, outputs, scalars=0, operands=0, scratch=(), cost=None):
    vmem = pl.BlockSpec(memory_space=pltpu.VMEM)
    smem = pl.BlockSpec(memory_space=pltpu.SMEM)
    return pl.pallas_call(
        kernel,
        out_shape=outputs,
        in_specs=[smem] * scalars + [vmem] * operands,
        out_specs=jax.tree.map(lambda _: vmem, outputs),
        scratch_shapes=list(scratch),
        cost_estimate=cost,
        compiler_params=pltpu.CompilerParams(vmem_limit_bytes=40 * 1024 * 1024),
    )


def paired(block, axis, first):
    count = lax.axis_size(axis)
    target = list(range(count))
    for i in range(first, count - 1, 2):
        target[i], target[i + 1] = i + 1, i
    return lax.ppermute(block, axis, list(enumerate(target)))


def exchanged(block, orders, step):
    count = lax.axis_size("row") * lax.axis_size("col")
    pairs = [(i, i ^ (1 << orders[i % 2][step])) for i in range(count)]
    return lax.ppermute(block, ("row", "col"), pairs)


def per_device(object_field, probe, amplitudes, positions):
    planes, side, _ = object_field.shape
    length = probe.shape[1]
    margin = MARGIN
    reach = side + 2 * margin
    wide = side + LANES
    per = LANES // margin
    tiles = length // LANES
    measured = amplitudes[0, 0]
    frames = measured.shape[0]
    counts = lax.axis_size("row"), lax.axis_size("col")
    row = lax.axis_index("row").astype(jnp.int32)
    col = lax.axis_index("col").astype(jnp.int32)
    index = row * counts[1] + col
    col_bits = (counts[1] - 1).bit_length()
    across = list(range(1, col_bits))
    along = list(range(col_bits, col_bits + (counts[0] - 1).bit_length()))
    orders = (across + along, along + across)
    halvings = 2
    blocks = 2 << halvings
    rows = length // blocks
    homes = [
        sum(((index >> order[k]) & 1) << (halvings - 1 - k) for k in range(halvings))
        for order in orders
    ]
    core = index & 1
    homes[1] += blocks // 2
    place = jnp.stack(
        [
            jnp.where(core == 0, homes[0], homes[1]),
            row,
            col,
            jnp.where(core == 0, homes[1], homes[0]),
        ]
    )

    edge_rows = shape(planes, margin, side)
    inner = shape(planes, side // per, LANES)
    smem = pl.BlockSpec(memory_space=pltpu.SMEM)
    vmem = pl.BlockSpec(memory_space=pltpu.VMEM)
    field, rows_first, rows_second, inner_first, inner_second = pl.pallas_call(
        begin_kernel,
        out_shape=(shape(*object_field.shape), edge_rows, edge_rows, inner, inner),
        in_specs=[smem, pl.BlockSpec(memory_space=pl.ANY)],
        out_specs=(vmem,) * 5,
        scratch_shapes=[pltpu.SemaphoreType.DMA],
        compiler_params=pltpu.CompilerParams(vmem_limit_bytes=16 * 1024 * 1024),
    )(place, object_field)
    rows_first = paired(rows_first, "row", 0)
    rows_second = paired(rows_second, "row", 1)
    ordered, total = call(
        amplitude_kernel,
        (shape(frames, 2 * length, length // 2), shape(SUBLANES, LANES)),
        operands=1,
        scratch=(pltpu.VMEM((frames, 2, length, length // 2), f32),),
        cost=pl.CostEstimate(flops=10**9, bytes_accessed=2 * measured.size * 4, transcendentals=0),
    )(measured)
    packed = shape(planes, reach // per, LANES)
    above, below, columns_first, columns_second = call(
        functools.partial(corner_kernel, counts),
        (edge_rows, edge_rows, packed, packed),
        scalars=1,
        operands=4,
    )(place, rows_first, rows_second, inner_first, inner_second)
    columns_first = paired(columns_first, "col", 0)
    columns_second = paired(columns_second, "col", 1)

    matrices, row_turn, column_turn = tables(length)
    half_rows = blocks // 2 * 3 * tiles * rows
    depth = 3 * reach // per
    low, canvas, high, kept, sent, edge = call(
        functools.partial(frames_kernel, counts, blocks),
        (
            shape(3, margin, side),
            shape(3, side, side),
            shape(3, margin, side),
            shape(half_rows + SUBLANES, LANES),
            shape(half_rows + SUBLANES + depth, LANES),
            shape(depth, LANES),
        ),
        scalars=2,
        operands=11,
        scratch=(
            pltpu.VMEM((2, reach + SUBLANES, wide), f32),
            pltpu.VMEM((3, reach + SUBLANES, wide), f32),
            pltpu.VMEM((3, length, length), f32),
        ),
    )(
        place,
        positions[0, 0],
        field,
        above,
        below,
        columns_first,
        columns_second,
        probe,
        ordered,
        total,
        jnp.asarray(matrices),
        jnp.asarray(row_turn),
        jnp.asarray(column_turn),
    )

    arrived = paired(sent, "col", 0)
    current = kept + arrived[: half_rows + SUBLANES]
    first = arrived[half_rows + SUBLANES :]
    second = paired(edge, "col", 1)
    for step in range(len(orders[0])):
        if step == 1:
            current, second = lax.optimization_barrier((current, second))
            out = shape(3 * tiles * margin, LANES)
            row_first, row_second = call(
                functools.partial(row_edge_kernel, counts), (out, out), scalars=1, operands=4
            )(
                place, low, high, first, second
            )
            row_first = paired(row_first, "row", 0)
            row_second = paired(row_second, "row", 1)
        if step == 3:
            current, row_first, row_second = lax.optimization_barrier(
                (current, row_first, row_second)
            )
        count = current.shape[0] - SUBLANES
        if step < halvings:
            sent = jnp.concatenate([current[count // 2 : count], current[count:]], 0)
            kept = jnp.concatenate([current[: count // 2], current[count:]], 0)
        else:
            kept = sent = current
        current = kept + exchanged(sent, orders, step)
    size = tiles * rows
    weight = current[2 * size : 3 * size]
    stepped = current[: 2 * size] / jnp.concatenate([weight, weight], 0)
    object_next = call(
        functools.partial(object_kernel, counts),
        shape(*object_field.shape),
        scalars=1,
        operands=5,
    )(
        place, canvas, first, second, row_first, row_second
    )
    for step in reversed(range(halvings)):
        stepped = jnp.concatenate([stepped, exchanged(stepped, orders, step)], 0)
    stepped = jnp.concatenate([stepped, paired(stepped, "col", 0)], 0)
    frame_count = frames * counts[0] * counts[1]
    probe_next = call(
        functools.partial(probe_kernel, frame_count, blocks),
        shape(*probe.shape),
        scalars=1,
        operands=2,
    )(place, stepped, current[3 * size :])
    return (object_next, probe_next)


def solution(mesh):
    return jax.shard_map(
        per_device,
        mesh=mesh,
        in_specs=(
            P(None, "row", "col"),
            P(),
            P("row", "col", None, None, None),
            P("row", "col", None, None),
        ),
        out_specs=(P(None, "row", "col"), P()),
        check_vma=False,
    )
```

```python
import functools
import math

import jax
import jax.numpy as jnp
import numpy as np
from jax import lax
from jax.experimental import pallas as pl
from jax.experimental.pallas import tpu as pltpu
from jax.sharding import PartitionSpec as P

MARGIN = 32
LANES = 128
SUBLANES = 8

smoothing = 0.1
regular = 1.0
epsilon = 1e-06

f32 = jnp.float32
bf16 = jnp.bfloat16


def tables(length):
    half = length // 2
    scaling = 1.0 / math.sqrt(length)
    k = np.arange(half)
    phases = (k[:, None] * k[None, :] % half) * (2.0 * math.pi / half)
    cosine, sine = np.cos(phases) * scaling, np.sin(phases) * scaling
    right = np.block([[cosine, -sine], [sine, cosine]])
    left = np.block([[cosine, sine], [-sine, cosine]])
    both = np.stack([left, right]).astype(np.float32)
    high = both.astype(bf16)
    low = (both - high.astype(np.float32)).astype(bf16)
    matrices = np.stack([high, low], 1)
    angle = k * (2.0 * math.pi / length)
    turn = np.stack([np.cos(angle), np.sin(angle)]).astype(np.float32)
    rows = np.broadcast_to(turn[:, :, None], (2, half, LANES)).copy()
    columns = np.broadcast_to(turn[:, None, :], (2, SUBLANES, half)).copy()
    return matrices, rows, columns


def split(x):
    high = x.astype(bf16)
    return high, (x - high.astype(f32)).astype(bf16)


def dot(a, b):
    return jnp.dot(a, b, preferred_element_type=f32)


def times_matrix(data, matrix):
    high, low = split(data)
    return dot(
        jnp.concatenate([high, low, high], 1),
        jnp.concatenate([matrix[0], matrix[0], matrix[1]], 0),
    )


def matrix_times(matrix, data):
    high, low = split(data)
    return dot(
        jnp.concatenate([matrix[0], matrix[0], matrix[1]], 1),
        jnp.concatenate([high, low, high], 0),
    )


def turned(real, imag, cosine, sine):
    return real * cosine - imag * sine, real * sine + imag * cosine


def pack(chunks, lane, width):
    place = lax.broadcasted_iota(jnp.int32, chunks[0].shape, 1) // width
    out = jnp.zeros_like(chunks[0])
    for q, chunk in enumerate(chunks):
        shift = (q * width - lane) % LANES
        moved = pltpu.roll(chunk, shift, 1) if shift else chunk
        out = jnp.where(place == q, moved, out)
    return out


def pack_rows(rows, lane, width):
    count = rows.shape[0] * width // LANES
    return pack([rows[q : q + count] for q in range(0, rows.shape[0], count)], lane, width)


def unpack(packed, q, lane, width):
    shift = (lane - q * width) % LANES
    moved = pltpu.roll(packed, shift, 1) if shift else packed
    place = lax.broadcasted_iota(jnp.int32, packed.shape, 1)
    return jnp.where((place >= lane) & (place < lane + width), moved, 0.0)


def unpack_rows(packed, lane, width):
    return jnp.concatenate([unpack(packed, q, lane, width) for q in range(LANES // width)], 0)


def lifted(tile, shift):
    groups = tile.shape[0] // SUBLANES
    turned_rows = pltpu.roll(
        tile.reshape(groups, SUBLANES, LANES), lax.rem(SUBLANES - shift, SUBLANES), 1
    )
    place = lax.broadcasted_iota(jnp.int32, (groups - 1, SUBLANES, LANES), 1)
    picked = jnp.where(place < SUBLANES - shift, turned_rows[:-1], turned_rows[1:])
    return picked.reshape((groups - 1) * SUBLANES, LANES)


def lowered(tile, shift):
    groups = tile.shape[0] // SUBLANES
    moved = pltpu.roll(tile.reshape(groups, SUBLANES, LANES), shift, 1)
    none = jnp.zeros((1, SUBLANES, LANES), f32)
    place = lax.broadcasted_iota(jnp.int32, (groups + 1, SUBLANES, LANES), 1)
    picked = jnp.where(
        place >= shift, jnp.concatenate([moved, none], 0), jnp.concatenate([none, moved], 0)
    )
    return picked.reshape((groups + 1) * SUBLANES, LANES)


def spot(offsets, f, margin, taller):
    a, b = offsets[f, 0], offsets[f, 1]
    shift = lax.rem(a, SUBLANES)
    lane = b + LANES - margin
    tile = lane // LANES
    return pl.ds(pl.multiple_of(a - shift, SUBLANES), taller), shift, tile, lane - tile * LANES


def window_of(padded, plane, spot_of, tiles):
    at, shift, base, lane = spot_of
    moved = [
        pltpu.roll(padded[plane, base + t, at, :], lax.rem(LANES - lane, LANES), 1)
        for t in range(tiles + 1)
    ]
    place = lax.broadcasted_iota(jnp.int32, moved[0].shape, 1)
    parts = [
        lifted(jnp.where(place < LANES - lane, moved[t], moved[t + 1]), shift)
        for t in range(tiles)
    ]
    return jnp.concatenate(parts, 1)


def add_window(work, term, spot_of):
    at, shift, base, lane = spot_of
    tiles = term.shape[1] // LANES
    moved = [
        pltpu.roll(lowered(term[:, t * LANES : (t + 1) * LANES], shift), lane, 1)
        for t in range(tiles)
    ]
    none = jnp.zeros_like(moved[0])
    place = lax.broadcasted_iota(jnp.int32, none.shape, 1)
    for t in range(tiles + 1):
        here = moved[t] if t < tiles else none
        before = moved[t - 1] if t else none
        work[base + t, at, :] += jnp.where(place >= lane, here, before)


def neighbours(first, second, index, count):
    even = index % 2 == 0
    before = jnp.where(even, second, first)
    after = jnp.where(even, first, second)
    return jnp.where(index > 0, before, 0.0), jnp.where(index < count - 1, after, 0.0)


def begin_kernel(place, source, field, rows_first, rows_second, columns_first, columns_second, sem):
    copy = pltpu.make_async_copy(source, field, sem)
    copy.start()
    copy.wait()
    planes, side, _ = field.shape
    margin = rows_first.shape[1]
    even_row = place[1] % 2 == 0
    even_column = place[2] % 2 == 0
    for plane in range(planes):
        top, bottom = field[plane, :margin], field[plane, side - margin :]
        rows_first[plane] = jnp.where(even_row, bottom, top)
        rows_second[plane] = jnp.where(even_row, top, bottom)
        left = pack_rows(field[plane, :, :LANES], 0, margin)
        right = pack_rows(field[plane, :, side - LANES :], LANES - margin, margin)
        columns_first[plane] = jnp.where(even_column, right, left)
        columns_second[plane] = jnp.where(even_column, left, right)


def amplitude_kernel(margin, offsets, amplitude, probe, sorted_out, total_out, powers, held):
    frames, length, _ = amplitude.shape
    half = length // 2
    power = probe[0] * probe[0] + probe[1] * probe[1]
    powers[...] = jnp.zeros(powers.shape, f32)
    for f in range(frames):
        add_window(powers, power, spot(offsets, f, margin, length + SUBLANES))
    row = lax.broadcasted_iota(jnp.int32, (length, length), 0)
    column = lax.broadcasted_iota(jnp.int32, (length, length), 1)
    source = jnp.where(column < half, 2 * column, 2 * (column - half) + 1)
    order = jnp.where(row == source, 1.0, 0.0).astype(bf16)
    total = jnp.zeros((SUBLANES, length), f32)
    for f in range(frames):
        values = amplitude[f]
        total += jnp.sum((values * values).reshape(length // SUBLANES, SUBLANES, length), 0)
        high = values.astype(bf16)
        rest = values - high.astype(f32)
        middle = rest.astype(bf16)
        low = (rest - middle.astype(f32)).astype(bf16)
        placed = dot(high, order) + (dot(middle, order) + dot(low, order))
        for parity in range(2):
            held[f, parity] = placed[:, parity * half : (parity + 1) * half]
            for start in range(2):
                at = 2 * parity + start
                sorted_out[f, at * half : (at + 1) * half, :] = held[
                    f, parity, pl.ds(start, half, stride=2), :
                ]
    total_out[...] = sum(total[:, t * LANES : (t + 1) * LANES] for t in range(length // LANES))


def corner_kernel(
    counts, place, first, second, inner_first, inner_second, above, below, first_out, second_out
):
    planes, margin, side = first.shape
    inner = inner_first.shape[1]
    even = place[2] % 2 == 0
    for plane in range(planes):
        before, after = neighbours(first[plane], second[plane], place[1], counts[0])
        above[plane] = before
        below[plane] = after
        both = jnp.concatenate([before, after], 0)
        left = pack_rows(both[:, :LANES], 0, margin)
        right = pack_rows(both[:, side - LANES :], LANES - margin, margin)
        first_out[plane, :inner] = inner_first[plane]
        first_out[plane, inner:] = jnp.where(even, right, left)
        second_out[plane, :inner] = inner_second[plane]
        second_out[plane, inner:] = jnp.where(even, left, right)


def transform_pair(waves, row_turn, column_turn, matrices, amplitudes):
    length = waves[0][0].shape[0]
    half = length // 2
    row_cos, row_sin = row_turn
    column_cos, column_sin = column_turn

    mixed = []
    for real, imag in waves:
        odd = turned(real[:half] - real[half:], imag[:half] - imag[half:], row_cos, -row_sin)
        stacked = jnp.concatenate(
            [
                jnp.concatenate([real[:half] + real[half:], imag[:half] + imag[half:]], 0),
                jnp.concatenate(odd, 0),
            ],
            1,
        )
        mixed.append(matrix_times(matrices.at[0], stacked))

    far = []
    for value in mixed:
        evens, odds = [], []
        for parity in range(2):
            part = value[:, parity * length : (parity + 1) * length]
            real, imag = part[:half], part[half:]
            evens.append(
                jnp.concatenate(
                    [real[:, :half] + real[:, half:], imag[:, :half] + imag[:, half:]], 1
                )
            )
            odd = turned(
                real[:, :half] - real[:, half:],
                imag[:, :half] - imag[:, half:],
                column_cos,
                -column_sin,
            )
            odds.append(jnp.concatenate(odd, 1))
        far.append(times_matrix(jnp.concatenate(evens + odds, 0), matrices.at[1]))

    turned_back = []
    for value, amplitude in zip(far, amplitudes):
        real, imag = value[:, :half], value[:, half:]
        factor = amplitude * lax.rsqrt(real * real + imag * imag + smoothing)
        corrected = jnp.concatenate([real * factor, imag * factor], 1)
        turned_back.append(times_matrix(corrected, matrices.at[0]))

    near = []
    for value in turned_back:
        even, odd = value[:length], value[length:]
        odd_real, odd_imag = turned(odd[:, :half], odd[:, half:], column_cos, column_sin)
        even_real, even_imag = even[:, :half], even[:, half:]
        real = jnp.concatenate([even_real + odd_real, even_real - odd_real], 1)
        imag = jnp.concatenate([even_imag + odd_imag, even_imag - odd_imag], 1)
        stacked = jnp.concatenate(
            [
                jnp.concatenate([real[:half], imag[:half]], 0),
                jnp.concatenate([real[half:], imag[half:]], 0),
            ],
            1,
        )
        near.append(matrix_times(matrices.at[1], stacked))

    results = []
    for value in near:
        even, odd = value[:, :length], value[:, length:]
        odd_real, odd_imag = turned(odd[:half], odd[half:], row_cos, row_sin)
        results.append(
            (
                jnp.concatenate([even[:half] + odd_real, even[:half] - odd_real], 0),
                jnp.concatenate([even[half:] + odd_imag, even[half:] - odd_imag], 0),
            )
        )
    return results


def frames_kernel(
    counts,
    blocks,
    place,
    offsets,
    field,
    above,
    below,
    columns_first,
    columns_second,
    probe,
    amplitude,
    total,
    powers,
    matrices,
    row_turn,
    column_turn,
    work,
    kept,
    sent,
    later,
    padded,
    sums,
):
    frames = amplitude.shape[0]
    length = probe.shape[1]
    side = field.shape[1]
    margin = above.shape[1]
    reach = side + 2 * margin
    taller = length + SUBLANES
    per = LANES // margin
    inner = side // per
    tiles = length // LANES
    last = side // LANES + 1

    for plane in range(2):
        for tile in range(side // LANES):
            lanes = pl.ds(tile * LANES, LANES)
            padded[plane, tile + 1, :margin, :] = above[plane, :, lanes]
            padded[plane, tile + 1, margin : margin + side, :] = field[plane, :, lanes]
            padded[plane, tile + 1, margin + side : reach, :] = below[plane, :, lanes]
        left, right = neighbours(
            columns_first[plane], columns_second[plane], place[2], counts[1]
        )
        for tile, packed, lane in ((0, left, LANES - margin), (last, right, 0)):
            corners = unpack_rows(packed[inner:], lane, margin)
            padded[plane, tile, :margin, :] = corners[:margin]
            padded[plane, tile, margin : margin + side, :] = unpack_rows(
                packed[:inner], lane, margin
            )
            padded[plane, tile, margin + side : reach, :] = corners[margin:]
        padded[plane, :, reach:, :] = jnp.zeros((last + 1, SUBLANES, LANES), f32)
    work[...] = jnp.zeros(work.shape, f32)
    first = jnp.where(place[1] + place[2] == 0, 1.0, 0.0).astype(f32)
    sums[0] = probe[0] * first
    sums[1] = probe[1] * first
    sums[2] = jnp.full((length, length), regular, f32) * first

    row_cos, row_sin = (jnp.concatenate([row_turn[k]] * tiles, 1) for k in range(2))
    column_cos, column_sin = (column_turn[k, 0:1, :] for k in range(2))
    together = 2 if frames % 2 == 0 else 1

    def visit(step, carry):
        chosen = [step * together + k for k in range(together)]
        spots = [spot(offsets, f, margin, taller) for f in chosen]
        windows = [
            tuple(window_of(padded, plane, spot_of, tiles) for plane in range(2))
            for spot_of in spots
        ]
        probe_real, probe_imag = probe[0], probe[1]
        waves = [
            (
                probe_real * real - probe_imag * imag,
                probe_real * imag + probe_imag * real,
            )
            for real, imag in windows
        ]
        nears = transform_pair(
            waves,
            (row_cos, row_sin),
            (column_cos, column_sin),
            matrices,
            [amplitude[f] for f in chosen],
        )
        for (window_real, window_imag), (near_real, near_imag), spot_of in zip(
            windows, nears, spots
        ):
            sums[0] += window_real * near_real + window_imag * near_imag
            sums[1] += window_real * near_imag - window_imag * near_real
            sums[2] += window_real * window_real + window_imag * window_imag
            add_window(work.at[0], probe_real * near_real + probe_imag * near_imag, spot_of)
            add_window(work.at[1], probe_real * near_imag - probe_imag * near_real, spot_of)
        return carry

    lax.fori_loop(0, frames // together, visit, 0)

    rows = length // blocks
    half_rows = blocks // 2 * 3 * tiles * rows
    for p in range(blocks):
        out, q, base = (
            (kept, p, place[0]) if p < blocks // 2 else (sent, p - blocks // 2, place[3])
        )
        source = pl.multiple_of((base ^ q) * rows, rows)
        for plane in range(3):
            for tile in range(tiles):
                start = ((3 * q + plane) * tiles + tile) * rows
                out[start : start + rows, :] = sums[
                    plane, pl.ds(source, rows), pl.ds(tile * LANES, LANES)
                ]
    kept[half_rows:, :] = total[...]
    sent[half_rows : half_rows + SUBLANES, :] = total[...]
    even = place[2] % 2 == 0
    start = half_rows + SUBLANES
    depth = reach // per
    for plane in range(3):
        canvas = powers if plane == 2 else work.at[plane]
        right = pack_rows(canvas[last, :reach, :], 0, margin)
        left = pack_rows(canvas[0, :reach, :], LANES - margin, margin)
        at = start + plane * depth
        sent[at : at + depth, :] = jnp.where(even, right, left)
        later[plane * depth : (plane + 1) * depth, :] = jnp.where(even, left, right)


def row_edge_kernel(counts, margin, place, work, powers, first, second, first_out, second_out):
    planes = work.shape[0] + 1
    tiles = work.shape[1] - 2
    reach = work.shape[2] - SUBLANES
    depth = first.shape[0] // planes
    even = place[1] % 2 == 0
    for plane in range(planes):
        canvas = powers if plane == planes - 1 else work.at[plane]
        at = pl.ds(plane * depth, depth)
        before, after = neighbours(first[at, :], second[at, :], place[2], counts[1])
        last = LANES // margin - 1
        edges = []
        for begin, chunk, cut in (
            (0, 0, slice(None, margin)),
            (reach - margin, last, slice(depth - margin, None)),
        ):
            parts = [canvas[tile + 1, begin : begin + margin, :] for tile in range(tiles)]
            parts[0] += unpack(before, chunk, 0, margin)[cut]
            parts[-1] += unpack(after, chunk, LANES - margin, margin)[cut]
            edges.append(parts)
        for tile in range(tiles):
            at = pl.ds((plane * tiles + tile) * margin, margin)
            first_out[at, :] = jnp.where(even, edges[1][tile], edges[0][tile])
            second_out[at, :] = jnp.where(even, edges[0][tile], edges[1][tile])


def object_kernel(
    counts, margin, place, field, work, powers, first, second, row_first, row_second, out
):
    planes = work.shape[0] + 1
    tiles = work.shape[1] - 2
    side = field.shape[1]
    depth = first.shape[0] // planes
    for tile in range(tiles):
        lanes = pl.ds(tile * LANES, LANES)
        total = []
        for plane in range(planes):
            canvas = powers if plane == planes - 1 else work.at[plane]
            at = pl.ds((plane * tiles + tile) * margin, margin)
            above, below = neighbours(row_first[at, :], row_second[at, :], place[1], counts[0])
            part = canvas[tile + 1, margin : margin + side, :]
            at = pl.ds(plane * depth, depth)
            before, after = neighbours(first[at, :], second[at, :], place[2], counts[1])
            if tile == 0:
                part += unpack_rows(before, 0, margin)[margin : margin + side]
            if tile == tiles - 1:
                part += unpack_rows(after, LANES - margin, margin)[margin : margin + side]
            part = jnp.concatenate(
                [
                    part[:margin] + above,
                    part[margin : side - margin],
                    part[side - margin :] + below,
                ],
                0,
            )
            total.append(part)
        weight = 1.0 / (total[2] + regular)
        out[0, :, lanes] = (field[0, :, lanes] + total[0]) * weight
        out[1, :, lanes] = (field[1, :, lanes] + total[1]) * weight


def probe_kernel(frame_count, blocks, place, stepped, total, out):
    planes, length, _ = out.shape
    tiles = length // LANES
    rows = length // blocks
    values = stepped[...]
    power = jnp.sum(values * values)
    target = jnp.sum(total[...]) / frame_count
    scale = jnp.sqrt(jnp.full((rows, LANES), target / (power + epsilon), f32))
    for p in range(blocks):
        base, q = (place[0], p) if p < blocks // 2 else (place[3], p - blocks // 2)
        home = pl.multiple_of((base ^ q) * rows, rows)
        for plane in range(planes):
            for tile in range(tiles):
                start = ((planes * p + plane) * tiles + tile) * rows
                out[plane, pl.ds(home, rows), pl.ds(tile * LANES, LANES)] = (
                    values[start : start + rows] * scale
                )


def shape(*dims):
    return jax.ShapeDtypeStruct(dims, f32)


def call(kernel, outputs, scalars=0, operands=0, scratch=(), cost=None):
    vmem = pl.BlockSpec(memory_space=pltpu.VMEM)
    smem = pl.BlockSpec(memory_space=pltpu.SMEM)
    return pl.pallas_call(
        kernel,
        out_shape=outputs,
        in_specs=[smem] * scalars + [vmem] * operands,
        out_specs=jax.tree.map(lambda _: vmem, outputs),
        scratch_shapes=list(scratch),
        cost_estimate=cost,
        compiler_params=pltpu.CompilerParams(vmem_limit_bytes=40 * 1024 * 1024),
    )


def paired(block, axis, first):
    count = lax.axis_size(axis)
    target = list(range(count))
    for i in range(first, count - 1, 2):
        target[i], target[i + 1] = i + 1, i
    return lax.ppermute(block, axis, list(enumerate(target)))


def exchanged(block, orders, step):
    count = lax.axis_size("row") * lax.axis_size("col")
    pairs = [(i, i ^ (1 << orders[i % 2][step])) for i in range(count)]
    return lax.ppermute(block, ("row", "col"), pairs)


def per_device(object_field, probe, amplitudes, positions):
    planes, side, _ = object_field.shape
    length = probe.shape[1]
    margin = MARGIN
    reach = side + 2 * margin
    per = LANES // margin
    tiles = length // LANES
    measured = amplitudes[0, 0]
    frames = measured.shape[0]
    counts = lax.axis_size("row"), lax.axis_size("col")
    row = lax.axis_index("row").astype(jnp.int32)
    col = lax.axis_index("col").astype(jnp.int32)
    index = row * counts[1] + col
    col_bits = (counts[1] - 1).bit_length()
    across = list(range(1, col_bits))
    along = list(range(col_bits, col_bits + (counts[0] - 1).bit_length()))
    orders = (across + along, along + across)
    halvings = 2
    blocks = 2 << halvings
    rows = length // blocks
    homes = [
        sum(((index >> order[k]) & 1) << (halvings - 1 - k) for k in range(halvings))
        for order in orders
    ]
    core = index & 1
    homes[1] += blocks // 2
    place = jnp.stack(
        [
            jnp.where(core == 0, homes[0], homes[1]),
            row,
            col,
            jnp.where(core == 0, homes[1], homes[0]),
        ]
    )

    edge_rows = shape(planes, margin, side)
    inner = shape(planes, side // per, LANES)
    smem = pl.BlockSpec(memory_space=pltpu.SMEM)
    vmem = pl.BlockSpec(memory_space=pltpu.VMEM)
    field, rows_first, rows_second, inner_first, inner_second = pl.pallas_call(
        begin_kernel,
        out_shape=(shape(*object_field.shape), edge_rows, edge_rows, inner, inner),
        in_specs=[smem, pl.BlockSpec(memory_space=pl.ANY)],
        out_specs=(vmem,) * 5,
        scratch_shapes=[pltpu.SemaphoreType.DMA],
        compiler_params=pltpu.CompilerParams(vmem_limit_bytes=16 * 1024 * 1024),
    )(place, object_field)
    rows_first = paired(rows_first, "row", 0)
    rows_second = paired(rows_second, "row", 1)
    ordered, total, powers = call(
        functools.partial(amplitude_kernel, margin),
        (
            shape(frames, 2 * length, length // 2),
            shape(SUBLANES, LANES),
            shape(side // LANES + 2, reach + SUBLANES, LANES),
        ),
        scalars=1,
        operands=2,
        scratch=(pltpu.VMEM((frames, 2, length, length // 2), f32),),
        cost=pl.CostEstimate(flops=10**9, bytes_accessed=2 * measured.size * 4, transcendentals=0),
    )(positions[0, 0], measured, probe)
    packed = shape(planes, reach // per, LANES)
    above, below, columns_first, columns_second = call(
        functools.partial(corner_kernel, counts),
        (edge_rows, edge_rows, packed, packed),
        scalars=1,
        operands=4,
    )(place, rows_first, rows_second, inner_first, inner_second)
    columns_first = paired(columns_first, "col", 0)
    columns_second = paired(columns_second, "col", 1)

    matrices, row_turn, column_turn = tables(length)
    half_rows = blocks // 2 * 3 * tiles * rows
    depth = 3 * reach // per
    work, kept, sent, edge = call(
        functools.partial(frames_kernel, counts, blocks),
        (
            shape(2, side // LANES + 2, reach + SUBLANES, LANES),
            shape(half_rows + SUBLANES, LANES),
            shape(half_rows + SUBLANES + depth, LANES),
            shape(depth, LANES),
        ),
        scalars=2,
        operands=12,
        scratch=(
            pltpu.VMEM((2, side // LANES + 2, reach + SUBLANES, LANES), f32),
            pltpu.VMEM((3, length, length), f32),
        ),
    )(
        place,
        positions[0, 0],
        field,
        above,
        below,
        columns_first,
        columns_second,
        probe,
        ordered,
        total,
        powers,
        jnp.asarray(matrices),
        jnp.asarray(row_turn),
        jnp.asarray(column_turn),
    )

    arrived = paired(sent, "col", 0)
    current = kept + arrived[: half_rows + SUBLANES]
    first = arrived[half_rows + SUBLANES :]
    second = paired(edge, "col", 1)
    for step in range(len(orders[0])):
        if step == 1:
            current, second = lax.optimization_barrier((current, second))
            out = shape(3 * tiles * margin, LANES)
            row_first, row_second = call(
                functools.partial(row_edge_kernel, counts, margin), (out, out), scalars=1, operands=4
            )(
                place, work, powers, first, second
            )
            row_first = paired(row_first, "row", 0)
            row_second = paired(row_second, "row", 1)
        if step == 3:
            current, row_first, row_second = lax.optimization_barrier(
                (current, row_first, row_second)
            )
        count = current.shape[0] - SUBLANES
        if step < halvings:
            sent = jnp.concatenate([current[count // 2 : count], current[count:]], 0)
            kept = jnp.concatenate([current[: count // 2], current[count:]], 0)
        else:
            kept = sent = current
        current = kept + exchanged(sent, orders, step)
    size = tiles * rows
    weight = current[2 * size : 3 * size]
    stepped = current[: 2 * size] / jnp.concatenate([weight, weight], 0)
    object_next = call(
        functools.partial(object_kernel, counts, margin),
        shape(*object_field.shape),
        scalars=1,
        operands=7,
    )(
        place, field, work, powers, first, second, row_first, row_second
    )
    for step in reversed(range(halvings)):
        stepped = jnp.concatenate([stepped, exchanged(stepped, orders, step)], 0)
    stepped = jnp.concatenate([stepped, paired(stepped, "col", 0)], 0)
    frame_count = frames * counts[0] * counts[1]
    probe_next = call(
        functools.partial(probe_kernel, frame_count, blocks),
        shape(*probe.shape),
        scalars=1,
        operands=2,
    )(place, stepped, current[3 * size :])
    return (object_next, probe_next)


def solution(mesh):
    return jax.shard_map(
        per_device,
        mesh=mesh,
        in_specs=(
            P(None, "row", "col"),
            P(),
            P("row", "col", None, None, None),
            P("row", "col", None, None),
        ),
        out_specs=(P(None, "row", "col"), P()),
        check_vma=False,
    )
```

```python
import functools
import math

import jax
import jax.numpy as jnp
import numpy as np
from jax import lax
from jax.experimental import pallas as pl
from jax.experimental.pallas import tpu as pltpu
from jax.sharding import PartitionSpec as P

MARGIN = 32
LANES = 128
SUBLANES = 8

smoothing = 0.1
regular = 1.0
epsilon = 1e-06

f32 = jnp.float32
bf16 = jnp.bfloat16


def tables(length):
    half = length // 2
    scaling = 1.0 / math.sqrt(length)
    k = np.arange(half)
    phases = (k[:, None] * k[None, :] % half) * (2.0 * math.pi / half)
    cosine, sine = np.cos(phases) * scaling, np.sin(phases) * scaling
    right = np.block([[cosine, -sine], [sine, cosine]])
    left = np.block([[cosine, sine], [-sine, cosine]])
    both = np.stack([left, right]).astype(np.float32)
    high = both.astype(bf16)
    low = (both - high.astype(np.float32)).astype(bf16)
    matrices = np.stack([high, low], 1)
    angle = k * (2.0 * math.pi / length)
    turn = np.stack([np.cos(angle), np.sin(angle)]).astype(np.float32)
    rows = np.broadcast_to(turn[:, :, None], (2, half, LANES)).copy()
    columns = np.broadcast_to(turn[:, None, :], (2, SUBLANES, half)).copy()
    return matrices, rows, columns


def split(x):
    high = x.astype(bf16)
    return high, (x - high.astype(f32)).astype(bf16)


def dot(a, b):
    return jnp.dot(a, b, preferred_element_type=f32)


def times_matrix(data, matrix):
    high, low = split(data)
    return dot(
        jnp.concatenate([high, low, high], 1),
        jnp.concatenate([matrix[0], matrix[0], matrix[1]], 0),
    )


def matrix_times(matrix, data):
    high, low = split(data)
    return dot(
        jnp.concatenate([matrix[0], matrix[0], matrix[1]], 1),
        jnp.concatenate([high, low, high], 0),
    )


def turned(real, imag, cosine, sine):
    return real * cosine - imag * sine, real * sine + imag * cosine


def pack(chunks, lane, width):
    place = lax.broadcasted_iota(jnp.int32, chunks[0].shape, 1) // width
    out = jnp.zeros_like(chunks[0])
    for q, chunk in enumerate(chunks):
        shift = (q * width - lane) % LANES
        moved = pltpu.roll(chunk, shift, 1) if shift else chunk
        out = jnp.where(place == q, moved, out)
    return out


def pack_rows(rows, lane, width):
    count = rows.shape[0] * width // LANES
    return pack([rows[q : q + count] for q in range(0, rows.shape[0], count)], lane, width)


def unpack(packed, q, lane, width):
    shift = (lane - q * width) % LANES
    moved = pltpu.roll(packed, shift, 1) if shift else packed
    place = lax.broadcasted_iota(jnp.int32, packed.shape, 1)
    return jnp.where((place >= lane) & (place < lane + width), moved, 0.0)


def unpack_rows(packed, lane, width):
    return jnp.concatenate([unpack(packed, q, lane, width) for q in range(LANES // width)], 0)


def lifted(tile, shift):
    groups = tile.shape[0] // SUBLANES
    turned_rows = pltpu.roll(
        tile.reshape(groups, SUBLANES, LANES), lax.rem(SUBLANES - shift, SUBLANES), 1
    )
    place = lax.broadcasted_iota(jnp.int32, (groups - 1, SUBLANES, LANES), 1)
    picked = jnp.where(place < SUBLANES - shift, turned_rows[:-1], turned_rows[1:])
    return picked.reshape((groups - 1) * SUBLANES, LANES)


def lowered(tile, shift):
    groups = tile.shape[0] // SUBLANES
    moved = pltpu.roll(tile.reshape(groups, SUBLANES, LANES), shift, 1)
    none = jnp.zeros((1, SUBLANES, LANES), f32)
    place = lax.broadcasted_iota(jnp.int32, (groups + 1, SUBLANES, LANES), 1)
    picked = jnp.where(
        place >= shift, jnp.concatenate([moved, none], 0), jnp.concatenate([none, moved], 0)
    )
    return picked.reshape((groups + 1) * SUBLANES, LANES)


def spot(offsets, f, margin, taller):
    a, b = offsets[f, 0], offsets[f, 1]
    shift = lax.rem(a, SUBLANES)
    lane = b + LANES - margin
    tile = lane // LANES
    return pl.ds(pl.multiple_of(a - shift, SUBLANES), taller), shift, tile, lane - tile * LANES


def window_of(padded, plane, spot_of, tiles):
    at, shift, base, lane = spot_of
    moved = [
        pltpu.roll(padded[plane, base + t, at, :], lax.rem(LANES - lane, LANES), 1)
        for t in range(tiles + 1)
    ]
    place = lax.broadcasted_iota(jnp.int32, moved[0].shape, 1)
    parts = [
        lifted(jnp.where(place < LANES - lane, moved[t], moved[t + 1]), shift)
        for t in range(tiles)
    ]
    return jnp.concatenate(parts, 1)


def add_window(work, term, spot_of):
    at, shift, base, lane = spot_of
    tiles = term.shape[1] // LANES
    moved = [
        pltpu.roll(lowered(term[:, t * LANES : (t + 1) * LANES], shift), lane, 1)
        for t in range(tiles)
    ]
    none = jnp.zeros_like(moved[0])
    place = lax.broadcasted_iota(jnp.int32, none.shape, 1)
    for t in range(tiles + 1):
        here = moved[t] if t < tiles else none
        before = moved[t - 1] if t else none
        work[base + t, at, :] += jnp.where(place >= lane, here, before)


def neighbours(first, second, index, count):
    even = index % 2 == 0
    before = jnp.where(even, second, first)
    after = jnp.where(even, first, second)
    return jnp.where(index > 0, before, 0.0), jnp.where(index < count - 1, after, 0.0)


def begin_kernel(place, source, field, rows_first, rows_second, columns_first, columns_second, sem):
    copy = pltpu.make_async_copy(source, field, sem)
    copy.start()
    copy.wait()
    planes, side, _ = field.shape
    margin = rows_first.shape[1]
    even_row = place[1] % 2 == 0
    even_column = place[2] % 2 == 0
    for plane in range(planes):
        top, bottom = field[plane, :margin], field[plane, side - margin :]
        rows_first[plane] = jnp.where(even_row, bottom, top)
        rows_second[plane] = jnp.where(even_row, top, bottom)
        left = pack_rows(field[plane, :, :LANES], 0, margin)
        right = pack_rows(field[plane, :, side - LANES :], LANES - margin, margin)
        columns_first[plane] = jnp.where(even_column, right, left)
        columns_second[plane] = jnp.where(even_column, left, right)


def amplitude_kernel(margin, offsets, amplitude, probe, sorted_out, total_out, powers, held):
    frames, length, _ = amplitude.shape
    half = length // 2
    power = probe[0] * probe[0] + probe[1] * probe[1]
    powers[...] = jnp.zeros(powers.shape, f32)
    for f in range(frames):
        add_window(powers, power, spot(offsets, f, margin, length + SUBLANES))
    row = lax.broadcasted_iota(jnp.int32, (length, length), 0)
    column = lax.broadcasted_iota(jnp.int32, (length, length), 1)
    source = jnp.where(column < half, 2 * column, 2 * (column - half) + 1)
    order = jnp.where(row == source, 1.0, 0.0).astype(bf16)
    total = jnp.zeros((SUBLANES, length), f32)
    for f in range(frames):
        values = amplitude[f]
        total += jnp.sum((values * values).reshape(length // SUBLANES, SUBLANES, length), 0)
        high = values.astype(bf16)
        rest = values - high.astype(f32)
        middle = rest.astype(bf16)
        low = (rest - middle.astype(f32)).astype(bf16)
        placed = dot(high, order) + (dot(middle, order) + dot(low, order))
        for parity in range(2):
            held[f, parity] = placed[:, parity * half : (parity + 1) * half]
            for start in range(2):
                at = 2 * parity + start
                sorted_out[f, at * half : (at + 1) * half, :] = held[
                    f, parity, pl.ds(start, half, stride=2), :
                ]
    total_out[...] = sum(total[:, t * LANES : (t + 1) * LANES] for t in range(length // LANES))


def corner_kernel(
    counts, place, first, second, inner_first, inner_second, above, below, first_out, second_out
):
    planes, margin, side = first.shape
    inner = inner_first.shape[1]
    even = place[2] % 2 == 0
    for plane in range(planes):
        before, after = neighbours(first[plane], second[plane], place[1], counts[0])
        above[plane] = before
        below[plane] = after
        both = jnp.concatenate([before, after], 0)
        left = pack_rows(both[:, :LANES], 0, margin)
        right = pack_rows(both[:, side - LANES :], LANES - margin, margin)
        first_out[plane, :inner] = inner_first[plane]
        first_out[plane, inner:] = jnp.where(even, right, left)
        second_out[plane, :inner] = inner_second[plane]
        second_out[plane, inner:] = jnp.where(even, left, right)


def transform_pair(waves, row_turn, column_turn, matrices, amplitudes):
    length = waves[0][0].shape[0]
    half = length // 2
    row_cos, row_sin = row_turn
    column_cos, column_sin = column_turn

    mixed = []
    for real, imag in waves:
        odd = turned(real[:half] - real[half:], imag[:half] - imag[half:], row_cos, -row_sin)
        stacked = jnp.concatenate(
            [
                jnp.concatenate([real[:half] + real[half:], imag[:half] + imag[half:]], 0),
                jnp.concatenate(odd, 0),
            ],
            1,
        )
        mixed.append(matrix_times(matrices.at[0], stacked))

    far = []
    for value in mixed:
        evens, odds = [], []
        for parity in range(2):
            part = value[:, parity * length : (parity + 1) * length]
            real, imag = part[:half], part[half:]
            evens.append(
                jnp.concatenate(
                    [real[:, :half] + real[:, half:], imag[:, :half] + imag[:, half:]], 1
                )
            )
            odd = turned(
                real[:, :half] - real[:, half:],
                imag[:, :half] - imag[:, half:],
                column_cos,
                -column_sin,
            )
            odds.append(jnp.concatenate(odd, 1))
        far.append(times_matrix(jnp.concatenate(evens + odds, 0), matrices.at[1]))

    turned_back = []
    for value, amplitude in zip(far, amplitudes):
        real, imag = value[:, :half], value[:, half:]
        factor = amplitude * lax.rsqrt(real * real + imag * imag + smoothing)
        corrected = jnp.concatenate([real * factor, imag * factor], 1)
        turned_back.append(times_matrix(corrected, matrices.at[0]))

    near = []
    for value in turned_back:
        even, odd = value[:length], value[length:]
        odd_real, odd_imag = turned(odd[:, :half], odd[:, half:], column_cos, column_sin)
        even_real, even_imag = even[:, :half], even[:, half:]
        real = jnp.concatenate([even_real + odd_real, even_real - odd_real], 1)
        imag = jnp.concatenate([even_imag + odd_imag, even_imag - odd_imag], 1)
        stacked = jnp.concatenate(
            [
                jnp.concatenate([real[:half], imag[:half]], 0),
                jnp.concatenate([real[half:], imag[half:]], 0),
            ],
            1,
        )
        near.append(matrix_times(matrices.at[1], stacked))

    results = []
    for value in near:
        even, odd = value[:, :length], value[:, length:]
        odd_real, odd_imag = turned(odd[:half], odd[half:], row_cos, row_sin)
        results.append(
            (
                jnp.concatenate([even[:half] + odd_real, even[:half] - odd_real], 0),
                jnp.concatenate([even[half:] + odd_imag, even[half:] - odd_imag], 0),
            )
        )
    return results


def frames_kernel(
    counts,
    blocks,
    place,
    offsets,
    field,
    above,
    below,
    columns_first,
    columns_second,
    probe,
    amplitude,
    total,
    powers,
    matrices,
    row_turn,
    column_turn,
    work,
    kept,
    sent,
    later,
    padded,
    sums,
):
    frames = amplitude.shape[0]
    length = probe.shape[1]
    side = field.shape[1]
    margin = above.shape[1]
    reach = side + 2 * margin
    taller = length + SUBLANES
    per = LANES // margin
    inner = side // per
    tiles = length // LANES
    last = side // LANES + 1

    for plane in range(2):
        for tile in range(side // LANES):
            lanes = pl.ds(tile * LANES, LANES)
            padded[plane, tile + 1, :margin, :] = above[plane, :, lanes]
            padded[plane, tile + 1, margin : margin + side, :] = field[plane, :, lanes]
            padded[plane, tile + 1, margin + side : reach, :] = below[plane, :, lanes]
        left, right = neighbours(
            columns_first[plane], columns_second[plane], place[2], counts[1]
        )
        for tile, packed, lane in ((0, left, LANES - margin), (last, right, 0)):
            corners = unpack_rows(packed[inner:], lane, margin)
            padded[plane, tile, :margin, :] = corners[:margin]
            padded[plane, tile, margin : margin + side, :] = unpack_rows(
                packed[:inner], lane, margin
            )
            padded[plane, tile, margin + side : reach, :] = corners[margin:]
        padded[plane, :, reach:, :] = jnp.zeros((last + 1, SUBLANES, LANES), f32)
    work[...] = jnp.zeros(work.shape, f32)
    first = jnp.where(place[1] + place[2] == 0, 1.0, 0.0).astype(f32)
    sums[0] = probe[0] * first
    sums[1] = probe[1] * first
    sums[2] = jnp.full((length, length), regular, f32) * first

    row_cos, row_sin = (jnp.concatenate([row_turn[k]] * tiles, 1) for k in range(2))
    column_cos, column_sin = (column_turn[k, 0:1, :] for k in range(2))
    together = 2 if frames % 2 == 0 else 1

    def visit(step, carry):
        chosen = [step * together + k for k in range(together)]
        spots = [spot(offsets, f, margin, taller) for f in chosen]
        windows = [
            tuple(window_of(padded, plane, spot_of, tiles) for plane in range(2))
            for spot_of in spots
        ]
        probe_real, probe_imag = probe[0], probe[1]
        waves = [
            (
                probe_real * real - probe_imag * imag,
                probe_real * imag + probe_imag * real,
            )
            for real, imag in windows
        ]
        nears = transform_pair(
            waves,
            (row_cos, row_sin),
            (column_cos, column_sin),
            matrices,
            [amplitude[f] for f in chosen],
        )
        for (window_real, window_imag), (near_real, near_imag), spot_of in zip(
            windows, nears, spots
        ):
            sums[0] += window_real * near_real + window_imag * near_imag
            sums[1] += window_real * near_imag - window_imag * near_real
            sums[2] += window_real * window_real + window_imag * window_imag
            add_window(work.at[0], probe_real * near_real + probe_imag * near_imag, spot_of)
            add_window(work.at[1], probe_real * near_imag - probe_imag * near_real, spot_of)
        return carry

    lax.fori_loop(0, frames // together, visit, 0)

    rows = length // blocks
    half_rows = blocks // 2 * 3 * tiles * rows
    for p in range(blocks):
        out, q, base = (
            (kept, p, place[0]) if p < blocks // 2 else (sent, p - blocks // 2, place[3])
        )
        source = pl.multiple_of((base ^ q) * rows, rows)
        for plane in range(3):
            for tile in range(tiles):
                start = ((3 * q + plane) * tiles + tile) * rows
                out[start : start + rows, :] = sums[
                    plane, pl.ds(source, rows), pl.ds(tile * LANES, LANES)
                ]
    kept[half_rows:, :] = total[...]
    sent[half_rows : half_rows + SUBLANES, :] = total[...]
    even = place[2] % 2 == 0
    start = half_rows + SUBLANES
    depth = reach // per
    for plane in range(3):
        canvas = powers if plane == 2 else work.at[plane]
        right = pack_rows(canvas[last, :reach, :], 0, margin)
        left = pack_rows(canvas[0, :reach, :], LANES - margin, margin)
        at = start + plane * depth
        sent[at : at + depth, :] = jnp.where(even, right, left)
        later[plane * depth : (plane + 1) * depth, :] = jnp.where(even, left, right)


def row_edge_kernel(counts, margin, place, work, powers, first, second, first_out, second_out):
    planes = work.shape[0] + 1
    tiles = work.shape[1] - 2
    reach = work.shape[2] - SUBLANES
    depth = first.shape[0] // planes
    even = place[1] % 2 == 0
    for plane in range(planes):
        canvas = powers if plane == planes - 1 else work.at[plane]
        at = pl.ds(plane * depth, depth)
        before, after = neighbours(first[at, :], second[at, :], place[2], counts[1])
        last = LANES // margin - 1
        edges = []
        for begin, chunk, cut in (
            (0, 0, slice(None, margin)),
            (reach - margin, last, slice(depth - margin, None)),
        ):
            parts = [canvas[tile + 1, begin : begin + margin, :] for tile in range(tiles)]
            parts[0] += unpack(before, chunk, 0, margin)[cut]
            parts[-1] += unpack(after, chunk, LANES - margin, margin)[cut]
            edges.append(parts)
        for tile in range(tiles):
            at = pl.ds((plane * tiles + tile) * margin, margin)
            first_out[at, :] = jnp.where(even, edges[1][tile], edges[0][tile])
            second_out[at, :] = jnp.where(even, edges[0][tile], edges[1][tile])


def object_kernel(
    counts, margin, place, field, work, powers, first, second, row_first, row_second, out
):
    planes = work.shape[0] + 1
    tiles = work.shape[1] - 2
    side = field.shape[1]
    depth = first.shape[0] // planes
    for tile in range(tiles):
        lanes = pl.ds(tile * LANES, LANES)
        total = []
        for plane in range(planes):
            canvas = powers if plane == planes - 1 else work.at[plane]
            at = pl.ds((plane * tiles + tile) * margin, margin)
            above, below = neighbours(row_first[at, :], row_second[at, :], place[1], counts[0])
            part = canvas[tile + 1, margin : margin + side, :]
            at = pl.ds(plane * depth, depth)
            before, after = neighbours(first[at, :], second[at, :], place[2], counts[1])
            if tile == 0:
                part += unpack_rows(before, 0, margin)[margin : margin + side]
            if tile == tiles - 1:
                part += unpack_rows(after, LANES - margin, margin)[margin : margin + side]
            part = jnp.concatenate(
                [
                    part[:margin] + above,
                    part[margin : side - margin],
                    part[side - margin :] + below,
                ],
                0,
            )
            total.append(part)
        weight = 1.0 / (total[2] + regular)
        out[0, :, lanes] = (field[0, :, lanes] + total[0]) * weight
        out[1, :, lanes] = (field[1, :, lanes] + total[1]) * weight


def probe_kernel(frame_count, blocks, place, stepped, total, out):
    planes, length, _ = out.shape
    tiles = length // LANES
    rows = length // blocks
    values = stepped[...]
    power = jnp.sum(values * values)
    target = jnp.sum(total[...]) / frame_count
    scale = jnp.sqrt(jnp.full((rows, LANES), target / (power + epsilon), f32))
    for p in range(blocks):
        base, q = (place[0], p) if p < blocks // 2 else (place[3], p - blocks // 2)
        home = pl.multiple_of((base ^ q) * rows, rows)
        for plane in range(planes):
            for tile in range(tiles):
                start = ((planes * p + plane) * tiles + tile) * rows
                out[plane, pl.ds(home, rows), pl.ds(tile * LANES, LANES)] = (
                    values[start : start + rows] * scale
                )


def shape(*dims):
    return jax.ShapeDtypeStruct(dims, f32)


def call(kernel, outputs, scalars=0, operands=0, scratch=(), cost=None):
    vmem = pl.BlockSpec(memory_space=pltpu.VMEM)
    smem = pl.BlockSpec(memory_space=pltpu.SMEM)
    return pl.pallas_call(
        kernel,
        out_shape=outputs,
        in_specs=[smem] * scalars + [vmem] * operands,
        out_specs=jax.tree.map(lambda _: vmem, outputs),
        scratch_shapes=list(scratch),
        cost_estimate=cost,
        compiler_params=pltpu.CompilerParams(vmem_limit_bytes=40 * 1024 * 1024),
    )


def paired(block, axis, first):
    count = lax.axis_size(axis)
    target = list(range(count))
    for i in range(first, count - 1, 2):
        target[i], target[i + 1] = i + 1, i
    return lax.ppermute(block, axis, list(enumerate(target)))


def exchanged(block, orders, step):
    count = lax.axis_size("row") * lax.axis_size("col")
    pairs = [(i, i ^ (1 << orders[i % 2][step])) for i in range(count)]
    return lax.ppermute(block, ("row", "col"), pairs)


def per_device(object_field, probe, amplitudes, positions):
    planes, side, _ = object_field.shape
    length = probe.shape[1]
    margin = MARGIN
    reach = side + 2 * margin
    per = LANES // margin
    tiles = length // LANES
    measured = amplitudes[0, 0]
    frames = measured.shape[0]
    counts = lax.axis_size("row"), lax.axis_size("col")
    row = lax.axis_index("row").astype(jnp.int32)
    col = lax.axis_index("col").astype(jnp.int32)
    index = row * counts[1] + col
    col_bits = (counts[1] - 1).bit_length()
    across = list(range(1, col_bits))
    along = list(range(col_bits, col_bits + (counts[0] - 1).bit_length()))
    orders = (across + along, along + across)
    halvings = 2
    blocks = 2 << halvings
    rows = length // blocks
    homes = [
        sum(((index >> order[k]) & 1) << (halvings - 1 - k) for k in range(halvings))
        for order in orders
    ]
    core = index & 1
    homes[1] += blocks // 2
    place = jnp.stack(
        [
            jnp.where(core == 0, homes[0], homes[1]),
            row,
            col,
            jnp.where(core == 0, homes[1], homes[0]),
        ]
    )

    edge_rows = shape(planes, margin, side)
    inner = shape(planes, side // per, LANES)
    smem = pl.BlockSpec(memory_space=pltpu.SMEM)
    vmem = pl.BlockSpec(memory_space=pltpu.VMEM)
    field, rows_first, rows_second, inner_first, inner_second = pl.pallas_call(
        begin_kernel,
        out_shape=(shape(*object_field.shape), edge_rows, edge_rows, inner, inner),
        in_specs=[smem, pl.BlockSpec(memory_space=pl.ANY)],
        out_specs=(vmem,) * 5,
        scratch_shapes=[pltpu.SemaphoreType.DMA],
        compiler_params=pltpu.CompilerParams(vmem_limit_bytes=16 * 1024 * 1024),
    )(place, object_field)
    rows_second = paired(rows_second, "row", 1)
    rows_first = paired(rows_first, "row", 0)
    ordered, total, powers = call(
        functools.partial(amplitude_kernel, margin),
        (
            shape(frames, 2 * length, length // 2),
            shape(SUBLANES, LANES),
            shape(side // LANES + 2, reach + SUBLANES, LANES),
        ),
        scalars=1,
        operands=2,
        scratch=(pltpu.VMEM((frames, 2, length, length // 2), f32),),
        cost=pl.CostEstimate(flops=10**9, bytes_accessed=2 * measured.size * 4, transcendentals=0),
    )(positions[0, 0], measured, probe)
    rows_first, rows_second, ordered, powers = lax.optimization_barrier(
        (rows_first, rows_second, ordered, powers)
    )
    packed = shape(planes, reach // per, LANES)
    above, below, columns_first, columns_second = call(
        functools.partial(corner_kernel, counts),
        (edge_rows, edge_rows, packed, packed),
        scalars=1,
        operands=4,
    )(place, rows_first, rows_second, inner_first, inner_second)
    columns_second = paired(columns_second, "col", 1)
    columns_first = paired(columns_first, "col", 0)

    matrices, row_turn, column_turn = tables(length)
    half_rows = blocks // 2 * 3 * tiles * rows
    depth = 3 * reach // per
    work, kept, sent, edge = call(
        functools.partial(frames_kernel, counts, blocks),
        (
            shape(2, side // LANES + 2, reach + SUBLANES, LANES),
            shape(half_rows + SUBLANES, LANES),
            shape(half_rows + SUBLANES + depth, LANES),
            shape(depth, LANES),
        ),
        scalars=2,
        operands=12,
        scratch=(
            pltpu.VMEM((2, side // LANES + 2, reach + SUBLANES, LANES), f32),
            pltpu.VMEM((3, length, length), f32),
        ),
    )(
        place,
        positions[0, 0],
        field,
        above,
        below,
        columns_first,
        columns_second,
        probe,
        ordered,
        total,
        powers,
        jnp.asarray(matrices),
        jnp.asarray(row_turn),
        jnp.asarray(column_turn),
    )

    arrived = paired(sent, "col", 0)
    current = kept + arrived[: half_rows + SUBLANES]
    first = arrived[half_rows + SUBLANES :]
    second = paired(edge, "col", 1)
    out = shape(3 * tiles * margin, LANES)
    row_first, row_second = call(
        functools.partial(row_edge_kernel, counts, margin), (out, out), scalars=1, operands=4
    )(place, work, powers, first, second)
    for step in range(len(orders[0])):
        if step == 2:
            current, row_first, row_second = lax.optimization_barrier(
                (current, row_first, row_second)
            )
            row_second = paired(row_second, "row", 1)
            row_first = paired(row_first, "row", 0)
        count = current.shape[0] - SUBLANES
        if step < halvings:
            sent = jnp.concatenate([current[count // 2 : count], current[count:]], 0)
            kept = jnp.concatenate([current[: count // 2], current[count:]], 0)
        else:
            kept = sent = current
        current = kept + exchanged(sent, orders, step)
    size = tiles * rows
    weight = current[2 * size : 3 * size]
    stepped = current[: 2 * size] / jnp.concatenate([weight, weight], 0)
    stepped, row_first, row_second = lax.optimization_barrier((stepped, row_first, row_second))
    object_next = call(
        functools.partial(object_kernel, counts, margin),
        shape(*object_field.shape),
        scalars=1,
        operands=7,
    )(place, field, work, powers, first, second, row_first, row_second)
    for step in reversed(range(halvings)):
        stepped = jnp.concatenate([stepped, exchanged(stepped, orders, step)], 0)
    stepped = jnp.concatenate([stepped, paired(stepped, "col", 0)], 0)
    frame_count = frames * counts[0] * counts[1]
    probe_next = call(
        functools.partial(probe_kernel, frame_count, blocks),
        shape(*probe.shape),
        scalars=1,
        operands=2,
    )(place, stepped, current[3 * size :])
    return (object_next, probe_next)


def solution(mesh):
    return jax.shard_map(
        per_device,
        mesh=mesh,
        in_specs=(
            P(None, "row", "col"),
            P(),
            P("row", "col", None, None, None),
            P("row", "col", None, None),
        ),
        out_specs=(P(None, "row", "col"), P()),
        check_vma=False,
    )
```

```python
import functools
import math

import jax
import jax.numpy as jnp
import numpy as np
from jax import lax
from jax.experimental import pallas as pl
from jax.experimental.pallas import tpu as pltpu
from jax.sharding import PartitionSpec as P

MARGIN = 32
LANES = 128
SUBLANES = 8

smoothing = 0.1
regular = 1.0
epsilon = 1e-06

f32 = jnp.float32
bf16 = jnp.bfloat16


def tables(length):
    half = length // 2
    scaling = 1.0 / math.sqrt(length)
    k = np.arange(half)
    phases = (k[:, None] * k[None, :] % half) * (2.0 * math.pi / half)
    cosine, sine = np.cos(phases) * scaling, np.sin(phases) * scaling
    right = np.block([[cosine, -sine], [sine, cosine]])
    left = np.block([[cosine, sine], [-sine, cosine]])
    both = np.stack([left, right]).astype(np.float32)
    high = both.astype(bf16)
    low = (both - high.astype(np.float32)).astype(bf16)
    matrices = np.stack([high, low], 1)
    angle = k * (2.0 * math.pi / length)
    turn = np.stack([np.cos(angle), np.sin(angle)]).astype(np.float32)
    rows = np.broadcast_to(turn[:, :, None], (2, half, LANES)).copy()
    columns = np.broadcast_to(turn[:, None, :], (2, SUBLANES, half)).copy()
    return matrices, rows, columns


def split(x):
    high = x.astype(bf16)
    return high, (x - high.astype(f32)).astype(bf16)


def dot(a, b):
    return jnp.dot(a, b, preferred_element_type=f32)


def times_matrix(data, matrix):
    high, low = split(data)
    return dot(
        jnp.concatenate([high, low, high], 1),
        jnp.concatenate([matrix[0], matrix[0], matrix[1]], 0),
    )


def matrix_times(matrix, data):
    high, low = split(data)
    return dot(
        jnp.concatenate([matrix[0], matrix[0], matrix[1]], 1),
        jnp.concatenate([high, low, high], 0),
    )


def turned(real, imag, cosine, sine):
    return real * cosine - imag * sine, real * sine + imag * cosine


def pack(chunks, lane, width):
    place = lax.broadcasted_iota(jnp.int32, chunks[0].shape, 1) // width
    out = jnp.zeros_like(chunks[0])
    for q, chunk in enumerate(chunks):
        shift = (q * width - lane) % LANES
        moved = pltpu.roll(chunk, shift, 1) if shift else chunk
        out = jnp.where(place == q, moved, out)
    return out


def pack_rows(rows, lane, width):
    count = rows.shape[0] * width // LANES
    return pack([rows[q : q + count] for q in range(0, rows.shape[0], count)], lane, width)


def unpack(packed, q, lane, width):
    shift = (lane - q * width) % LANES
    moved = pltpu.roll(packed, shift, 1) if shift else packed
    place = lax.broadcasted_iota(jnp.int32, packed.shape, 1)
    return jnp.where((place >= lane) & (place < lane + width), moved, 0.0)


def unpack_rows(packed, lane, width):
    return jnp.concatenate([unpack(packed, q, lane, width) for q in range(LANES // width)], 0)


def lifted(tile, shift):
    groups = tile.shape[0] // SUBLANES
    turned_rows = pltpu.roll(
        tile.reshape(groups, SUBLANES, LANES), lax.rem(SUBLANES - shift, SUBLANES), 1
    )
    place = lax.broadcasted_iota(jnp.int32, (groups - 1, SUBLANES, LANES), 1)
    picked = jnp.where(place < SUBLANES - shift, turned_rows[:-1], turned_rows[1:])
    return picked.reshape((groups - 1) * SUBLANES, LANES)


def lowered(tile, shift):
    groups = tile.shape[0] // SUBLANES
    moved = pltpu.roll(tile.reshape(groups, SUBLANES, LANES), shift, 1)
    none = jnp.zeros((1, SUBLANES, LANES), f32)
    place = lax.broadcasted_iota(jnp.int32, (groups + 1, SUBLANES, LANES), 1)
    picked = jnp.where(
        place >= shift, jnp.concatenate([moved, none], 0), jnp.concatenate([none, moved], 0)
    )
    return picked.reshape((groups + 1) * SUBLANES, LANES)


def spot(offsets, f, margin, taller):
    a, b = offsets[f, 0], offsets[f, 1]
    shift = lax.rem(a, SUBLANES)
    lane = b + LANES - margin
    tile = lane // LANES
    return pl.ds(pl.multiple_of(a - shift, SUBLANES), taller), shift, tile, lane - tile * LANES


def window_of(padded, plane, spot_of, tiles):
    at, shift, base, lane = spot_of
    moved = [
        pltpu.roll(padded[plane, base + t, at, :], lax.rem(LANES - lane, LANES), 1)
        for t in range(tiles + 1)
    ]
    place = lax.broadcasted_iota(jnp.int32, moved[0].shape, 1)
    parts = [
        lifted(jnp.where(place < LANES - lane, moved[t], moved[t + 1]), shift)
        for t in range(tiles)
    ]
    return jnp.concatenate(parts, 1)


def add_window(work, term, spot_of):
    at, shift, base, lane = spot_of
    tiles = term.shape[1] // LANES
    moved = [
        pltpu.roll(lowered(term[:, t * LANES : (t + 1) * LANES], shift), lane, 1)
        for t in range(tiles)
    ]
    none = jnp.zeros_like(moved[0])
    place = lax.broadcasted_iota(jnp.int32, none.shape, 1)
    for t in range(tiles + 1):
        here = moved[t] if t < tiles else none
        before = moved[t - 1] if t else none
        work[base + t, at, :] += jnp.where(place >= lane, here, before)


def neighbours(first, second, index, count):
    even = index % 2 == 0
    before = jnp.where(even, second, first)
    after = jnp.where(even, first, second)
    return jnp.where(index > 0, before, 0.0), jnp.where(index < count - 1, after, 0.0)


def begin_kernel(place, source, rows_first, rows_second, sems):
    margin = rows_first.shape[1]
    last = source.shape[1] - margin
    odd = place[1] % 2
    copies = [
        pltpu.make_async_copy(
            source.at[:, pl.ds(pl.multiple_of(start, SUBLANES), margin), :], target, sems.at[k]
        )
        for k, (start, target) in enumerate(
            ((last - odd * last, rows_first), (odd * last, rows_second))
        )
    ]
    for copy in copies:
        copy.start()
    for copy in copies:
        copy.wait()


def prepare_kernel(
    margin,
    place,
    offsets,
    source,
    measured,
    light,
    field,
    probe,
    columns_first,
    columns_second,
    sorted_out,
    total_out,
    powers,
    amplitude,
    held,
    sems,
):
    frames, length, _ = amplitude.shape
    half = length // 2
    planes, side, _ = field.shape
    fetches = [
        pltpu.make_async_copy(light, probe, sems.at[0]),
        pltpu.make_async_copy(source, field, sems.at[1]),
    ] + [
        pltpu.make_async_copy(measured.at[f], amplitude.at[f], sems.at[2 + f])
        for f in range(frames)
    ]
    for fetch in fetches:
        fetch.start()
    powers[...] = jnp.zeros(powers.shape, f32)
    row = lax.broadcasted_iota(jnp.int32, (length, length), 0)
    column = lax.broadcasted_iota(jnp.int32, (length, length), 1)
    origin = jnp.where(column < half, 2 * column, 2 * (column - half) + 1)
    order = jnp.where(row == origin, 1.0, 0.0).astype(bf16)

    fetches[0].wait()
    power = probe[0] * probe[0] + probe[1] * probe[1]
    for f in range(frames):
        add_window(powers, power, spot(offsets, f, margin, length + SUBLANES))

    fetches[1].wait()
    even = place[2] % 2 == 0
    for plane in range(planes):
        left = pack_rows(field[plane, :, :LANES], 0, margin)
        right = pack_rows(field[plane, :, side - LANES :], LANES - margin, margin)
        columns_first[plane] = jnp.where(even, right, left)
        columns_second[plane] = jnp.where(even, left, right)

    total = jnp.zeros((SUBLANES, length), f32)
    for f in range(frames):
        fetches[2 + f].wait()
        values = amplitude[f]
        total += jnp.sum((values * values).reshape(length // SUBLANES, SUBLANES, length), 0)
        high = values.astype(bf16)
        rest = values - high.astype(f32)
        middle = rest.astype(bf16)
        low = (rest - middle.astype(f32)).astype(bf16)
        placed = dot(high, order) + (dot(middle, order) + dot(low, order))
        for parity in range(2):
            held[f, parity] = placed[:, parity * half : (parity + 1) * half]
            for start in range(2):
                at = 2 * parity + start
                sorted_out[f, at * half : (at + 1) * half, :] = held[
                    f, parity, pl.ds(start, half, stride=2), :
                ]
    total_out[...] = sum(total[:, t * LANES : (t + 1) * LANES] for t in range(length // LANES))


def corner_kernel(
    counts, place, second, first, inner_second, inner_first, above, below, second_out, first_out
):
    planes, margin, side = first.shape
    inner = inner_first.shape[1]
    even = place[2] % 2 == 0
    for plane in range(planes):
        before, after = neighbours(first[plane], second[plane], place[1], counts[0])
        above[plane] = before
        below[plane] = after
        both = jnp.concatenate([before, after], 0)
        left = pack_rows(both[:, :LANES], 0, margin)
        right = pack_rows(both[:, side - LANES :], LANES - margin, margin)
        first_out[plane, :inner] = inner_first[plane]
        first_out[plane, inner:] = jnp.where(even, right, left)
        second_out[plane, :inner] = inner_second[plane]
        second_out[plane, inner:] = jnp.where(even, left, right)


def transform_pair(waves, row_turn, column_turn, matrices, amplitudes):
    length = waves[0][0].shape[0]
    half = length // 2
    row_cos, row_sin = row_turn
    column_cos, column_sin = column_turn

    mixed = []
    for real, imag in waves:
        odd = turned(real[:half] - real[half:], imag[:half] - imag[half:], row_cos, -row_sin)
        stacked = jnp.concatenate(
            [
                jnp.concatenate([real[:half] + real[half:], imag[:half] + imag[half:]], 0),
                jnp.concatenate(odd, 0),
            ],
            1,
        )
        mixed.append(matrix_times(matrices.at[0], stacked))

    far = []
    for value in mixed:
        evens, odds = [], []
        for parity in range(2):
            part = value[:, parity * length : (parity + 1) * length]
            real, imag = part[:half], part[half:]
            evens.append(
                jnp.concatenate(
                    [real[:, :half] + real[:, half:], imag[:, :half] + imag[:, half:]], 1
                )
            )
            odd = turned(
                real[:, :half] - real[:, half:],
                imag[:, :half] - imag[:, half:],
                column_cos,
                -column_sin,
            )
            odds.append(jnp.concatenate(odd, 1))
        far.append(times_matrix(jnp.concatenate(evens + odds, 0), matrices.at[1]))

    turned_back = []
    for value, amplitude in zip(far, amplitudes):
        real, imag = value[:, :half], value[:, half:]
        factor = amplitude * lax.rsqrt(real * real + imag * imag + smoothing)
        corrected = jnp.concatenate([real * factor, imag * factor], 1)
        turned_back.append(times_matrix(corrected, matrices.at[0]))

    near = []
    for value in turned_back:
        even, odd = value[:length], value[length:]
        odd_real, odd_imag = turned(odd[:, :half], odd[:, half:], column_cos, column_sin)
        even_real, even_imag = even[:, :half], even[:, half:]
        real = jnp.concatenate([even_real + odd_real, even_real - odd_real], 1)
        imag = jnp.concatenate([even_imag + odd_imag, even_imag - odd_imag], 1)
        stacked = jnp.concatenate(
            [
                jnp.concatenate([real[:half], imag[:half]], 0),
                jnp.concatenate([real[half:], imag[half:]], 0),
            ],
            1,
        )
        near.append(matrix_times(matrices.at[1], stacked))

    results = []
    for value in near:
        even, odd = value[:, :length], value[:, length:]
        odd_real, odd_imag = turned(odd[:half], odd[half:], row_cos, row_sin)
        results.append(
            (
                jnp.concatenate([even[:half] + odd_real, even[:half] - odd_real], 0),
                jnp.concatenate([even[half:] + odd_imag, even[half:] - odd_imag], 0),
            )
        )
    return results


def frames_kernel(
    counts,
    blocks,
    place,
    offsets,
    field,
    above,
    below,
    columns_second,
    columns_first,
    probe,
    amplitude,
    total,
    powers,
    matrices,
    row_turn,
    column_turn,
    work,
    kept,
    sent,
    later,
    padded,
    sums,
):
    frames = amplitude.shape[0]
    length = probe.shape[1]
    side = field.shape[1]
    margin = above.shape[1]
    reach = side + 2 * margin
    taller = length + SUBLANES
    per = LANES // margin
    inner = side // per
    tiles = length // LANES
    last = side // LANES + 1

    for plane in range(2):
        for tile in range(side // LANES):
            lanes = pl.ds(tile * LANES, LANES)
            padded[plane, tile + 1, :margin, :] = above[plane, :, lanes]
            padded[plane, tile + 1, margin : margin + side, :] = field[plane, :, lanes]
            padded[plane, tile + 1, margin + side : reach, :] = below[plane, :, lanes]
        left, right = neighbours(
            columns_first[plane], columns_second[plane], place[2], counts[1]
        )
        for tile, packed, lane in ((0, left, LANES - margin), (last, right, 0)):
            corners = unpack_rows(packed[inner:], lane, margin)
            padded[plane, tile, :margin, :] = corners[:margin]
            padded[plane, tile, margin : margin + side, :] = unpack_rows(
                packed[:inner], lane, margin
            )
            padded[plane, tile, margin + side : reach, :] = corners[margin:]
        padded[plane, :, reach:, :] = jnp.zeros((last + 1, SUBLANES, LANES), f32)
    work[...] = jnp.zeros(work.shape, f32)
    first = jnp.where(place[1] + place[2] == 0, 1.0, 0.0).astype(f32)
    sums[0] = probe[0] * first
    sums[1] = probe[1] * first
    sums[2] = jnp.full((length, length), regular, f32) * first

    row_cos, row_sin = (jnp.concatenate([row_turn[k]] * tiles, 1) for k in range(2))
    column_cos, column_sin = (column_turn[k, 0:1, :] for k in range(2))
    together = 2 if frames % 2 == 0 else 1

    def visit(step, carry):
        chosen = [step * together + k for k in range(together)]
        spots = [spot(offsets, f, margin, taller) for f in chosen]
        windows = [
            tuple(window_of(padded, plane, spot_of, tiles) for plane in range(2))
            for spot_of in spots
        ]
        probe_real, probe_imag = probe[0], probe[1]
        waves = [
            (
                probe_real * real - probe_imag * imag,
                probe_real * imag + probe_imag * real,
            )
            for real, imag in windows
        ]
        nears = transform_pair(
            waves,
            (row_cos, row_sin),
            (column_cos, column_sin),
            matrices,
            [amplitude[f] for f in chosen],
        )
        for (window_real, window_imag), (near_real, near_imag), spot_of in zip(
            windows, nears, spots
        ):
            sums[0] += window_real * near_real + window_imag * near_imag
            sums[1] += window_real * near_imag - window_imag * near_real
            sums[2] += window_real * window_real + window_imag * window_imag
            add_window(work.at[0], probe_real * near_real + probe_imag * near_imag, spot_of)
            add_window(work.at[1], probe_real * near_imag - probe_imag * near_real, spot_of)
        return carry

    lax.fori_loop(0, frames // together, visit, 0)

    rows = length // blocks
    half_rows = blocks // 2 * 3 * tiles * rows
    for p in range(blocks):
        out, q, base = (
            (kept, p, place[0]) if p < blocks // 2 else (sent, p - blocks // 2, place[3])
        )
        source = pl.multiple_of((base ^ q) * rows, rows)
        for plane in range(3):
            for tile in range(tiles):
                start = ((3 * q + plane) * tiles + tile) * rows
                out[start : start + rows, :] = sums[
                    plane, pl.ds(source, rows), pl.ds(tile * LANES, LANES)
                ]
    kept[half_rows:, :] = total[...]
    sent[half_rows : half_rows + SUBLANES, :] = total[...]
    even = place[2] % 2 == 0
    start = half_rows + SUBLANES
    depth = reach // per
    for plane in range(3):
        canvas = powers if plane == 2 else work.at[plane]
        right = pack_rows(canvas[last, :reach, :], 0, margin)
        left = pack_rows(canvas[0, :reach, :], LANES - margin, margin)
        at = start + plane * depth
        sent[at : at + depth, :] = jnp.where(even, right, left)
        later[plane * depth : (plane + 1) * depth, :] = jnp.where(even, left, right)


def row_edge_kernel(counts, margin, place, work, powers, first, second, first_out, second_out):
    planes = work.shape[0] + 1
    tiles = work.shape[1] - 2
    reach = work.shape[2] - SUBLANES
    depth = first.shape[0] // planes
    even = place[1] % 2 == 0
    for plane in range(planes):
        canvas = powers if plane == planes - 1 else work.at[plane]
        at = pl.ds(plane * depth, depth)
        before, after = neighbours(first[at, :], second[at, :], place[2], counts[1])
        last = LANES // margin - 1
        edges = []
        for begin, chunk, cut in (
            (0, 0, slice(None, margin)),
            (reach - margin, last, slice(depth - margin, None)),
        ):
            parts = [canvas[tile + 1, begin : begin + margin, :] for tile in range(tiles)]
            parts[0] += unpack(before, chunk, 0, margin)[cut]
            parts[-1] += unpack(after, chunk, LANES - margin, margin)[cut]
            edges.append(parts)
        for tile in range(tiles):
            at = pl.ds((plane * tiles + tile) * margin, margin)
            first_out[at, :] = jnp.where(even, edges[1][tile], edges[0][tile])
            second_out[at, :] = jnp.where(even, edges[0][tile], edges[1][tile])


def object_kernel(
    counts, margin, place, field, work, powers, first, second, row_first, row_second, out
):
    planes = work.shape[0] + 1
    tiles = work.shape[1] - 2
    side = field.shape[1]
    depth = first.shape[0] // planes
    for tile in range(tiles):
        lanes = pl.ds(tile * LANES, LANES)
        total = []
        for plane in range(planes):
            canvas = powers if plane == planes - 1 else work.at[plane]
            at = pl.ds((plane * tiles + tile) * margin, margin)
            above, below = neighbours(row_first[at, :], row_second[at, :], place[1], counts[0])
            part = canvas[tile + 1, margin : margin + side, :]
            at = pl.ds(plane * depth, depth)
            before, after = neighbours(first[at, :], second[at, :], place[2], counts[1])
            if tile == 0:
                part += unpack_rows(before, 0, margin)[margin : margin + side]
            if tile == tiles - 1:
                part += unpack_rows(after, LANES - margin, margin)[margin : margin + side]
            part = jnp.concatenate(
                [
                    part[:margin] + above,
                    part[margin : side - margin],
                    part[side - margin :] + below,
                ],
                0,
            )
            total.append(part)
        weight = 1.0 / (total[2] + regular)
        out[0, :, lanes] = (field[0, :, lanes] + total[0]) * weight
        out[1, :, lanes] = (field[1, :, lanes] + total[1]) * weight


def probe_kernel(frame_count, blocks, place, stepped, total, out):
    planes, length, _ = out.shape
    tiles = length // LANES
    rows = length // blocks
    values = stepped[...]
    power = jnp.sum(values * values)
    target = jnp.sum(total[...]) / frame_count
    scale = jnp.sqrt(jnp.full((rows, LANES), target / (power + epsilon), f32))
    for p in range(blocks):
        base, q = (place[0], p) if p < blocks // 2 else (place[3], p - blocks // 2)
        home = pl.multiple_of((base ^ q) * rows, rows)
        for plane in range(planes):
            for tile in range(tiles):
                start = ((planes * p + plane) * tiles + tile) * rows
                out[plane, pl.ds(home, rows), pl.ds(tile * LANES, LANES)] = (
                    values[start : start + rows] * scale
                )


def shape(*dims):
    return jax.ShapeDtypeStruct(dims, f32)


def call(kernel, outputs, scalars=0, operands=0, scratch=(), cost=None):
    vmem = pl.BlockSpec(memory_space=pltpu.VMEM)
    smem = pl.BlockSpec(memory_space=pltpu.SMEM)
    return pl.pallas_call(
        kernel,
        out_shape=outputs,
        in_specs=[smem] * scalars + [vmem] * operands,
        out_specs=jax.tree.map(lambda _: vmem, outputs),
        scratch_shapes=list(scratch),
        cost_estimate=cost,
        compiler_params=pltpu.CompilerParams(vmem_limit_bytes=40 * 1024 * 1024),
    )


def paired(block, axis, first):
    count = lax.axis_size(axis)
    target = list(range(count))
    for i in range(first, count - 1, 2):
        target[i], target[i + 1] = i + 1, i
    return lax.ppermute(block, axis, list(enumerate(target)))


def exchanged(block, orders, step):
    count = lax.axis_size("row") * lax.axis_size("col")
    pairs = [(i, i ^ (1 << orders[i % 2][step])) for i in range(count)]
    return lax.ppermute(block, ("row", "col"), pairs)


def per_device(object_field, probe, amplitudes, positions):
    planes, side, _ = object_field.shape
    length = probe.shape[1]
    margin = MARGIN
    reach = side + 2 * margin
    per = LANES // margin
    tiles = length // LANES
    measured = amplitudes[0, 0]
    frames = measured.shape[0]
    counts = lax.axis_size("row"), lax.axis_size("col")
    row = lax.axis_index("row").astype(jnp.int32)
    col = lax.axis_index("col").astype(jnp.int32)
    index = row * counts[1] + col
    col_bits = (counts[1] - 1).bit_length()
    across = list(range(1, col_bits))
    along = list(range(col_bits, col_bits + (counts[0] - 1).bit_length()))
    orders = (across + along, along + across)
    halvings = 2
    blocks = 2 << halvings
    rows = length // blocks
    homes = [
        sum(((index >> order[k]) & 1) << (halvings - 1 - k) for k in range(halvings))
        for order in orders
    ]
    core = index & 1
    homes[1] += blocks // 2
    place = jnp.stack(
        [
            jnp.where(core == 0, homes[0], homes[1]),
            row,
            col,
            jnp.where(core == 0, homes[1], homes[0]),
        ]
    )

    edge_rows = shape(planes, margin, side)
    inner = shape(planes, side // per, LANES)
    smem = pl.BlockSpec(memory_space=pltpu.SMEM)
    vmem = pl.BlockSpec(memory_space=pltpu.VMEM)
    hbm = pl.BlockSpec(memory_space=pltpu.HBM)
    rows_first, rows_second = pl.pallas_call(
        begin_kernel,
        out_shape=(edge_rows, edge_rows),
        in_specs=[smem, hbm],
        out_specs=(vmem, vmem),
        scratch_shapes=[pltpu.SemaphoreType.DMA((2,))],
    )(place, object_field)
    rows_second = paired(rows_second, "row", 1)
    rows_first = paired(rows_first, "row", 0)
    field, probe, inner_first, inner_second, ordered, total, powers = pl.pallas_call(
        functools.partial(prepare_kernel, margin),
        out_shape=(
            shape(*object_field.shape),
            shape(*probe.shape),
            inner,
            inner,
            shape(frames, 2 * length, length // 2),
            shape(SUBLANES, LANES),
            shape(side // LANES + 2, reach + SUBLANES, LANES),
        ),
        in_specs=[smem, smem, hbm, hbm, hbm],
        out_specs=(vmem,) * 7,
        scratch_shapes=[
            pltpu.VMEM((frames, length, length), f32),
            pltpu.VMEM((frames, 2, length, length // 2), f32),
            pltpu.SemaphoreType.DMA((2 + frames,)),
        ],
        cost_estimate=pl.CostEstimate(
            flops=10**9, bytes_accessed=2 * measured.size * 4, transcendentals=0
        ),
    )(place, positions[0, 0], object_field, measured, probe)
    packed = shape(planes, reach // per, LANES)
    above, below, columns_second, columns_first = call(
        functools.partial(corner_kernel, counts),
        (edge_rows, edge_rows, packed, packed),
        scalars=1,
        operands=4,
    )(place, rows_second, rows_first, inner_second, inner_first)
    columns_second = paired(columns_second, "col", 1)
    columns_first = paired(columns_first, "col", 0)

    matrices, row_turn, column_turn = tables(length)
    half_rows = blocks // 2 * 3 * tiles * rows
    depth = 3 * reach // per
    work, kept, sent, edge = call(
        functools.partial(frames_kernel, counts, blocks),
        (
            shape(2, side // LANES + 2, reach + SUBLANES, LANES),
            shape(half_rows + SUBLANES, LANES),
            shape(half_rows + SUBLANES + depth, LANES),
            shape(depth, LANES),
        ),
        scalars=2,
        operands=12,
        scratch=(
            pltpu.VMEM((2, side // LANES + 2, reach + SUBLANES, LANES), f32),
            pltpu.VMEM((3, length, length), f32),
        ),
    )(
        place,
        positions[0, 0],
        field,
        above,
        below,
        columns_second,
        columns_first,
        probe,
        ordered,
        total,
        powers,
        jnp.asarray(matrices),
        jnp.asarray(row_turn),
        jnp.asarray(column_turn),
    )

    arrived = paired(sent, "col", 0)
    current = kept + arrived[: half_rows + SUBLANES]
    first = arrived[half_rows + SUBLANES :]
    second = paired(edge, "col", 1)
    out = shape(3 * tiles * margin, LANES)
    row_first, row_second = call(
        functools.partial(row_edge_kernel, counts, margin), (out, out), scalars=1, operands=4
    )(place, work, powers, first, second)
    for step in range(len(orders[0])):
        if step == 1:
            current, row_first, row_second = lax.optimization_barrier(
                (current, row_first, row_second)
            )
            row_first = paired(row_first, "row", 0)
        if step == 2:
            current, row_first, row_second = lax.optimization_barrier(
                (current, row_first, row_second)
            )
            row_second = paired(row_second, "row", 1)
        if step == 3:
            current, row_second = lax.optimization_barrier((current, row_second))
        count = current.shape[0] - SUBLANES
        if step < halvings:
            sent = jnp.concatenate([current[count // 2 : count], current[count:]], 0)
            kept = jnp.concatenate([current[: count // 2], current[count:]], 0)
        else:
            kept = sent = current
        current = kept + exchanged(sent, orders, step)
    size = tiles * rows
    weight = current[2 * size : 3 * size]
    stepped = current[: 2 * size] / jnp.concatenate([weight, weight], 0)
    object_next = call(
        functools.partial(object_kernel, counts, margin),
        shape(*object_field.shape),
        scalars=1,
        operands=7,
    )(place, field, work, powers, first, second, row_first, row_second)
    for step in reversed(range(halvings)):
        stepped = jnp.concatenate([stepped, exchanged(stepped, orders, step)], 0)
    stepped = jnp.concatenate([stepped, paired(stepped, "col", 0)], 0)
    frame_count = frames * counts[0] * counts[1]
    probe_next = call(
        functools.partial(probe_kernel, frame_count, blocks),
        shape(*probe.shape),
        scalars=1,
        operands=2,
    )(place, stepped, current[3 * size :])
    return (object_next, probe_next)


def solution(mesh):
    return jax.shard_map(
        per_device,
        mesh=mesh,
        in_specs=(
            P(None, "row", "col"),
            P(),
            P("row", "col", None, None, None),
            P("row", "col", None, None),
        ),
        out_specs=(P(None, "row", "col"), P()),
        check_vma=False,
    )
```

```python
import functools
import math

import jax
import jax.numpy as jnp
import numpy as np
from jax import lax
from jax.experimental import pallas as pl
from jax.experimental.pallas import tpu as pltpu
from jax.sharding import PartitionSpec as P

MARGIN = 32
LANES = 128
SUBLANES = 8

smoothing = 0.1
regular = 1.0
epsilon = 1e-06

f32 = jnp.float32
bf16 = jnp.bfloat16


def tables(length):
    half = length // 2
    scaling = 1.0 / math.sqrt(length)
    k = np.arange(half)
    phases = (k[:, None] * k[None, :] % half) * (2.0 * math.pi / half)
    cosine, sine = np.cos(phases) * scaling, np.sin(phases) * scaling
    right = np.block([[cosine, -sine], [sine, cosine]])
    left = np.block([[cosine, sine], [-sine, cosine]])
    both = np.stack([left, right]).astype(np.float32)
    high = both.astype(bf16)
    low = (both - high.astype(np.float32)).astype(bf16)
    matrices = np.stack([high, low], 1)
    angle = k * (2.0 * math.pi / length)
    turn = np.stack([np.cos(angle), np.sin(angle)]).astype(np.float32)
    rows = np.broadcast_to(turn[:, :, None], (2, half, LANES)).copy()
    columns = np.broadcast_to(turn[:, None, :], (2, SUBLANES, half)).copy()
    return matrices, rows, columns


def split(x):
    high = x.astype(bf16)
    return high, (x - high.astype(f32)).astype(bf16)


def dot(a, b):
    return jnp.dot(a, b, preferred_element_type=f32)


def times_matrix(data, matrix):
    high, low = split(data)
    return dot(
        jnp.concatenate([high, low, high], 1),
        jnp.concatenate([matrix[0], matrix[0], matrix[1]], 0),
    )


def matrix_times(matrix, data):
    high, low = split(data)
    return dot(
        jnp.concatenate([matrix[0], matrix[0], matrix[1]], 1),
        jnp.concatenate([high, low, high], 0),
    )


def turned(real, imag, cosine, sine):
    return real * cosine - imag * sine, real * sine + imag * cosine


def pack(chunks, lane, width):
    place = lax.broadcasted_iota(jnp.int32, chunks[0].shape, 1) // width
    out = jnp.zeros_like(chunks[0])
    for q, chunk in enumerate(chunks):
        shift = (q * width - lane) % LANES
        moved = pltpu.roll(chunk, shift, 1) if shift else chunk
        out = jnp.where(place == q, moved, out)
    return out


def pack_rows(rows, lane, width):
    count = rows.shape[0] * width // LANES
    return pack([rows[q : q + count] for q in range(0, rows.shape[0], count)], lane, width)


def unpack(packed, q, lane, width):
    shift = (lane - q * width) % LANES
    moved = pltpu.roll(packed, shift, 1) if shift else packed
    place = lax.broadcasted_iota(jnp.int32, packed.shape, 1)
    return jnp.where((place >= lane) & (place < lane + width), moved, 0.0)


def unpack_rows(packed, lane, width):
    return jnp.concatenate([unpack(packed, q, lane, width) for q in range(LANES // width)], 0)


def lifted(tile, shift):
    groups = tile.shape[0] // SUBLANES
    turned_rows = pltpu.roll(
        tile.reshape(groups, SUBLANES, LANES), lax.rem(SUBLANES - shift, SUBLANES), 1
    )
    place = lax.broadcasted_iota(jnp.int32, (groups - 1, SUBLANES, LANES), 1)
    picked = jnp.where(place < SUBLANES - shift, turned_rows[:-1], turned_rows[1:])
    return picked.reshape((groups - 1) * SUBLANES, LANES)


def lowered(tile, shift):
    groups = tile.shape[0] // SUBLANES
    moved = pltpu.roll(tile.reshape(groups, SUBLANES, LANES), shift, 1)
    none = jnp.zeros((1, SUBLANES, LANES), f32)
    place = lax.broadcasted_iota(jnp.int32, (groups + 1, SUBLANES, LANES), 1)
    picked = jnp.where(
        place >= shift, jnp.concatenate([moved, none], 0), jnp.concatenate([none, moved], 0)
    )
    return picked.reshape((groups + 1) * SUBLANES, LANES)


def spot(offsets, f, margin, taller):
    a, b = offsets[f, 0], offsets[f, 1]
    shift = lax.rem(a, SUBLANES)
    lane = b + LANES - margin
    tile = lane // LANES
    return pl.ds(pl.multiple_of(a - shift, SUBLANES), taller), shift, tile, lane - tile * LANES


def window_of(padded, plane, spot_of, tiles):
    at, shift, base, lane = spot_of
    moved = [
        pltpu.roll(padded[plane, base + t, at, :], lax.rem(LANES - lane, LANES), 1)
        for t in range(tiles + 1)
    ]
    place = lax.broadcasted_iota(jnp.int32, moved[0].shape, 1)
    parts = [
        lifted(jnp.where(place < LANES - lane, moved[t], moved[t + 1]), shift)
        for t in range(tiles)
    ]
    return jnp.concatenate(parts, 1)


def add_window(work, term, spot_of):
    at, shift, base, lane = spot_of
    tiles = term.shape[1] // LANES
    moved = [
        pltpu.roll(lowered(term[:, t * LANES : (t + 1) * LANES], shift), lane, 1)
        for t in range(tiles)
    ]
    none = jnp.zeros_like(moved[0])
    place = lax.broadcasted_iota(jnp.int32, none.shape, 1)
    for t in range(tiles + 1):
        here = moved[t] if t < tiles else none
        before = moved[t - 1] if t else none
        work[base + t, at, :] += jnp.where(place >= lane, here, before)


def neighbours(first, second, index, count):
    even = index % 2 == 0
    before = jnp.where(even, second, first)
    after = jnp.where(even, first, second)
    return jnp.where(index > 0, before, 0.0), jnp.where(index < count - 1, after, 0.0)


def begin_kernel(place, source, field, rows_first, rows_second, columns_first, columns_second, sem):
    copy = pltpu.make_async_copy(source, field, sem)
    copy.start()
    copy.wait()
    planes, side, _ = field.shape
    margin = rows_first.shape[1]
    even_row = place[1] % 2 == 0
    even_column = place[2] % 2 == 0
    for plane in range(planes):
        top, bottom = field[plane, :margin], field[plane, side - margin :]
        rows_first[plane] = jnp.where(even_row, bottom, top)
        rows_second[plane] = jnp.where(even_row, top, bottom)
        left = pack_rows(field[plane, :, :LANES], 0, margin)
        right = pack_rows(field[plane, :, side - LANES :], LANES - margin, margin)
        columns_first[plane] = jnp.where(even_column, right, left)
        columns_second[plane] = jnp.where(even_column, left, right)


def amplitude_kernel(margin, offsets, amplitude, probe, sorted_out, total_out, powers, held):
    frames, length, _ = amplitude.shape
    half = length // 2
    power = probe[0] * probe[0] + probe[1] * probe[1]
    powers[...] = jnp.zeros(powers.shape, f32)
    for f in range(frames):
        add_window(powers, power, spot(offsets, f, margin, length + SUBLANES))
    row = lax.broadcasted_iota(jnp.int32, (length, length), 0)
    column = lax.broadcasted_iota(jnp.int32, (length, length), 1)
    source = jnp.where(column < half, 2 * column, 2 * (column - half) + 1)
    order = jnp.where(row == source, 1.0, 0.0).astype(bf16)
    total = jnp.zeros((SUBLANES, length), f32)
    for f in range(frames):
        values = amplitude[f]
        total += jnp.sum((values * values).reshape(length // SUBLANES, SUBLANES, length), 0)
        high = values.astype(bf16)
        rest = values - high.astype(f32)
        middle = rest.astype(bf16)
        low = (rest - middle.astype(f32)).astype(bf16)
        placed = dot(high, order) + (dot(middle, order) + dot(low, order))
        for parity in range(2):
            held[f, parity] = placed[:, parity * half : (parity + 1) * half]
            for start in range(2):
                at = 2 * parity + start
                sorted_out[f, at * half : (at + 1) * half, :] = held[
                    f, parity, pl.ds(start, half, stride=2), :
                ]
    total_out[...] = sum(total[:, t * LANES : (t + 1) * LANES] for t in range(length // LANES))


def corner_kernel(counts, place, first, second, inner_first, inner_second, above, below, out):
    planes, margin, side = first.shape
    inner = inner_first.shape[1]
    even = place[2] % 2 == 0
    for plane in range(planes):
        before, after = neighbours(first[plane], second[plane], place[1], counts[0])
        above[plane] = before
        below[plane] = after
        both = jnp.concatenate([before, after], 0)
        left = pack_rows(both[:, :LANES], 0, margin)
        right = pack_rows(both[:, side - LANES :], LANES - margin, margin)
        out[plane, :inner] = inner_first[plane]
        out[plane, inner:] = jnp.where(even, right, left)
        out[planes + plane, :inner] = inner_second[plane]
        out[planes + plane, inner:] = jnp.where(even, left, right)


def transform_pair(waves, row_turn, column_turn, matrices, amplitudes):
    length = waves[0][0].shape[0]
    half = length // 2
    row_cos, row_sin = row_turn
    column_cos, column_sin = column_turn

    mixed = []
    for real, imag in waves:
        odd = turned(real[:half] - real[half:], imag[:half] - imag[half:], row_cos, -row_sin)
        stacked = jnp.concatenate(
            [
                jnp.concatenate([real[:half] + real[half:], imag[:half] + imag[half:]], 0),
                jnp.concatenate(odd, 0),
            ],
            1,
        )
        mixed.append(matrix_times(matrices.at[0], stacked))

    far = []
    for value in mixed:
        evens, odds = [], []
        for parity in range(2):
            part = value[:, parity * length : (parity + 1) * length]
            real, imag = part[:half], part[half:]
            evens.append(
                jnp.concatenate(
                    [real[:, :half] + real[:, half:], imag[:, :half] + imag[:, half:]], 1
                )
            )
            odd = turned(
                real[:, :half] - real[:, half:],
                imag[:, :half] - imag[:, half:],
                column_cos,
                -column_sin,
            )
            odds.append(jnp.concatenate(odd, 1))
        far.append(times_matrix(jnp.concatenate(evens + odds, 0), matrices.at[1]))

    turned_back = []
    for value, amplitude in zip(far, amplitudes):
        real, imag = value[:, :half], value[:, half:]
        factor = amplitude * lax.rsqrt(real * real + imag * imag + smoothing)
        corrected = jnp.concatenate([real * factor, imag * factor], 1)
        turned_back.append(times_matrix(corrected, matrices.at[0]))

    near = []
    for value in turned_back:
        even, odd = value[:length], value[length:]
        odd_real, odd_imag = turned(odd[:, :half], odd[:, half:], column_cos, column_sin)
        even_real, even_imag = even[:, :half], even[:, half:]
        real = jnp.concatenate([even_real + odd_real, even_real - odd_real], 1)
        imag = jnp.concatenate([even_imag + odd_imag, even_imag - odd_imag], 1)
        stacked = jnp.concatenate(
            [
                jnp.concatenate([real[:half], imag[:half]], 0),
                jnp.concatenate([real[half:], imag[half:]], 0),
            ],
            1,
        )
        near.append(matrix_times(matrices.at[1], stacked))

    results = []
    for value in near:
        even, odd = value[:, :length], value[:, length:]
        odd_real, odd_imag = turned(odd[:half], odd[half:], row_cos, row_sin)
        results.append(
            (
                jnp.concatenate([even[:half] + odd_real, even[:half] - odd_real], 0),
                jnp.concatenate([even[half:] + odd_imag, even[half:] - odd_imag], 0),
            )
        )
    return results


def frames_kernel(
    counts,
    blocks,
    place,
    offsets,
    field,
    above,
    below,
    columns_first,
    columns_second,
    probe,
    amplitude,
    total,
    powers,
    matrices,
    row_turn,
    column_turn,
    work,
    kept,
    sent,
    padded,
    sums,
):
    frames = amplitude.shape[0]
    length = probe.shape[1]
    side = field.shape[1]
    margin = above.shape[1]
    reach = side + 2 * margin
    taller = length + SUBLANES
    per = LANES // margin
    inner = side // per
    tiles = length // LANES
    last = side // LANES + 1

    for plane in range(2):
        for tile in range(side // LANES):
            lanes = pl.ds(tile * LANES, LANES)
            padded[plane, tile + 1, :margin, :] = above[plane, :, lanes]
            padded[plane, tile + 1, margin : margin + side, :] = field[plane, :, lanes]
            padded[plane, tile + 1, margin + side : reach, :] = below[plane, :, lanes]
        left, right = neighbours(
            columns_first[plane], columns_second[plane], place[2], counts[1]
        )
        for tile, packed, lane in ((0, left, LANES - margin), (last, right, 0)):
            corners = unpack_rows(packed[inner:], lane, margin)
            padded[plane, tile, :margin, :] = corners[:margin]
            padded[plane, tile, margin : margin + side, :] = unpack_rows(
                packed[:inner], lane, margin
            )
            padded[plane, tile, margin + side : reach, :] = corners[margin:]
        padded[plane, :, reach:, :] = jnp.zeros((last + 1, SUBLANES, LANES), f32)
    work[...] = jnp.zeros(work.shape, f32)
    first = jnp.where(place[1] + place[2] == 0, 1.0, 0.0).astype(f32)
    sums[0] = probe[0] * first
    sums[1] = probe[1] * first
    sums[2] = jnp.full((length, length), regular, f32) * first

    row_cos, row_sin = (jnp.concatenate([row_turn[k]] * tiles, 1) for k in range(2))
    column_cos, column_sin = (column_turn[k, 0:1, :] for k in range(2))
    together = 2 if frames % 2 == 0 else 1

    def visit(step, carry):
        chosen = [step * together + k for k in range(together)]
        spots = [spot(offsets, f, margin, taller) for f in chosen]
        windows = [
            tuple(window_of(padded, plane, spot_of, tiles) for plane in range(2))
            for spot_of in spots
        ]
        probe_real, probe_imag = probe[0], probe[1]
        waves = [
            (
                probe_real * real - probe_imag * imag,
                probe_real * imag + probe_imag * real,
            )
            for real, imag in windows
        ]
        nears = transform_pair(
            waves,
            (row_cos, row_sin),
            (column_cos, column_sin),
            matrices,
            [amplitude[f] for f in chosen],
        )
        for (window_real, window_imag), (near_real, near_imag), spot_of in zip(
            windows, nears, spots
        ):
            sums[0] += window_real * near_real + window_imag * near_imag
            sums[1] += window_real * near_imag - window_imag * near_real
            sums[2] += window_real * window_real + window_imag * window_imag
            add_window(work.at[0], probe_real * near_real + probe_imag * near_imag, spot_of)
            add_window(work.at[1], probe_real * near_imag - probe_imag * near_real, spot_of)
        return carry

    lax.fori_loop(0, frames // together, visit, 0)

    rows = length // blocks
    half_rows = blocks // 2 * 3 * tiles * rows
    for p in range(blocks):
        out, q, base = (
            (kept, p, place[0]) if p < blocks // 2 else (sent, p - blocks // 2, place[3])
        )
        source = pl.multiple_of((base ^ q) * rows, rows)
        for plane in range(3):
            for tile in range(tiles):
                start = ((3 * q + plane) * tiles + tile) * rows
                out[start : start + rows, :] = sums[
                    plane, pl.ds(source, rows), pl.ds(tile * LANES, LANES)
                ]
    kept[half_rows:, :] = total[...]
    sent[half_rows : half_rows + SUBLANES, :] = total[...]
    even = place[2] % 2 == 0
    start = half_rows + SUBLANES
    depth = reach // per
    for plane in range(3):
        canvas = powers if plane == 2 else work.at[plane]
        right = pack_rows(canvas[last, :reach, :], 0, margin)
        left = pack_rows(canvas[0, :reach, :], LANES - margin, margin)
        at = start + plane * depth
        sent[at : at + depth, :] = jnp.where(even, right, left)
        at += 3 * depth
        sent[at : at + depth, :] = jnp.where(even, left, right)


def row_edge_kernel(counts, margin, place, work, powers, first, second, first_out, second_out):
    planes = work.shape[0] + 1
    tiles = work.shape[1] - 2
    reach = work.shape[2] - SUBLANES
    depth = first.shape[0] // planes
    even = place[1] % 2 == 0
    for plane in range(planes):
        canvas = powers if plane == planes - 1 else work.at[plane]
        at = pl.ds(plane * depth, depth)
        before, after = neighbours(first[at, :], second[at, :], place[2], counts[1])
        last = LANES // margin - 1
        edges = []
        for begin, chunk, cut in (
            (0, 0, slice(None, margin)),
            (reach - margin, last, slice(depth - margin, None)),
        ):
            parts = [canvas[tile + 1, begin : begin + margin, :] for tile in range(tiles)]
            parts[0] += unpack(before, chunk, 0, margin)[cut]
            parts[-1] += unpack(after, chunk, LANES - margin, margin)[cut]
            edges.append(parts)
        for tile in range(tiles):
            at = pl.ds((plane * tiles + tile) * margin, margin)
            first_out[at, :] = jnp.where(even, edges[1][tile], edges[0][tile])
            second_out[at, :] = jnp.where(even, edges[0][tile], edges[1][tile])


def object_kernel(
    counts, margin, place, field, work, powers, first, second, row_first, row_second, out
):
    planes = work.shape[0] + 1
    tiles = work.shape[1] - 2
    side = field.shape[1]
    depth = first.shape[0] // planes
    for tile in range(tiles):
        lanes = pl.ds(tile * LANES, LANES)
        total = []
        for plane in range(planes):
            canvas = powers if plane == planes - 1 else work.at[plane]
            at = pl.ds((plane * tiles + tile) * margin, margin)
            above, below = neighbours(row_first[at, :], row_second[at, :], place[1], counts[0])
            part = canvas[tile + 1, margin : margin + side, :]
            at = pl.ds(plane * depth, depth)
            before, after = neighbours(first[at, :], second[at, :], place[2], counts[1])
            if tile == 0:
                part += unpack_rows(before, 0, margin)[margin : margin + side]
            if tile == tiles - 1:
                part += unpack_rows(after, LANES - margin, margin)[margin : margin + side]
            part = jnp.concatenate(
                [
                    part[:margin] + above,
                    part[margin : side - margin],
                    part[side - margin :] + below,
                ],
                0,
            )
            total.append(part)
        weight = 1.0 / (total[2] + regular)
        out[0, :, lanes] = (field[0, :, lanes] + total[0]) * weight
        out[1, :, lanes] = (field[1, :, lanes] + total[1]) * weight


def probe_kernel(frame_count, blocks, place, stepped, total, out):
    planes, length, _ = out.shape
    tiles = length // LANES
    rows = length // blocks
    values = stepped[...]
    power = jnp.sum(values * values)
    target = jnp.sum(total[...]) / frame_count
    scale = jnp.sqrt(jnp.full((rows, LANES), target / (power + epsilon), f32))
    for p in range(blocks):
        base, q = (place[0], p) if p < blocks // 2 else (place[3], p - blocks // 2)
        home = pl.multiple_of((base ^ q) * rows, rows)
        for plane in range(planes):
            for tile in range(tiles):
                start = ((planes * p + plane) * tiles + tile) * rows
                out[plane, pl.ds(home, rows), pl.ds(tile * LANES, LANES)] = (
                    values[start : start + rows] * scale
                )


def shape(*dims):
    return jax.ShapeDtypeStruct(dims, f32)


def call(kernel, outputs, scalars=0, operands=0, scratch=(), cost=None):
    vmem = pl.BlockSpec(memory_space=pltpu.VMEM)
    smem = pl.BlockSpec(memory_space=pltpu.SMEM)
    return pl.pallas_call(
        kernel,
        out_shape=outputs,
        in_specs=[smem] * scalars + [vmem] * operands,
        out_specs=jax.tree.map(lambda _: vmem, outputs),
        scratch_shapes=list(scratch),
        cost_estimate=cost,
        compiler_params=pltpu.CompilerParams(vmem_limit_bytes=40 * 1024 * 1024),
    )


def paired(block, axis, first):
    count = lax.axis_size(axis)
    target = list(range(count))
    for i in range(first, count - 1, 2):
        target[i], target[i + 1] = i + 1, i
    return lax.ppermute(block, axis, list(enumerate(target)))


def relayed(block):
    chips = lax.axis_size("col") // 2
    return lax.ppermute(
        block,
        "col",
        [
            (2 * chip + core, 2 * ((chip + 1 - 2 * core) % chips) + core)
            for chip in range(chips)
            for core in range(2)
        ],
    )


def exchanged(block, orders, step):
    count = lax.axis_size("row") * lax.axis_size("col")
    pairs = [(i, i ^ (1 << orders[i % 2][step])) for i in range(count)]
    return lax.ppermute(block, ("row", "col"), pairs)


def per_device(object_field, probe, amplitudes, positions):
    planes, side, _ = object_field.shape
    length = probe.shape[1]
    margin = MARGIN
    reach = side + 2 * margin
    per = LANES // margin
    tiles = length // LANES
    measured = amplitudes[0, 0]
    frames = measured.shape[0]
    counts = lax.axis_size("row"), lax.axis_size("col")
    row = lax.axis_index("row").astype(jnp.int32)
    col = lax.axis_index("col").astype(jnp.int32)
    index = row * counts[1] + col
    col_bits = (counts[1] - 1).bit_length()
    across = list(range(1, col_bits))
    along = list(range(col_bits, col_bits + (counts[0] - 1).bit_length()))
    orders = (across + along, along + across)
    halvings = 2
    blocks = 2 << halvings
    rows = length // blocks
    homes = [
        sum(((index >> order[k]) & 1) << (halvings - 1 - k) for k in range(halvings))
        for order in orders
    ]
    core = index & 1
    homes[1] += blocks // 2
    place = jnp.stack(
        [
            jnp.where(core == 0, homes[0], homes[1]),
            row,
            col,
            jnp.where(core == 0, homes[1], homes[0]),
        ]
    )

    edge_rows = shape(planes, margin, side)
    inner = shape(planes, side // per, LANES)
    smem = pl.BlockSpec(memory_space=pltpu.SMEM)
    vmem = pl.BlockSpec(memory_space=pltpu.VMEM)
    field, rows_first, rows_second, inner_first, inner_second = pl.pallas_call(
        begin_kernel,
        out_shape=(shape(*object_field.shape), edge_rows, edge_rows, inner, inner),
        in_specs=[smem, pl.BlockSpec(memory_space=pl.ANY)],
        out_specs=(vmem,) * 5,
        scratch_shapes=[pltpu.SemaphoreType.DMA],
        compiler_params=pltpu.CompilerParams(vmem_limit_bytes=16 * 1024 * 1024),
    )(place, object_field)
    rows_second = paired(rows_second, "row", 1)
    rows_first = paired(rows_first, "row", 0)
    ordered, total, powers = call(
        functools.partial(amplitude_kernel, margin),
        (
            shape(frames, 2 * length, length // 2),
            shape(SUBLANES, LANES),
            shape(side // LANES + 2, reach + SUBLANES, LANES),
        ),
        scalars=1,
        operands=2,
        scratch=(pltpu.VMEM((frames, 2, length, length // 2), f32),),
        cost=pl.CostEstimate(flops=10**9, bytes_accessed=2 * measured.size * 4, transcendentals=0),
    )(positions[0, 0], measured, probe)
    rows_first, rows_second, ordered, powers = lax.optimization_barrier(
        (rows_first, rows_second, ordered, powers)
    )
    above, below, columns = call(
        functools.partial(corner_kernel, counts),
        (edge_rows, edge_rows, shape(2 * planes, reach // per, LANES)),
        scalars=1,
        operands=4,
    )(place, rows_first, rows_second, inner_first, inner_second)
    columns = paired(columns, "col", 0)
    relay = relayed(columns[planes:])

    matrices, row_turn, column_turn = tables(length)
    half_rows = blocks // 2 * 3 * tiles * rows
    depth = 3 * reach // per
    work, kept, sent = call(
        functools.partial(frames_kernel, counts, blocks),
        (
            shape(2, side // LANES + 2, reach + SUBLANES, LANES),
            shape(half_rows + SUBLANES, LANES),
            shape(half_rows + SUBLANES + 2 * depth, LANES),
        ),
        scalars=2,
        operands=12,
        scratch=(
            pltpu.VMEM((2, side // LANES + 2, reach + SUBLANES, LANES), f32),
            pltpu.VMEM((3, length, length), f32),
        ),
    )(
        place,
        positions[0, 0],
        field,
        above,
        below,
        columns,
        relay,
        probe,
        ordered,
        total,
        powers,
        jnp.asarray(matrices),
        jnp.asarray(row_turn),
        jnp.asarray(column_turn),
    )

    arrived = paired(sent, "col", 0)
    current = kept + arrived[: half_rows + SUBLANES]
    first = arrived[half_rows + SUBLANES : half_rows + SUBLANES + depth]
    second = relayed(arrived[half_rows + SUBLANES + depth :])
    for step in range(len(orders[0])):
        if step == 2:
            current, second = lax.optimization_barrier((current, second))
            out = shape(3 * tiles * margin, LANES)
            row_first, row_second = call(
                functools.partial(row_edge_kernel, counts, margin),
                (out, out),
                scalars=1,
                operands=4,
            )(place, work, powers, first, second)
            row_first = paired(row_first, "row", 0)
        if step == 3:
            current, row_first, row_second = lax.optimization_barrier(
                (current, row_first, row_second)
            )
            row_second = paired(row_second, "row", 1)
        count = current.shape[0] - SUBLANES
        if step < halvings:
            sent = jnp.concatenate([current[count // 2 : count], current[count:]], 0)
            kept = jnp.concatenate([current[: count // 2], current[count:]], 0)
        else:
            kept = sent = current
        current = kept + exchanged(sent, orders, step)
    size = tiles * rows
    weight = current[2 * size : 3 * size]
    stepped = current[: 2 * size] / jnp.concatenate([weight, weight], 0)
    stepped, row_second = lax.optimization_barrier((stepped, row_second))
    object_next = call(
        functools.partial(object_kernel, counts, margin),
        shape(*object_field.shape),
        scalars=1,
        operands=7,
    )(place, field, work, powers, first, second, row_first, row_second)
    for step in reversed(range(halvings)):
        stepped = jnp.concatenate([stepped, exchanged(stepped, orders, step)], 0)
    stepped = jnp.concatenate([stepped, paired(stepped, "col", 0)], 0)
    frame_count = frames * counts[0] * counts[1]
    probe_next = call(
        functools.partial(probe_kernel, frame_count, blocks),
        shape(*probe.shape),
        scalars=1,
        operands=2,
    )(place, stepped, current[3 * size :])
    return (object_next, probe_next)


def solution(mesh):
    return jax.shard_map(
        per_device,
        mesh=mesh,
        in_specs=(
            P(None, "row", "col"),
            P(),
            P("row", "col", None, None, None),
            P("row", "col", None, None),
        ),
        out_specs=(P(None, "row", "col"), P()),
        check_vma=False,
    )
```

```python
import functools
import math

import jax
import jax.numpy as jnp
import numpy as np
from jax import lax
from jax.experimental import pallas as pl
from jax.experimental.pallas import tpu as pltpu
from jax.sharding import PartitionSpec as P

MARGIN = 32
LANES = 128
SUBLANES = 8

smoothing = 0.1
regular = 1.0
epsilon = 1e-06

f32 = jnp.float32
bf16 = jnp.bfloat16


def tables(length):
    half = length // 2
    scaling = 1.0 / math.sqrt(length)
    k = np.arange(half)
    phases = (k[:, None] * k[None, :] % half) * (2.0 * math.pi / half)
    cosine, sine = np.cos(phases) * scaling, np.sin(phases) * scaling
    right = np.block([[cosine, -sine], [sine, cosine]])
    left = np.block([[cosine, sine], [-sine, cosine]])
    both = np.stack([left, right]).astype(np.float32)
    high = both.astype(bf16)
    low = (both - high.astype(np.float32)).astype(bf16)
    matrices = np.stack([high, low], 1)
    angle = k * (2.0 * math.pi / length)
    turn = np.stack([np.cos(angle), np.sin(angle)]).astype(np.float32)
    rows = np.broadcast_to(turn[:, :, None], (2, half, LANES)).copy()
    columns = np.broadcast_to(turn[:, None, :], (2, SUBLANES, half)).copy()
    return matrices, rows, columns


def split(x):
    high = x.astype(bf16)
    return high, (x - high.astype(f32)).astype(bf16)


def dot(a, b):
    return jnp.dot(a, b, preferred_element_type=f32)


def times_matrix(data, matrix):
    high, low = split(data)
    return dot(
        jnp.concatenate([high, low, high], 1),
        jnp.concatenate([matrix[0], matrix[0], matrix[1]], 0),
    )


def matrix_times(matrix, data):
    high, low = split(data)
    return dot(
        jnp.concatenate([matrix[0], matrix[0], matrix[1]], 1),
        jnp.concatenate([high, low, high], 0),
    )


def turned(real, imag, cosine, sine):
    return real * cosine - imag * sine, real * sine + imag * cosine


def pack(chunks, lane, width):
    place = lax.broadcasted_iota(jnp.int32, chunks[0].shape, 1) // width
    out = jnp.zeros_like(chunks[0])
    for q, chunk in enumerate(chunks):
        shift = (q * width - lane) % LANES
        moved = pltpu.roll(chunk, shift, 1) if shift else chunk
        out = jnp.where(place == q, moved, out)
    return out


def pack_rows(rows, lane, width):
    count = rows.shape[0] * width // LANES
    return pack([rows[q : q + count] for q in range(0, rows.shape[0], count)], lane, width)


def unpack(packed, q, lane, width):
    shift = (lane - q * width) % LANES
    moved = pltpu.roll(packed, shift, 1) if shift else packed
    place = lax.broadcasted_iota(jnp.int32, packed.shape, 1)
    return jnp.where((place >= lane) & (place < lane + width), moved, 0.0)


def unpack_rows(packed, lane, width):
    return jnp.concatenate([unpack(packed, q, lane, width) for q in range(LANES // width)], 0)


def lifted(tile, shift):
    groups = tile.shape[0] // SUBLANES
    turned_rows = pltpu.roll(
        tile.reshape(groups, SUBLANES, LANES), lax.rem(SUBLANES - shift, SUBLANES), 1
    )
    place = lax.broadcasted_iota(jnp.int32, (groups - 1, SUBLANES, LANES), 1)
    picked = jnp.where(place < SUBLANES - shift, turned_rows[:-1], turned_rows[1:])
    return picked.reshape((groups - 1) * SUBLANES, LANES)


def lowered(tile, shift):
    groups = tile.shape[0] // SUBLANES
    moved = pltpu.roll(tile.reshape(groups, SUBLANES, LANES), shift, 1)
    none = jnp.zeros((1, SUBLANES, LANES), f32)
    place = lax.broadcasted_iota(jnp.int32, (groups + 1, SUBLANES, LANES), 1)
    picked = jnp.where(
        place >= shift, jnp.concatenate([moved, none], 0), jnp.concatenate([none, moved], 0)
    )
    return picked.reshape((groups + 1) * SUBLANES, LANES)


def spot(offsets, f, margin, taller):
    a, b = offsets[f, 0], offsets[f, 1]
    shift = lax.rem(a, SUBLANES)
    lane = b + LANES - margin
    tile = lane // LANES
    return pl.ds(pl.multiple_of(a - shift, SUBLANES), taller), shift, tile, lane - tile * LANES


def window_of(padded, plane, spot_of, tiles):
    at, shift, base, lane = spot_of
    moved = [
        pltpu.roll(padded[plane, base + t, at, :], lax.rem(LANES - lane, LANES), 1)
        for t in range(tiles + 1)
    ]
    place = lax.broadcasted_iota(jnp.int32, moved[0].shape, 1)
    parts = [
        lifted(jnp.where(place < LANES - lane, moved[t], moved[t + 1]), shift)
        for t in range(tiles)
    ]
    return jnp.concatenate(parts, 1)


def add_window(work, term, spot_of):
    at, shift, base, lane = spot_of
    tiles = term.shape[1] // LANES
    moved = [
        pltpu.roll(lowered(term[:, t * LANES : (t + 1) * LANES], shift), lane, 1)
        for t in range(tiles)
    ]
    none = jnp.zeros_like(moved[0])
    place = lax.broadcasted_iota(jnp.int32, none.shape, 1)
    for t in range(tiles + 1):
        here = moved[t] if t < tiles else none
        before = moved[t - 1] if t else none
        work[base + t, at, :] += jnp.where(place >= lane, here, before)


def neighbours(first, second, index, count):
    even = index % 2 == 0
    before = jnp.where(even, second, first)
    after = jnp.where(even, first, second)
    return jnp.where(index > 0, before, 0.0), jnp.where(index < count - 1, after, 0.0)


def prepare_kernel(
    place, field, amplitude, columns_first, columns_second, sorted_out, total_out, held
):
    frames, length, _ = amplitude.shape
    half = length // 2
    planes, side, _ = field.shape
    margin = MARGIN
    even = place[2] % 2 == 0
    for plane in range(planes):
        left = pack_rows(field[plane, :, :LANES], 0, margin)
        right = pack_rows(field[plane, :, side - LANES :], LANES - margin, margin)
        columns_first[plane] = jnp.where(even, right, left)
        columns_second[plane] = jnp.where(even, left, right)
    row = lax.broadcasted_iota(jnp.int32, (length, length), 0)
    column = lax.broadcasted_iota(jnp.int32, (length, length), 1)
    source = jnp.where(column < half, 2 * column, 2 * (column - half) + 1)
    order = jnp.where(row == source, 1.0, 0.0).astype(bf16)
    total = jnp.zeros((SUBLANES, length), f32)
    for f in range(frames):
        values = amplitude[f]
        total += jnp.sum((values * values).reshape(length // SUBLANES, SUBLANES, length), 0)
        high = values.astype(bf16)
        rest = values - high.astype(f32)
        middle = rest.astype(bf16)
        low = (rest - middle.astype(f32)).astype(bf16)
        placed = dot(high, order) + (dot(middle, order) + dot(low, order))
        for parity in range(2):
            held[f, parity] = placed[:, parity * half : (parity + 1) * half]
            for start in range(2):
                at = 2 * parity + start
                sorted_out[f, at * half : (at + 1) * half, :] = held[
                    f, parity, pl.ds(start, half, stride=2), :
                ]
    total_out[...] = sum(total[:, t * LANES : (t + 1) * LANES] for t in range(length // LANES))


def powers_kernel(frames, margin, offsets, probe, powers):
    length = probe.shape[1]
    power = probe[0] * probe[0] + probe[1] * probe[1]
    powers[...] = jnp.zeros(powers.shape, f32)
    for f in range(frames):
        add_window(powers, power, spot(offsets, f, margin, length + SUBLANES))


def corner_kernel(
    counts, place, first, second, inner_first, inner_second, above, below, first_out, second_out
):
    planes, margin, side = first.shape
    inner = inner_first.shape[1]
    even = place[2] % 2 == 0
    for plane in range(planes):
        before, after = neighbours(first[plane], second[plane], place[1], counts[0])
        above[plane] = before
        below[plane] = after
        both = jnp.concatenate([before, after], 0)
        left = pack_rows(both[:, :LANES], 0, margin)
        right = pack_rows(both[:, side - LANES :], LANES - margin, margin)
        first_out[plane, :inner] = inner_first[plane]
        first_out[plane, inner:] = jnp.where(even, right, left)
        second_out[plane, :inner] = inner_second[plane]
        second_out[plane, inner:] = jnp.where(even, left, right)


def transform_pair(waves, row_turn, column_turn, matrices, amplitudes):
    length = waves[0][0].shape[0]
    half = length // 2
    row_cos, row_sin = row_turn
    column_cos, column_sin = column_turn

    mixed = []
    for real, imag in waves:
        odd = turned(real[:half] - real[half:], imag[:half] - imag[half:], row_cos, -row_sin)
        stacked = jnp.concatenate(
            [
                jnp.concatenate([real[:half] + real[half:], imag[:half] + imag[half:]], 0),
                jnp.concatenate(odd, 0),
            ],
            1,
        )
        mixed.append(matrix_times(matrices.at[0], stacked))

    far = []
    for value in mixed:
        evens, odds = [], []
        for parity in range(2):
            part = value[:, parity * length : (parity + 1) * length]
            real, imag = part[:half], part[half:]
            evens.append(
                jnp.concatenate(
                    [real[:, :half] + real[:, half:], imag[:, :half] + imag[:, half:]], 1
                )
            )
            odd = turned(
                real[:, :half] - real[:, half:],
                imag[:, :half] - imag[:, half:],
                column_cos,
                -column_sin,
            )
            odds.append(jnp.concatenate(odd, 1))
        far.append(times_matrix(jnp.concatenate(evens + odds, 0), matrices.at[1]))

    turned_back = []
    for value, amplitude in zip(far, amplitudes):
        real, imag = value[:, :half], value[:, half:]
        factor = amplitude * lax.rsqrt(real * real + imag * imag + smoothing)
        corrected = jnp.concatenate([real * factor, imag * factor], 1)
        turned_back.append(times_matrix(corrected, matrices.at[0]))

    near = []
    for value in turned_back:
        even, odd = value[:length], value[length:]
        odd_real, odd_imag = turned(odd[:, :half], odd[:, half:], column_cos, column_sin)
        even_real, even_imag = even[:, :half], even[:, half:]
        real = jnp.concatenate([even_real + odd_real, even_real - odd_real], 1)
        imag = jnp.concatenate([even_imag + odd_imag, even_imag - odd_imag], 1)
        stacked = jnp.concatenate(
            [
                jnp.concatenate([real[:half], imag[:half]], 0),
                jnp.concatenate([real[half:], imag[half:]], 0),
            ],
            1,
        )
        near.append(matrix_times(matrices.at[1], stacked))

    results = []
    for value in near:
        even, odd = value[:, :length], value[:, length:]
        odd_real, odd_imag = turned(odd[:half], odd[half:], row_cos, row_sin)
        results.append(
            (
                jnp.concatenate([even[:half] + odd_real, even[:half] - odd_real], 0),
                jnp.concatenate([even[half:] + odd_imag, even[half:] - odd_imag], 0),
            )
        )
    return results


def frames_kernel(
    counts,
    blocks,
    place,
    offsets,
    field,
    above,
    below,
    columns_first,
    columns_second,
    probe,
    amplitude,
    total,
    powers,
    matrices,
    row_turn,
    column_turn,
    work,
    kept,
    sent,
    later,
    padded,
    sums,
):
    frames = amplitude.shape[0]
    length = probe.shape[1]
    side = field.shape[1]
    margin = above.shape[1]
    reach = side + 2 * margin
    taller = length + SUBLANES
    per = LANES // margin
    inner = side // per
    tiles = length // LANES
    last = side // LANES + 1

    for plane in range(2):
        for tile in range(side // LANES):
            lanes = pl.ds(tile * LANES, LANES)
            padded[plane, tile + 1, :margin, :] = above[plane, :, lanes]
            padded[plane, tile + 1, margin : margin + side, :] = field[plane, :, lanes]
            padded[plane, tile + 1, margin + side : reach, :] = below[plane, :, lanes]
        left, right = neighbours(
            columns_first[plane], columns_second[plane], place[2], counts[1]
        )
        for tile, packed, lane in ((0, left, LANES - margin), (last, right, 0)):
            corners = unpack_rows(packed[inner:], lane, margin)
            padded[plane, tile, :margin, :] = corners[:margin]
            padded[plane, tile, margin : margin + side, :] = unpack_rows(
                packed[:inner], lane, margin
            )
            padded[plane, tile, margin + side : reach, :] = corners[margin:]
        padded[plane, :, reach:, :] = jnp.zeros((last + 1, SUBLANES, LANES), f32)
    work[...] = jnp.zeros(work.shape, f32)
    first = jnp.where(place[1] + place[2] == 0, 1.0, 0.0).astype(f32)
    sums[0] = probe[0] * first
    sums[1] = probe[1] * first
    sums[2] = jnp.full((length, length), regular, f32) * first

    row_cos, row_sin = (jnp.concatenate([row_turn[k]] * tiles, 1) for k in range(2))
    column_cos, column_sin = (column_turn[k, 0:1, :] for k in range(2))
    together = 2 if frames % 2 == 0 else 1

    def visit(step, carry):
        chosen = [step * together + k for k in range(together)]
        spots = [spot(offsets, f, margin, taller) for f in chosen]
        windows = [
            tuple(window_of(padded, plane, spot_of, tiles) for plane in range(2))
            for spot_of in spots
        ]
        probe_real, probe_imag = probe[0], probe[1]
        waves = [
            (
                probe_real * real - probe_imag * imag,
                probe_real * imag + probe_imag * real,
            )
            for real, imag in windows
        ]
        nears = transform_pair(
            waves,
            (row_cos, row_sin),
            (column_cos, column_sin),
            matrices,
            [amplitude[f] for f in chosen],
        )
        for (window_real, window_imag), (near_real, near_imag), spot_of in zip(
            windows, nears, spots
        ):
            sums[0] += window_real * near_real + window_imag * near_imag
            sums[1] += window_real * near_imag - window_imag * near_real
            sums[2] += window_real * window_real + window_imag * window_imag
            add_window(work.at[0], probe_real * near_real + probe_imag * near_imag, spot_of)
            add_window(work.at[1], probe_real * near_imag - probe_imag * near_real, spot_of)
        return carry

    lax.fori_loop(0, frames // together, visit, 0)

    rows = length // blocks
    half_rows = blocks // 2 * 3 * tiles * rows
    for p in range(blocks):
        out, q, base = (
            (kept, p, place[0]) if p < blocks // 2 else (sent, p - blocks // 2, place[3])
        )
        source = pl.multiple_of((base ^ q) * rows, rows)
        for plane in range(3):
            for tile in range(tiles):
                start = ((3 * q + plane) * tiles + tile) * rows
                out[start : start + rows, :] = sums[
                    plane, pl.ds(source, rows), pl.ds(tile * LANES, LANES)
                ]
    kept[half_rows:, :] = total[...]
    sent[half_rows : half_rows + SUBLANES, :] = total[...]
    even = place[2] % 2 == 0
    start = half_rows + SUBLANES
    depth = reach // per
    for plane in range(3):
        canvas = powers if plane == 2 else work.at[plane]
        right = pack_rows(canvas[last, :reach, :], 0, margin)
        left = pack_rows(canvas[0, :reach, :], LANES - margin, margin)
        at = start + plane * depth
        sent[at : at + depth, :] = jnp.where(even, right, left)
        later[plane * depth : (plane + 1) * depth, :] = jnp.where(even, left, right)


def row_edge_kernel(counts, margin, place, work, powers, first, second, first_out, second_out):
    planes = work.shape[0] + 1
    tiles = work.shape[1] - 2
    reach = work.shape[2] - SUBLANES
    depth = first.shape[0] // planes
    even = place[1] % 2 == 0
    for plane in range(planes):
        canvas = powers if plane == planes - 1 else work.at[plane]
        at = pl.ds(plane * depth, depth)
        before, after = neighbours(first[at, :], second[at, :], place[2], counts[1])
        last = LANES // margin - 1
        edges = []
        for begin, chunk, cut in (
            (0, 0, slice(None, margin)),
            (reach - margin, last, slice(depth - margin, None)),
        ):
            parts = [canvas[tile + 1, begin : begin + margin, :] for tile in range(tiles)]
            parts[0] += unpack(before, chunk, 0, margin)[cut]
            parts[-1] += unpack(after, chunk, LANES - margin, margin)[cut]
            edges.append(parts)
        for tile in range(tiles):
            at = pl.ds((plane * tiles + tile) * margin, margin)
            first_out[at, :] = jnp.where(even, edges[1][tile], edges[0][tile])
            second_out[at, :] = jnp.where(even, edges[0][tile], edges[1][tile])


def object_kernel(
    counts, margin, place, field, work, powers, first, second, row_first, row_second, out
):
    planes = work.shape[0] + 1
    tiles = work.shape[1] - 2
    side = field.shape[1]
    depth = first.shape[0] // planes
    for tile in range(tiles):
        lanes = pl.ds(tile * LANES, LANES)
        total = []
        for plane in range(planes):
            canvas = powers if plane == planes - 1 else work.at[plane]
            at = pl.ds((plane * tiles + tile) * margin, margin)
            above, below = neighbours(row_first[at, :], row_second[at, :], place[1], counts[0])
            part = canvas[tile + 1, margin : margin + side, :]
            at = pl.ds(plane * depth, depth)
            before, after = neighbours(first[at, :], second[at, :], place[2], counts[1])
            if tile == 0:
                part += unpack_rows(before, 0, margin)[margin : margin + side]
            if tile == tiles - 1:
                part += unpack_rows(after, LANES - margin, margin)[margin : margin + side]
            part = jnp.concatenate(
                [
                    part[:margin] + above,
                    part[margin : side - margin],
                    part[side - margin :] + below,
                ],
                0,
            )
            total.append(part)
        weight = 1.0 / (total[2] + regular)
        out[0, :, lanes] = (field[0, :, lanes] + total[0]) * weight
        out[1, :, lanes] = (field[1, :, lanes] + total[1]) * weight


def probe_kernel(frame_count, blocks, place, stepped, total, out):
    planes, length, _ = out.shape
    tiles = length // LANES
    rows = length // blocks
    values = stepped[...]
    power = jnp.sum(values * values)
    target = jnp.sum(total[...]) / frame_count
    scale = jnp.sqrt(jnp.full((rows, LANES), target / (power + epsilon), f32))
    for p in range(blocks):
        base, q = (place[0], p) if p < blocks // 2 else (place[3], p - blocks // 2)
        home = pl.multiple_of((base ^ q) * rows, rows)
        for plane in range(planes):
            for tile in range(tiles):
                start = ((planes * p + plane) * tiles + tile) * rows
                out[plane, pl.ds(home, rows), pl.ds(tile * LANES, LANES)] = (
                    values[start : start + rows] * scale
                )


def shape(*dims):
    return jax.ShapeDtypeStruct(dims, f32)


def call(kernel, outputs, scalars=0, operands=0, scratch=(), cost=None):
    vmem = pl.BlockSpec(memory_space=pltpu.VMEM)
    smem = pl.BlockSpec(memory_space=pltpu.SMEM)
    return pl.pallas_call(
        kernel,
        out_shape=outputs,
        in_specs=[smem] * scalars + [vmem] * operands,
        out_specs=jax.tree.map(lambda _: vmem, outputs),
        scratch_shapes=list(scratch),
        cost_estimate=cost,
        compiler_params=pltpu.CompilerParams(vmem_limit_bytes=40 * 1024 * 1024),
    )


def paired(block, axis, first):
    count = lax.axis_size(axis)
    target = list(range(count))
    for i in range(first, count - 1, 2):
        target[i], target[i + 1] = i + 1, i
    return lax.ppermute(block, axis, list(enumerate(target)))


def exchanged(block, orders, distance):
    count = lax.axis_size("row") * lax.axis_size("col")
    masks = [
        sum(1 << bit for k, bit in enumerate(order) if distance >> k & 1) for order in orders
    ]
    return lax.ppermute(block, ("row", "col"), [(i, i ^ masks[i % 2]) for i in range(count)])


def per_device(object_field, probe, amplitudes, positions):
    planes, side, _ = object_field.shape
    length = probe.shape[1]
    margin = MARGIN
    reach = side + 2 * margin
    per = LANES // margin
    tiles = length // LANES
    measured = amplitudes[0, 0]
    frames = measured.shape[0]
    counts = lax.axis_size("row"), lax.axis_size("col")
    row = lax.axis_index("row").astype(jnp.int32)
    col = lax.axis_index("col").astype(jnp.int32)
    index = row * counts[1] + col
    col_bits = (counts[1] - 1).bit_length()
    across = list(range(1, col_bits))
    along = list(range(col_bits, col_bits + (counts[0] - 1).bit_length()))
    orders = (across + along, along + across)
    halvings = 2
    blocks = 2 << halvings
    rows = length // blocks
    homes = [
        sum(((index >> order[k]) & 1) << k for k in range(halvings))
        for order in orders
    ]
    core = index & 1
    homes[1] += blocks // 2
    place = jnp.stack(
        [
            jnp.where(core == 0, homes[0], homes[1]),
            row,
            col,
            jnp.where(core == 0, homes[1], homes[0]),
        ]
    )

    edge_rows = shape(planes, margin, side)
    inner = shape(planes, side // per, LANES)
    odd = row & 1
    last = side - margin
    rows_first = lax.dynamic_slice_in_dim(object_field, last - odd * last, margin, 1)
    rows_second = lax.dynamic_slice_in_dim(object_field, odd * last, margin, 1)
    rows_second = paired(rows_second, "row", 1)
    rows_first = paired(rows_first, "row", 0)
    inner_first, inner_second, ordered, total = call(
        prepare_kernel,
        (inner, inner, shape(frames, 2 * length, length // 2), shape(SUBLANES, LANES)),
        scalars=1,
        operands=2,
        scratch=(pltpu.VMEM((frames, 2, length, length // 2), f32),),
        cost=pl.CostEstimate(flops=10**9, bytes_accessed=2 * measured.size * 4, transcendentals=0),
    )(place, object_field, measured)
    packed = shape(planes, reach // per, LANES)
    above, below, columns_first, columns_second = call(
        functools.partial(corner_kernel, counts),
        (edge_rows, edge_rows, packed, packed),
        scalars=1,
        operands=4,
    )(place, rows_first, rows_second, inner_first, inner_second)
    columns_second = paired(columns_second, "col", 1)
    columns_first = paired(columns_first, "col", 0)

    powers = call(
        functools.partial(powers_kernel, frames, margin),
        shape(side // LANES + 2, reach + SUBLANES, LANES),
        scalars=1,
        operands=1,
        cost=pl.CostEstimate(flops=10**9, bytes_accessed=2 * measured.size * 4, transcendentals=0),
    )(positions[0, 0], probe)
    matrices, row_turn, column_turn = tables(length)
    half_rows = blocks // 2 * 3 * tiles * rows
    depth = 3 * reach // per
    work, kept, sent, edge = call(
        functools.partial(frames_kernel, counts, blocks),
        (
            shape(2, side // LANES + 2, reach + SUBLANES, LANES),
            shape(half_rows + SUBLANES, LANES),
            shape(half_rows + SUBLANES + depth, LANES),
            shape(depth, LANES),
        ),
        scalars=2,
        operands=12,
        scratch=(
            pltpu.VMEM((2, side // LANES + 2, reach + SUBLANES, LANES), f32),
            pltpu.VMEM((3, length, length), f32),
        ),
    )(
        place,
        positions[0, 0],
        object_field,
        above,
        below,
        columns_first,
        columns_second,
        probe,
        ordered,
        total,
        powers,
        jnp.asarray(matrices),
        jnp.asarray(row_turn),
        jnp.asarray(column_turn),
    )

    arrived = paired(sent, "col", 0)
    current = kept + arrived[: half_rows + SUBLANES]
    first = arrived[half_rows + SUBLANES :]
    second = paired(edge, "col", 1)
    block = 3 * tiles * rows
    total = current[-SUBLANES:]
    quarters = [
        jnp.concatenate([current[d * block : (d + 1) * block], total], 0) for d in range(blocks // 2)
    ]
    terms = quarters[:1] + [exchanged(quarters[d], orders, d) for d in range(1, blocks // 2)]
    while len(terms) > 1:
        terms = [terms[k] + terms[k + 1] for k in range(0, len(terms), 2)]
    current = terms[0]
    current, second = lax.optimization_barrier((current, second))
    out = shape(3 * tiles * margin, LANES)
    row_first, row_second = call(
        functools.partial(row_edge_kernel, counts, margin), (out, out), scalars=1, operands=4
    )(place, work, powers, first, second)
    row_first = paired(row_first, "row", 0)
    for step in range(halvings, len(orders[0])):
        if step == halvings + 1:
            current, row_first, row_second = lax.optimization_barrier(
                (current, row_first, row_second)
            )
            row_second = paired(row_second, "row", 1)
        current = current + exchanged(current, orders, 1 << step)
    size = tiles * rows
    weight = current[2 * size : 3 * size]
    stepped = current[: 2 * size] / jnp.concatenate([weight, weight], 0)
    stepped = jnp.concatenate(
        [stepped] + [exchanged(stepped, orders, d) for d in range(1, blocks // 2)], 0
    )
    stepped, row_second = lax.optimization_barrier((stepped, row_second))
    object_next = call(
        functools.partial(object_kernel, counts, margin),
        shape(*object_field.shape),
        scalars=1,
        operands=7,
    )(place, object_field, work, powers, first, second, row_first, row_second)
    stepped = jnp.concatenate([stepped, paired(stepped, "col", 0)], 0)
    frame_count = frames * counts[0] * counts[1]
    probe_next = call(
        functools.partial(probe_kernel, frame_count, blocks),
        shape(*probe.shape),
        scalars=1,
        operands=2,
    )(place, stepped, current[3 * size :])
    return (object_next, probe_next)


def solution(mesh):
    return jax.shard_map(
        per_device,
        mesh=mesh,
        in_specs=(
            P(None, "row", "col"),
            P(),
            P("row", "col", None, None, None),
            P("row", "col", None, None),
        ),
        out_specs=(P(None, "row", "col"), P()),
        check_vma=False,
    )
```

```python
import functools
import math

import jax
import jax.numpy as jnp
import numpy as np
from jax import lax
from jax.experimental import pallas as pl
from jax.experimental.pallas import tpu as pltpu
from jax.sharding import PartitionSpec as P

MARGIN = 32
LANES = 128
SUBLANES = 8

smoothing = 0.1
regular = 1.0
epsilon = 1e-06

f32 = jnp.float32
bf16 = jnp.bfloat16


def tables(length):
    half = length // 2
    scaling = 1.0 / math.sqrt(length)
    k = np.arange(half)
    phases = (k[:, None] * k[None, :] % half) * (2.0 * math.pi / half)
    cosine, sine = np.cos(phases) * scaling, np.sin(phases) * scaling
    right = np.block([[cosine, -sine], [sine, cosine]])
    left = np.block([[cosine, sine], [-sine, cosine]])
    both = np.stack([left, right]).astype(np.float32)
    high = both.astype(bf16)
    low = (both - high.astype(np.float32)).astype(bf16)
    matrices = np.stack([high, low], 1)
    angle = k * (2.0 * math.pi / length)
    turn = np.stack([np.cos(angle), np.sin(angle)]).astype(np.float32)
    rows = np.broadcast_to(turn[:, :, None], (2, half, LANES)).copy()
    columns = np.broadcast_to(turn[:, None, :], (2, SUBLANES, half)).copy()
    return matrices, rows, columns


def split(x):
    high = x.astype(bf16)
    return high, (x - high.astype(f32)).astype(bf16)


def dot(a, b):
    return jnp.dot(a, b, preferred_element_type=f32)


def times_matrix(data, matrix):
    high, low = split(data)
    return dot(
        jnp.concatenate([high, low, high], 1),
        jnp.concatenate([matrix[0], matrix[0], matrix[1]], 0),
    )


def matrix_times(matrix, data):
    high, low = split(data)
    return dot(
        jnp.concatenate([matrix[0], matrix[0], matrix[1]], 1),
        jnp.concatenate([high, low, high], 0),
    )


def turned(real, imag, cosine, sine):
    return real * cosine - imag * sine, real * sine + imag * cosine


def pack(chunks, lane, width):
    place = lax.broadcasted_iota(jnp.int32, chunks[0].shape, 1) // width
    out = jnp.zeros_like(chunks[0])
    for q, chunk in enumerate(chunks):
        shift = (q * width - lane) % LANES
        moved = pltpu.roll(chunk, shift, 1) if shift else chunk
        out = jnp.where(place == q, moved, out)
    return out


def pack_rows(rows, lane, width):
    count = rows.shape[0] * width // LANES
    return pack([rows[q : q + count] for q in range(0, rows.shape[0], count)], lane, width)


def unpack(packed, q, lane, width):
    shift = (lane - q * width) % LANES
    moved = pltpu.roll(packed, shift, 1) if shift else packed
    place = lax.broadcasted_iota(jnp.int32, packed.shape, 1)
    return jnp.where((place >= lane) & (place < lane + width), moved, 0.0)


def unpack_rows(packed, lane, width):
    return jnp.concatenate([unpack(packed, q, lane, width) for q in range(LANES // width)], 0)


def lifted(tile, shift):
    groups = tile.shape[0] // SUBLANES
    turned_rows = pltpu.roll(
        tile.reshape(groups, SUBLANES, LANES), lax.rem(SUBLANES - shift, SUBLANES), 1
    )
    place = lax.broadcasted_iota(jnp.int32, (groups - 1, SUBLANES, LANES), 1)
    picked = jnp.where(place < SUBLANES - shift, turned_rows[:-1], turned_rows[1:])
    return picked.reshape((groups - 1) * SUBLANES, LANES)


def lowered(tile, shift):
    groups = tile.shape[0] // SUBLANES
    moved = pltpu.roll(tile.reshape(groups, SUBLANES, LANES), shift, 1)
    none = jnp.zeros((1, SUBLANES, LANES), f32)
    place = lax.broadcasted_iota(jnp.int32, (groups + 1, SUBLANES, LANES), 1)
    picked = jnp.where(
        place >= shift, jnp.concatenate([moved, none], 0), jnp.concatenate([none, moved], 0)
    )
    return picked.reshape((groups + 1) * SUBLANES, LANES)


def spot(offsets, f, margin, taller):
    a, b = offsets[f, 0], offsets[f, 1]
    shift = lax.rem(a, SUBLANES)
    lane = b + LANES - margin
    tile = lane // LANES
    return pl.ds(pl.multiple_of(a - shift, SUBLANES), taller), shift, tile, lane - tile * LANES


def window_of(padded, plane, spot_of, tiles):
    at, shift, base, lane = spot_of
    moved = [
        pltpu.roll(padded[plane, base + t, at, :], lax.rem(LANES - lane, LANES), 1)
        for t in range(tiles + 1)
    ]
    place = lax.broadcasted_iota(jnp.int32, moved[0].shape, 1)
    parts = [
        lifted(jnp.where(place < LANES - lane, moved[t], moved[t + 1]), shift)
        for t in range(tiles)
    ]
    return jnp.concatenate(parts, 1)


def add_window(work, term, spot_of):
    at, shift, base, lane = spot_of
    tiles = term.shape[1] // LANES
    moved = [
        pltpu.roll(lowered(term[:, t * LANES : (t + 1) * LANES], shift), lane, 1)
        for t in range(tiles)
    ]
    none = jnp.zeros_like(moved[0])
    place = lax.broadcasted_iota(jnp.int32, none.shape, 1)
    for t in range(tiles + 1):
        here = moved[t] if t < tiles else none
        before = moved[t - 1] if t else none
        work[base + t, at, :] += jnp.where(place >= lane, here, before)


def neighbours(first, second, index, count):
    even = index % 2 == 0
    before = jnp.where(even, second, first)
    after = jnp.where(even, first, second)
    return jnp.where(index > 0, before, 0.0), jnp.where(index < count - 1, after, 0.0)


def pack_kernel(margin, place, field, columns_first, columns_second):
    planes, side, _ = field.shape
    even = place[2] % 2 == 0
    for plane in range(planes):
        left = pack_rows(field[plane, :, :LANES], 0, margin)
        right = pack_rows(field[plane, :, side - LANES :], LANES - margin, margin)
        columns_first[plane] = jnp.where(even, right, left)
        columns_second[plane] = jnp.where(even, left, right)


def prepare_kernel(margin, offsets, amplitude, probe, sorted_out, total_out, powers, held):
    frames, length, _ = amplitude.shape
    half = length // 2
    power = probe[0] * probe[0] + probe[1] * probe[1]
    powers[...] = jnp.zeros(powers.shape, f32)
    for f in range(frames):
        add_window(powers, power, spot(offsets, f, margin, length + SUBLANES))
    row = lax.broadcasted_iota(jnp.int32, (length, length), 0)
    column = lax.broadcasted_iota(jnp.int32, (length, length), 1)
    source = jnp.where(column < half, 2 * column, 2 * (column - half) + 1)
    order = jnp.where(row == source, 1.0, 0.0).astype(bf16)
    total = jnp.zeros((SUBLANES, length), f32)
    for f in range(frames):
        values = amplitude[f]
        total += jnp.sum((values * values).reshape(length // SUBLANES, SUBLANES, length), 0)
        high = values.astype(bf16)
        rest = values - high.astype(f32)
        middle = rest.astype(bf16)
        low = (rest - middle.astype(f32)).astype(bf16)
        placed = dot(high, order) + (dot(middle, order) + dot(low, order))
        for parity in range(2):
            held[f, parity] = placed[:, parity * half : (parity + 1) * half]
            for start in range(2):
                at = 2 * parity + start
                sorted_out[f, at * half : (at + 1) * half, :] = held[
                    f, parity, pl.ds(start, half, stride=2), :
                ]
    total_out[...] = sum(total[:, t * LANES : (t + 1) * LANES] for t in range(length // LANES))


def corner_kernel(
    counts, place, first, second, inner_first, inner_second, above, below, first_out, second_out
):
    planes, margin, side = first.shape
    inner = inner_first.shape[1]
    even = place[2] % 2 == 0
    for plane in range(planes):
        before, after = neighbours(first[plane], second[plane], place[1], counts[0])
        above[plane] = before
        below[plane] = after
        both = jnp.concatenate([before, after], 0)
        left = pack_rows(both[:, :LANES], 0, margin)
        right = pack_rows(both[:, side - LANES :], LANES - margin, margin)
        first_out[plane, :inner] = inner_first[plane]
        first_out[plane, inner:] = jnp.where(even, right, left)
        second_out[plane, :inner] = inner_second[plane]
        second_out[plane, inner:] = jnp.where(even, left, right)


def transform_pair(waves, row_turn, column_turn, matrices, amplitudes):
    length = waves[0][0].shape[0]
    half = length // 2
    row_cos, row_sin = row_turn
    column_cos, column_sin = column_turn

    mixed = []
    for real, imag in waves:
        odd = turned(real[:half] - real[half:], imag[:half] - imag[half:], row_cos, -row_sin)
        stacked = jnp.concatenate(
            [
                jnp.concatenate([real[:half] + real[half:], imag[:half] + imag[half:]], 0),
                jnp.concatenate(odd, 0),
            ],
            1,
        )
        mixed.append(matrix_times(matrices.at[0], stacked))

    far = []
    for value in mixed:
        evens, odds = [], []
        for parity in range(2):
            part = value[:, parity * length : (parity + 1) * length]
            real, imag = part[:half], part[half:]
            evens.append(
                jnp.concatenate(
                    [real[:, :half] + real[:, half:], imag[:, :half] + imag[:, half:]], 1
                )
            )
            odd = turned(
                real[:, :half] - real[:, half:],
                imag[:, :half] - imag[:, half:],
                column_cos,
                -column_sin,
            )
            odds.append(jnp.concatenate(odd, 1))
        far.append(times_matrix(jnp.concatenate(evens + odds, 0), matrices.at[1]))

    turned_back = []
    for value, amplitude in zip(far, amplitudes):
        real, imag = value[:, :half], value[:, half:]
        factor = amplitude * lax.rsqrt(real * real + imag * imag + smoothing)
        corrected = jnp.concatenate([real * factor, imag * factor], 1)
        turned_back.append(times_matrix(corrected, matrices.at[0]))

    near = []
    for value in turned_back:
        even, odd = value[:length], value[length:]
        odd_real, odd_imag = turned(odd[:, :half], odd[:, half:], column_cos, column_sin)
        even_real, even_imag = even[:, :half], even[:, half:]
        real = jnp.concatenate([even_real + odd_real, even_real - odd_real], 1)
        imag = jnp.concatenate([even_imag + odd_imag, even_imag - odd_imag], 1)
        stacked = jnp.concatenate(
            [
                jnp.concatenate([real[:half], imag[:half]], 0),
                jnp.concatenate([real[half:], imag[half:]], 0),
            ],
            1,
        )
        near.append(matrix_times(matrices.at[1], stacked))

    results = []
    for value in near:
        even, odd = value[:, :length], value[:, length:]
        odd_real, odd_imag = turned(odd[:half], odd[half:], row_cos, row_sin)
        results.append(
            (
                jnp.concatenate([even[:half] + odd_real, even[:half] - odd_real], 0),
                jnp.concatenate([even[half:] + odd_imag, even[half:] - odd_imag], 0),
            )
        )
    return results


def frames_kernel(
    counts,
    blocks,
    place,
    offsets,
    field,
    above,
    below,
    columns_first,
    columns_second,
    probe,
    amplitude,
    total,
    powers,
    matrices,
    row_turn,
    column_turn,
    work,
    kept,
    sent,
    later,
    padded,
    sums,
):
    frames = amplitude.shape[0]
    length = probe.shape[1]
    side = field.shape[1]
    margin = above.shape[1]
    reach = side + 2 * margin
    taller = length + SUBLANES
    per = LANES // margin
    inner = side // per
    tiles = length // LANES
    last = side // LANES + 1

    for plane in range(2):
        for tile in range(side // LANES):
            lanes = pl.ds(tile * LANES, LANES)
            padded[plane, tile + 1, :margin, :] = above[plane, :, lanes]
            padded[plane, tile + 1, margin : margin + side, :] = field[plane, :, lanes]
            padded[plane, tile + 1, margin + side : reach, :] = below[plane, :, lanes]
        left, right = neighbours(
            columns_first[plane], columns_second[plane], place[2], counts[1]
        )
        for tile, packed, lane in ((0, left, LANES - margin), (last, right, 0)):
            corners = unpack_rows(packed[inner:], lane, margin)
            padded[plane, tile, :margin, :] = corners[:margin]
            padded[plane, tile, margin : margin + side, :] = unpack_rows(
                packed[:inner], lane, margin
            )
            padded[plane, tile, margin + side : reach, :] = corners[margin:]
        padded[plane, :, reach:, :] = jnp.zeros((last + 1, SUBLANES, LANES), f32)
    work[...] = jnp.zeros(work.shape, f32)
    first = jnp.where(place[1] + place[2] == 0, 1.0, 0.0).astype(f32)
    sums[0] = probe[0] * first
    sums[1] = probe[1] * first
    sums[2] = jnp.full((length, length), regular, f32) * first

    row_cos, row_sin = (jnp.concatenate([row_turn[k]] * tiles, 1) for k in range(2))
    column_cos, column_sin = (column_turn[k, 0:1, :] for k in range(2))
    together = 2 if frames % 2 == 0 else 1

    def visit(step, carry):
        chosen = [step * together + k for k in range(together)]
        spots = [spot(offsets, f, margin, taller) for f in chosen]
        windows = [
            tuple(window_of(padded, plane, spot_of, tiles) for plane in range(2))
            for spot_of in spots
        ]
        probe_real, probe_imag = probe[0], probe[1]
        waves = [
            (
                probe_real * real - probe_imag * imag,
                probe_real * imag + probe_imag * real,
            )
            for real, imag in windows
        ]
        nears = transform_pair(
            waves,
            (row_cos, row_sin),
            (column_cos, column_sin),
            matrices,
            [amplitude[f] for f in chosen],
        )
        for (window_real, window_imag), (near_real, near_imag), spot_of in zip(
            windows, nears, spots
        ):
            sums[0] += window_real * near_real + window_imag * near_imag
            sums[1] += window_real * near_imag - window_imag * near_real
            sums[2] += window_real * window_real + window_imag * window_imag
            add_window(work.at[0], probe_real * near_real + probe_imag * near_imag, spot_of)
            add_window(work.at[1], probe_real * near_imag - probe_imag * near_real, spot_of)
        return carry

    lax.fori_loop(0, frames // together, visit, 0)

    rows = length // blocks
    half_rows = blocks // 2 * 3 * tiles * rows
    for p in range(blocks):
        out, q, base = (
            (kept, p, place[0]) if p < blocks // 2 else (sent, p - blocks // 2, place[3])
        )
        source = pl.multiple_of((base ^ q) * rows, rows)
        for plane in range(3):
            for tile in range(tiles):
                start = ((3 * q + plane) * tiles + tile) * rows
                out[start : start + rows, :] = sums[
                    plane, pl.ds(source, rows), pl.ds(tile * LANES, LANES)
                ]
    kept[half_rows:, :] = total[...]
    sent[half_rows : half_rows + SUBLANES, :] = total[...]
    even = place[2] % 2 == 0
    start = half_rows + SUBLANES
    depth = reach // per
    for plane in range(3):
        canvas = powers if plane == 2 else work.at[plane]
        right = pack_rows(canvas[last, :reach, :], 0, margin)
        left = pack_rows(canvas[0, :reach, :], LANES - margin, margin)
        at = start + plane * depth
        sent[at : at + depth, :] = jnp.where(even, right, left)
        later[plane * depth : (plane + 1) * depth, :] = jnp.where(even, left, right)


def row_edge_kernel(counts, margin, place, work, powers, first, second, first_out, second_out):
    planes = work.shape[0] + 1
    tiles = work.shape[1] - 2
    reach = work.shape[2] - SUBLANES
    depth = first.shape[0] // planes
    even = place[1] % 2 == 0
    for plane in range(planes):
        canvas = powers if plane == planes - 1 else work.at[plane]
        at = pl.ds(plane * depth, depth)
        before, after = neighbours(first[at, :], second[at, :], place[2], counts[1])
        last = LANES // margin - 1
        edges = []
        for begin, chunk, cut in (
            (0, 0, slice(None, margin)),
            (reach - margin, last, slice(depth - margin, None)),
        ):
            parts = [canvas[tile + 1, begin : begin + margin, :] for tile in range(tiles)]
            parts[0] += unpack(before, chunk, 0, margin)[cut]
            parts[-1] += unpack(after, chunk, LANES - margin, margin)[cut]
            edges.append(parts)
        for tile in range(tiles):
            at = pl.ds((plane * tiles + tile) * margin, margin)
            first_out[at, :] = jnp.where(even, edges[1][tile], edges[0][tile])
            second_out[at, :] = jnp.where(even, edges[0][tile], edges[1][tile])


def object_kernel(
    counts, margin, place, field, work, powers, first, second, row_first, row_second, out
):
    planes = work.shape[0] + 1
    tiles = work.shape[1] - 2
    side = field.shape[1]
    depth = first.shape[0] // planes
    for tile in range(tiles):
        lanes = pl.ds(tile * LANES, LANES)
        total = []
        for plane in range(planes):
            canvas = powers if plane == planes - 1 else work.at[plane]
            at = pl.ds((plane * tiles + tile) * margin, margin)
            above, below = neighbours(row_first[at, :], row_second[at, :], place[1], counts[0])
            part = canvas[tile + 1, margin : margin + side, :]
            at = pl.ds(plane * depth, depth)
            before, after = neighbours(first[at, :], second[at, :], place[2], counts[1])
            if tile == 0:
                part += unpack_rows(before, 0, margin)[margin : margin + side]
            if tile == tiles - 1:
                part += unpack_rows(after, LANES - margin, margin)[margin : margin + side]
            part = jnp.concatenate(
                [
                    part[:margin] + above,
                    part[margin : side - margin],
                    part[side - margin :] + below,
                ],
                0,
            )
            total.append(part)
        weight = 1.0 / (total[2] + regular)
        out[0, :, lanes] = (field[0, :, lanes] + total[0]) * weight
        out[1, :, lanes] = (field[1, :, lanes] + total[1]) * weight


def probe_kernel(frame_count, blocks, place, stepped, total, out):
    planes, length, _ = out.shape
    tiles = length // LANES
    rows = length // blocks
    values = stepped[...]
    power = jnp.sum(values * values)
    target = jnp.sum(total[...]) / frame_count
    scale = jnp.sqrt(jnp.full((rows, LANES), target / (power + epsilon), f32))
    for p in range(blocks):
        base, q = (place[0], p) if p < blocks // 2 else (place[3], p - blocks // 2)
        home = pl.multiple_of((base ^ q) * rows, rows)
        for plane in range(planes):
            for tile in range(tiles):
                start = ((planes * p + plane) * tiles + tile) * rows
                out[plane, pl.ds(home, rows), pl.ds(tile * LANES, LANES)] = (
                    values[start : start + rows] * scale
                )


def shape(*dims):
    return jax.ShapeDtypeStruct(dims, f32)


def call(kernel, outputs, scalars=0, operands=0, scratch=(), cost=None):
    vmem = pl.BlockSpec(memory_space=pltpu.VMEM)
    smem = pl.BlockSpec(memory_space=pltpu.SMEM)
    return pl.pallas_call(
        kernel,
        out_shape=outputs,
        in_specs=[smem] * scalars + [vmem] * operands,
        out_specs=jax.tree.map(lambda _: vmem, outputs),
        scratch_shapes=list(scratch),
        cost_estimate=cost,
        compiler_params=pltpu.CompilerParams(vmem_limit_bytes=40 * 1024 * 1024),
    )


def paired(block, axis, first):
    count = lax.axis_size(axis)
    target = list(range(count))
    for i in range(first, count - 1, 2):
        target[i], target[i + 1] = i + 1, i
    return lax.ppermute(block, axis, list(enumerate(target)))


def exchanged(block, orders, distance):
    count = lax.axis_size("row") * lax.axis_size("col")
    masks = [
        sum(1 << bit for k, bit in enumerate(order) if distance >> k & 1) for order in orders
    ]
    return lax.ppermute(block, ("row", "col"), [(i, i ^ masks[i % 2]) for i in range(count)])


def per_device(object_field, probe, amplitudes, positions):
    planes, side, _ = object_field.shape
    length = probe.shape[1]
    margin = MARGIN
    reach = side + 2 * margin
    per = LANES // margin
    tiles = length // LANES
    measured = amplitudes[0, 0]
    frames = measured.shape[0]
    counts = lax.axis_size("row"), lax.axis_size("col")
    row = lax.axis_index("row").astype(jnp.int32)
    col = lax.axis_index("col").astype(jnp.int32)
    index = row * counts[1] + col
    col_bits = (counts[1] - 1).bit_length()
    across = list(range(1, col_bits))
    along = list(range(col_bits, col_bits + (counts[0] - 1).bit_length()))
    orders = (across + along, along + across)
    halvings = 2
    blocks = 2 << halvings
    rows = length // blocks
    homes = [
        sum(((index >> order[k]) & 1) << k for k in range(halvings))
        for order in orders
    ]
    core = index & 1
    homes[1] += blocks // 2
    place = jnp.stack(
        [
            jnp.where(core == 0, homes[0], homes[1]),
            row,
            col,
            jnp.where(core == 0, homes[1], homes[0]),
        ]
    )

    edge_rows = shape(planes, margin, side)
    inner = shape(planes, side // per, LANES)
    odd = row & 1
    last = side - margin
    rows_first = lax.dynamic_slice_in_dim(object_field, last - odd * last, margin, 1)
    rows_second = lax.dynamic_slice_in_dim(object_field, odd * last, margin, 1)
    rows_second = paired(rows_second, "row", 1)
    rows_first = paired(rows_first, "row", 0)
    inner_first, inner_second = call(
        functools.partial(pack_kernel, margin), (inner, inner), scalars=1, operands=1
    )(place, object_field)
    packed = shape(planes, reach // per, LANES)
    above, below, columns_first, columns_second = call(
        functools.partial(corner_kernel, counts),
        (edge_rows, edge_rows, packed, packed),
        scalars=1,
        operands=4,
    )(place, rows_first, rows_second, inner_first, inner_second)
    columns_second = paired(columns_second, "col", 1)
    columns_first = paired(columns_first, "col", 0)

    ordered, total, powers = call(
        functools.partial(prepare_kernel, margin),
        (
            shape(frames, 2 * length, length // 2),
            shape(SUBLANES, LANES),
            shape(side // LANES + 2, reach + SUBLANES, LANES),
        ),
        scalars=1,
        operands=2,
        scratch=(pltpu.VMEM((frames, 2, length, length // 2), f32),),
        cost=pl.CostEstimate(flops=10**9, bytes_accessed=2 * measured.size * 4, transcendentals=0),
    )(positions[0, 0], measured, probe)
    matrices, row_turn, column_turn = tables(length)
    half_rows = blocks // 2 * 3 * tiles * rows
    depth = 3 * reach // per
    work, kept, sent, edge = call(
        functools.partial(frames_kernel, counts, blocks),
        (
            shape(2, side // LANES + 2, reach + SUBLANES, LANES),
            shape(half_rows + SUBLANES, LANES),
            shape(half_rows + SUBLANES + depth, LANES),
            shape(depth, LANES),
        ),
        scalars=2,
        operands=12,
        scratch=(
            pltpu.VMEM((2, side // LANES + 2, reach + SUBLANES, LANES), f32),
            pltpu.VMEM((3, length, length), f32),
        ),
    )(
        place,
        positions[0, 0],
        object_field,
        above,
        below,
        columns_first,
        columns_second,
        probe,
        ordered,
        total,
        powers,
        jnp.asarray(matrices),
        jnp.asarray(row_turn),
        jnp.asarray(column_turn),
    )

    arrived = paired(sent, "col", 0)
    current = kept + arrived[: half_rows + SUBLANES]
    first = arrived[half_rows + SUBLANES :]
    second = paired(edge, "col", 1)
    block = 3 * tiles * rows
    total = current[-SUBLANES:]
    quarters = [
        jnp.concatenate([current[d * block : (d + 1) * block], total], 0) for d in range(blocks // 2)
    ]
    terms = quarters[:1] + [exchanged(quarters[d], orders, d) for d in range(1, blocks // 2)]
    while len(terms) > 1:
        terms = [terms[k] + terms[k + 1] for k in range(0, len(terms), 2)]
    current = terms[0]
    current, second = lax.optimization_barrier((current, second))
    out = shape(3 * tiles * margin, LANES)
    row_first, row_second = call(
        functools.partial(row_edge_kernel, counts, margin), (out, out), scalars=1, operands=4
    )(place, work, powers, first, second)
    row_first = paired(row_first, "row", 0)
    for step in range(halvings, len(orders[0])):
        if step == halvings + 1:
            current, row_first, row_second = lax.optimization_barrier(
                (current, row_first, row_second)
            )
            row_second = paired(row_second, "row", 1)
        current = current + exchanged(current, orders, 1 << step)
    size = tiles * rows
    weight = current[2 * size : 3 * size]
    stepped = current[: 2 * size] / jnp.concatenate([weight, weight], 0)
    whole = [stepped] + [exchanged(stepped, orders, d) for d in range(2, blocks // 2)]
    stepped, row_second = lax.optimization_barrier((stepped, row_second))
    whole.insert(1, exchanged(stepped, orders, 1))
    stepped = jnp.concatenate(whole, 0)
    object_next = call(
        functools.partial(object_kernel, counts, margin),
        shape(*object_field.shape),
        scalars=1,
        operands=7,
    )(place, object_field, work, powers, first, second, row_first, row_second)
    stepped = jnp.concatenate([stepped, paired(stepped, "col", 0)], 0)
    frame_count = frames * counts[0] * counts[1]
    probe_next = call(
        functools.partial(probe_kernel, frame_count, blocks),
        shape(*probe.shape),
        scalars=1,
        operands=2,
    )(place, stepped, current[3 * size :])
    return (object_next, probe_next)


def solution(mesh):
    return jax.shard_map(
        per_device,
        mesh=mesh,
        in_specs=(
            P(None, "row", "col"),
            P(),
            P("row", "col", None, None, None),
            P("row", "col", None, None),
        ),
        out_specs=(P(None, "row", "col"), P()),
        check_vma=False,
    )
```

```python
import functools
import math

import jax
import jax.numpy as jnp
import numpy as np
from jax import lax
from jax.experimental import pallas as pl
from jax.experimental.pallas import tpu as pltpu
from jax.sharding import PartitionSpec as P

MARGIN = 32
LANES = 128
SUBLANES = 8

smoothing = 0.1
regular = 1.0
epsilon = 1e-06

f32 = jnp.float32
bf16 = jnp.bfloat16


def tables(length):
    half = length // 2
    scaling = 1.0 / math.sqrt(length)
    k = np.arange(half)
    phases = (k[:, None] * k[None, :] % half) * (2.0 * math.pi / half)
    cosine, sine = np.cos(phases) * scaling, np.sin(phases) * scaling
    right = np.block([[cosine, -sine], [sine, cosine]])
    left = np.block([[cosine, sine], [-sine, cosine]])
    both = np.stack([left, right]).astype(np.float32)
    high = both.astype(bf16)
    low = (both - high.astype(np.float32)).astype(bf16)
    matrices = np.stack([high, low], 1)
    angle = k * (2.0 * math.pi / length)
    turn = np.stack([np.cos(angle), np.sin(angle)]).astype(np.float32)
    rows = np.broadcast_to(turn[:, :, None], (2, half, LANES)).copy()
    columns = np.broadcast_to(turn[:, None, :], (2, SUBLANES, half)).copy()
    return matrices, rows, columns


def split(x):
    high = x.astype(bf16)
    return high, (x - high.astype(f32)).astype(bf16)


def dot(a, b):
    return jnp.dot(a, b, preferred_element_type=f32)


def times_matrix(data, matrix):
    high, low = split(data)
    return dot(
        jnp.concatenate([high, low, high], 1),
        jnp.concatenate([matrix[0], matrix[0], matrix[1]], 0),
    )


def matrix_times(matrix, data):
    high, low = split(data)
    return dot(
        jnp.concatenate([matrix[0], matrix[0], matrix[1]], 1),
        jnp.concatenate([high, low, high], 0),
    )


def turned(real, imag, cosine, sine):
    return real * cosine - imag * sine, real * sine + imag * cosine


def pack(chunks, lane, width):
    place = lax.broadcasted_iota(jnp.int32, chunks[0].shape, 1) // width
    out = jnp.zeros_like(chunks[0])
    for q, chunk in enumerate(chunks):
        shift = (q * width - lane) % LANES
        moved = pltpu.roll(chunk, shift, 1) if shift else chunk
        out = jnp.where(place == q, moved, out)
    return out


def pack_rows(rows, lane, width):
    count = rows.shape[0] * width // LANES
    return pack([rows[q : q + count] for q in range(0, rows.shape[0], count)], lane, width)


def unpack(packed, q, lane, width):
    shift = (lane - q * width) % LANES
    moved = pltpu.roll(packed, shift, 1) if shift else packed
    place = lax.broadcasted_iota(jnp.int32, packed.shape, 1)
    return jnp.where((place >= lane) & (place < lane + width), moved, 0.0)


def unpack_rows(packed, lane, width):
    return jnp.concatenate([unpack(packed, q, lane, width) for q in range(LANES // width)], 0)


def lifted(tile, shift):
    groups = tile.shape[0] // SUBLANES
    turned_rows = pltpu.roll(
        tile.reshape(groups, SUBLANES, LANES), lax.rem(SUBLANES - shift, SUBLANES), 1
    )
    place = lax.broadcasted_iota(jnp.int32, (groups - 1, SUBLANES, LANES), 1)
    picked = jnp.where(place < SUBLANES - shift, turned_rows[:-1], turned_rows[1:])
    return picked.reshape((groups - 1) * SUBLANES, LANES)


def lowered(tile, shift):
    groups = tile.shape[0] // SUBLANES
    moved = pltpu.roll(tile.reshape(groups, SUBLANES, LANES), shift, 1)
    none = jnp.zeros((1, SUBLANES, LANES), f32)
    place = lax.broadcasted_iota(jnp.int32, (groups + 1, SUBLANES, LANES), 1)
    picked = jnp.where(
        place >= shift, jnp.concatenate([moved, none], 0), jnp.concatenate([none, moved], 0)
    )
    return picked.reshape((groups + 1) * SUBLANES, LANES)


def spot(offsets, f, margin, taller):
    a, b = offsets[f, 0], offsets[f, 1]
    shift = lax.rem(a, SUBLANES)
    lane = b + LANES - margin
    tile = lane // LANES
    return pl.ds(pl.multiple_of(a - shift, SUBLANES), taller), shift, tile, lane - tile * LANES


def window_of(padded, plane, spot_of, tiles):
    at, shift, base, lane = spot_of
    moved = [
        pltpu.roll(padded[plane, base + t, at, :], lax.rem(LANES - lane, LANES), 1)
        for t in range(tiles + 1)
    ]
    place = lax.broadcasted_iota(jnp.int32, moved[0].shape, 1)
    parts = [
        lifted(jnp.where(place < LANES - lane, moved[t], moved[t + 1]), shift)
        for t in range(tiles)
    ]
    return jnp.concatenate(parts, 1)


def add_window(work, term, spot_of):
    at, shift, base, lane = spot_of
    tiles = term.shape[1] // LANES
    moved = [
        pltpu.roll(lowered(term[:, t * LANES : (t + 1) * LANES], shift), lane, 1)
        for t in range(tiles)
    ]
    none = jnp.zeros_like(moved[0])
    place = lax.broadcasted_iota(jnp.int32, none.shape, 1)
    for t in range(tiles + 1):
        here = moved[t] if t < tiles else none
        before = moved[t - 1] if t else none
        work[base + t, at, :] += jnp.where(place >= lane, here, before)


def neighbours(first, second, index, count):
    even = index % 2 == 0
    before = jnp.where(even, second, first)
    after = jnp.where(even, first, second)
    return jnp.where(index > 0, before, 0.0), jnp.where(index < count - 1, after, 0.0)


def pack_kernel(margin, place, field, columns_first, columns_second):
    planes, side, _ = field.shape
    even = place[2] % 2 == 0
    for plane in range(planes):
        left = pack_rows(field[plane, :, :LANES], 0, margin)
        right = pack_rows(field[plane, :, side - LANES :], LANES - margin, margin)
        columns_first[plane] = jnp.where(even, right, left)
        columns_second[plane] = jnp.where(even, left, right)


def prepare_kernel(margin, offsets, amplitude, probe, sorted_out, total_out, powers, held):
    frames, length, _ = amplitude.shape
    half = length // 2
    power = probe[0] * probe[0] + probe[1] * probe[1]
    powers[...] = jnp.zeros(powers.shape, f32)
    for f in range(frames):
        add_window(powers, power, spot(offsets, f, margin, length + SUBLANES))
    row = lax.broadcasted_iota(jnp.int32, (length, length), 0)
    column = lax.broadcasted_iota(jnp.int32, (length, length), 1)
    source = jnp.where(column < half, 2 * column, 2 * (column - half) + 1)
    order = jnp.where(row == source, 1.0, 0.0).astype(bf16)
    total = jnp.zeros((SUBLANES, length), f32)
    for f in range(frames):
        values = amplitude[f]
        total += jnp.sum((values * values).reshape(length // SUBLANES, SUBLANES, length), 0)
        high = values.astype(bf16)
        rest = values - high.astype(f32)
        middle = rest.astype(bf16)
        low = (rest - middle.astype(f32)).astype(bf16)
        placed = dot(high, order) + (dot(middle, order) + dot(low, order))
        for parity in range(2):
            held[f, parity] = placed[:, parity * half : (parity + 1) * half]
            for start in range(2):
                at = 2 * parity + start
                sorted_out[f, at * half : (at + 1) * half, :] = held[
                    f, parity, pl.ds(start, half, stride=2), :
                ]
    total_out[...] = sum(total[:, t * LANES : (t + 1) * LANES] for t in range(length // LANES))


def corner_kernel(counts, place, first, second, inner_first, inner_second, above, below, out):
    planes, margin, side = first.shape
    inner = inner_first.shape[1]
    even = place[2] % 2 == 0
    for plane in range(planes):
        before, after = neighbours(first[plane], second[plane], place[1], counts[0])
        above[plane] = before
        below[plane] = after
        both = jnp.concatenate([before, after], 0)
        left = pack_rows(both[:, :LANES], 0, margin)
        right = pack_rows(both[:, side - LANES :], LANES - margin, margin)
        out[plane, :inner] = inner_first[plane]
        out[plane, inner:] = jnp.where(even, right, left)
        out[planes + plane, :inner] = inner_second[plane]
        out[planes + plane, inner:] = jnp.where(even, left, right)


def transform_pair(waves, row_turn, column_turn, matrices, amplitudes):
    length = waves[0][0].shape[0]
    half = length // 2
    row_cos, row_sin = row_turn
    column_cos, column_sin = column_turn

    mixed = []
    for real, imag in waves:
        odd = turned(real[:half] - real[half:], imag[:half] - imag[half:], row_cos, -row_sin)
        stacked = jnp.concatenate(
            [
                jnp.concatenate([real[:half] + real[half:], imag[:half] + imag[half:]], 0),
                jnp.concatenate(odd, 0),
            ],
            1,
        )
        mixed.append(matrix_times(matrices.at[0], stacked))

    far = []
    for value in mixed:
        evens, odds = [], []
        for parity in range(2):
            part = value[:, parity * length : (parity + 1) * length]
            real, imag = part[:half], part[half:]
            evens.append(
                jnp.concatenate(
                    [real[:, :half] + real[:, half:], imag[:, :half] + imag[:, half:]], 1
                )
            )
            odd = turned(
                real[:, :half] - real[:, half:],
                imag[:, :half] - imag[:, half:],
                column_cos,
                -column_sin,
            )
            odds.append(jnp.concatenate(odd, 1))
        far.append(times_matrix(jnp.concatenate(evens + odds, 0), matrices.at[1]))

    turned_back = []
    for value, amplitude in zip(far, amplitudes):
        real, imag = value[:, :half], value[:, half:]
        factor = amplitude * lax.rsqrt(real * real + imag * imag + smoothing)
        corrected = jnp.concatenate([real * factor, imag * factor], 1)
        turned_back.append(times_matrix(corrected, matrices.at[0]))

    near = []
    for value in turned_back:
        even, odd = value[:length], value[length:]
        odd_real, odd_imag = turned(odd[:, :half], odd[:, half:], column_cos, column_sin)
        even_real, even_imag = even[:, :half], even[:, half:]
        real = jnp.concatenate([even_real + odd_real, even_real - odd_real], 1)
        imag = jnp.concatenate([even_imag + odd_imag, even_imag - odd_imag], 1)
        stacked = jnp.concatenate(
            [
                jnp.concatenate([real[:half], imag[:half]], 0),
                jnp.concatenate([real[half:], imag[half:]], 0),
            ],
            1,
        )
        near.append(matrix_times(matrices.at[1], stacked))

    results = []
    for value in near:
        even, odd = value[:, :length], value[:, length:]
        odd_real, odd_imag = turned(odd[:half], odd[half:], row_cos, row_sin)
        results.append(
            (
                jnp.concatenate([even[:half] + odd_real, even[:half] - odd_real], 0),
                jnp.concatenate([even[half:] + odd_imag, even[half:] - odd_imag], 0),
            )
        )
    return results


def frames_kernel(
    counts,
    blocks,
    place,
    offsets,
    field,
    above,
    below,
    columns_first,
    columns_second,
    probe,
    amplitude,
    total,
    powers,
    matrices,
    row_turn,
    column_turn,
    work,
    kept,
    sent,
    padded,
    sums,
):
    frames = amplitude.shape[0]
    length = probe.shape[1]
    side = field.shape[1]
    margin = above.shape[1]
    reach = side + 2 * margin
    taller = length + SUBLANES
    per = LANES // margin
    inner = side // per
    tiles = length // LANES
    last = side // LANES + 1

    for plane in range(2):
        for tile in range(side // LANES):
            lanes = pl.ds(tile * LANES, LANES)
            padded[plane, tile + 1, :margin, :] = above[plane, :, lanes]
            padded[plane, tile + 1, margin : margin + side, :] = field[plane, :, lanes]
            padded[plane, tile + 1, margin + side : reach, :] = below[plane, :, lanes]
        left, right = neighbours(
            columns_first[plane], columns_second[plane], place[2], counts[1]
        )
        for tile, packed, lane in ((0, left, LANES - margin), (last, right, 0)):
            corners = unpack_rows(packed[inner:], lane, margin)
            padded[plane, tile, :margin, :] = corners[:margin]
            padded[plane, tile, margin : margin + side, :] = unpack_rows(
                packed[:inner], lane, margin
            )
            padded[plane, tile, margin + side : reach, :] = corners[margin:]
        padded[plane, :, reach:, :] = jnp.zeros((last + 1, SUBLANES, LANES), f32)
    work[...] = jnp.zeros(work.shape, f32)
    first = jnp.where(place[1] + place[2] == 0, 1.0, 0.0).astype(f32)
    sums[0] = probe[0] * first
    sums[1] = probe[1] * first
    sums[2] = jnp.full((length, length), regular, f32) * first

    row_cos, row_sin = (jnp.concatenate([row_turn[k]] * tiles, 1) for k in range(2))
    column_cos, column_sin = (column_turn[k, 0:1, :] for k in range(2))
    together = 2 if frames % 2 == 0 else 1

    def visit(step, carry):
        chosen = [step * together + k for k in range(together)]
        spots = [spot(offsets, f, margin, taller) for f in chosen]
        windows = [
            tuple(window_of(padded, plane, spot_of, tiles) for plane in range(2))
            for spot_of in spots
        ]
        probe_real, probe_imag = probe[0], probe[1]
        waves = [
            (
                probe_real * real - probe_imag * imag,
                probe_real * imag + probe_imag * real,
            )
            for real, imag in windows
        ]
        nears = transform_pair(
            waves,
            (row_cos, row_sin),
            (column_cos, column_sin),
            matrices,
            [amplitude[f] for f in chosen],
        )
        for (window_real, window_imag), (near_real, near_imag), spot_of in zip(
            windows, nears, spots
        ):
            sums[0] += window_real * near_real + window_imag * near_imag
            sums[1] += window_real * near_imag - window_imag * near_real
            sums[2] += window_real * window_real + window_imag * window_imag
            add_window(work.at[0], probe_real * near_real + probe_imag * near_imag, spot_of)
            add_window(work.at[1], probe_real * near_imag - probe_imag * near_real, spot_of)
        return carry

    lax.fori_loop(0, frames // together, visit, 0)

    rows = length // blocks
    half_rows = blocks // 2 * 3 * tiles * rows
    for p in range(blocks):
        out, q, base = (
            (kept, p, place[0]) if p < blocks // 2 else (sent, p - blocks // 2, place[3])
        )
        source = pl.multiple_of((base ^ q) * rows, rows)
        for plane in range(3):
            for tile in range(tiles):
                start = ((3 * q + plane) * tiles + tile) * rows
                out[start : start + rows, :] = sums[
                    plane, pl.ds(source, rows), pl.ds(tile * LANES, LANES)
                ]
    kept[half_rows:, :] = total[...]
    sent[half_rows : half_rows + SUBLANES, :] = total[...]
    even = place[2] % 2 == 0
    start = half_rows + SUBLANES
    depth = reach // per
    for plane in range(3):
        canvas = powers if plane == 2 else work.at[plane]
        right = pack_rows(canvas[last, :reach, :], 0, margin)
        left = pack_rows(canvas[0, :reach, :], LANES - margin, margin)
        at = start + plane * depth
        sent[at : at + depth, :] = jnp.where(even, right, left)
        at += 3 * depth
        sent[at : at + depth, :] = jnp.where(even, left, right)


def row_edge_kernel(counts, margin, place, work, powers, first, second, out):
    planes = work.shape[0] + 1
    tiles = work.shape[1] - 2
    reach = work.shape[2] - SUBLANES
    depth = first.shape[0] // planes
    even = place[1] % 2 == 0
    for plane in range(planes):
        canvas = powers if plane == planes - 1 else work.at[plane]
        at = pl.ds(plane * depth, depth)
        before, after = neighbours(first[at, :], second[at, :], place[2], counts[1])
        last = LANES // margin - 1
        edges = []
        for begin, chunk, cut in (
            (0, 0, slice(None, margin)),
            (reach - margin, last, slice(depth - margin, None)),
        ):
            parts = [canvas[tile + 1, begin : begin + margin, :] for tile in range(tiles)]
            parts[0] += unpack(before, chunk, 0, margin)[cut]
            parts[-1] += unpack(after, chunk, LANES - margin, margin)[cut]
            edges.append(parts)
        for tile in range(tiles):
            at = pl.ds((plane * tiles + tile) * margin, margin)
            out[at, :] = jnp.where(even, edges[1][tile], edges[0][tile])
            at = pl.ds(((planes + plane) * tiles + tile) * margin, margin)
            out[at, :] = jnp.where(even, edges[0][tile], edges[1][tile])


def object_kernel(
    counts, margin, place, field, work, powers, first, second, row_first, row_second, out
):
    planes = work.shape[0] + 1
    tiles = work.shape[1] - 2
    side = field.shape[1]
    depth = first.shape[0] // planes
    for tile in range(tiles):
        lanes = pl.ds(tile * LANES, LANES)
        total = []
        for plane in range(planes):
            canvas = powers if plane == planes - 1 else work.at[plane]
            at = pl.ds((plane * tiles + tile) * margin, margin)
            above, below = neighbours(row_first[at, :], row_second[at, :], place[1], counts[0])
            part = canvas[tile + 1, margin : margin + side, :]
            at = pl.ds(plane * depth, depth)
            before, after = neighbours(first[at, :], second[at, :], place[2], counts[1])
            if tile == 0:
                part += unpack_rows(before, 0, margin)[margin : margin + side]
            if tile == tiles - 1:
                part += unpack_rows(after, LANES - margin, margin)[margin : margin + side]
            part = jnp.concatenate(
                [
                    part[:margin] + above,
                    part[margin : side - margin],
                    part[side - margin :] + below,
                ],
                0,
            )
            total.append(part)
        weight = 1.0 / (total[2] + regular)
        out[0, :, lanes] = (field[0, :, lanes] + total[0]) * weight
        out[1, :, lanes] = (field[1, :, lanes] + total[1]) * weight


def probe_kernel(frame_count, blocks, place, stepped, total, out):
    planes, length, _ = out.shape
    tiles = length // LANES
    rows = length // blocks
    values = stepped[...]
    power = jnp.sum(values * values)
    target = jnp.sum(total[...]) / frame_count
    scale = jnp.sqrt(jnp.full((rows, LANES), target / (power + epsilon), f32))
    for p in range(blocks):
        base, q = (place[0], p) if p < blocks // 2 else (place[3], p - blocks // 2)
        home = pl.multiple_of((base ^ q) * rows, rows)
        for plane in range(planes):
            for tile in range(tiles):
                start = ((planes * p + plane) * tiles + tile) * rows
                out[plane, pl.ds(home, rows), pl.ds(tile * LANES, LANES)] = (
                    values[start : start + rows] * scale
                )


def shape(*dims):
    return jax.ShapeDtypeStruct(dims, f32)


def call(kernel, outputs, scalars=0, operands=0, scratch=(), cost=None):
    vmem = pl.BlockSpec(memory_space=pltpu.VMEM)
    smem = pl.BlockSpec(memory_space=pltpu.SMEM)
    return pl.pallas_call(
        kernel,
        out_shape=outputs,
        in_specs=[smem] * scalars + [vmem] * operands,
        out_specs=jax.tree.map(lambda _: vmem, outputs),
        scratch_shapes=list(scratch),
        cost_estimate=cost,
        compiler_params=pltpu.CompilerParams(vmem_limit_bytes=40 * 1024 * 1024),
    )


def paired(block, axis, first):
    count = lax.axis_size(axis)
    target = list(range(count))
    for i in range(first, count - 1, 2):
        target[i], target[i + 1] = i + 1, i
    return lax.ppermute(block, axis, list(enumerate(target)))


def relayed(block, axis):
    count = lax.axis_size(axis)
    target = {i: i + 2 if i % 2 == 0 else i - 2 for i in range(count)}
    target[count - 2], target[1] = count - 1, 0
    return lax.ppermute(block, axis, list(target.items()))


def exchanged(block, orders, distance):
    count = lax.axis_size("row") * lax.axis_size("col")
    masks = [
        sum(1 << bit for k, bit in enumerate(order) if distance >> k & 1) for order in orders
    ]
    return lax.ppermute(block, ("row", "col"), [(i, i ^ masks[i % 2]) for i in range(count)])


def per_device(object_field, probe, amplitudes, positions):
    planes, side, _ = object_field.shape
    length = probe.shape[1]
    margin = MARGIN
    reach = side + 2 * margin
    per = LANES // margin
    tiles = length // LANES
    measured = amplitudes[0, 0]
    frames = measured.shape[0]
    counts = lax.axis_size("row"), lax.axis_size("col")
    row = lax.axis_index("row").astype(jnp.int32)
    col = lax.axis_index("col").astype(jnp.int32)
    index = row * counts[1] + col
    col_bits = (counts[1] - 1).bit_length()
    across = list(range(1, col_bits))
    along = list(range(col_bits, col_bits + (counts[0] - 1).bit_length()))
    orders = (across + along, along + across)
    halvings = 2
    blocks = 2 << halvings
    rows = length // blocks
    homes = [
        sum(((index >> order[k]) & 1) << k for k in range(halvings))
        for order in orders
    ]
    core = index & 1
    homes[1] += blocks // 2
    place = jnp.stack(
        [
            jnp.where(core == 0, homes[0], homes[1]),
            row,
            col,
            jnp.where(core == 0, homes[1], homes[0]),
        ]
    )

    edge_rows = shape(planes, margin, side)
    inner = shape(planes, side // per, LANES)
    odd = row & 1
    last = side - margin
    rows_first = lax.dynamic_slice_in_dim(object_field, last - odd * last, margin, 1)
    rows_second = lax.dynamic_slice_in_dim(object_field, odd * last, margin, 1)
    rows_second = paired(rows_second, "row", 1)
    rows_first = paired(rows_first, "row", 0)
    inner_first, inner_second = call(
        functools.partial(pack_kernel, margin), (inner, inner), scalars=1, operands=1
    )(place, object_field)
    above, below, columns = call(
        functools.partial(corner_kernel, counts),
        (edge_rows, edge_rows, shape(2 * planes, reach // per, LANES)),
        scalars=1,
        operands=4,
    )(place, rows_first, rows_second, inner_first, inner_second)
    columns = paired(columns, "col", 0)
    relay = relayed(columns[planes:], "col")

    ordered, total, powers = call(
        functools.partial(prepare_kernel, margin),
        (
            shape(frames, 2 * length, length // 2),
            shape(SUBLANES, LANES),
            shape(side // LANES + 2, reach + SUBLANES, LANES),
        ),
        scalars=1,
        operands=2,
        scratch=(pltpu.VMEM((frames, 2, length, length // 2), f32),),
        cost=pl.CostEstimate(flops=10**9, bytes_accessed=2 * measured.size * 4, transcendentals=0),
    )(positions[0, 0], measured, probe)
    matrices, row_turn, column_turn = tables(length)
    half_rows = blocks // 2 * 3 * tiles * rows
    depth = 3 * reach // per
    work, kept, sent = call(
        functools.partial(frames_kernel, counts, blocks),
        (
            shape(2, side // LANES + 2, reach + SUBLANES, LANES),
            shape(half_rows + SUBLANES, LANES),
            shape(half_rows + SUBLANES + 2 * depth, LANES),
        ),
        scalars=2,
        operands=12,
        scratch=(
            pltpu.VMEM((2, side // LANES + 2, reach + SUBLANES, LANES), f32),
            pltpu.VMEM((3, length, length), f32),
        ),
    )(
        place,
        positions[0, 0],
        object_field,
        above,
        below,
        columns,
        relay,
        probe,
        ordered,
        total,
        powers,
        jnp.asarray(matrices),
        jnp.asarray(row_turn),
        jnp.asarray(column_turn),
    )

    arrived = paired(sent, "col", 0)
    current = kept + arrived[: half_rows + SUBLANES]
    first = arrived[half_rows + SUBLANES : half_rows + SUBLANES + depth]
    second = relayed(arrived[half_rows + SUBLANES + depth :], "col")
    block = 3 * tiles * rows
    total = current[-SUBLANES:]
    quarters = [
        jnp.concatenate([current[d * block : (d + 1) * block], total], 0) for d in range(blocks // 2)
    ]
    terms = quarters[:1] + [exchanged(quarters[d], orders, d) for d in range(1, blocks // 2)]
    while len(terms) > 1:
        terms = [terms[k] + terms[k + 1] for k in range(0, len(terms), 2)]
    current = terms[0]
    current, second = lax.optimization_barrier((current, second))
    count = 3 * tiles * margin
    edges = call(
        functools.partial(row_edge_kernel, counts, margin),
        shape(2 * count, LANES),
        scalars=1,
        operands=4,
    )(place, work, powers, first, second)
    edges = paired(edges, "row", 0)
    for step in range(halvings, len(orders[0])):
        if step == halvings + 1:
            current, edges = lax.optimization_barrier((current, edges))
            row_first = edges[:count]
            row_second = relayed(edges[count:], "row")
        current = current + exchanged(current, orders, 1 << step)
    size = tiles * rows
    weight = current[2 * size : 3 * size]
    stepped = current[: 2 * size] / jnp.concatenate([weight, weight], 0)
    whole = [stepped] + [exchanged(stepped, orders, d) for d in range(2, blocks // 2)]
    stepped, row_second = lax.optimization_barrier((stepped, row_second))
    whole.insert(1, exchanged(stepped, orders, 1))
    stepped = jnp.concatenate(whole, 0)
    object_next = call(
        functools.partial(object_kernel, counts, margin),
        shape(*object_field.shape),
        scalars=1,
        operands=7,
    )(place, object_field, work, powers, first, second, row_first, row_second)
    stepped = jnp.concatenate([stepped, paired(stepped, "col", 0)], 0)
    frame_count = frames * counts[0] * counts[1]
    probe_next = call(
        functools.partial(probe_kernel, frame_count, blocks),
        shape(*probe.shape),
        scalars=1,
        operands=2,
    )(place, stepped, current[3 * size :])
    return (object_next, probe_next)


def solution(mesh):
    return jax.shard_map(
        per_device,
        mesh=mesh,
        in_specs=(
            P(None, "row", "col"),
            P(),
            P("row", "col", None, None, None),
            P("row", "col", None, None),
        ),
        out_specs=(P(None, "row", "col"), P()),
        check_vma=False,
    )
```

```python
import functools
import math

import jax
import jax.numpy as jnp
import numpy as np
from jax import lax
from jax.experimental import pallas as pl
from jax.experimental.pallas import tpu as pltpu
from jax.sharding import PartitionSpec as P

MARGIN = 32
LANES = 128
SUBLANES = 8

smoothing = 0.1
regular = 1.0
epsilon = 1e-06

f32 = jnp.float32
bf16 = jnp.bfloat16


def tables(length):
    half = length // 2
    scaling = 1.0 / math.sqrt(length)
    k = np.arange(half)
    phases = (k[:, None] * k[None, :] % half) * (2.0 * math.pi / half)
    cosine, sine = np.cos(phases) * scaling, np.sin(phases) * scaling
    right = np.block([[cosine, -sine], [sine, cosine]])
    left = np.block([[cosine, sine], [-sine, cosine]])
    both = np.stack([left, right]).astype(np.float32)
    high = both.astype(bf16)
    low = (both - high.astype(np.float32)).astype(bf16)
    matrices = np.stack([high, low], 1)
    angle = k * (2.0 * math.pi / length)
    turn = np.stack([np.cos(angle), np.sin(angle)]).astype(np.float32)
    rows = np.broadcast_to(turn[:, :, None], (2, half, LANES)).copy()
    columns = np.broadcast_to(turn[:, None, :], (2, SUBLANES, half)).copy()
    return matrices, rows, columns


def split(x):
    high = x.astype(bf16)
    return high, (x - high.astype(f32)).astype(bf16)


def dot(a, b):
    return jnp.dot(a, b, preferred_element_type=f32)


def times_matrix(data, matrix):
    high, low = split(data)
    return dot(
        jnp.concatenate([high, low, high], 1),
        jnp.concatenate([matrix[0], matrix[0], matrix[1]], 0),
    )


def matrix_times(matrix, data):
    high, low = split(data)
    return dot(
        jnp.concatenate([matrix[0], matrix[0], matrix[1]], 1),
        jnp.concatenate([high, low, high], 0),
    )


def turned(real, imag, cosine, sine):
    return real * cosine - imag * sine, real * sine + imag * cosine


def pack(chunks, lane, width):
    place = lax.broadcasted_iota(jnp.int32, chunks[0].shape, 1) // width
    out = jnp.zeros_like(chunks[0])
    for q, chunk in enumerate(chunks):
        shift = (q * width - lane) % LANES
        moved = pltpu.roll(chunk, shift, 1) if shift else chunk
        out = jnp.where(place == q, moved, out)
    return out


def pack_rows(rows, lane, width):
    count = rows.shape[0] * width // LANES
    return pack([rows[q : q + count] for q in range(0, rows.shape[0], count)], lane, width)


def unpack(packed, q, lane, width):
    shift = (lane - q * width) % LANES
    moved = pltpu.roll(packed, shift, 1) if shift else packed
    place = lax.broadcasted_iota(jnp.int32, packed.shape, 1)
    return jnp.where((place >= lane) & (place < lane + width), moved, 0.0)


def unpack_rows(packed, lane, width):
    return jnp.concatenate([unpack(packed, q, lane, width) for q in range(LANES // width)], 0)


def lifted(tile, shift):
    groups = tile.shape[0] // SUBLANES
    turned_rows = pltpu.roll(
        tile.reshape(groups, SUBLANES, LANES), lax.rem(SUBLANES - shift, SUBLANES), 1
    )
    place = lax.broadcasted_iota(jnp.int32, (groups - 1, SUBLANES, LANES), 1)
    picked = jnp.where(place < SUBLANES - shift, turned_rows[:-1], turned_rows[1:])
    return picked.reshape((groups - 1) * SUBLANES, LANES)


def lowered(tile, shift):
    groups = tile.shape[0] // SUBLANES
    moved = pltpu.roll(tile.reshape(groups, SUBLANES, LANES), shift, 1)
    none = jnp.zeros((1, SUBLANES, LANES), f32)
    place = lax.broadcasted_iota(jnp.int32, (groups + 1, SUBLANES, LANES), 1)
    picked = jnp.where(
        place >= shift, jnp.concatenate([moved, none], 0), jnp.concatenate([none, moved], 0)
    )
    return picked.reshape((groups + 1) * SUBLANES, LANES)


def spot(offsets, f, margin, taller):
    a, b = offsets[f, 0], offsets[f, 1]
    shift = lax.rem(a, SUBLANES)
    lane = b + LANES - margin
    tile = lane // LANES
    return pl.ds(pl.multiple_of(a - shift, SUBLANES), taller), shift, tile, lane - tile * LANES


def window_of(padded, plane, spot_of, tiles):
    at, shift, base, lane = spot_of
    moved = [
        pltpu.roll(padded[plane, base + t, at, :], lax.rem(LANES - lane, LANES), 1)
        for t in range(tiles + 1)
    ]
    place = lax.broadcasted_iota(jnp.int32, moved[0].shape, 1)
    parts = [
        lifted(jnp.where(place < LANES - lane, moved[t], moved[t + 1]), shift)
        for t in range(tiles)
    ]
    return jnp.concatenate(parts, 1)


def add_window(work, term, spot_of):
    at, shift, base, lane = spot_of
    tiles = term.shape[1] // LANES
    moved = [
        pltpu.roll(lowered(term[:, t * LANES : (t + 1) * LANES], shift), lane, 1)
        for t in range(tiles)
    ]
    none = jnp.zeros_like(moved[0])
    place = lax.broadcasted_iota(jnp.int32, none.shape, 1)
    for t in range(tiles + 1):
        here = moved[t] if t < tiles else none
        before = moved[t - 1] if t else none
        work[base + t, at, :] += jnp.where(place >= lane, here, before)


def neighbours(first, second, index, count):
    even = index % 2 == 0
    before = jnp.where(even, second, first)
    after = jnp.where(even, first, second)
    return jnp.where(index > 0, before, 0.0), jnp.where(index < count - 1, after, 0.0)


def pack_kernel(margin, place, field, columns_first, columns_second):
    planes, side, _ = field.shape
    even = place[2] % 2 == 0
    for plane in range(planes):
        left = pack_rows(field[plane, :, :LANES], 0, margin)
        right = pack_rows(field[plane, :, side - LANES :], LANES - margin, margin)
        columns_first[plane] = jnp.where(even, right, left)
        columns_second[plane] = jnp.where(even, left, right)


def prepare_kernel(margin, offsets, amplitude, probe, sorted_out, total_out, powers, held):
    frames, length, _ = amplitude.shape
    half = length // 2
    power = probe[0] * probe[0] + probe[1] * probe[1]
    powers[...] = jnp.zeros(powers.shape, f32)
    for f in range(frames):
        add_window(powers, power, spot(offsets, f, margin, length + SUBLANES))
    row = lax.broadcasted_iota(jnp.int32, (length, length), 0)
    column = lax.broadcasted_iota(jnp.int32, (length, length), 1)
    source = jnp.where(column < half, 2 * column, 2 * (column - half) + 1)
    order = jnp.where(row == source, 1.0, 0.0).astype(bf16)
    total = jnp.zeros((SUBLANES, length), f32)
    for f in range(frames):
        values = amplitude[f]
        total += jnp.sum((values * values).reshape(length // SUBLANES, SUBLANES, length), 0)
        high = values.astype(bf16)
        rest = values - high.astype(f32)
        middle = rest.astype(bf16)
        low = (rest - middle.astype(f32)).astype(bf16)
        placed = dot(high, order) + (dot(middle, order) + dot(low, order))
        for parity in range(2):
            held[f, parity] = placed[:, parity * half : (parity + 1) * half]
            for start in range(2):
                at = 2 * parity + start
                sorted_out[f, at * half : (at + 1) * half, :] = held[
                    f, parity, pl.ds(start, half, stride=2), :
                ]
    total_out[...] = sum(total[:, t * LANES : (t + 1) * LANES] for t in range(length // LANES))


def corner_kernel(counts, place, first, second, inner_first, inner_second, above, below, out):
    planes, margin, side = first.shape
    inner = inner_first.shape[1]
    even = place[2] % 2 == 0
    for plane in range(planes):
        before, after = neighbours(first[plane], second[plane], place[1], counts[0])
        above[plane] = before
        below[plane] = after
        both = jnp.concatenate([before, after], 0)
        left = pack_rows(both[:, :LANES], 0, margin)
        right = pack_rows(both[:, side - LANES :], LANES - margin, margin)
        out[plane, :inner] = inner_first[plane]
        out[plane, inner:] = jnp.where(even, right, left)
        out[planes + plane, :inner] = inner_second[plane]
        out[planes + plane, inner:] = jnp.where(even, left, right)


def transform_pair(waves, row_turn, column_turn, matrices, amplitudes):
    length = waves[0][0].shape[0]
    half = length // 2
    row_cos, row_sin = row_turn
    column_cos, column_sin = column_turn

    mixed = []
    for real, imag in waves:
        odd = turned(real[:half] - real[half:], imag[:half] - imag[half:], row_cos, -row_sin)
        stacked = jnp.concatenate(
            [
                jnp.concatenate([real[:half] + real[half:], imag[:half] + imag[half:]], 0),
                jnp.concatenate(odd, 0),
            ],
            1,
        )
        mixed.append(matrix_times(matrices.at[0], stacked))

    far = []
    for value in mixed:
        evens, odds = [], []
        for parity in range(2):
            part = value[:, parity * length : (parity + 1) * length]
            real, imag = part[:half], part[half:]
            evens.append(
                jnp.concatenate(
                    [real[:, :half] + real[:, half:], imag[:, :half] + imag[:, half:]], 1
                )
            )
            odd = turned(
                real[:, :half] - real[:, half:],
                imag[:, :half] - imag[:, half:],
                column_cos,
                -column_sin,
            )
            odds.append(jnp.concatenate(odd, 1))
        far.append(times_matrix(jnp.concatenate(evens + odds, 0), matrices.at[1]))

    turned_back = []
    for value, amplitude in zip(far, amplitudes):
        real, imag = value[:, :half], value[:, half:]
        factor = amplitude * lax.rsqrt(real * real + imag * imag + smoothing)
        corrected = jnp.concatenate([real * factor, imag * factor], 1)
        turned_back.append(times_matrix(corrected, matrices.at[0]))

    near = []
    for value in turned_back:
        even, odd = value[:length], value[length:]
        odd_real, odd_imag = turned(odd[:, :half], odd[:, half:], column_cos, column_sin)
        even_real, even_imag = even[:, :half], even[:, half:]
        real = jnp.concatenate([even_real + odd_real, even_real - odd_real], 1)
        imag = jnp.concatenate([even_imag + odd_imag, even_imag - odd_imag], 1)
        stacked = jnp.concatenate(
            [
                jnp.concatenate([real[:half], imag[:half]], 0),
                jnp.concatenate([real[half:], imag[half:]], 0),
            ],
            1,
        )
        near.append(matrix_times(matrices.at[1], stacked))

    results = []
    for value in near:
        even, odd = value[:, :length], value[:, length:]
        odd_real, odd_imag = turned(odd[:half], odd[half:], row_cos, row_sin)
        results.append(
            (
                jnp.concatenate([even[:half] + odd_real, even[:half] - odd_real], 0),
                jnp.concatenate([even[half:] + odd_imag, even[half:] - odd_imag], 0),
            )
        )
    return results


def frames_kernel(
    counts,
    blocks,
    place,
    offsets,
    field,
    above,
    below,
    columns_first,
    columns_second,
    probe,
    amplitude,
    total,
    powers,
    matrices,
    row_turn,
    column_turn,
    work,
    kept,
    sent,
    padded,
    sums,
):
    frames = amplitude.shape[0]
    length = probe.shape[1]
    side = field.shape[1]
    margin = above.shape[1]
    reach = side + 2 * margin
    taller = length + SUBLANES
    per = LANES // margin
    inner = side // per
    tiles = length // LANES
    last = side // LANES + 1

    for plane in range(2):
        for tile in range(side // LANES):
            lanes = pl.ds(tile * LANES, LANES)
            padded[plane, tile + 1, :margin, :] = above[plane, :, lanes]
            padded[plane, tile + 1, margin : margin + side, :] = field[plane, :, lanes]
            padded[plane, tile + 1, margin + side : reach, :] = below[plane, :, lanes]
        left, right = neighbours(
            columns_first[plane], columns_second[plane], place[2], counts[1]
        )
        for tile, packed, lane in ((0, left, LANES - margin), (last, right, 0)):
            corners = unpack_rows(packed[inner:], lane, margin)
            padded[plane, tile, :margin, :] = corners[:margin]
            padded[plane, tile, margin : margin + side, :] = unpack_rows(
                packed[:inner], lane, margin
            )
            padded[plane, tile, margin + side : reach, :] = corners[margin:]
        padded[plane, :, reach:, :] = jnp.zeros((last + 1, SUBLANES, LANES), f32)
    work[...] = jnp.zeros(work.shape, f32)
    first = jnp.where(place[1] + place[2] == 0, 1.0, 0.0).astype(f32)
    sums[0] = probe[0] * first
    sums[1] = probe[1] * first
    sums[2] = jnp.full((length, length), regular, f32) * first

    row_cos, row_sin = (jnp.concatenate([row_turn[k]] * tiles, 1) for k in range(2))
    column_cos, column_sin = (column_turn[k, 0:1, :] for k in range(2))
    together = max(k for k in (1, 2, 4) if frames % k == 0)

    def visit(step, carry):
        chosen = [step * together + k for k in range(together)]
        spots = [spot(offsets, f, margin, taller) for f in chosen]
        windows = [
            tuple(window_of(padded, plane, spot_of, tiles) for plane in range(2))
            for spot_of in spots
        ]
        probe_real, probe_imag = probe[0], probe[1]
        waves = [
            (
                probe_real * real - probe_imag * imag,
                probe_real * imag + probe_imag * real,
            )
            for real, imag in windows
        ]
        nears = transform_pair(
            waves,
            (row_cos, row_sin),
            (column_cos, column_sin),
            matrices,
            [amplitude[f] for f in chosen],
        )
        for (window_real, window_imag), (near_real, near_imag), spot_of in zip(
            windows, nears, spots
        ):
            sums[0] += window_real * near_real + window_imag * near_imag
            sums[1] += window_real * near_imag - window_imag * near_real
            sums[2] += window_real * window_real + window_imag * window_imag
            add_window(work.at[0], probe_real * near_real + probe_imag * near_imag, spot_of)
            add_window(work.at[1], probe_real * near_imag - probe_imag * near_real, spot_of)
        return carry

    lax.fori_loop(0, frames // together, visit, 0)

    rows = length // blocks
    half_rows = blocks // 2 * 3 * tiles * rows
    for p in range(blocks):
        out, q, base = (
            (kept, p, place[0]) if p < blocks // 2 else (sent, p - blocks // 2, place[3])
        )
        source = pl.multiple_of((base ^ q) * rows, rows)
        for plane in range(3):
            for tile in range(tiles):
                start = ((3 * q + plane) * tiles + tile) * rows
                out[start : start + rows, :] = sums[
                    plane, pl.ds(source, rows), pl.ds(tile * LANES, LANES)
                ]
    kept[half_rows:, :] = total[...]
    sent[half_rows : half_rows + SUBLANES, :] = total[...]
    even = place[2] % 2 == 0
    start = half_rows + SUBLANES
    depth = reach // per
    for plane in range(3):
        canvas = powers if plane == 2 else work.at[plane]
        right = pack_rows(canvas[last, :reach, :], 0, margin)
        left = pack_rows(canvas[0, :reach, :], LANES - margin, margin)
        at = start + plane * depth
        sent[at : at + depth, :] = jnp.where(even, right, left)
        at += 3 * depth
        sent[at : at + depth, :] = jnp.where(even, left, right)


def row_edge_kernel(counts, margin, place, work, powers, first, second, out):
    planes = work.shape[0] + 1
    tiles = work.shape[1] - 2
    reach = work.shape[2] - SUBLANES
    depth = first.shape[0] // planes
    even = place[1] % 2 == 0
    for plane in range(planes):
        canvas = powers if plane == planes - 1 else work.at[plane]
        at = pl.ds(plane * depth, depth)
        before, after = neighbours(first[at, :], second[at, :], place[2], counts[1])
        last = LANES // margin - 1
        edges = []
        for begin, chunk, cut in (
            (0, 0, slice(None, margin)),
            (reach - margin, last, slice(depth - margin, None)),
        ):
            parts = [canvas[tile + 1, begin : begin + margin, :] for tile in range(tiles)]
            parts[0] += unpack(before, chunk, 0, margin)[cut]
            parts[-1] += unpack(after, chunk, LANES - margin, margin)[cut]
            edges.append(parts)
        for tile in range(tiles):
            at = pl.ds((plane * tiles + tile) * margin, margin)
            out[at, :] = jnp.where(even, edges[1][tile], edges[0][tile])
            at = pl.ds(((planes + plane) * tiles + tile) * margin, margin)
            out[at, :] = jnp.where(even, edges[0][tile], edges[1][tile])


def object_kernel(
    counts, margin, place, field, work, powers, first, second, row_first, row_second, out
):
    planes = work.shape[0] + 1
    tiles = work.shape[1] - 2
    side = field.shape[1]
    depth = first.shape[0] // planes
    for tile in range(tiles):
        lanes = pl.ds(tile * LANES, LANES)
        total = []
        for plane in range(planes):
            canvas = powers if plane == planes - 1 else work.at[plane]
            at = pl.ds((plane * tiles + tile) * margin, margin)
            above, below = neighbours(row_first[at, :], row_second[at, :], place[1], counts[0])
            part = canvas[tile + 1, margin : margin + side, :]
            at = pl.ds(plane * depth, depth)
            before, after = neighbours(first[at, :], second[at, :], place[2], counts[1])
            if tile == 0:
                part += unpack_rows(before, 0, margin)[margin : margin + side]
            if tile == tiles - 1:
                part += unpack_rows(after, LANES - margin, margin)[margin : margin + side]
            part = jnp.concatenate(
                [
                    part[:margin] + above,
                    part[margin : side - margin],
                    part[side - margin :] + below,
                ],
                0,
            )
            total.append(part)
        weight = 1.0 / (total[2] + regular)
        out[0, :, lanes] = (field[0, :, lanes] + total[0]) * weight
        out[1, :, lanes] = (field[1, :, lanes] + total[1]) * weight


def probe_kernel(frame_count, blocks, place, stepped, total, out):
    planes, length, _ = out.shape
    tiles = length // LANES
    rows = length // blocks
    values = stepped[...]
    power = jnp.sum(values * values)
    target = jnp.sum(total[...]) / frame_count
    scale = jnp.sqrt(jnp.full((rows, LANES), target / (power + epsilon), f32))
    for p in range(blocks):
        base, q = (place[0], p) if p < blocks // 2 else (place[3], p - blocks // 2)
        home = pl.multiple_of((base ^ q) * rows, rows)
        for plane in range(planes):
            for tile in range(tiles):
                start = ((planes * p + plane) * tiles + tile) * rows
                out[plane, pl.ds(home, rows), pl.ds(tile * LANES, LANES)] = (
                    values[start : start + rows] * scale
                )


def shape(*dims):
    return jax.ShapeDtypeStruct(dims, f32)


def call(kernel, outputs, scalars=0, operands=0, scratch=(), cost=None):
    vmem = pl.BlockSpec(memory_space=pltpu.VMEM)
    smem = pl.BlockSpec(memory_space=pltpu.SMEM)
    return pl.pallas_call(
        kernel,
        out_shape=outputs,
        in_specs=[smem] * scalars + [vmem] * operands,
        out_specs=jax.tree.map(lambda _: vmem, outputs),
        scratch_shapes=list(scratch),
        cost_estimate=cost,
        compiler_params=pltpu.CompilerParams(vmem_limit_bytes=40 * 1024 * 1024),
    )


def paired(block, axis, first):
    count = lax.axis_size(axis)
    target = list(range(count))
    for i in range(first, count - 1, 2):
        target[i], target[i + 1] = i + 1, i
    return lax.ppermute(block, axis, list(enumerate(target)))


def relayed(block, axis):
    count = lax.axis_size(axis)
    target = {i: i + 2 if i % 2 == 0 else i - 2 for i in range(count)}
    target[count - 2], target[1] = count - 1, 0
    return lax.ppermute(block, axis, list(target.items()))


def exchanged(block, orders, distance):
    count = lax.axis_size("row") * lax.axis_size("col")
    masks = [
        sum(1 << bit for k, bit in enumerate(order) if distance >> k & 1) for order in orders
    ]
    return lax.ppermute(block, ("row", "col"), [(i, i ^ masks[i % 2]) for i in range(count)])


def per_device(object_field, probe, amplitudes, positions):
    planes, side, _ = object_field.shape
    length = probe.shape[1]
    margin = MARGIN
    reach = side + 2 * margin
    per = LANES // margin
    tiles = length // LANES
    measured = amplitudes[0, 0]
    frames = measured.shape[0]
    counts = lax.axis_size("row"), lax.axis_size("col")
    row = lax.axis_index("row").astype(jnp.int32)
    col = lax.axis_index("col").astype(jnp.int32)
    index = row * counts[1] + col
    col_bits = (counts[1] - 1).bit_length()
    across = list(range(1, col_bits))
    along = list(range(col_bits, col_bits + (counts[0] - 1).bit_length()))
    orders = (across + along, along + across)
    halvings = 2
    blocks = 2 << halvings
    rows = length // blocks
    homes = [
        sum(((index >> order[k]) & 1) << k for k in range(halvings))
        for order in orders
    ]
    core = index & 1
    homes[1] += blocks // 2
    place = jnp.stack(
        [
            jnp.where(core == 0, homes[0], homes[1]),
            row,
            col,
            jnp.where(core == 0, homes[1], homes[0]),
        ]
    )

    edge_rows = shape(planes, margin, side)
    inner = shape(planes, side // per, LANES)
    odd = row & 1
    last = side - margin
    rows_first = lax.dynamic_slice_in_dim(object_field, last - odd * last, margin, 1)
    rows_second = lax.dynamic_slice_in_dim(object_field, odd * last, margin, 1)
    rows_second = paired(rows_second, "row", 1)
    rows_first = paired(rows_first, "row", 0)
    inner_first, inner_second = call(
        functools.partial(pack_kernel, margin), (inner, inner), scalars=1, operands=1
    )(place, object_field)
    above, below, columns = call(
        functools.partial(corner_kernel, counts),
        (edge_rows, edge_rows, shape(2 * planes, reach // per, LANES)),
        scalars=1,
        operands=4,
    )(place, rows_first, rows_second, inner_first, inner_second)
    columns = paired(columns, "col", 0)
    relay = relayed(columns[planes:], "col")

    ordered, total, powers = call(
        functools.partial(prepare_kernel, margin),
        (
            shape(frames, 2 * length, length // 2),
            shape(SUBLANES, LANES),
            shape(side // LANES + 2, reach + SUBLANES, LANES),
        ),
        scalars=1,
        operands=2,
        scratch=(pltpu.VMEM((frames, 2, length, length // 2), f32),),
        cost=pl.CostEstimate(flops=10**9, bytes_accessed=2 * measured.size * 4, transcendentals=0),
    )(positions[0, 0], measured, probe)
    matrices, row_turn, column_turn = tables(length)
    half_rows = blocks // 2 * 3 * tiles * rows
    depth = 3 * reach // per
    work, kept, sent = call(
        functools.partial(frames_kernel, counts, blocks),
        (
            shape(2, side // LANES + 2, reach + SUBLANES, LANES),
            shape(half_rows + SUBLANES, LANES),
            shape(half_rows + SUBLANES + 2 * depth, LANES),
        ),
        scalars=2,
        operands=12,
        scratch=(
            pltpu.VMEM((2, side // LANES + 2, reach + SUBLANES, LANES), f32),
            pltpu.VMEM((3, length, length), f32),
        ),
    )(
        place,
        positions[0, 0],
        object_field,
        above,
        below,
        columns,
        relay,
        probe,
        ordered,
        total,
        powers,
        jnp.asarray(matrices),
        jnp.asarray(row_turn),
        jnp.asarray(column_turn),
    )

    arrived = paired(sent, "col", 0)
    current = kept + arrived[: half_rows + SUBLANES]
    first = arrived[half_rows + SUBLANES : half_rows + SUBLANES + depth]
    second = relayed(arrived[half_rows + SUBLANES + depth :], "col")
    block = 3 * tiles * rows
    total = current[-SUBLANES:]
    quarters = [
        jnp.concatenate([current[d * block : (d + 1) * block], total], 0) for d in range(blocks // 2)
    ]
    terms = quarters[:1] + [exchanged(quarters[d], orders, d) for d in range(1, blocks // 2)]
    while len(terms) > 1:
        terms = [terms[k] + terms[k + 1] for k in range(0, len(terms), 2)]
    current = terms[0]
    current, second = lax.optimization_barrier((current, second))
    count = 3 * tiles * margin
    edges = call(
        functools.partial(row_edge_kernel, counts, margin),
        shape(2 * count, LANES),
        scalars=1,
        operands=4,
    )(place, work, powers, first, second)
    edges = paired(edges, "row", 0)
    for step in range(halvings, len(orders[0])):
        if step == halvings + 1:
            current, edges = lax.optimization_barrier((current, edges))
            row_first = edges[:count]
            row_second = relayed(edges[count:], "row")
        current = current + exchanged(current, orders, 1 << step)
    size = tiles * rows
    weight = current[2 * size : 3 * size]
    stepped = current[: 2 * size] / jnp.concatenate([weight, weight], 0)
    stepped = jnp.concatenate(
        [stepped] + [exchanged(stepped, orders, d) for d in range(1, blocks // 2)], 0
    )
    stepped, row_second = lax.optimization_barrier((stepped, row_second))
    object_next = call(
        functools.partial(object_kernel, counts, margin),
        shape(*object_field.shape),
        scalars=1,
        operands=7,
    )(place, object_field, work, powers, first, second, row_first, row_second)
    stepped = jnp.concatenate([stepped, paired(stepped, "col", 0)], 0)
    frame_count = frames * counts[0] * counts[1]
    probe_next = call(
        functools.partial(probe_kernel, frame_count, blocks),
        shape(*probe.shape),
        scalars=1,
        operands=2,
    )(place, stepped, current[3 * size :])
    return (object_next, probe_next)


def solution(mesh):
    return jax.shard_map(
        per_device,
        mesh=mesh,
        in_specs=(
            P(None, "row", "col"),
            P(),
            P("row", "col", None, None, None),
            P("row", "col", None, None),
        ),
        out_specs=(P(None, "row", "col"), P()),
        check_vma=False,
    )
```

```python
import functools
import math

import jax
import jax.numpy as jnp
import numpy as np
from jax import lax
from jax.experimental import pallas as pl
from jax.experimental.pallas import tpu as pltpu
from jax.sharding import PartitionSpec as P

MARGIN = 32
LANES = 128
SUBLANES = 8

smoothing = 0.1
regular = 1.0
epsilon = 1e-06

f32 = jnp.float32
bf16 = jnp.bfloat16


def tables(length):
    half = length // 2
    scaling = 1.0 / math.sqrt(length)
    k = np.arange(half)
    phases = (k[:, None] * k[None, :] % half) * (2.0 * math.pi / half)
    cosine, sine = np.cos(phases) * scaling, np.sin(phases) * scaling
    right = np.block([[cosine, -sine], [sine, cosine]])
    left = np.block([[cosine, sine], [-sine, cosine]])
    both = np.stack([left, right]).astype(np.float32)
    high = both.astype(bf16)
    low = (both - high.astype(np.float32)).astype(bf16)
    matrices = np.stack([high, low], 1)
    angle = k * (2.0 * math.pi / length)
    turn = np.stack([np.cos(angle), np.sin(angle)]).astype(np.float32)
    rows = np.broadcast_to(turn[:, :, None], (2, half, LANES)).copy()
    columns = np.broadcast_to(turn[:, None, :], (2, SUBLANES, half)).copy()
    return matrices, rows, columns


def split(x):
    high = x.astype(bf16)
    return high, (x - high.astype(f32)).astype(bf16)


def dot(a, b):
    return jnp.dot(a, b, preferred_element_type=f32)


def times_matrix(data, matrix):
    high, low = split(data)
    return dot(
        jnp.concatenate([high, low, high], 1),
        jnp.concatenate([matrix[0], matrix[0], matrix[1]], 0),
    )


def matrix_times(matrix, data):
    high, low = split(data)
    return dot(
        jnp.concatenate([matrix[0], matrix[0], matrix[1]], 1),
        jnp.concatenate([high, low, high], 0),
    )


def turned(real, imag, cosine, sine):
    return real * cosine - imag * sine, real * sine + imag * cosine


def pack(chunks, lane, width):
    place = lax.broadcasted_iota(jnp.int32, chunks[0].shape, 1) // width
    out = jnp.zeros_like(chunks[0])
    for q, chunk in enumerate(chunks):
        shift = (q * width - lane) % LANES
        moved = pltpu.roll(chunk, shift, 1) if shift else chunk
        out = jnp.where(place == q, moved, out)
    return out


def pack_rows(rows, lane, width):
    count = rows.shape[0] * width // LANES
    return pack([rows[q : q + count] for q in range(0, rows.shape[0], count)], lane, width)


def unpack(packed, q, lane, width):
    shift = (lane - q * width) % LANES
    moved = pltpu.roll(packed, shift, 1) if shift else packed
    place = lax.broadcasted_iota(jnp.int32, packed.shape, 1)
    return jnp.where((place >= lane) & (place < lane + width), moved, 0.0)


def unpack_rows(packed, lane, width):
    return jnp.concatenate([unpack(packed, q, lane, width) for q in range(LANES // width)], 0)


def lifted(tile, shift):
    groups = tile.shape[0] // SUBLANES
    turned_rows = pltpu.roll(
        tile.reshape(groups, SUBLANES, LANES), lax.rem(SUBLANES - shift, SUBLANES), 1
    )
    place = lax.broadcasted_iota(jnp.int32, (groups - 1, SUBLANES, LANES), 1)
    picked = jnp.where(place < SUBLANES - shift, turned_rows[:-1], turned_rows[1:])
    return picked.reshape((groups - 1) * SUBLANES, LANES)


def lowered(tile, shift):
    groups = tile.shape[0] // SUBLANES
    moved = pltpu.roll(tile.reshape(groups, SUBLANES, LANES), shift, 1)
    none = jnp.zeros((1, SUBLANES, LANES), f32)
    place = lax.broadcasted_iota(jnp.int32, (groups + 1, SUBLANES, LANES), 1)
    picked = jnp.where(
        place >= shift, jnp.concatenate([moved, none], 0), jnp.concatenate([none, moved], 0)
    )
    return picked.reshape((groups + 1) * SUBLANES, LANES)


def spot(offsets, f, margin, taller):
    a, b = offsets[f, 0], offsets[f, 1]
    shift = lax.rem(a, SUBLANES)
    lane = b + LANES - margin
    tile = lane // LANES
    return pl.ds(pl.multiple_of(a - shift, SUBLANES), taller), shift, tile, lane - tile * LANES


def window_of(padded, plane, spot_of, tiles):
    at, shift, base, lane = spot_of
    moved = [
        pltpu.roll(padded[plane, base + t, at, :], lax.rem(LANES - lane, LANES), 1)
        for t in range(tiles + 1)
    ]
    place = lax.broadcasted_iota(jnp.int32, moved[0].shape, 1)
    parts = [
        lifted(jnp.where(place < LANES - lane, moved[t], moved[t + 1]), shift)
        for t in range(tiles)
    ]
    return jnp.concatenate(parts, 1)


def add_window(work, term, spot_of):
    at, shift, base, lane = spot_of
    tiles = term.shape[1] // LANES
    moved = [
        pltpu.roll(lowered(term[:, t * LANES : (t + 1) * LANES], shift), lane, 1)
        for t in range(tiles)
    ]
    none = jnp.zeros_like(moved[0])
    place = lax.broadcasted_iota(jnp.int32, none.shape, 1)
    for t in range(tiles + 1):
        here = moved[t] if t < tiles else none
        before = moved[t - 1] if t else none
        work[base + t, at, :] += jnp.where(place >= lane, here, before)


def neighbours(first, second, index, count):
    even = index % 2 == 0
    before = jnp.where(even, second, first)
    after = jnp.where(even, first, second)
    return jnp.where(index > 0, before, 0.0), jnp.where(index < count - 1, after, 0.0)


def pack_kernel(margin, place, field, columns_first, columns_second):
    planes, side, _ = field.shape
    even = place[2] % 2 == 0
    for plane in range(planes):
        left = pack_rows(field[plane, :, :LANES], 0, margin)
        right = pack_rows(field[plane, :, side - LANES :], LANES - margin, margin)
        columns_first[plane] = jnp.where(even, right, left)
        columns_second[plane] = jnp.where(even, left, right)


def prepare_kernel(margin, offsets, amplitude, probe, sorted_out, total_out, powers, held):
    frames, length, _ = amplitude.shape
    half = length // 2
    power = probe[0] * probe[0] + probe[1] * probe[1]
    powers[...] = jnp.zeros(powers.shape, f32)
    for f in range(frames):
        add_window(powers, power, spot(offsets, f, margin, length + SUBLANES))
    row = lax.broadcasted_iota(jnp.int32, (length, length), 0)
    column = lax.broadcasted_iota(jnp.int32, (length, length), 1)
    source = jnp.where(column < half, 2 * column, 2 * (column - half) + 1)
    order = jnp.where(row == source, 1.0, 0.0).astype(bf16)
    total = jnp.zeros((SUBLANES, length), f32)
    for f in range(frames):
        values = amplitude[f]
        total += jnp.sum((values * values).reshape(length // SUBLANES, SUBLANES, length), 0)
        high = values.astype(bf16)
        rest = values - high.astype(f32)
        middle = rest.astype(bf16)
        low = (rest - middle.astype(f32)).astype(bf16)
        placed = dot(high, order) + (dot(middle, order) + dot(low, order))
        for parity in range(2):
            held[f, parity] = placed[:, parity * half : (parity + 1) * half]
            for start in range(2):
                at = 2 * parity + start
                sorted_out[f, at * half : (at + 1) * half, :] = held[
                    f, parity, pl.ds(start, half, stride=2), :
                ]
    total_out[...] = sum(total[:, t * LANES : (t + 1) * LANES] for t in range(length // LANES))


def corner_kernel(counts, place, first, second, inner_first, inner_second, above, below, out):
    planes, margin, side = first.shape
    inner = inner_first.shape[1]
    even = place[2] % 2 == 0
    for plane in range(planes):
        before, after = neighbours(first[plane], second[plane], place[1], counts[0])
        above[plane] = before
        below[plane] = after
        both = jnp.concatenate([before, after], 0)
        left = pack_rows(both[:, :LANES], 0, margin)
        right = pack_rows(both[:, side - LANES :], LANES - margin, margin)
        out[plane, :inner] = inner_first[plane]
        out[plane, inner:] = jnp.where(even, right, left)
        out[planes + plane, :inner] = inner_second[plane]
        out[planes + plane, inner:] = jnp.where(even, left, right)


def transform_pair(waves, row_turn, column_turn, matrices, amplitudes):
    length = waves[0][0].shape[0]
    half = length // 2
    row_cos, row_sin = row_turn
    column_cos, column_sin = column_turn

    mixed = []
    for real, imag in waves:
        odd = turned(real[:half] - real[half:], imag[:half] - imag[half:], row_cos, -row_sin)
        stacked = jnp.concatenate(
            [
                jnp.concatenate([real[:half] + real[half:], imag[:half] + imag[half:]], 0),
                jnp.concatenate(odd, 0),
            ],
            1,
        )
        mixed.append(matrix_times(matrices.at[0], stacked))

    far = []
    for value in mixed:
        evens, odds = [], []
        for parity in range(2):
            part = value[:, parity * length : (parity + 1) * length]
            real, imag = part[:half], part[half:]
            evens.append(
                jnp.concatenate(
                    [real[:, :half] + real[:, half:], imag[:, :half] + imag[:, half:]], 1
                )
            )
            odd = turned(
                real[:, :half] - real[:, half:],
                imag[:, :half] - imag[:, half:],
                column_cos,
                -column_sin,
            )
            odds.append(jnp.concatenate(odd, 1))
        far.append(times_matrix(jnp.concatenate(evens + odds, 0), matrices.at[1]))

    turned_back = []
    for value, amplitude in zip(far, amplitudes):
        real, imag = value[:, :half], value[:, half:]
        factor = amplitude * lax.rsqrt(real * real + imag * imag + smoothing)
        corrected = jnp.concatenate([real * factor, imag * factor], 1)
        turned_back.append(times_matrix(corrected, matrices.at[0]))

    near = []
    for value in turned_back:
        even, odd = value[:length], value[length:]
        odd_real, odd_imag = turned(odd[:, :half], odd[:, half:], column_cos, column_sin)
        even_real, even_imag = even[:, :half], even[:, half:]
        real = jnp.concatenate([even_real + odd_real, even_real - odd_real], 1)
        imag = jnp.concatenate([even_imag + odd_imag, even_imag - odd_imag], 1)
        stacked = jnp.concatenate(
            [
                jnp.concatenate([real[:half], imag[:half]], 0),
                jnp.concatenate([real[half:], imag[half:]], 0),
            ],
            1,
        )
        near.append(matrix_times(matrices.at[1], stacked))

    results = []
    for value in near:
        even, odd = value[:, :length], value[:, length:]
        odd_real, odd_imag = turned(odd[:half], odd[half:], row_cos, row_sin)
        results.append(
            (
                jnp.concatenate([even[:half] + odd_real, even[:half] - odd_real], 0),
                jnp.concatenate([even[half:] + odd_imag, even[half:] - odd_imag], 0),
            )
        )
    return results


def frames_kernel(
    counts,
    blocks,
    place,
    offsets,
    field,
    above,
    below,
    columns_first,
    columns_second,
    probe,
    amplitude,
    total,
    powers,
    matrices,
    row_turn,
    column_turn,
    work,
    kept,
    sent,
    padded,
    sums,
):
    frames = amplitude.shape[0]
    length = probe.shape[1]
    side = field.shape[1]
    margin = above.shape[1]
    reach = side + 2 * margin
    taller = length + SUBLANES
    per = LANES // margin
    inner = side // per
    tiles = length // LANES
    last = side // LANES + 1

    for plane in range(2):
        for tile in range(side // LANES):
            lanes = pl.ds(tile * LANES, LANES)
            padded[plane, tile + 1, :margin, :] = above[plane, :, lanes]
            padded[plane, tile + 1, margin : margin + side, :] = field[plane, :, lanes]
            padded[plane, tile + 1, margin + side : reach, :] = below[plane, :, lanes]
        left, right = neighbours(
            columns_first[plane], columns_second[plane], place[2], counts[1]
        )
        for tile, packed, lane in ((0, left, LANES - margin), (last, right, 0)):
            corners = unpack_rows(packed[inner:], lane, margin)
            padded[plane, tile, :margin, :] = corners[:margin]
            padded[plane, tile, margin : margin + side, :] = unpack_rows(
                packed[:inner], lane, margin
            )
            padded[plane, tile, margin + side : reach, :] = corners[margin:]
        padded[plane, :, reach:, :] = jnp.zeros((last + 1, SUBLANES, LANES), f32)
    work[...] = jnp.zeros(work.shape, f32)
    first = jnp.where(place[1] + place[2] == 0, 1.0, 0.0).astype(f32)
    sums[0] = probe[0] * first
    sums[1] = probe[1] * first
    sums[2] = jnp.full((length, length), regular, f32) * first

    row_cos, row_sin = (jnp.concatenate([row_turn[k]] * tiles, 1) for k in range(2))
    column_cos, column_sin = (column_turn[k, 0:1, :] for k in range(2))
    together = max(k for k in (1, 2, 4) if frames % k == 0)

    def visit(step, carry):
        chosen = [step * together + k for k in range(together)]
        spots = [spot(offsets, f, margin, taller) for f in chosen]
        windows = [
            tuple(window_of(padded, plane, spot_of, tiles) for plane in range(2))
            for spot_of in spots
        ]
        probe_real, probe_imag = probe[0], probe[1]
        waves = [
            (
                probe_real * real - probe_imag * imag,
                probe_real * imag + probe_imag * real,
            )
            for real, imag in windows
        ]
        nears = transform_pair(
            waves,
            (row_cos, row_sin),
            (column_cos, column_sin),
            matrices,
            [amplitude[f] for f in chosen],
        )
        for (window_real, window_imag), (near_real, near_imag), spot_of in zip(
            windows, nears, spots
        ):
            sums[0] += window_real * near_real + window_imag * near_imag
            sums[1] += window_real * near_imag - window_imag * near_real
            sums[2] += window_real * window_real + window_imag * window_imag
            add_window(work.at[0], probe_real * near_real + probe_imag * near_imag, spot_of)
            add_window(work.at[1], probe_real * near_imag - probe_imag * near_real, spot_of)
        return carry

    lax.fori_loop(0, frames // together, visit, 0)

    rows = length // blocks
    half_rows = blocks // 2 * 3 * tiles * rows
    for p in range(blocks):
        out, q, base = (
            (kept, p, place[0]) if p < blocks // 2 else (sent, p - blocks // 2, place[3])
        )
        source = pl.multiple_of((base ^ q) * rows, rows)
        for plane in range(3):
            for tile in range(tiles):
                start = ((3 * q + plane) * tiles + tile) * rows
                out[start : start + rows, :] = sums[
                    plane, pl.ds(source, rows), pl.ds(tile * LANES, LANES)
                ]
    kept[half_rows:, :] = total[...]
    sent[half_rows : half_rows + SUBLANES, :] = total[...]
    even = place[2] % 2 == 0
    start = half_rows + SUBLANES
    depth = reach // per
    for plane in range(3):
        canvas = powers if plane == 2 else work.at[plane]
        right = pack_rows(canvas[last, :reach, :], 0, margin)
        left = pack_rows(canvas[0, :reach, :], LANES - margin, margin)
        at = start + plane * depth
        sent[at : at + depth, :] = jnp.where(even, right, left)
        at += 3 * depth
        sent[at : at + depth, :] = jnp.where(even, left, right)


def row_edge_kernel(counts, margin, place, work, powers, first, second, out):
    planes = work.shape[0] + 1
    tiles = work.shape[1] - 2
    reach = work.shape[2] - SUBLANES
    depth = first.shape[0] // planes
    even = place[1] % 2 == 0
    for plane in range(planes):
        canvas = powers if plane == planes - 1 else work.at[plane]
        at = pl.ds(plane * depth, depth)
        before, after = neighbours(first[at, :], second[at, :], place[2], counts[1])
        last = LANES // margin - 1
        edges = []
        for begin, chunk, cut in (
            (0, 0, slice(None, margin)),
            (reach - margin, last, slice(depth - margin, None)),
        ):
            parts = [canvas[tile + 1, begin : begin + margin, :] for tile in range(tiles)]
            parts[0] += unpack(before, chunk, 0, margin)[cut]
            parts[-1] += unpack(after, chunk, LANES - margin, margin)[cut]
            edges.append(parts)
        for tile in range(tiles):
            at = pl.ds((plane * tiles + tile) * margin, margin)
            out[at, :] = jnp.where(even, edges[1][tile], edges[0][tile])
            at = pl.ds(((planes + plane) * tiles + tile) * margin, margin)
            out[at, :] = jnp.where(even, edges[0][tile], edges[1][tile])


def object_kernel(
    counts, margin, place, field, work, powers, first, second, row_first, row_second, out
):
    planes = work.shape[0] + 1
    tiles = work.shape[1] - 2
    side = field.shape[1]
    depth = first.shape[0] // planes
    for tile in range(tiles):
        lanes = pl.ds(tile * LANES, LANES)
        total = []
        for plane in range(planes):
            canvas = powers if plane == planes - 1 else work.at[plane]
            at = pl.ds((plane * tiles + tile) * margin, margin)
            above, below = neighbours(row_first[at, :], row_second[at, :], place[1], counts[0])
            part = canvas[tile + 1, margin : margin + side, :]
            at = pl.ds(plane * depth, depth)
            before, after = neighbours(first[at, :], second[at, :], place[2], counts[1])
            if tile == 0:
                part += unpack_rows(before, 0, margin)[margin : margin + side]
            if tile == tiles - 1:
                part += unpack_rows(after, LANES - margin, margin)[margin : margin + side]
            part = jnp.concatenate(
                [
                    part[:margin] + above,
                    part[margin : side - margin],
                    part[side - margin :] + below,
                ],
                0,
            )
            total.append(part)
        weight = 1.0 / (total[2] + regular)
        out[0, :, lanes] = (field[0, :, lanes] + total[0]) * weight
        out[1, :, lanes] = (field[1, :, lanes] + total[1]) * weight


def probe_kernel(frame_count, blocks, place, stepped, total, out):
    planes, length, _ = out.shape
    tiles = length // LANES
    rows = length // blocks
    values = stepped[...]
    power = jnp.sum(values * values)
    target = jnp.sum(total[...]) / frame_count
    scale = jnp.sqrt(jnp.full((rows, LANES), target / (power + epsilon), f32))
    for p in range(blocks):
        base, q = (place[0], p) if p < blocks // 2 else (place[3], p - blocks // 2)
        home = pl.multiple_of((base ^ q) * rows, rows)
        for plane in range(planes):
            for tile in range(tiles):
                start = ((planes * p + plane) * tiles + tile) * rows
                out[plane, pl.ds(home, rows), pl.ds(tile * LANES, LANES)] = (
                    values[start : start + rows] * scale
                )


def shape(*dims):
    return jax.ShapeDtypeStruct(dims, f32)


def call(kernel, outputs, scalars=0, operands=0, scratch=(), cost=None):
    vmem = pl.BlockSpec(memory_space=pltpu.VMEM)
    smem = pl.BlockSpec(memory_space=pltpu.SMEM)
    return pl.pallas_call(
        kernel,
        out_shape=outputs,
        in_specs=[smem] * scalars + [vmem] * operands,
        out_specs=jax.tree.map(lambda _: vmem, outputs),
        scratch_shapes=list(scratch),
        cost_estimate=cost,
        compiler_params=pltpu.CompilerParams(vmem_limit_bytes=40 * 1024 * 1024),
    )


def paired(block, axis, first):
    count = lax.axis_size(axis)
    target = list(range(count))
    for i in range(first, count - 1, 2):
        target[i], target[i + 1] = i + 1, i
    return lax.ppermute(block, axis, list(enumerate(target)))


def relayed(block, axis):
    count = lax.axis_size(axis)
    target = {i: i + 2 if i % 2 == 0 else i - 2 for i in range(count)}
    target[count - 2], target[1] = count - 1, 0
    return lax.ppermute(block, axis, list(target.items()))


def exchanged(block, orders, distance):
    count = lax.axis_size("row") * lax.axis_size("col")
    masks = [
        sum(1 << bit for k, bit in enumerate(order) if distance >> k & 1) for order in orders
    ]
    return lax.ppermute(block, ("row", "col"), [(i, i ^ masks[i % 2]) for i in range(count)])


def per_device(object_field, probe, amplitudes, positions):
    planes, side, _ = object_field.shape
    length = probe.shape[1]
    margin = MARGIN
    reach = side + 2 * margin
    per = LANES // margin
    tiles = length // LANES
    measured = amplitudes[0, 0]
    frames = measured.shape[0]
    counts = lax.axis_size("row"), lax.axis_size("col")
    row = lax.axis_index("row").astype(jnp.int32)
    col = lax.axis_index("col").astype(jnp.int32)
    index = row * counts[1] + col
    col_bits = (counts[1] - 1).bit_length()
    across = list(range(1, col_bits))
    along = list(range(col_bits, col_bits + (counts[0] - 1).bit_length()))
    halvings = 2
    orders = tuple(
        order[:halvings] + order[halvings:][::-1] for order in (across + along, along + across)
    )
    blocks = 2 << halvings
    rows = length // blocks
    homes = [
        sum(((index >> order[k]) & 1) << k for k in range(halvings))
        for order in orders
    ]
    core = index & 1
    homes[1] += blocks // 2
    place = jnp.stack(
        [
            jnp.where(core == 0, homes[0], homes[1]),
            row,
            col,
            jnp.where(core == 0, homes[1], homes[0]),
        ]
    )

    edge_rows = shape(planes, margin, side)
    inner = shape(planes, side // per, LANES)
    odd = row & 1
    last = side - margin
    rows_first = lax.dynamic_slice_in_dim(object_field, last - odd * last, margin, 1)
    rows_second = lax.dynamic_slice_in_dim(object_field, odd * last, margin, 1)
    rows_second = paired(rows_second, "row", 1)
    rows_first = paired(rows_first, "row", 0)
    inner_first, inner_second = call(
        functools.partial(pack_kernel, margin), (inner, inner), scalars=1, operands=1
    )(place, object_field)
    above, below, columns = call(
        functools.partial(corner_kernel, counts),
        (edge_rows, edge_rows, shape(2 * planes, reach // per, LANES)),
        scalars=1,
        operands=4,
    )(place, rows_first, rows_second, inner_first, inner_second)
    columns = paired(columns, "col", 0)
    relay = relayed(columns[planes:], "col")

    ordered, total, powers = call(
        functools.partial(prepare_kernel, margin),
        (
            shape(frames, 2 * length, length // 2),
            shape(SUBLANES, LANES),
            shape(side // LANES + 2, reach + SUBLANES, LANES),
        ),
        scalars=1,
        operands=2,
        scratch=(pltpu.VMEM((frames, 2, length, length // 2), f32),),
        cost=pl.CostEstimate(flops=10**9, bytes_accessed=2 * measured.size * 4, transcendentals=0),
    )(positions[0, 0], measured, probe)
    matrices, row_turn, column_turn = tables(length)
    half_rows = blocks // 2 * 3 * tiles * rows
    depth = 3 * reach // per
    work, kept, sent = call(
        functools.partial(frames_kernel, counts, blocks),
        (
            shape(2, side // LANES + 2, reach + SUBLANES, LANES),
            shape(half_rows + SUBLANES, LANES),
            shape(half_rows + SUBLANES + 2 * depth, LANES),
        ),
        scalars=2,
        operands=12,
        scratch=(
            pltpu.VMEM((2, side // LANES + 2, reach + SUBLANES, LANES), f32),
            pltpu.VMEM((3, length, length), f32),
        ),
    )(
        place,
        positions[0, 0],
        object_field,
        above,
        below,
        columns,
        relay,
        probe,
        ordered,
        total,
        powers,
        jnp.asarray(matrices),
        jnp.asarray(row_turn),
        jnp.asarray(column_turn),
    )

    arrived = paired(sent, "col", 0)
    current = kept + arrived[: half_rows + SUBLANES]
    first = arrived[half_rows + SUBLANES : half_rows + SUBLANES + depth]
    second = relayed(arrived[half_rows + SUBLANES + depth :], "col")
    block = 3 * tiles * rows
    total = current[-SUBLANES:]
    quarters = [
        jnp.concatenate([current[d * block : (d + 1) * block], total], 0) for d in range(blocks // 2)
    ]
    terms = quarters[:1] + [exchanged(quarters[d], orders, d) for d in range(1, blocks // 2)]
    while len(terms) > 1:
        terms = [terms[k] + terms[k + 1] for k in range(0, len(terms), 2)]
    current = terms[0]
    current, second = lax.optimization_barrier((current, second))
    count = 3 * tiles * margin
    edges = call(
        functools.partial(row_edge_kernel, counts, margin),
        shape(2 * count, LANES),
        scalars=1,
        operands=4,
    )(place, work, powers, first, second)
    edges = paired(edges, "row", 0)
    for step in range(halvings, len(orders[0])):
        if step == halvings + 1:
            current, edges = lax.optimization_barrier((current, edges))
            row_first = edges[:count]
            row_second = relayed(edges[count:], "row")
        current = current + exchanged(current, orders, 1 << step)
    size = tiles * rows
    weight = current[2 * size : 3 * size]
    stepped = current[: 2 * size] / jnp.concatenate([weight, weight], 0)
    stepped = jnp.concatenate(
        [stepped] + [exchanged(stepped, orders, d) for d in range(1, blocks // 2)], 0
    )
    stepped, row_second = lax.optimization_barrier((stepped, row_second))
    object_next = call(
        functools.partial(object_kernel, counts, margin),
        shape(*object_field.shape),
        scalars=1,
        operands=7,
    )(place, object_field, work, powers, first, second, row_first, row_second)
    stepped = jnp.concatenate([stepped, paired(stepped, "col", 0)], 0)
    frame_count = frames * counts[0] * counts[1]
    probe_next = call(
        functools.partial(probe_kernel, frame_count, blocks),
        shape(*probe.shape),
        scalars=1,
        operands=2,
    )(place, stepped, current[3 * size :])
    return (object_next, probe_next)


def solution(mesh):
    return jax.shard_map(
        per_device,
        mesh=mesh,
        in_specs=(
            P(None, "row", "col"),
            P(),
            P("row", "col", None, None, None),
            P("row", "col", None, None),
        ),
        out_specs=(P(None, "row", "col"), P()),
        check_vma=False,
    )
```

```python
import functools
import math

import jax
import jax.numpy as jnp
import numpy as np
from jax import lax
from jax.experimental import pallas as pl
from jax.experimental.pallas import tpu as pltpu
from jax.sharding import PartitionSpec as P

MARGIN = 32
LANES = 128
SUBLANES = 8

smoothing = 0.1
regular = 1.0
epsilon = 1e-06

f32 = jnp.float32
bf16 = jnp.bfloat16


def tables(length):
    half = length // 2
    scaling = 1.0 / math.sqrt(length)
    k = np.arange(half)
    phases = (k[:, None] * k[None, :] % half) * (2.0 * math.pi / half)
    cosine, sine = np.cos(phases) * scaling, np.sin(phases) * scaling
    right = np.block([[cosine, -sine], [sine, cosine]])
    left = np.block([[cosine, sine], [-sine, cosine]])
    both = np.stack([left, right]).astype(np.float32)
    high = both.astype(bf16)
    low = (both - high.astype(np.float32)).astype(bf16)
    matrices = np.stack([high, low], 1)
    angle = k * (2.0 * math.pi / length)
    turn = np.stack([np.cos(angle), np.sin(angle)]).astype(np.float32)
    rows = np.broadcast_to(turn[:, :, None], (2, half, LANES)).copy()
    columns = np.broadcast_to(turn[:, None, :], (2, SUBLANES, half)).copy()
    return matrices, rows, columns


def split(x):
    high = x.astype(bf16)
    return high, (x - high.astype(f32)).astype(bf16)


def dot(a, b):
    return jnp.dot(a, b, preferred_element_type=f32)


def times_matrix(data, matrix):
    high, low = split(data)
    return dot(
        jnp.concatenate([high, low, high], 1),
        jnp.concatenate([matrix[0], matrix[0], matrix[1]], 0),
    )


def matrix_times(matrix, data):
    high, low = split(data)
    return dot(
        jnp.concatenate([matrix[0], matrix[0], matrix[1]], 1),
        jnp.concatenate([high, low, high], 0),
    )


def turned(real, imag, cosine, sine):
    return real * cosine - imag * sine, real * sine + imag * cosine


def pack(chunks, lane, width):
    place = lax.broadcasted_iota(jnp.int32, chunks[0].shape, 1) // width
    out = jnp.zeros_like(chunks[0])
    for q, chunk in enumerate(chunks):
        shift = (q * width - lane) % LANES
        moved = pltpu.roll(chunk, shift, 1) if shift else chunk
        out = jnp.where(place == q, moved, out)
    return out


def pack_rows(rows, lane, width):
    count = rows.shape[0] * width // LANES
    return pack([rows[q : q + count] for q in range(0, rows.shape[0], count)], lane, width)


def unpack(packed, q, lane, width):
    shift = (lane - q * width) % LANES
    moved = pltpu.roll(packed, shift, 1) if shift else packed
    place = lax.broadcasted_iota(jnp.int32, packed.shape, 1)
    return jnp.where((place >= lane) & (place < lane + width), moved, 0.0)


def unpack_rows(packed, lane, width):
    return jnp.concatenate([unpack(packed, q, lane, width) for q in range(LANES // width)], 0)


def lifted(tile, shift):
    groups = tile.shape[0] // SUBLANES
    turned_rows = pltpu.roll(
        tile.reshape(groups, SUBLANES, LANES), lax.rem(SUBLANES - shift, SUBLANES), 1
    )
    place = lax.broadcasted_iota(jnp.int32, (groups - 1, SUBLANES, LANES), 1)
    picked = jnp.where(place < SUBLANES - shift, turned_rows[:-1], turned_rows[1:])
    return picked.reshape((groups - 1) * SUBLANES, LANES)


def lowered(tile, shift):
    groups = tile.shape[0] // SUBLANES
    moved = pltpu.roll(tile.reshape(groups, SUBLANES, LANES), shift, 1)
    none = jnp.zeros((1, SUBLANES, LANES), f32)
    place = lax.broadcasted_iota(jnp.int32, (groups + 1, SUBLANES, LANES), 1)
    picked = jnp.where(
        place >= shift, jnp.concatenate([moved, none], 0), jnp.concatenate([none, moved], 0)
    )
    return picked.reshape((groups + 1) * SUBLANES, LANES)


def spot(offsets, f, margin, taller):
    a, b = offsets[f, 0], offsets[f, 1]
    shift = lax.rem(a, SUBLANES)
    lane = b + LANES - margin
    tile = lane // LANES
    return pl.ds(pl.multiple_of(a - shift, SUBLANES), taller), shift, tile, lane - tile * LANES


def window_of(padded, plane, spot_of, tiles):
    at, shift, base, lane = spot_of
    moved = [
        pltpu.roll(padded[plane, base + t, at, :], lax.rem(LANES - lane, LANES), 1)
        for t in range(tiles + 1)
    ]
    place = lax.broadcasted_iota(jnp.int32, moved[0].shape, 1)
    parts = [
        lifted(jnp.where(place < LANES - lane, moved[t], moved[t + 1]), shift)
        for t in range(tiles)
    ]
    return jnp.concatenate(parts, 1)


def add_window(work, term, spot_of):
    at, shift, base, lane = spot_of
    tiles = term.shape[1] // LANES
    moved = [
        pltpu.roll(lowered(term[:, t * LANES : (t + 1) * LANES], shift), lane, 1)
        for t in range(tiles)
    ]
    none = jnp.zeros_like(moved[0])
    place = lax.broadcasted_iota(jnp.int32, none.shape, 1)
    for t in range(tiles + 1):
        here = moved[t] if t < tiles else none
        before = moved[t - 1] if t else none
        work[base + t, at, :] += jnp.where(place >= lane, here, before)


def neighbours(first, second, index, count):
    even = index % 2 == 0
    before = jnp.where(even, second, first)
    after = jnp.where(even, first, second)
    return jnp.where(index > 0, before, 0.0), jnp.where(index < count - 1, after, 0.0)


def pack_kernel(margin, place, field, columns_first, columns_second):
    planes, side, _ = field.shape
    even = place[2] % 2 == 0
    for plane in range(planes):
        left = pack_rows(field[plane, :, :LANES], 0, margin)
        right = pack_rows(field[plane, :, side - LANES :], LANES - margin, margin)
        columns_first[plane] = jnp.where(even, right, left)
        columns_second[plane] = jnp.where(even, left, right)


def prepare_kernel(margin, offsets, amplitude, probe, sorted_out, total_out, powers, held):
    frames, length, _ = amplitude.shape
    half = length // 2
    power = probe[0] * probe[0] + probe[1] * probe[1]
    powers[...] = jnp.zeros(powers.shape, f32)
    for f in range(frames):
        add_window(powers, power, spot(offsets, f, margin, length + SUBLANES))
    row = lax.broadcasted_iota(jnp.int32, (length, length), 0)
    column = lax.broadcasted_iota(jnp.int32, (length, length), 1)
    source = jnp.where(column < half, 2 * column, 2 * (column - half) + 1)
    order = jnp.where(row == source, 1.0, 0.0).astype(bf16)
    total = jnp.zeros((SUBLANES, length), f32)
    for f in range(frames):
        values = amplitude[f]
        total += jnp.sum((values * values).reshape(length // SUBLANES, SUBLANES, length), 0)
        high = values.astype(bf16)
        rest = values - high.astype(f32)
        middle = rest.astype(bf16)
        low = (rest - middle.astype(f32)).astype(bf16)
        placed = dot(high, order) + (dot(middle, order) + dot(low, order))
        for parity in range(2):
            held[f, parity] = placed[:, parity * half : (parity + 1) * half]
            for start in range(2):
                at = 2 * parity + start
                sorted_out[f, at * half : (at + 1) * half, :] = held[
                    f, parity, pl.ds(start, half, stride=2), :
                ]
    total_out[...] = sum(total[:, t * LANES : (t + 1) * LANES] for t in range(length // LANES))


def corner_kernel(counts, place, first, second, inner_first, inner_second, above, below, out):
    planes, margin, side = first.shape
    inner = inner_first.shape[1]
    even = place[2] % 2 == 0
    for plane in range(planes):
        before, after = neighbours(first[plane], second[plane], place[1], counts[0])
        above[plane] = before
        below[plane] = after
        both = jnp.concatenate([before, after], 0)
        left = pack_rows(both[:, :LANES], 0, margin)
        right = pack_rows(both[:, side - LANES :], LANES - margin, margin)
        out[plane, :inner] = inner_first[plane]
        out[plane, inner:] = jnp.where(even, right, left)
        out[planes + plane, :inner] = inner_second[plane]
        out[planes + plane, inner:] = jnp.where(even, left, right)


def transform_pair(waves, row_turn, column_turn, matrices, amplitudes):
    length = waves[0][0].shape[0]
    half = length // 2
    row_cos, row_sin = row_turn
    column_cos, column_sin = column_turn

    mixed = []
    for real, imag in waves:
        odd = turned(real[:half] - real[half:], imag[:half] - imag[half:], row_cos, -row_sin)
        stacked = jnp.concatenate(
            [
                jnp.concatenate([real[:half] + real[half:], imag[:half] + imag[half:]], 0),
                jnp.concatenate(odd, 0),
            ],
            1,
        )
        mixed.append(matrix_times(matrices.at[0], stacked))

    far = []
    for value in mixed:
        evens, odds = [], []
        for parity in range(2):
            part = value[:, parity * length : (parity + 1) * length]
            real, imag = part[:half], part[half:]
            evens.append(
                jnp.concatenate(
                    [real[:, :half] + real[:, half:], imag[:, :half] + imag[:, half:]], 1
                )
            )
            odd = turned(
                real[:, :half] - real[:, half:],
                imag[:, :half] - imag[:, half:],
                column_cos,
                -column_sin,
            )
            odds.append(jnp.concatenate(odd, 1))
        far.append(times_matrix(jnp.concatenate(evens + odds, 0), matrices.at[1]))

    turned_back = []
    for value, amplitude in zip(far, amplitudes):
        real, imag = value[:, :half], value[:, half:]
        factor = amplitude * lax.rsqrt(real * real + imag * imag + smoothing)
        corrected = jnp.concatenate([real * factor, imag * factor], 1)
        turned_back.append(times_matrix(corrected, matrices.at[0]))

    near = []
    for value in turned_back:
        even, odd = value[:length], value[length:]
        odd_real, odd_imag = turned(odd[:, :half], odd[:, half:], column_cos, column_sin)
        even_real, even_imag = even[:, :half], even[:, half:]
        real = jnp.concatenate([even_real + odd_real, even_real - odd_real], 1)
        imag = jnp.concatenate([even_imag + odd_imag, even_imag - odd_imag], 1)
        stacked = jnp.concatenate(
            [
                jnp.concatenate([real[:half], imag[:half]], 0),
                jnp.concatenate([real[half:], imag[half:]], 0),
            ],
            1,
        )
        near.append(matrix_times(matrices.at[1], stacked))

    results = []
    for value in near:
        even, odd = value[:, :length], value[:, length:]
        odd_real, odd_imag = turned(odd[:half], odd[half:], row_cos, row_sin)
        results.append(
            (
                jnp.concatenate([even[:half] + odd_real, even[:half] - odd_real], 0),
                jnp.concatenate([even[half:] + odd_imag, even[half:] - odd_imag], 0),
            )
        )
    return results


def frames_kernel(
    counts,
    blocks,
    place,
    offsets,
    field,
    above,
    below,
    columns_first,
    columns_second,
    probe,
    amplitude,
    total,
    powers,
    matrices,
    row_turn,
    column_turn,
    work,
    kept,
    sent,
    padded,
    sums,
):
    frames = amplitude.shape[0]
    length = probe.shape[1]
    side = field.shape[1]
    margin = above.shape[1]
    reach = side + 2 * margin
    taller = length + SUBLANES
    per = LANES // margin
    inner = side // per
    tiles = length // LANES
    last = side // LANES + 1

    for plane in range(2):
        for tile in range(side // LANES):
            lanes = pl.ds(tile * LANES, LANES)
            padded[plane, tile + 1, :margin, :] = above[plane, :, lanes]
            padded[plane, tile + 1, margin : margin + side, :] = field[plane, :, lanes]
            padded[plane, tile + 1, margin + side : reach, :] = below[plane, :, lanes]
        left, right = neighbours(
            columns_first[plane], columns_second[plane], place[2], counts[1]
        )
        for tile, packed, lane in ((0, left, LANES - margin), (last, right, 0)):
            corners = unpack_rows(packed[inner:], lane, margin)
            padded[plane, tile, :margin, :] = corners[:margin]
            padded[plane, tile, margin : margin + side, :] = unpack_rows(
                packed[:inner], lane, margin
            )
            padded[plane, tile, margin + side : reach, :] = corners[margin:]
        padded[plane, :, reach:, :] = jnp.zeros((last + 1, SUBLANES, LANES), f32)
    work[...] = jnp.zeros(work.shape, f32)
    first = jnp.where(place[1] + place[2] == 0, 1.0, 0.0).astype(f32)
    sums[0] = probe[0] * first
    sums[1] = probe[1] * first
    sums[2] = jnp.full((length, length), regular, f32) * first

    row_cos, row_sin = (jnp.concatenate([row_turn[k]] * tiles, 1) for k in range(2))
    column_cos, column_sin = (column_turn[k, 0:1, :] for k in range(2))
    together = max(k for k in (1, 2, 4) if frames % k == 0)

    def visit(step, carry):
        chosen = [step * together + k for k in range(together)]
        spots = [spot(offsets, f, margin, taller) for f in chosen]
        windows = [
            tuple(window_of(padded, plane, spot_of, tiles) for plane in range(2))
            for spot_of in spots
        ]
        probe_real, probe_imag = probe[0], probe[1]
        waves = [
            (
                probe_real * real - probe_imag * imag,
                probe_real * imag + probe_imag * real,
            )
            for real, imag in windows
        ]
        nears = transform_pair(
            waves,
            (row_cos, row_sin),
            (column_cos, column_sin),
            matrices,
            [amplitude[f] for f in chosen],
        )
        for (window_real, window_imag), (near_real, near_imag), spot_of in zip(
            windows, nears, spots
        ):
            sums[0] += window_real * near_real + window_imag * near_imag
            sums[1] += window_real * near_imag - window_imag * near_real
            sums[2] += window_real * window_real + window_imag * window_imag
            add_window(work.at[0], probe_real * near_real + probe_imag * near_imag, spot_of)
            add_window(work.at[1], probe_real * near_imag - probe_imag * near_real, spot_of)
        return carry

    lax.fori_loop(0, frames // together, visit, 0)

    rows = length // blocks
    half_rows = blocks // 2 * 3 * tiles * rows
    for p in range(blocks):
        out, q, base = (
            (kept, p, place[0]) if p < blocks // 2 else (sent, p - blocks // 2, place[3])
        )
        source = pl.multiple_of((base ^ q) * rows, rows)
        for plane in range(3):
            for tile in range(tiles):
                start = ((3 * q + plane) * tiles + tile) * rows
                out[start : start + rows, :] = sums[
                    plane, pl.ds(source, rows), pl.ds(tile * LANES, LANES)
                ]
    kept[half_rows:, :] = total[...]
    sent[half_rows : half_rows + SUBLANES, :] = total[...]
    even = place[2] % 2 == 0
    start = half_rows + SUBLANES
    depth = reach // per
    for plane in range(3):
        canvas = powers if plane == 2 else work.at[plane]
        right = pack_rows(canvas[last, :reach, :], 0, margin)
        left = pack_rows(canvas[0, :reach, :], LANES - margin, margin)
        at = start + plane * depth
        sent[at : at + depth, :] = jnp.where(even, right, left)
        at += 3 * depth
        sent[at : at + depth, :] = jnp.where(even, left, right)


def row_edge_kernel(counts, margin, place, work, powers, first, second, out):
    planes = work.shape[0] + 1
    tiles = work.shape[1] - 2
    reach = work.shape[2] - SUBLANES
    depth = first.shape[0] // planes
    even = place[1] % 2 == 0
    for plane in range(planes):
        canvas = powers if plane == planes - 1 else work.at[plane]
        at = pl.ds(plane * depth, depth)
        before, after = neighbours(first[at, :], second[at, :], place[2], counts[1])
        last = LANES // margin - 1
        edges = []
        for begin, chunk, cut in (
            (0, 0, slice(None, margin)),
            (reach - margin, last, slice(depth - margin, None)),
        ):
            parts = [canvas[tile + 1, begin : begin + margin, :] for tile in range(tiles)]
            parts[0] += unpack(before, chunk, 0, margin)[cut]
            parts[-1] += unpack(after, chunk, LANES - margin, margin)[cut]
            edges.append(parts)
        for tile in range(tiles):
            at = pl.ds((plane * tiles + tile) * margin, margin)
            out[at, :] = jnp.where(even, edges[1][tile], edges[0][tile])
            at = pl.ds(((planes + plane) * tiles + tile) * margin, margin)
            out[at, :] = jnp.where(even, edges[0][tile], edges[1][tile])


def object_kernel(
    counts, margin, place, field, work, powers, first, second, row_first, row_second, out
):
    planes = work.shape[0] + 1
    tiles = work.shape[1] - 2
    side = field.shape[1]
    depth = first.shape[0] // planes
    for tile in range(tiles):
        lanes = pl.ds(tile * LANES, LANES)
        total = []
        for plane in range(planes):
            canvas = powers if plane == planes - 1 else work.at[plane]
            at = pl.ds((plane * tiles + tile) * margin, margin)
            above, below = neighbours(row_first[at, :], row_second[at, :], place[1], counts[0])
            part = canvas[tile + 1, margin : margin + side, :]
            at = pl.ds(plane * depth, depth)
            before, after = neighbours(first[at, :], second[at, :], place[2], counts[1])
            if tile == 0:
                part += unpack_rows(before, 0, margin)[margin : margin + side]
            if tile == tiles - 1:
                part += unpack_rows(after, LANES - margin, margin)[margin : margin + side]
            part = jnp.concatenate(
                [
                    part[:margin] + above,
                    part[margin : side - margin],
                    part[side - margin :] + below,
                ],
                0,
            )
            total.append(part)
        weight = 1.0 / (total[2] + regular)
        out[0, :, lanes] = (field[0, :, lanes] + total[0]) * weight
        out[1, :, lanes] = (field[1, :, lanes] + total[1]) * weight


def probe_kernel(frame_count, blocks, place, stepped, total, out):
    planes, length, _ = out.shape
    tiles = length // LANES
    rows = length // blocks
    values = stepped[...]
    power = jnp.sum(values * values)
    target = jnp.sum(total[...]) / frame_count
    scale = jnp.sqrt(jnp.full((rows, LANES), target / (power + epsilon), f32))
    for p in range(blocks):
        base, q = (place[0], p) if p < blocks // 2 else (place[3], p - blocks // 2)
        home = pl.multiple_of((base ^ q) * rows, rows)
        for plane in range(planes):
            for tile in range(tiles):
                start = ((planes * p + plane) * tiles + tile) * rows
                out[plane, pl.ds(home, rows), pl.ds(tile * LANES, LANES)] = (
                    values[start : start + rows] * scale
                )


def shape(*dims):
    return jax.ShapeDtypeStruct(dims, f32)


def call(kernel, outputs, scalars=0, operands=0, scratch=(), cost=None):
    vmem = pl.BlockSpec(memory_space=pltpu.VMEM)
    smem = pl.BlockSpec(memory_space=pltpu.SMEM)
    return pl.pallas_call(
        kernel,
        out_shape=outputs,
        in_specs=[smem] * scalars + [vmem] * operands,
        out_specs=jax.tree.map(lambda _: vmem, outputs),
        scratch_shapes=list(scratch),
        cost_estimate=cost,
        compiler_params=pltpu.CompilerParams(vmem_limit_bytes=40 * 1024 * 1024),
    )


def paired(block, axis, first):
    count = lax.axis_size(axis)
    target = list(range(count))
    for i in range(first, count - 1, 2):
        target[i], target[i + 1] = i + 1, i
    return lax.ppermute(block, axis, list(enumerate(target)))


def relayed(block, axis):
    count = lax.axis_size(axis)
    target = {i: i + 2 if i % 2 == 0 else i - 2 for i in range(count)}
    target[count - 2], target[1] = count - 1, 0
    return lax.ppermute(block, axis, list(target.items()))


def exchanged(block, orders, distance):
    count = lax.axis_size("row") * lax.axis_size("col")
    masks = [
        sum(1 << bit for k, bit in enumerate(order) if distance >> k & 1) for order in orders
    ]
    return lax.ppermute(block, ("row", "col"), [(i, i ^ masks[i % 2]) for i in range(count)])


def per_device(object_field, probe, amplitudes, positions):
    planes, side, _ = object_field.shape
    length = probe.shape[1]
    margin = MARGIN
    reach = side + 2 * margin
    per = LANES // margin
    tiles = length // LANES
    measured = amplitudes[0, 0]
    frames = measured.shape[0]
    counts = lax.axis_size("row"), lax.axis_size("col")
    row = lax.axis_index("row").astype(jnp.int32)
    col = lax.axis_index("col").astype(jnp.int32)
    index = row * counts[1] + col
    col_bits = (counts[1] - 1).bit_length()
    across = list(range(1, col_bits))
    along = list(range(col_bits, col_bits + (counts[0] - 1).bit_length()))
    halvings = 2
    orders = tuple(
        order[:halvings] + order[halvings:][::-1] for order in (across + along, along + across)
    )
    blocks = 2 << halvings
    rows = length // blocks
    homes = [
        sum(((index >> order[k]) & 1) << k for k in range(halvings))
        for order in orders
    ]
    core = index & 1
    homes[1] += blocks // 2
    place = jnp.stack(
        [
            jnp.where(core == 0, homes[0], homes[1]),
            row,
            col,
            jnp.where(core == 0, homes[1], homes[0]),
        ]
    )

    edge_rows = shape(planes, margin, side)
    inner = shape(planes, side // per, LANES)
    odd = row & 1
    last = side - margin
    rows_first = lax.dynamic_slice_in_dim(object_field, last - odd * last, margin, 1)
    rows_second = lax.dynamic_slice_in_dim(object_field, odd * last, margin, 1)
    rows_second = paired(rows_second, "row", 1)
    rows_first = paired(rows_first, "row", 0)
    inner_first, inner_second = call(
        functools.partial(pack_kernel, margin), (inner, inner), scalars=1, operands=1
    )(place, object_field)
    above, below, columns = call(
        functools.partial(corner_kernel, counts),
        (edge_rows, edge_rows, shape(2 * planes, reach // per, LANES)),
        scalars=1,
        operands=4,
    )(place, rows_first, rows_second, inner_first, inner_second)
    columns = paired(columns, "col", 0)
    relay = relayed(columns[planes:], "col")

    ordered, total, powers = call(
        functools.partial(prepare_kernel, margin),
        (
            shape(frames, 2 * length, length // 2),
            shape(SUBLANES, LANES),
            shape(side // LANES + 2, reach + SUBLANES, LANES),
        ),
        scalars=1,
        operands=2,
        scratch=(pltpu.VMEM((frames, 2, length, length // 2), f32),),
        cost=pl.CostEstimate(flops=10**9, bytes_accessed=2 * measured.size * 4, transcendentals=0),
    )(positions[0, 0], measured, probe)
    matrices, row_turn, column_turn = tables(length)
    half_rows = blocks // 2 * 3 * tiles * rows
    depth = 3 * reach // per
    work, kept, sent = call(
        functools.partial(frames_kernel, counts, blocks),
        (
            shape(2, side // LANES + 2, reach + SUBLANES, LANES),
            shape(half_rows + SUBLANES, LANES),
            shape(half_rows + SUBLANES + 2 * depth, LANES),
        ),
        scalars=2,
        operands=12,
        scratch=(
            pltpu.VMEM((2, side // LANES + 2, reach + SUBLANES, LANES), f32),
            pltpu.VMEM((3, length, length), f32),
        ),
    )(
        place,
        positions[0, 0],
        object_field,
        above,
        below,
        columns,
        relay,
        probe,
        ordered,
        total,
        powers,
        jnp.asarray(matrices),
        jnp.asarray(row_turn),
        jnp.asarray(column_turn),
    )

    arrived = paired(sent, "col", 0)
    current = kept + arrived[: half_rows + SUBLANES]
    first = arrived[half_rows + SUBLANES : half_rows + SUBLANES + depth]
    second = relayed(arrived[half_rows + SUBLANES + depth :], "col")
    block = 3 * tiles * rows
    total = current[-SUBLANES:]
    quarters = [
        jnp.concatenate([current[d * block : (d + 1) * block], total], 0) for d in range(blocks // 2)
    ]
    terms = quarters[:1] + [exchanged(quarters[d], orders, d) for d in range(1, blocks // 2)]
    while len(terms) > 1:
        terms = [terms[k] + terms[k + 1] for k in range(0, len(terms), 2)]
    current = terms[0]
    current, second = lax.optimization_barrier((current, second))
    count = 3 * tiles * margin
    edges = call(
        functools.partial(row_edge_kernel, counts, margin),
        shape(2 * count, LANES),
        scalars=1,
        operands=4,
    )(place, work, powers, first, second)
    edges = paired(edges, "row", 0)
    for step in range(halvings, len(orders[0])):
        if step == halvings + 1:
            current, edges = lax.optimization_barrier((current, edges))
            row_first = edges[:count]
            row_second = relayed(edges[count:], "row")
        current = current + exchanged(current, orders, 1 << step)
    size = tiles * rows
    weight = current[2 * size : 3 * size]
    stepped = current[: 2 * size] / jnp.concatenate([weight, weight], 0)
    stepped = jnp.concatenate(
        [stepped] + [exchanged(stepped, orders, d) for d in range(1, blocks // 2)], 0
    )
    object_next = call(
        functools.partial(object_kernel, counts, margin),
        shape(*object_field.shape),
        scalars=1,
        operands=7,
    )(place, object_field, work, powers, first, second, row_first, row_second)
    stepped = jnp.concatenate([stepped, paired(stepped, "col", 0)], 0)
    frame_count = frames * counts[0] * counts[1]
    probe_next = call(
        functools.partial(probe_kernel, frame_count, blocks),
        shape(*probe.shape),
        scalars=1,
        operands=2,
    )(place, stepped, current[3 * size :])
    return (object_next, probe_next)


def solution(mesh):
    return jax.shard_map(
        per_device,
        mesh=mesh,
        in_specs=(
            P(None, "row", "col"),
            P(),
            P("row", "col", None, None, None),
            P("row", "col", None, None),
        ),
        out_specs=(P(None, "row", "col"), P()),
        check_vma=False,
    )
```

```python
import functools
import math

import jax
import jax.numpy as jnp
import numpy as np
from jax import lax
from jax.experimental import pallas as pl
from jax.experimental.pallas import tpu as pltpu
from jax.sharding import PartitionSpec as P

MARGIN = 32
LANES = 128
SUBLANES = 8

smoothing = 0.1
regular = 1.0
epsilon = 1e-06

f32 = jnp.float32
bf16 = jnp.bfloat16


def tables(length):
    half = length // 2
    scaling = 1.0 / math.sqrt(length)
    k = np.arange(half)
    phases = (k[:, None] * k[None, :] % half) * (2.0 * math.pi / half)
    cosine, sine = np.cos(phases) * scaling, np.sin(phases) * scaling
    right = np.block([[cosine, -sine], [sine, cosine]])
    left = np.block([[cosine, sine], [-sine, cosine]])
    both = np.stack([left, right]).astype(np.float32)
    high = both.astype(bf16)
    low = (both - high.astype(np.float32)).astype(bf16)
    matrices = np.stack([high, low], 1)
    angle = k * (2.0 * math.pi / length)
    turn = np.stack([np.cos(angle), np.sin(angle)]).astype(np.float32)
    rows = np.broadcast_to(turn[:, :, None], (2, half, LANES)).copy()
    columns = np.broadcast_to(turn[:, None, :], (2, SUBLANES, half)).copy()
    return matrices, rows, columns


def split(x):
    high = x.astype(bf16)
    return high, (x - high.astype(f32)).astype(bf16)


def dot(a, b):
    return jnp.dot(a, b, preferred_element_type=f32)


def times_matrix(data, matrix):
    high, low = split(data)
    return dot(
        jnp.concatenate([high, low, high], 1),
        jnp.concatenate([matrix[0], matrix[0], matrix[1]], 0),
    )


def matrix_times(matrix, data):
    high, low = split(data)
    return dot(
        jnp.concatenate([matrix[0], matrix[0], matrix[1]], 1),
        jnp.concatenate([high, low, high], 0),
    )


def turned(real, imag, cosine, sine):
    return real * cosine - imag * sine, real * sine + imag * cosine


def pack(chunks, lane, width):
    place = lax.broadcasted_iota(jnp.int32, chunks[0].shape, 1) // width
    out = jnp.zeros_like(chunks[0])
    for q, chunk in enumerate(chunks):
        shift = (q * width - lane) % LANES
        moved = pltpu.roll(chunk, shift, 1) if shift else chunk
        out = jnp.where(place == q, moved, out)
    return out


def pack_rows(rows, lane, width):
    count = rows.shape[0] * width // LANES
    return pack([rows[q : q + count] for q in range(0, rows.shape[0], count)], lane, width)


def unpack(packed, q, lane, width):
    shift = (lane - q * width) % LANES
    moved = pltpu.roll(packed, shift, 1) if shift else packed
    place = lax.broadcasted_iota(jnp.int32, packed.shape, 1)
    return jnp.where((place >= lane) & (place < lane + width), moved, 0.0)


def unpack_rows(packed, lane, width):
    return jnp.concatenate([unpack(packed, q, lane, width) for q in range(LANES // width)], 0)


def lifted(tile, shift):
    groups = tile.shape[0] // SUBLANES
    turned_rows = pltpu.roll(
        tile.reshape(groups, SUBLANES, LANES), lax.rem(SUBLANES - shift, SUBLANES), 1
    )
    place = lax.broadcasted_iota(jnp.int32, (groups - 1, SUBLANES, LANES), 1)
    picked = jnp.where(place < SUBLANES - shift, turned_rows[:-1], turned_rows[1:])
    return picked.reshape((groups - 1) * SUBLANES, LANES)


def lowered(tile, shift):
    groups = tile.shape[0] // SUBLANES
    moved = pltpu.roll(tile.reshape(groups, SUBLANES, LANES), shift, 1)
    none = jnp.zeros((1, SUBLANES, LANES), f32)
    place = lax.broadcasted_iota(jnp.int32, (groups + 1, SUBLANES, LANES), 1)
    picked = jnp.where(
        place >= shift, jnp.concatenate([moved, none], 0), jnp.concatenate([none, moved], 0)
    )
    return picked.reshape((groups + 1) * SUBLANES, LANES)


def spot(offsets, f, margin, taller):
    a, b = offsets[f, 0], offsets[f, 1]
    shift = lax.rem(a, SUBLANES)
    lane = b + LANES - margin
    tile = lane // LANES
    return pl.ds(pl.multiple_of(a - shift, SUBLANES), taller), shift, tile, lane - tile * LANES


def window_of(padded, plane, spot_of, tiles):
    at, shift, base, lane = spot_of
    moved = [
        pltpu.roll(padded[plane, base + t, at, :], lax.rem(LANES - lane, LANES), 1)
        for t in range(tiles + 1)
    ]
    place = lax.broadcasted_iota(jnp.int32, moved[0].shape, 1)
    parts = [
        lifted(jnp.where(place < LANES - lane, moved[t], moved[t + 1]), shift)
        for t in range(tiles)
    ]
    return jnp.concatenate(parts, 1)


def add_window(work, term, spot_of):
    at, shift, base, lane = spot_of
    tiles = term.shape[1] // LANES
    moved = [
        pltpu.roll(lowered(term[:, t * LANES : (t + 1) * LANES], shift), lane, 1)
        for t in range(tiles)
    ]
    none = jnp.zeros_like(moved[0])
    place = lax.broadcasted_iota(jnp.int32, none.shape, 1)
    for t in range(tiles + 1):
        here = moved[t] if t < tiles else none
        before = moved[t - 1] if t else none
        work[base + t, at, :] += jnp.where(place >= lane, here, before)


def neighbours(first, second, index, count):
    even = index % 2 == 0
    before = jnp.where(even, second, first)
    after = jnp.where(even, first, second)
    return jnp.where(index > 0, before, 0.0), jnp.where(index < count - 1, after, 0.0)


def pack_kernel(margin, place, field, columns_first, columns_second):
    planes, side, _ = field.shape
    even = place[2] % 2 == 0
    for plane in range(planes):
        left = pack_rows(field[plane, :, :LANES], 0, margin)
        right = pack_rows(field[plane, :, side - LANES :], LANES - margin, margin)
        columns_first[plane] = jnp.where(even, right, left)
        columns_second[plane] = jnp.where(even, left, right)


def prepare_kernel(margin, offsets, amplitude, probe, sorted_out, total_out, powers, held):
    frames, length, _ = amplitude.shape
    half = length // 2
    power = probe[0] * probe[0] + probe[1] * probe[1]
    powers[...] = jnp.zeros(powers.shape, f32)
    for f in range(frames):
        add_window(powers, power, spot(offsets, f, margin, length + SUBLANES))
    row = lax.broadcasted_iota(jnp.int32, (length, length), 0)
    column = lax.broadcasted_iota(jnp.int32, (length, length), 1)
    source = jnp.where(column < half, 2 * column, 2 * (column - half) + 1)
    order = jnp.where(row == source, 1.0, 0.0).astype(bf16)
    total = jnp.zeros((SUBLANES, length), f32)
    for f in range(frames):
        values = amplitude[f]
        total += jnp.sum((values * values).reshape(length // SUBLANES, SUBLANES, length), 0)
        high = values.astype(bf16)
        rest = values - high.astype(f32)
        middle = rest.astype(bf16)
        low = (rest - middle.astype(f32)).astype(bf16)
        placed = dot(high, order) + (dot(middle, order) + dot(low, order))
        for parity in range(2):
            held[f, parity] = placed[:, parity * half : (parity + 1) * half]
            for start in range(2):
                at = 2 * parity + start
                sorted_out[f, at * half : (at + 1) * half, :] = held[
                    f, parity, pl.ds(start, half, stride=2), :
                ]
    total_out[...] = sum(total[:, t * LANES : (t + 1) * LANES] for t in range(length // LANES))


def corner_kernel(counts, place, first, second, inner_first, inner_second, above, below, out):
    planes, margin, side = first.shape
    inner = inner_first.shape[1]
    even = place[2] % 2 == 0
    for plane in range(planes):
        before, after = neighbours(first[plane], second[plane], place[1], counts[0])
        above[plane] = before
        below[plane] = after
        both = jnp.concatenate([before, after], 0)
        left = pack_rows(both[:, :LANES], 0, margin)
        right = pack_rows(both[:, side - LANES :], LANES - margin, margin)
        out[plane, :inner] = inner_first[plane]
        out[plane, inner:] = jnp.where(even, right, left)
        out[planes + plane, :inner] = inner_second[plane]
        out[planes + plane, inner:] = jnp.where(even, left, right)


def transform_pair(waves, row_turn, column_turn, matrices, amplitudes):
    length = waves[0][0].shape[0]
    half = length // 2
    row_cos, row_sin = row_turn
    column_cos, column_sin = column_turn

    mixed = []
    for real, imag in waves:
        odd = turned(real[:half] - real[half:], imag[:half] - imag[half:], row_cos, -row_sin)
        stacked = jnp.concatenate(
            [
                jnp.concatenate([real[:half] + real[half:], imag[:half] + imag[half:]], 0),
                jnp.concatenate(odd, 0),
            ],
            1,
        )
        mixed.append(matrix_times(matrices.at[0], stacked))

    far = []
    for value in mixed:
        evens, odds = [], []
        for parity in range(2):
            part = value[:, parity * length : (parity + 1) * length]
            real, imag = part[:half], part[half:]
            evens.append(
                jnp.concatenate(
                    [real[:, :half] + real[:, half:], imag[:, :half] + imag[:, half:]], 1
                )
            )
            odd = turned(
                real[:, :half] - real[:, half:],
                imag[:, :half] - imag[:, half:],
                column_cos,
                -column_sin,
            )
            odds.append(jnp.concatenate(odd, 1))
        far.append(times_matrix(jnp.concatenate(evens + odds, 0), matrices.at[1]))

    turned_back = []
    for value, amplitude in zip(far, amplitudes):
        real, imag = value[:, :half], value[:, half:]
        factor = amplitude * lax.rsqrt(real * real + imag * imag + smoothing)
        corrected = jnp.concatenate([real * factor, imag * factor], 1)
        turned_back.append(times_matrix(corrected, matrices.at[0]))

    near = []
    for value in turned_back:
        even, odd = value[:length], value[length:]
        odd_real, odd_imag = turned(odd[:, :half], odd[:, half:], column_cos, column_sin)
        even_real, even_imag = even[:, :half], even[:, half:]
        real = jnp.concatenate([even_real + odd_real, even_real - odd_real], 1)
        imag = jnp.concatenate([even_imag + odd_imag, even_imag - odd_imag], 1)
        stacked = jnp.concatenate(
            [
                jnp.concatenate([real[:half], imag[:half]], 0),
                jnp.concatenate([real[half:], imag[half:]], 0),
            ],
            1,
        )
        near.append(matrix_times(matrices.at[1], stacked))

    results = []
    for value in near:
        even, odd = value[:, :length], value[:, length:]
        odd_real, odd_imag = turned(odd[:half], odd[half:], row_cos, row_sin)
        results.append(
            (
                jnp.concatenate([even[:half] + odd_real, even[:half] - odd_real], 0),
                jnp.concatenate([even[half:] + odd_imag, even[half:] - odd_imag], 0),
            )
        )
    return results


def frames_kernel(
    counts,
    blocks,
    place,
    offsets,
    field,
    above,
    below,
    columns_first,
    columns_second,
    probe,
    amplitude,
    total,
    powers,
    matrices,
    row_turn,
    column_turn,
    work,
    kept,
    sent,
    padded,
    sums,
):
    frames = amplitude.shape[0]
    length = probe.shape[1]
    side = field.shape[1]
    margin = above.shape[1]
    reach = side + 2 * margin
    taller = length + SUBLANES
    per = LANES // margin
    inner = side // per
    tiles = length // LANES
    last = side // LANES + 1

    for plane in range(2):
        for tile in range(side // LANES):
            lanes = pl.ds(tile * LANES, LANES)
            padded[plane, tile + 1, :margin, :] = above[plane, :, lanes]
            padded[plane, tile + 1, margin : margin + side, :] = field[plane, :, lanes]
            padded[plane, tile + 1, margin + side : reach, :] = below[plane, :, lanes]
        left, right = neighbours(
            columns_first[plane], columns_second[plane], place[2], counts[1]
        )
        for tile, packed, lane in ((0, left, LANES - margin), (last, right, 0)):
            corners = unpack_rows(packed[inner:], lane, margin)
            padded[plane, tile, :margin, :] = corners[:margin]
            padded[plane, tile, margin : margin + side, :] = unpack_rows(
                packed[:inner], lane, margin
            )
            padded[plane, tile, margin + side : reach, :] = corners[margin:]
        padded[plane, :, reach:, :] = jnp.zeros((last + 1, SUBLANES, LANES), f32)
    work[...] = jnp.zeros(work.shape, f32)
    first = jnp.where(place[1] + place[2] == 0, 1.0, 0.0).astype(f32)
    sums[0] = probe[0] * first
    sums[1] = probe[1] * first
    sums[2] = jnp.full((length, length), regular, f32) * first

    row_cos, row_sin = (jnp.concatenate([row_turn[k]] * tiles, 1) for k in range(2))
    column_cos, column_sin = (column_turn[k, 0:1, :] for k in range(2))
    together = max(k for k in (1, 2, 4) if frames % k == 0)

    def visit(step, carry):
        chosen = [step * together + k for k in range(together)]
        spots = [spot(offsets, f, margin, taller) for f in chosen]
        windows = [
            tuple(window_of(padded, plane, spot_of, tiles) for plane in range(2))
            for spot_of in spots
        ]
        probe_real, probe_imag = probe[0], probe[1]
        waves = [
            (
                probe_real * real - probe_imag * imag,
                probe_real * imag + probe_imag * real,
            )
            for real, imag in windows
        ]
        nears = transform_pair(
            waves,
            (row_cos, row_sin),
            (column_cos, column_sin),
            matrices,
            [amplitude[f] for f in chosen],
        )
        for (window_real, window_imag), (near_real, near_imag), spot_of in zip(
            windows, nears, spots
        ):
            sums[0] += window_real * near_real + window_imag * near_imag
            sums[1] += window_real * near_imag - window_imag * near_real
            sums[2] += window_real * window_real + window_imag * window_imag
            add_window(work.at[0], probe_real * near_real + probe_imag * near_imag, spot_of)
            add_window(work.at[1], probe_real * near_imag - probe_imag * near_real, spot_of)
        return carry

    lax.fori_loop(0, frames // together, visit, 0)

    rows = length // blocks
    half_rows = blocks // 2 * 3 * tiles * rows
    for p in range(blocks):
        out, q, base = (
            (kept, p, place[0]) if p < blocks // 2 else (sent, p - blocks // 2, place[3])
        )
        source = pl.multiple_of((base ^ q) * rows, rows)
        for plane in range(3):
            for tile in range(tiles):
                start = ((3 * q + plane) * tiles + tile) * rows
                out[start : start + rows, :] = sums[
                    plane, pl.ds(source, rows), pl.ds(tile * LANES, LANES)
                ]
    kept[half_rows:, :] = total[...]
    sent[half_rows : half_rows + SUBLANES, :] = total[...]
    even = place[2] % 2 == 0
    start = half_rows + SUBLANES
    depth = reach // per
    for plane in range(3):
        canvas = powers if plane == 2 else work.at[plane]
        right = pack_rows(canvas[last, :reach, :], 0, margin)
        left = pack_rows(canvas[0, :reach, :], LANES - margin, margin)
        at = start + plane * depth
        sent[at : at + depth, :] = jnp.where(even, right, left)
        at += 3 * depth
        sent[at : at + depth, :] = jnp.where(even, left, right)


def row_edge_kernel(counts, margin, place, work, powers, first, second, out):
    planes = work.shape[0] + 1
    tiles = work.shape[1] - 2
    reach = work.shape[2] - SUBLANES
    depth = first.shape[0] // planes
    even = place[1] % 2 == 0
    for plane in range(planes):
        canvas = powers if plane == planes - 1 else work.at[plane]
        at = pl.ds(plane * depth, depth)
        before, after = neighbours(first[at, :], second[at, :], place[2], counts[1])
        last = LANES // margin - 1
        edges = []
        for begin, chunk, cut in (
            (0, 0, slice(None, margin)),
            (reach - margin, last, slice(depth - margin, None)),
        ):
            parts = [canvas[tile + 1, begin : begin + margin, :] for tile in range(tiles)]
            parts[0] += unpack(before, chunk, 0, margin)[cut]
            parts[-1] += unpack(after, chunk, LANES - margin, margin)[cut]
            edges.append(parts)
        for tile in range(tiles):
            at = pl.ds((plane * tiles + tile) * margin, margin)
            out[at, :] = jnp.where(even, edges[1][tile], edges[0][tile])
            at = pl.ds(((planes + plane) * tiles + tile) * margin, margin)
            out[at, :] = jnp.where(even, edges[0][tile], edges[1][tile])


def object_kernel(
    counts, margin, place, field, work, powers, first, second, row_first, row_second, out
):
    planes = work.shape[0] + 1
    tiles = work.shape[1] - 2
    side = field.shape[1]
    depth = first.shape[0] // planes
    for tile in range(tiles):
        lanes = pl.ds(tile * LANES, LANES)
        total = []
        for plane in range(planes):
            canvas = powers if plane == planes - 1 else work.at[plane]
            at = pl.ds((plane * tiles + tile) * margin, margin)
            above, below = neighbours(row_first[at, :], row_second[at, :], place[1], counts[0])
            part = canvas[tile + 1, margin : margin + side, :]
            at = pl.ds(plane * depth, depth)
            before, after = neighbours(first[at, :], second[at, :], place[2], counts[1])
            if tile == 0:
                part += unpack_rows(before, 0, margin)[margin : margin + side]
            if tile == tiles - 1:
                part += unpack_rows(after, LANES - margin, margin)[margin : margin + side]
            part = jnp.concatenate(
                [
                    part[:margin] + above,
                    part[margin : side - margin],
                    part[side - margin :] + below,
                ],
                0,
            )
            total.append(part)
        weight = 1.0 / (total[2] + regular)
        out[0, :, lanes] = (field[0, :, lanes] + total[0]) * weight
        out[1, :, lanes] = (field[1, :, lanes] + total[1]) * weight


def probe_kernel(frame_count, blocks, place, stepped, total, out):
    planes, length, _ = out.shape
    tiles = length // LANES
    rows = length // blocks
    values = stepped[...]
    power = jnp.sum(values * values)
    target = jnp.sum(total[...]) / frame_count
    scale = jnp.sqrt(jnp.full((rows, LANES), target / (power + epsilon), f32))
    for p in range(blocks):
        base, q = (place[0], p) if p < blocks // 2 else (place[3], p - blocks // 2)
        home = pl.multiple_of((base ^ q) * rows, rows)
        for plane in range(planes):
            for tile in range(tiles):
                start = ((planes * p + plane) * tiles + tile) * rows
                out[plane, pl.ds(home, rows), pl.ds(tile * LANES, LANES)] = (
                    values[start : start + rows] * scale
                )


def shape(*dims):
    return jax.ShapeDtypeStruct(dims, f32)


def call(kernel, outputs, scalars=0, operands=0, scratch=(), cost=None):
    vmem = pl.BlockSpec(memory_space=pltpu.VMEM)
    smem = pl.BlockSpec(memory_space=pltpu.SMEM)
    return pl.pallas_call(
        kernel,
        out_shape=outputs,
        in_specs=[smem] * scalars + [vmem] * operands,
        out_specs=jax.tree.map(lambda _: vmem, outputs),
        scratch_shapes=list(scratch),
        cost_estimate=cost,
        compiler_params=pltpu.CompilerParams(vmem_limit_bytes=40 * 1024 * 1024),
    )


def paired(block, axis, first):
    count = lax.axis_size(axis)
    target = list(range(count))
    for i in range(first, count - 1, 2):
        target[i], target[i + 1] = i + 1, i
    return lax.ppermute(block, axis, list(enumerate(target)))


def relayed(block, axis):
    count = lax.axis_size(axis)
    target = {i: i + 2 if i % 2 == 0 else i - 2 for i in range(count)}
    target[count - 2], target[1] = count - 1, 0
    return lax.ppermute(block, axis, list(target.items()))


def exchanged(block, orders, distance):
    count = lax.axis_size("row") * lax.axis_size("col")
    masks = [
        sum(1 << bit for k, bit in enumerate(order) if distance >> k & 1) for order in orders
    ]
    return lax.ppermute(block, ("row", "col"), [(i, i ^ masks[i % 2]) for i in range(count)])


def per_device(object_field, probe, amplitudes, positions):
    planes, side, _ = object_field.shape
    length = probe.shape[1]
    margin = MARGIN
    reach = side + 2 * margin
    per = LANES // margin
    tiles = length // LANES
    measured = amplitudes[0, 0]
    frames = measured.shape[0]
    counts = lax.axis_size("row"), lax.axis_size("col")
    row = lax.axis_index("row").astype(jnp.int32)
    col = lax.axis_index("col").astype(jnp.int32)
    index = row * counts[1] + col
    col_bits = (counts[1] - 1).bit_length()
    across = list(range(1, col_bits))
    along = list(range(col_bits, col_bits + (counts[0] - 1).bit_length()))
    halvings = 2
    orders = tuple(
        order[:halvings] + order[halvings:][::-1] for order in (across + along, along[::-1] + across)
    )
    blocks = 2 << halvings
    rows = length // blocks
    homes = [
        sum(((index >> order[k]) & 1) << k for k in range(halvings))
        for order in orders
    ]
    core = index & 1
    homes[1] += blocks // 2
    place = jnp.stack(
        [
            jnp.where(core == 0, homes[0], homes[1]),
            row,
            col,
            jnp.where(core == 0, homes[1], homes[0]),
        ]
    )

    edge_rows = shape(planes, margin, side)
    inner = shape(planes, side // per, LANES)
    odd = row & 1
    last = side - margin
    rows_first = lax.dynamic_slice_in_dim(object_field, last - odd * last, margin, 1)
    rows_second = lax.dynamic_slice_in_dim(object_field, odd * last, margin, 1)
    rows_second = paired(rows_second, "row", 1)
    rows_first = paired(rows_first, "row", 0)
    inner_first, inner_second = call(
        functools.partial(pack_kernel, margin), (inner, inner), scalars=1, operands=1
    )(place, object_field)
    above, below, columns = call(
        functools.partial(corner_kernel, counts),
        (edge_rows, edge_rows, shape(2 * planes, reach // per, LANES)),
        scalars=1,
        operands=4,
    )(place, rows_first, rows_second, inner_first, inner_second)
    columns = paired(columns, "col", 0)
    relay = relayed(columns[planes:], "col")

    ordered, total, powers = call(
        functools.partial(prepare_kernel, margin),
        (
            shape(frames, 2 * length, length // 2),
            shape(SUBLANES, LANES),
            shape(side // LANES + 2, reach + SUBLANES, LANES),
        ),
        scalars=1,
        operands=2,
        scratch=(pltpu.VMEM((frames, 2, length, length // 2), f32),),
        cost=pl.CostEstimate(flops=10**9, bytes_accessed=2 * measured.size * 4, transcendentals=0),
    )(positions[0, 0], measured, probe)
    matrices, row_turn, column_turn = tables(length)
    half_rows = blocks // 2 * 3 * tiles * rows
    depth = 3 * reach // per
    work, kept, sent = call(
        functools.partial(frames_kernel, counts, blocks),
        (
            shape(2, side // LANES + 2, reach + SUBLANES, LANES),
            shape(half_rows + SUBLANES, LANES),
            shape(half_rows + SUBLANES + 2 * depth, LANES),
        ),
        scalars=2,
        operands=12,
        scratch=(
            pltpu.VMEM((2, side // LANES + 2, reach + SUBLANES, LANES), f32),
            pltpu.VMEM((3, length, length), f32),
        ),
    )(
        place,
        positions[0, 0],
        object_field,
        above,
        below,
        columns,
        relay,
        probe,
        ordered,
        total,
        powers,
        jnp.asarray(matrices),
        jnp.asarray(row_turn),
        jnp.asarray(column_turn),
    )

    arrived = paired(sent, "col", 0)
    current = kept + arrived[: half_rows + SUBLANES]
    first = arrived[half_rows + SUBLANES : half_rows + SUBLANES + depth]
    second = relayed(arrived[half_rows + SUBLANES + depth :], "col")
    block = 3 * tiles * rows
    total = current[-SUBLANES:]
    quarters = [
        jnp.concatenate([current[d * block : (d + 1) * block], total], 0) for d in range(blocks // 2)
    ]
    terms = quarters[:1] + [exchanged(quarters[d], orders, d) for d in range(1, blocks // 2)]
    while len(terms) > 1:
        terms = [terms[k] + terms[k + 1] for k in range(0, len(terms), 2)]
    current = terms[0]
    current, second = lax.optimization_barrier((current, second))
    count = 3 * tiles * margin
    edges = call(
        functools.partial(row_edge_kernel, counts, margin),
        shape(2 * count, LANES),
        scalars=1,
        operands=4,
    )(place, work, powers, first, second)
    edges = paired(edges, "row", 0)
    for step in range(halvings, len(orders[0])):
        if step == halvings + 1:
            current, edges = lax.optimization_barrier((current, edges))
            row_first = edges[:count]
            row_second = relayed(edges[count:], "row")
        current = current + exchanged(current, orders, 1 << step)
    size = tiles * rows
    weight = current[2 * size : 3 * size]
    stepped = current[: 2 * size] / jnp.concatenate([weight, weight], 0)
    stepped = jnp.concatenate(
        [stepped] + [exchanged(stepped, orders, d) for d in range(1, blocks // 2)], 0
    )
    object_next = call(
        functools.partial(object_kernel, counts, margin),
        shape(*object_field.shape),
        scalars=1,
        operands=7,
    )(place, object_field, work, powers, first, second, row_first, row_second)
    stepped = jnp.concatenate([stepped, paired(stepped, "col", 0)], 0)
    frame_count = frames * counts[0] * counts[1]
    probe_next = call(
        functools.partial(probe_kernel, frame_count, blocks),
        shape(*probe.shape),
        scalars=1,
        operands=2,
    )(place, stepped, current[3 * size :])
    return (object_next, probe_next)


def solution(mesh):
    return jax.shard_map(
        per_device,
        mesh=mesh,
        in_specs=(
            P(None, "row", "col"),
            P(),
            P("row", "col", None, None, None),
            P("row", "col", None, None),
        ),
        out_specs=(P(None, "row", "col"), P()),
        check_vma=False,
    )
```

```python
import functools
import math

import jax
import jax.numpy as jnp
import numpy as np
from jax import lax
from jax.experimental import pallas as pl
from jax.experimental.pallas import tpu as pltpu
from jax.sharding import PartitionSpec as P

MARGIN = 32
LANES = 128
SUBLANES = 8

smoothing = 0.1
regular = 1.0
epsilon = 1e-06

f32 = jnp.float32
bf16 = jnp.bfloat16


def tables(length):
    half = length // 2
    scaling = 1.0 / math.sqrt(length)
    k = np.arange(half)
    phases = (k[:, None] * k[None, :] % half) * (2.0 * math.pi / half)
    cosine, sine = np.cos(phases) * scaling, np.sin(phases) * scaling
    right = np.block([[cosine, -sine], [sine, cosine]])
    left = np.block([[cosine, sine], [-sine, cosine]])
    both = np.stack([left, right]).astype(np.float32)
    high = both.astype(bf16)
    low = (both - high.astype(np.float32)).astype(bf16)
    matrices = np.stack([high, low], 1)
    angle = k * (2.0 * math.pi / length)
    turn = np.stack([np.cos(angle), np.sin(angle)]).astype(np.float32)
    rows = np.broadcast_to(turn[:, :, None], (2, half, LANES)).copy()
    columns = np.broadcast_to(turn[:, None, :], (2, SUBLANES, half)).copy()
    return matrices, rows, columns


def split(x):
    high = x.astype(bf16)
    return high, (x - high.astype(f32)).astype(bf16)


def dot(a, b):
    return jnp.dot(a, b, preferred_element_type=f32)


def times_matrix(data, matrix):
    high, low = split(data)
    return dot(
        jnp.concatenate([high, low, high], 1),
        jnp.concatenate([matrix[0], matrix[0], matrix[1]], 0),
    )


def matrix_times(matrix, data):
    high, low = split(data)
    return dot(
        jnp.concatenate([matrix[0], matrix[0], matrix[1]], 1),
        jnp.concatenate([high, low, high], 0),
    )


def turned(real, imag, cosine, sine):
    return real * cosine - imag * sine, real * sine + imag * cosine


def pack(chunks, lane, width):
    place = lax.broadcasted_iota(jnp.int32, chunks[0].shape, 1) // width
    out = jnp.zeros_like(chunks[0])
    for q, chunk in enumerate(chunks):
        shift = (q * width - lane) % LANES
        moved = pltpu.roll(chunk, shift, 1) if shift else chunk
        out = jnp.where(place == q, moved, out)
    return out


def pack_rows(rows, lane, width):
    count = rows.shape[0] * width // LANES
    return pack([rows[q : q + count] for q in range(0, rows.shape[0], count)], lane, width)


def unpack(packed, q, lane, width):
    shift = (lane - q * width) % LANES
    moved = pltpu.roll(packed, shift, 1) if shift else packed
    place = lax.broadcasted_iota(jnp.int32, packed.shape, 1)
    return jnp.where((place >= lane) & (place < lane + width), moved, 0.0)


def unpack_rows(packed, lane, width):
    return jnp.concatenate([unpack(packed, q, lane, width) for q in range(LANES // width)], 0)


def lifted(tile, shift):
    groups = tile.shape[0] // SUBLANES
    turned_rows = pltpu.roll(
        tile.reshape(groups, SUBLANES, LANES), lax.rem(SUBLANES - shift, SUBLANES), 1
    )
    place = lax.broadcasted_iota(jnp.int32, (groups - 1, SUBLANES, LANES), 1)
    picked = jnp.where(place < SUBLANES - shift, turned_rows[:-1], turned_rows[1:])
    return picked.reshape((groups - 1) * SUBLANES, LANES)


def lowered(tile, shift):
    groups = tile.shape[0] // SUBLANES
    moved = pltpu.roll(tile.reshape(groups, SUBLANES, LANES), shift, 1)
    none = jnp.zeros((1, SUBLANES, LANES), f32)
    place = lax.broadcasted_iota(jnp.int32, (groups + 1, SUBLANES, LANES), 1)
    picked = jnp.where(
        place >= shift, jnp.concatenate([moved, none], 0), jnp.concatenate([none, moved], 0)
    )
    return picked.reshape((groups + 1) * SUBLANES, LANES)


def spot(offsets, f, margin, taller):
    a, b = offsets[f, 0], offsets[f, 1]
    shift = lax.rem(a, SUBLANES)
    lane = b + LANES - margin
    tile = lane // LANES
    return pl.ds(pl.multiple_of(a - shift, SUBLANES), taller), shift, tile, lane - tile * LANES


def window_of(padded, plane, spot_of, tiles):
    at, shift, base, lane = spot_of
    moved = [
        pltpu.roll(padded[plane, base + t, at, :], lax.rem(LANES - lane, LANES), 1)
        for t in range(tiles + 1)
    ]
    place = lax.broadcasted_iota(jnp.int32, moved[0].shape, 1)
    parts = [
        lifted(jnp.where(place < LANES - lane, moved[t], moved[t + 1]), shift)
        for t in range(tiles)
    ]
    return jnp.concatenate(parts, 1)


def add_window(work, term, spot_of):
    at, shift, base, lane = spot_of
    tiles = term.shape[1] // LANES
    moved = [
        pltpu.roll(lowered(term[:, t * LANES : (t + 1) * LANES], shift), lane, 1)
        for t in range(tiles)
    ]
    none = jnp.zeros_like(moved[0])
    place = lax.broadcasted_iota(jnp.int32, none.shape, 1)
    for t in range(tiles + 1):
        here = moved[t] if t < tiles else none
        before = moved[t - 1] if t else none
        work[base + t, at, :] += jnp.where(place >= lane, here, before)


def neighbours(first, second, index, count):
    even = index % 2 == 0
    before = jnp.where(even, second, first)
    after = jnp.where(even, first, second)
    return jnp.where(index > 0, before, 0.0), jnp.where(index < count - 1, after, 0.0)


def pack_kernel(margin, place, field, columns_first, columns_second):
    planes, side, _ = field.shape
    even = place[2] % 2 == 0
    for plane in range(planes):
        left = pack_rows(field[plane, :, :LANES], 0, margin)
        right = pack_rows(field[plane, :, side - LANES :], LANES - margin, margin)
        columns_first[plane] = jnp.where(even, right, left)
        columns_second[plane] = jnp.where(even, left, right)


def prepare_kernel(margin, offsets, amplitude, probe, sorted_out, total_out, powers, held):
    frames, length, _ = amplitude.shape
    half = length // 2
    power = probe[0] * probe[0] + probe[1] * probe[1]
    powers[...] = jnp.zeros(powers.shape, f32)
    for f in range(frames):
        add_window(powers, power, spot(offsets, f, margin, length + SUBLANES))
    row = lax.broadcasted_iota(jnp.int32, (length, length), 0)
    column = lax.broadcasted_iota(jnp.int32, (length, length), 1)
    source = jnp.where(column < half, 2 * column, 2 * (column - half) + 1)
    order = jnp.where(row == source, 1.0, 0.0).astype(bf16)
    total = jnp.zeros((SUBLANES, length), f32)
    for f in range(frames):
        values = amplitude[f]
        total += jnp.sum((values * values).reshape(length // SUBLANES, SUBLANES, length), 0)
        high = values.astype(bf16)
        rest = values - high.astype(f32)
        middle = rest.astype(bf16)
        low = (rest - middle.astype(f32)).astype(bf16)
        placed = dot(high, order) + (dot(middle, order) + dot(low, order))
        for parity in range(2):
            held[f, parity] = placed[:, parity * half : (parity + 1) * half]
            for start in range(2):
                at = 2 * parity + start
                sorted_out[f, at * half : (at + 1) * half, :] = held[
                    f, parity, pl.ds(start, half, stride=2), :
                ]
    total_out[...] = sum(total[:, t * LANES : (t + 1) * LANES] for t in range(length // LANES))


def corner_kernel(counts, place, first, second, inner_first, inner_second, above, below, out):
    planes, margin, side = first.shape
    inner = inner_first.shape[1]
    even = place[2] % 2 == 0
    for plane in range(planes):
        before, after = neighbours(first[plane], second[plane], place[1], counts[0])
        above[plane] = before
        below[plane] = after
        both = jnp.concatenate([before, after], 0)
        left = pack_rows(both[:, :LANES], 0, margin)
        right = pack_rows(both[:, side - LANES :], LANES - margin, margin)
        out[plane, :inner] = inner_first[plane]
        out[plane, inner:] = jnp.where(even, right, left)
        out[planes + plane, :inner] = inner_second[plane]
        out[planes + plane, inner:] = jnp.where(even, left, right)


def transform_pair(waves, row_turn, column_turn, matrices, amplitudes):
    length = waves[0][0].shape[0]
    half = length // 2
    row_cos, row_sin = row_turn
    column_cos, column_sin = column_turn

    mixed = []
    for real, imag in waves:
        odd = turned(real[:half] - real[half:], imag[:half] - imag[half:], row_cos, -row_sin)
        stacked = jnp.concatenate(
            [
                jnp.concatenate([real[:half] + real[half:], imag[:half] + imag[half:]], 0),
                jnp.concatenate(odd, 0),
            ],
            1,
        )
        mixed.append(matrix_times(matrices.at[0], stacked))

    far = []
    for value in mixed:
        evens, odds = [], []
        for parity in range(2):
            part = value[:, parity * length : (parity + 1) * length]
            real, imag = part[:half], part[half:]
            evens.append(
                jnp.concatenate(
                    [real[:, :half] + real[:, half:], imag[:, :half] + imag[:, half:]], 1
                )
            )
            odd = turned(
                real[:, :half] - real[:, half:],
                imag[:, :half] - imag[:, half:],
                column_cos,
                -column_sin,
            )
            odds.append(jnp.concatenate(odd, 1))
        far.append(times_matrix(jnp.concatenate(evens + odds, 0), matrices.at[1]))

    turned_back = []
    for value, amplitude in zip(far, amplitudes):
        real, imag = value[:, :half], value[:, half:]
        factor = amplitude * lax.rsqrt(real * real + imag * imag + smoothing)
        corrected = jnp.concatenate([real * factor, imag * factor], 1)
        turned_back.append(times_matrix(corrected, matrices.at[0]))

    near = []
    for value in turned_back:
        even, odd = value[:length], value[length:]
        odd_real, odd_imag = turned(odd[:, :half], odd[:, half:], column_cos, column_sin)
        even_real, even_imag = even[:, :half], even[:, half:]
        real = jnp.concatenate([even_real + odd_real, even_real - odd_real], 1)
        imag = jnp.concatenate([even_imag + odd_imag, even_imag - odd_imag], 1)
        stacked = jnp.concatenate(
            [
                jnp.concatenate([real[:half], imag[:half]], 0),
                jnp.concatenate([real[half:], imag[half:]], 0),
            ],
            1,
        )
        near.append(matrix_times(matrices.at[1], stacked))

    results = []
    for value in near:
        even, odd = value[:, :length], value[:, length:]
        odd_real, odd_imag = turned(odd[:half], odd[half:], row_cos, row_sin)
        results.append(
            (
                jnp.concatenate([even[:half] + odd_real, even[:half] - odd_real], 0),
                jnp.concatenate([even[half:] + odd_imag, even[half:] - odd_imag], 0),
            )
        )
    return results


def frames_kernel(
    counts,
    blocks,
    place,
    offsets,
    field,
    above,
    below,
    columns_first,
    columns_second,
    probe,
    amplitude,
    total,
    powers,
    matrices,
    row_turn,
    column_turn,
    work,
    kept,
    sent,
    padded,
    sums,
):
    frames = amplitude.shape[0]
    length = probe.shape[1]
    side = field.shape[1]
    margin = above.shape[1]
    reach = side + 2 * margin
    taller = length + SUBLANES
    per = LANES // margin
    inner = side // per
    tiles = length // LANES
    last = side // LANES + 1

    for plane in range(2):
        for tile in range(side // LANES):
            lanes = pl.ds(tile * LANES, LANES)
            padded[plane, tile + 1, :margin, :] = above[plane, :, lanes]
            padded[plane, tile + 1, margin : margin + side, :] = field[plane, :, lanes]
            padded[plane, tile + 1, margin + side : reach, :] = below[plane, :, lanes]
        left, right = neighbours(
            columns_first[plane], columns_second[plane], place[2], counts[1]
        )
        for tile, packed, lane in ((0, left, LANES - margin), (last, right, 0)):
            corners = unpack_rows(packed[inner:], lane, margin)
            padded[plane, tile, :margin, :] = corners[:margin]
            padded[plane, tile, margin : margin + side, :] = unpack_rows(
                packed[:inner], lane, margin
            )
            padded[plane, tile, margin + side : reach, :] = corners[margin:]
        padded[plane, :, reach:, :] = jnp.zeros((last + 1, SUBLANES, LANES), f32)
    work[...] = jnp.zeros(work.shape, f32)
    first = jnp.where(place[1] + place[2] == 0, 1.0, 0.0).astype(f32)
    sums[0] = probe[0] * first
    sums[1] = probe[1] * first
    sums[2] = jnp.full((length, length), regular, f32) * first

    row_cos, row_sin = (jnp.concatenate([row_turn[k]] * tiles, 1) for k in range(2))
    column_cos, column_sin = (column_turn[k, 0:1, :] for k in range(2))
    together = max(k for k in (1, 2, 4) if frames % k == 0)

    def visit(step, carry):
        chosen = [step * together + k for k in range(together)]
        spots = [spot(offsets, f, margin, taller) for f in chosen]
        windows = [
            tuple(window_of(padded, plane, spot_of, tiles) for plane in range(2))
            for spot_of in spots
        ]
        probe_real, probe_imag = probe[0], probe[1]
        waves = [
            (
                probe_real * real - probe_imag * imag,
                probe_real * imag + probe_imag * real,
            )
            for real, imag in windows
        ]
        nears = transform_pair(
            waves,
            (row_cos, row_sin),
            (column_cos, column_sin),
            matrices,
            [amplitude[f] for f in chosen],
        )
        for (window_real, window_imag), (near_real, near_imag), spot_of in zip(
            windows, nears, spots
        ):
            sums[0] += window_real * near_real + window_imag * near_imag
            sums[1] += window_real * near_imag - window_imag * near_real
            sums[2] += window_real * window_real + window_imag * window_imag
            add_window(work.at[0], probe_real * near_real + probe_imag * near_imag, spot_of)
            add_window(work.at[1], probe_real * near_imag - probe_imag * near_real, spot_of)
        return carry

    lax.fori_loop(0, frames // together, visit, 0)

    rows = length // blocks
    half_rows = blocks // 2 * 3 * tiles * rows
    for p in range(blocks):
        out, q, base = (
            (kept, p, place[0]) if p < blocks // 2 else (sent, p - blocks // 2, place[3])
        )
        source = pl.multiple_of((base ^ q) * rows, rows)
        for plane in range(3):
            for tile in range(tiles):
                start = ((3 * q + plane) * tiles + tile) * rows
                out[start : start + rows, :] = sums[
                    plane, pl.ds(source, rows), pl.ds(tile * LANES, LANES)
                ]
    kept[half_rows:, :] = total[...]
    sent[half_rows : half_rows + SUBLANES, :] = total[...]
    even = place[2] % 2 == 0
    start = half_rows + SUBLANES
    depth = reach // per
    for plane in range(3):
        canvas = powers if plane == 2 else work.at[plane]
        right = pack_rows(canvas[last, :reach, :], 0, margin)
        left = pack_rows(canvas[0, :reach, :], LANES - margin, margin)
        at = start + plane * depth
        sent[at : at + depth, :] = jnp.where(even, right, left)
        at += 3 * depth
        sent[at : at + depth, :] = jnp.where(even, left, right)


def row_edge_kernel(counts, margin, place, work, powers, first, second, out):
    planes = work.shape[0] + 1
    tiles = work.shape[1] - 2
    reach = work.shape[2] - SUBLANES
    depth = first.shape[0] // planes
    even = place[1] % 2 == 0
    for plane in range(planes):
        canvas = powers if plane == planes - 1 else work.at[plane]
        at = pl.ds(plane * depth, depth)
        before, after = neighbours(first[at, :], second[at, :], place[2], counts[1])
        last = LANES // margin - 1
        edges = []
        for begin, chunk, cut in (
            (0, 0, slice(None, margin)),
            (reach - margin, last, slice(depth - margin, None)),
        ):
            parts = [canvas[tile + 1, begin : begin + margin, :] for tile in range(tiles)]
            parts[0] += unpack(before, chunk, 0, margin)[cut]
            parts[-1] += unpack(after, chunk, LANES - margin, margin)[cut]
            edges.append(parts)
        for tile in range(tiles):
            at = pl.ds((plane * tiles + tile) * margin, margin)
            out[at, :] = jnp.where(even, edges[1][tile], edges[0][tile])
            at = pl.ds(((planes + plane) * tiles + tile) * margin, margin)
            out[at, :] = jnp.where(even, edges[0][tile], edges[1][tile])


def object_kernel(
    counts, margin, place, field, work, powers, first, second, row_first, row_second, out
):
    planes = work.shape[0] + 1
    tiles = work.shape[1] - 2
    side = field.shape[1]
    depth = first.shape[0] // planes
    for tile in range(tiles):
        lanes = pl.ds(tile * LANES, LANES)
        total = []
        for plane in range(planes):
            canvas = powers if plane == planes - 1 else work.at[plane]
            at = pl.ds((plane * tiles + tile) * margin, margin)
            above, below = neighbours(row_first[at, :], row_second[at, :], place[1], counts[0])
            part = canvas[tile + 1, margin : margin + side, :]
            at = pl.ds(plane * depth, depth)
            before, after = neighbours(first[at, :], second[at, :], place[2], counts[1])
            if tile == 0:
                part += unpack_rows(before, 0, margin)[margin : margin + side]
            if tile == tiles - 1:
                part += unpack_rows(after, LANES - margin, margin)[margin : margin + side]
            part = jnp.concatenate(
                [
                    part[:margin] + above,
                    part[margin : side - margin],
                    part[side - margin :] + below,
                ],
                0,
            )
            total.append(part)
        weight = 1.0 / (total[2] + regular)
        out[0, :, lanes] = (field[0, :, lanes] + total[0]) * weight
        out[1, :, lanes] = (field[1, :, lanes] + total[1]) * weight


def probe_kernel(frame_count, blocks, place, stepped, total, out):
    planes, length, _ = out.shape
    tiles = length // LANES
    rows = length // blocks
    values = stepped[...]
    power = jnp.sum(values * values)
    target = jnp.sum(total[...]) / frame_count
    scale = jnp.sqrt(jnp.full((rows, LANES), target / (power + epsilon), f32))
    for p in range(blocks):
        base, q = (place[0], p) if p < blocks // 2 else (place[3], p - blocks // 2)
        home = pl.multiple_of((base ^ q) * rows, rows)
        for plane in range(planes):
            for tile in range(tiles):
                start = ((planes * p + plane) * tiles + tile) * rows
                out[plane, pl.ds(home, rows), pl.ds(tile * LANES, LANES)] = (
                    values[start : start + rows] * scale
                )


def shape(*dims):
    return jax.ShapeDtypeStruct(dims, f32)


def call(kernel, outputs, scalars=0, operands=0, scratch=(), cost=None):
    vmem = pl.BlockSpec(memory_space=pltpu.VMEM)
    smem = pl.BlockSpec(memory_space=pltpu.SMEM)
    return pl.pallas_call(
        kernel,
        out_shape=outputs,
        in_specs=[smem] * scalars + [vmem] * operands,
        out_specs=jax.tree.map(lambda _: vmem, outputs),
        scratch_shapes=list(scratch),
        cost_estimate=cost,
        compiler_params=pltpu.CompilerParams(vmem_limit_bytes=40 * 1024 * 1024),
    )


def paired(block, axis, first):
    count = lax.axis_size(axis)
    target = list(range(count))
    for i in range(first, count - 1, 2):
        target[i], target[i + 1] = i + 1, i
    return lax.ppermute(block, axis, list(enumerate(target)))


def relayed(block, axis):
    count = lax.axis_size(axis)
    target = {i: i + 2 if i % 2 == 0 else i - 2 for i in range(count)}
    target[count - 2], target[1] = count - 1, 0
    return lax.ppermute(block, axis, list(target.items()))


def exchanged(block, orders, distance):
    count = lax.axis_size("row") * lax.axis_size("col")
    masks = [
        sum(1 << bit for k, bit in enumerate(order) if distance >> k & 1) for order in orders
    ]
    return lax.ppermute(block, ("row", "col"), [(i, i ^ masks[i % 2]) for i in range(count)])


def per_device(object_field, probe, amplitudes, positions):
    planes, side, _ = object_field.shape
    length = probe.shape[1]
    margin = MARGIN
    reach = side + 2 * margin
    per = LANES // margin
    tiles = length // LANES
    measured = amplitudes[0, 0]
    frames = measured.shape[0]
    counts = lax.axis_size("row"), lax.axis_size("col")
    row = lax.axis_index("row").astype(jnp.int32)
    col = lax.axis_index("col").astype(jnp.int32)
    index = row * counts[1] + col
    col_bits = (counts[1] - 1).bit_length()
    across = list(range(1, col_bits))
    along = list(range(col_bits, col_bits + (counts[0] - 1).bit_length()))
    halvings = 2
    orders = tuple(
        order[:halvings] + order[halvings:][::-1] for order in (across + along, along[::-1] + across)
    )
    blocks = 2 << halvings
    rows = length // blocks
    homes = [
        sum(((index >> order[k]) & 1) << k for k in range(halvings))
        for order in orders
    ]
    core = index & 1
    homes[1] += blocks // 2
    place = jnp.stack(
        [
            jnp.where(core == 0, homes[0], homes[1]),
            row,
            col,
            jnp.where(core == 0, homes[1], homes[0]),
        ]
    )

    edge_rows = shape(planes, margin, side)
    inner = shape(planes, side // per, LANES)
    odd = row & 1
    last = side - margin
    rows_first = lax.dynamic_slice_in_dim(object_field, last - odd * last, margin, 1)
    rows_second = lax.dynamic_slice_in_dim(object_field, odd * last, margin, 1)
    rows_second = paired(rows_second, "row", 1)
    rows_first = paired(rows_first, "row", 0)
    inner_first, inner_second = call(
        functools.partial(pack_kernel, margin), (inner, inner), scalars=1, operands=1
    )(place, object_field)
    above, below, columns = call(
        functools.partial(corner_kernel, counts),
        (edge_rows, edge_rows, shape(2 * planes, reach // per, LANES)),
        scalars=1,
        operands=4,
    )(place, rows_first, rows_second, inner_first, inner_second)
    columns = paired(columns, "col", 0)
    relay = relayed(columns[planes:], "col")

    ordered, total, powers = call(
        functools.partial(prepare_kernel, margin),
        (
            shape(frames, 2 * length, length // 2),
            shape(SUBLANES, LANES),
            shape(side // LANES + 2, reach + SUBLANES, LANES),
        ),
        scalars=1,
        operands=2,
        scratch=(pltpu.VMEM((frames, 2, length, length // 2), f32),),
        cost=pl.CostEstimate(flops=10**9, bytes_accessed=2 * measured.size * 4, transcendentals=0),
    )(positions[0, 0], measured, probe)
    matrices, row_turn, column_turn = tables(length)
    half_rows = blocks // 2 * 3 * tiles * rows
    depth = 3 * reach // per
    work, kept, sent = call(
        functools.partial(frames_kernel, counts, blocks),
        (
            shape(2, side // LANES + 2, reach + SUBLANES, LANES),
            shape(half_rows + SUBLANES, LANES),
            shape(half_rows + SUBLANES + 2 * depth, LANES),
        ),
        scalars=2,
        operands=12,
        scratch=(
            pltpu.VMEM((2, side // LANES + 2, reach + SUBLANES, LANES), f32),
            pltpu.VMEM((3, length, length), f32),
        ),
    )(
        place,
        positions[0, 0],
        object_field,
        above,
        below,
        columns,
        relay,
        probe,
        ordered,
        total,
        powers,
        jnp.asarray(matrices),
        jnp.asarray(row_turn),
        jnp.asarray(column_turn),
    )

    arrived = paired(sent, "col", 0)
    current = kept + arrived[: half_rows + SUBLANES]
    first = arrived[half_rows + SUBLANES : half_rows + SUBLANES + depth]
    second = relayed(arrived[half_rows + SUBLANES + depth :], "col")
    block = 3 * tiles * rows
    total = current[-SUBLANES:]
    quarters = [
        jnp.concatenate([current[d * block : (d + 1) * block], total], 0) for d in range(blocks // 2)
    ]
    terms = [exchanged(quarters[d], orders, d) for d in range(2, blocks // 2)]
    near_quarter, second = lax.optimization_barrier((quarters[1], second))
    terms = [quarters[0], exchanged(near_quarter, orders, 1)] + terms
    while len(terms) > 1:
        terms = [terms[k] + terms[k + 1] for k in range(0, len(terms), 2)]
    current = terms[0]
    count = 3 * tiles * margin
    edges = call(
        functools.partial(row_edge_kernel, counts, margin),
        shape(2 * count, LANES),
        scalars=1,
        operands=4,
    )(place, work, powers, first, second)
    current, edges = lax.optimization_barrier((current, edges))
    edges = paired(edges, "row", 0)
    for step in range(halvings, len(orders[0])):
        if step == halvings + 1:
            current, edges = lax.optimization_barrier((current, edges))
            row_first = edges[:count]
            row_second = relayed(edges[count:], "row")
        current = current + exchanged(current, orders, 1 << step)
    size = tiles * rows
    weight = current[2 * size : 3 * size]
    stepped = current[: 2 * size] / jnp.concatenate([weight, weight], 0)
    stepped = jnp.concatenate(
        [stepped] + [exchanged(stepped, orders, d) for d in range(1, blocks // 2)], 0
    )
    object_next = call(
        functools.partial(object_kernel, counts, margin),
        shape(*object_field.shape),
        scalars=1,
        operands=7,
    )(place, object_field, work, powers, first, second, row_first, row_second)
    stepped = jnp.concatenate([stepped, paired(stepped, "col", 0)], 0)
    frame_count = frames * counts[0] * counts[1]
    probe_next = call(
        functools.partial(probe_kernel, frame_count, blocks),
        shape(*probe.shape),
        scalars=1,
        operands=2,
    )(place, stepped, current[3 * size :])
    return (object_next, probe_next)


def solution(mesh):
    return jax.shard_map(
        per_device,
        mesh=mesh,
        in_specs=(
            P(None, "row", "col"),
            P(),
            P("row", "col", None, None, None),
            P("row", "col", None, None),
        ),
        out_specs=(P(None, "row", "col"), P()),
        check_vma=False,
    )
```

```python
import functools
import math

import jax
import jax.numpy as jnp
import numpy as np
from jax import lax
from jax.experimental import pallas as pl
from jax.experimental.pallas import tpu as pltpu
from jax.sharding import PartitionSpec as P

MARGIN = 32
LANES = 128
SUBLANES = 8

smoothing = 0.1
regular = 1.0
epsilon = 1e-06

f32 = jnp.float32
bf16 = jnp.bfloat16


def tables(length):
    half = length // 2
    scaling = 1.0 / math.sqrt(length)
    k = np.arange(half)
    phases = (k[:, None] * k[None, :] % half) * (2.0 * math.pi / half)
    cosine, sine = np.cos(phases) * scaling, np.sin(phases) * scaling
    right = np.block([[cosine, -sine], [sine, cosine]])
    left = np.block([[cosine, sine], [-sine, cosine]])
    both = np.stack([left, right]).astype(np.float32)
    high = both.astype(bf16)
    low = (both - high.astype(np.float32)).astype(bf16)
    matrices = np.stack([high, low], 1)
    angle = k * (2.0 * math.pi / length)
    turn = np.stack([np.cos(angle), np.sin(angle)]).astype(np.float32)
    rows = np.broadcast_to(turn[:, :, None], (2, half, LANES)).copy()
    columns = np.broadcast_to(turn[:, None, :], (2, SUBLANES, half)).copy()
    return matrices, rows, columns


def split(x):
    high = x.astype(bf16)
    return high, (x - high.astype(f32)).astype(bf16)


def dot(a, b):
    return jnp.dot(a, b, preferred_element_type=f32)


def times_matrix(data, matrix):
    high, low = split(data)
    return dot(
        jnp.concatenate([high, low, high], 1),
        jnp.concatenate([matrix[0], matrix[0], matrix[1]], 0),
    )


def matrix_times(matrix, data):
    high, low = split(data)
    return dot(
        jnp.concatenate([matrix[0], matrix[0], matrix[1]], 1),
        jnp.concatenate([high, low, high], 0),
    )


def turned(real, imag, cosine, sine):
    return real * cosine - imag * sine, real * sine + imag * cosine


def pack(chunks, lane, width):
    place = lax.broadcasted_iota(jnp.int32, chunks[0].shape, 1) // width
    out = jnp.zeros_like(chunks[0])
    for q, chunk in enumerate(chunks):
        shift = (q * width - lane) % LANES
        moved = pltpu.roll(chunk, shift, 1) if shift else chunk
        out = jnp.where(place == q, moved, out)
    return out


def pack_rows(rows, lane, width):
    count = rows.shape[0] * width // LANES
    return pack([rows[q : q + count] for q in range(0, rows.shape[0], count)], lane, width)


def unpack(packed, q, lane, width):
    shift = (lane - q * width) % LANES
    moved = pltpu.roll(packed, shift, 1) if shift else packed
    place = lax.broadcasted_iota(jnp.int32, packed.shape, 1)
    return jnp.where((place >= lane) & (place < lane + width), moved, 0.0)


def unpack_rows(packed, lane, width):
    return jnp.concatenate([unpack(packed, q, lane, width) for q in range(LANES // width)], 0)


def lifted(tile, shift):
    groups = tile.shape[0] // SUBLANES
    turned_rows = pltpu.roll(
        tile.reshape(groups, SUBLANES, LANES), lax.rem(SUBLANES - shift, SUBLANES), 1
    )
    place = lax.broadcasted_iota(jnp.int32, (groups - 1, SUBLANES, LANES), 1)
    picked = jnp.where(place < SUBLANES - shift, turned_rows[:-1], turned_rows[1:])
    return picked.reshape((groups - 1) * SUBLANES, LANES)


def lowered(tile, shift):
    groups = tile.shape[0] // SUBLANES
    moved = pltpu.roll(tile.reshape(groups, SUBLANES, LANES), shift, 1)
    none = jnp.zeros((1, SUBLANES, LANES), f32)
    place = lax.broadcasted_iota(jnp.int32, (groups + 1, SUBLANES, LANES), 1)
    picked = jnp.where(
        place >= shift, jnp.concatenate([moved, none], 0), jnp.concatenate([none, moved], 0)
    )
    return picked.reshape((groups + 1) * SUBLANES, LANES)


def spot(offsets, f, margin, taller):
    a, b = offsets[f, 0], offsets[f, 1]
    shift = lax.rem(a, SUBLANES)
    lane = b + LANES - margin
    tile = lane // LANES
    return pl.ds(pl.multiple_of(a - shift, SUBLANES), taller), shift, tile, lane - tile * LANES


def window_of(padded, plane, spot_of, tiles):
    at, shift, base, lane = spot_of
    moved = [
        pltpu.roll(padded[plane, base + t, at, :], lax.rem(LANES - lane, LANES), 1)
        for t in range(tiles + 1)
    ]
    place = lax.broadcasted_iota(jnp.int32, moved[0].shape, 1)
    parts = [
        lifted(jnp.where(place < LANES - lane, moved[t], moved[t + 1]), shift)
        for t in range(tiles)
    ]
    return jnp.concatenate(parts, 1)


def add_window(work, term, spot_of):
    at, shift, base, lane = spot_of
    tiles = term.shape[1] // LANES
    moved = [
        pltpu.roll(lowered(term[:, t * LANES : (t + 1) * LANES], shift), lane, 1)
        for t in range(tiles)
    ]
    none = jnp.zeros_like(moved[0])
    place = lax.broadcasted_iota(jnp.int32, none.shape, 1)
    for t in range(tiles + 1):
        here = moved[t] if t < tiles else none
        before = moved[t - 1] if t else none
        work[base + t, at, :] += jnp.where(place >= lane, here, before)


def neighbours(first, second, index, count):
    even = index % 2 == 0
    before = jnp.where(even, second, first)
    after = jnp.where(even, first, second)
    return jnp.where(index > 0, before, 0.0), jnp.where(index < count - 1, after, 0.0)


def pack_kernel(margin, place, field, columns_first, columns_second):
    planes, side, _ = field.shape
    even = place[2] % 2 == 0
    for plane in range(planes):
        left = pack_rows(field[plane, :, :LANES], 0, margin)
        right = pack_rows(field[plane, :, side - LANES :], LANES - margin, margin)
        columns_first[plane] = jnp.where(even, right, left)
        columns_second[plane] = jnp.where(even, left, right)


def prepare_kernel(margin, offsets, amplitude, probe, sorted_out, total_out, powers, held):
    frames, length, _ = amplitude.shape
    half = length // 2
    power = probe[0] * probe[0] + probe[1] * probe[1]
    powers[...] = jnp.zeros(powers.shape, f32)
    for f in range(frames):
        add_window(powers, power, spot(offsets, f, margin, length + SUBLANES))
    row = lax.broadcasted_iota(jnp.int32, (length, length), 0)
    column = lax.broadcasted_iota(jnp.int32, (length, length), 1)
    source = jnp.where(column < half, 2 * column, 2 * (column - half) + 1)
    order = jnp.where(row == source, 1.0, 0.0).astype(bf16)
    total = jnp.zeros((SUBLANES, length), f32)
    for f in range(frames):
        values = amplitude[f]
        total += jnp.sum((values * values).reshape(length // SUBLANES, SUBLANES, length), 0)
        high = values.astype(bf16)
        rest = values - high.astype(f32)
        middle = rest.astype(bf16)
        low = (rest - middle.astype(f32)).astype(bf16)
        placed = dot(high, order) + (dot(middle, order) + dot(low, order))
        for parity in range(2):
            held[f, parity] = placed[:, parity * half : (parity + 1) * half]
            for start in range(2):
                at = 2 * parity + start
                sorted_out[f, at * half : (at + 1) * half, :] = held[
                    f, parity, pl.ds(start, half, stride=2), :
                ]
    total_out[...] = sum(total[:, t * LANES : (t + 1) * LANES] for t in range(length // LANES))


def corner_kernel(counts, place, first, second, inner_first, inner_second, above, below, out):
    planes, margin, side = first.shape
    inner = inner_first.shape[1]
    even = place[2] % 2 == 0
    for plane in range(planes):
        before, after = neighbours(first[plane], second[plane], place[1], counts[0])
        above[plane] = before
        below[plane] = after
        both = jnp.concatenate([before, after], 0)
        left = pack_rows(both[:, :LANES], 0, margin)
        right = pack_rows(both[:, side - LANES :], LANES - margin, margin)
        out[plane, :inner] = inner_first[plane]
        out[plane, inner:] = jnp.where(even, right, left)
        out[planes + plane, :inner] = inner_second[plane]
        out[planes + plane, inner:] = jnp.where(even, left, right)


def transform_pair(waves, row_turn, column_turn, matrices, amplitudes):
    length = waves[0][0].shape[0]
    half = length // 2
    row_cos, row_sin = row_turn
    column_cos, column_sin = column_turn

    mixed = []
    for real, imag in waves:
        odd = turned(real[:half] - real[half:], imag[:half] - imag[half:], row_cos, -row_sin)
        stacked = jnp.concatenate(
            [
                jnp.concatenate([real[:half] + real[half:], imag[:half] + imag[half:]], 0),
                jnp.concatenate(odd, 0),
            ],
            1,
        )
        mixed.append(matrix_times(matrices.at[0], stacked))

    far = []
    for value in mixed:
        evens, odds = [], []
        for parity in range(2):
            part = value[:, parity * length : (parity + 1) * length]
            real, imag = part[:half], part[half:]
            evens.append(
                jnp.concatenate(
                    [real[:, :half] + real[:, half:], imag[:, :half] + imag[:, half:]], 1
                )
            )
            odd = turned(
                real[:, :half] - real[:, half:],
                imag[:, :half] - imag[:, half:],
                column_cos,
                -column_sin,
            )
            odds.append(jnp.concatenate(odd, 1))
        far.append(times_matrix(jnp.concatenate(evens + odds, 0), matrices.at[1]))

    turned_back = []
    for value, amplitude in zip(far, amplitudes):
        real, imag = value[:, :half], value[:, half:]
        factor = amplitude * lax.rsqrt(real * real + imag * imag + smoothing)
        corrected = jnp.concatenate([real * factor, imag * factor], 1)
        turned_back.append(times_matrix(corrected, matrices.at[0]))

    near = []
    for value in turned_back:
        even, odd = value[:length], value[length:]
        odd_real, odd_imag = turned(odd[:, :half], odd[:, half:], column_cos, column_sin)
        even_real, even_imag = even[:, :half], even[:, half:]
        real = jnp.concatenate([even_real + odd_real, even_real - odd_real], 1)
        imag = jnp.concatenate([even_imag + odd_imag, even_imag - odd_imag], 1)
        stacked = jnp.concatenate(
            [
                jnp.concatenate([real[:half], imag[:half]], 0),
                jnp.concatenate([real[half:], imag[half:]], 0),
            ],
            1,
        )
        near.append(matrix_times(matrices.at[1], stacked))

    results = []
    for value in near:
        even, odd = value[:, :length], value[:, length:]
        odd_real, odd_imag = turned(odd[:half], odd[half:], row_cos, row_sin)
        results.append(
            (
                jnp.concatenate([even[:half] + odd_real, even[:half] - odd_real], 0),
                jnp.concatenate([even[half:] + odd_imag, even[half:] - odd_imag], 0),
            )
        )
    return results


def frames_kernel(
    counts,
    blocks,
    place,
    offsets,
    field,
    above,
    below,
    columns_first,
    columns_second,
    probe,
    amplitude,
    total,
    powers,
    matrices,
    row_turn,
    column_turn,
    work,
    kept,
    sent,
    padded,
    sums,
):
    frames = amplitude.shape[0]
    length = probe.shape[1]
    side = field.shape[1]
    margin = above.shape[1]
    reach = side + 2 * margin
    taller = length + SUBLANES
    per = LANES // margin
    inner = side // per
    tiles = length // LANES
    last = side // LANES + 1

    for plane in range(2):
        for tile in range(side // LANES):
            lanes = pl.ds(tile * LANES, LANES)
            padded[plane, tile + 1, :margin, :] = above[plane, :, lanes]
            padded[plane, tile + 1, margin : margin + side, :] = field[plane, :, lanes]
            padded[plane, tile + 1, margin + side : reach, :] = below[plane, :, lanes]
        left, right = neighbours(
            columns_first[plane], columns_second[plane], place[2], counts[1]
        )
        for tile, packed, lane in ((0, left, LANES - margin), (last, right, 0)):
            corners = unpack_rows(packed[inner:], lane, margin)
            padded[plane, tile, :margin, :] = corners[:margin]
            padded[plane, tile, margin : margin + side, :] = unpack_rows(
                packed[:inner], lane, margin
            )
            padded[plane, tile, margin + side : reach, :] = corners[margin:]
        padded[plane, :, reach:, :] = jnp.zeros((last + 1, SUBLANES, LANES), f32)
    work[...] = jnp.zeros(work.shape, f32)
    first = jnp.where(place[1] + place[2] == 0, 1.0, 0.0).astype(f32)
    sums[0] = probe[0] * first
    sums[1] = probe[1] * first
    sums[2] = jnp.full((length, length), regular, f32) * first

    row_cos, row_sin = (jnp.concatenate([row_turn[k]] * tiles, 1) for k in range(2))
    column_cos, column_sin = (column_turn[k, 0:1, :] for k in range(2))
    together = max(k for k in (1, 2, 4) if frames % k == 0)

    def visit(step, carry):
        chosen = [step * together + k for k in range(together)]
        spots = [spot(offsets, f, margin, taller) for f in chosen]
        windows = [
            tuple(window_of(padded, plane, spot_of, tiles) for plane in range(2))
            for spot_of in spots
        ]
        probe_real, probe_imag = probe[0], probe[1]
        waves = [
            (
                probe_real * real - probe_imag * imag,
                probe_real * imag + probe_imag * real,
            )
            for real, imag in windows
        ]
        nears = transform_pair(
            waves,
            (row_cos, row_sin),
            (column_cos, column_sin),
            matrices,
            [amplitude[f] for f in chosen],
        )
        for (window_real, window_imag), (near_real, near_imag), spot_of in zip(
            windows, nears, spots
        ):
            sums[0] += window_real * near_real + window_imag * near_imag
            sums[1] += window_real * near_imag - window_imag * near_real
            sums[2] += window_real * window_real + window_imag * window_imag
            add_window(work.at[0], probe_real * near_real + probe_imag * near_imag, spot_of)
            add_window(work.at[1], probe_real * near_imag - probe_imag * near_real, spot_of)
        return carry

    lax.fori_loop(0, frames // together, visit, 0)

    rows = length // blocks
    half_rows = blocks // 2 * 3 * tiles * rows
    for p in range(blocks):
        out, q, base = (
            (kept, p, place[0]) if p < blocks // 2 else (sent, p - blocks // 2, place[3])
        )
        source = pl.multiple_of((base ^ q) * rows, rows)
        for plane in range(3):
            for tile in range(tiles):
                start = ((3 * q + plane) * tiles + tile) * rows
                out[start : start + rows, :] = sums[
                    plane, pl.ds(source, rows), pl.ds(tile * LANES, LANES)
                ]
    kept[half_rows:, :] = total[...]
    sent[half_rows : half_rows + SUBLANES, :] = total[...]
    even = place[2] % 2 == 0
    start = half_rows + SUBLANES
    depth = reach // per
    for plane in range(3):
        canvas = powers if plane == 2 else work.at[plane]
        right = pack_rows(canvas[last, :reach, :], 0, margin)
        left = pack_rows(canvas[0, :reach, :], LANES - margin, margin)
        at = start + plane * depth
        sent[at : at + depth, :] = jnp.where(even, right, left)
        at += 3 * depth
        sent[at : at + depth, :] = jnp.where(even, left, right)


def row_edge_kernel(counts, margin, place, work, powers, first, second, out):
    planes = work.shape[0] + 1
    tiles = work.shape[1] - 2
    reach = work.shape[2] - SUBLANES
    depth = first.shape[0] // planes
    even = place[1] % 2 == 0
    for plane in range(planes):
        canvas = powers if plane == planes - 1 else work.at[plane]
        at = pl.ds(plane * depth, depth)
        before, after = neighbours(first[at, :], second[at, :], place[2], counts[1])
        last = LANES // margin - 1
        edges = []
        for begin, chunk, cut in (
            (0, 0, slice(None, margin)),
            (reach - margin, last, slice(depth - margin, None)),
        ):
            parts = [canvas[tile + 1, begin : begin + margin, :] for tile in range(tiles)]
            parts[0] += unpack(before, chunk, 0, margin)[cut]
            parts[-1] += unpack(after, chunk, LANES - margin, margin)[cut]
            edges.append(parts)
        for tile in range(tiles):
            at = pl.ds((plane * tiles + tile) * margin, margin)
            out[at, :] = jnp.where(even, edges[1][tile], edges[0][tile])
            at = pl.ds(((planes + plane) * tiles + tile) * margin, margin)
            out[at, :] = jnp.where(even, edges[0][tile], edges[1][tile])


def object_kernel(
    counts, margin, place, field, work, powers, first, second, row_first, row_second, out
):
    planes = work.shape[0] + 1
    tiles = work.shape[1] - 2
    side = field.shape[1]
    depth = first.shape[0] // planes
    for tile in range(tiles):
        lanes = pl.ds(tile * LANES, LANES)
        total = []
        for plane in range(planes):
            canvas = powers if plane == planes - 1 else work.at[plane]
            at = pl.ds((plane * tiles + tile) * margin, margin)
            above, below = neighbours(row_first[at, :], row_second[at, :], place[1], counts[0])
            part = canvas[tile + 1, margin : margin + side, :]
            at = pl.ds(plane * depth, depth)
            before, after = neighbours(first[at, :], second[at, :], place[2], counts[1])
            if tile == 0:
                part += unpack_rows(before, 0, margin)[margin : margin + side]
            if tile == tiles - 1:
                part += unpack_rows(after, LANES - margin, margin)[margin : margin + side]
            part = jnp.concatenate(
                [
                    part[:margin] + above,
                    part[margin : side - margin],
                    part[side - margin :] + below,
                ],
                0,
            )
            total.append(part)
        weight = 1.0 / (total[2] + regular)
        out[0, :, lanes] = (field[0, :, lanes] + total[0]) * weight
        out[1, :, lanes] = (field[1, :, lanes] + total[1]) * weight


def probe_kernel(frame_count, blocks, place, stepped, total, out):
    planes, length, _ = out.shape
    tiles = length // LANES
    rows = length // blocks
    values = stepped[...]
    power = jnp.sum(values * values)
    target = jnp.sum(total[...]) / frame_count
    scale = jnp.sqrt(jnp.full((rows, LANES), target / (power + epsilon), f32))
    for p in range(blocks):
        base, q = (place[0], p) if p < blocks // 2 else (place[3], p - blocks // 2)
        home = pl.multiple_of((base ^ q) * rows, rows)
        for plane in range(planes):
            for tile in range(tiles):
                start = ((planes * p + plane) * tiles + tile) * rows
                out[plane, pl.ds(home, rows), pl.ds(tile * LANES, LANES)] = (
                    values[start : start + rows] * scale
                )


def shape(*dims):
    return jax.ShapeDtypeStruct(dims, f32)


def call(kernel, outputs, scalars=0, operands=0, scratch=(), cost=None):
    vmem = pl.BlockSpec(memory_space=pltpu.VMEM)
    smem = pl.BlockSpec(memory_space=pltpu.SMEM)
    return pl.pallas_call(
        kernel,
        out_shape=outputs,
        in_specs=[smem] * scalars + [vmem] * operands,
        out_specs=jax.tree.map(lambda _: vmem, outputs),
        scratch_shapes=list(scratch),
        cost_estimate=cost,
        compiler_params=pltpu.CompilerParams(vmem_limit_bytes=40 * 1024 * 1024),
    )


def paired(block, axis, first):
    count = lax.axis_size(axis)
    target = list(range(count))
    for i in range(first, count - 1, 2):
        target[i], target[i + 1] = i + 1, i
    return lax.ppermute(block, axis, list(enumerate(target)))


def relayed(block, axis):
    count = lax.axis_size(axis)
    target = {i: i + 2 if i % 2 == 0 else i - 2 for i in range(count)}
    target[count - 2], target[1] = count - 1, 0
    return lax.ppermute(block, axis, list(target.items()))


def exchanged(block, orders, distance):
    count = lax.axis_size("row") * lax.axis_size("col")
    masks = [
        sum(1 << bit for k, bit in enumerate(order) if distance >> k & 1) for order in orders
    ]
    return lax.ppermute(block, ("row", "col"), [(i, i ^ masks[i % 2]) for i in range(count)])


def per_device(object_field, probe, amplitudes, positions):
    planes, side, _ = object_field.shape
    length = probe.shape[1]
    margin = MARGIN
    reach = side + 2 * margin
    per = LANES // margin
    tiles = length // LANES
    measured = amplitudes[0, 0]
    frames = measured.shape[0]
    counts = lax.axis_size("row"), lax.axis_size("col")
    row = lax.axis_index("row").astype(jnp.int32)
    col = lax.axis_index("col").astype(jnp.int32)
    index = row * counts[1] + col
    col_bits = (counts[1] - 1).bit_length()
    across = list(range(1, col_bits))
    along = list(range(col_bits, col_bits + (counts[0] - 1).bit_length()))
    halvings = 2
    orders = tuple(
        order[:halvings] + order[halvings:][::-1] for order in (across + along, along[::-1] + across)
    )
    blocks = 2 << halvings
    rows = length // blocks
    homes = [
        sum(((index >> order[k]) & 1) << k for k in range(halvings))
        for order in orders
    ]
    core = index & 1
    homes[1] += blocks // 2
    place = jnp.stack(
        [
            jnp.where(core == 0, homes[0], homes[1]),
            row,
            col,
            jnp.where(core == 0, homes[1], homes[0]),
        ]
    )

    edge_rows = shape(planes, margin, side)
    inner = shape(planes, side // per, LANES)
    odd = row & 1
    last = side - margin
    rows_first = lax.dynamic_slice_in_dim(object_field, last - odd * last, margin, 1)
    rows_second = lax.dynamic_slice_in_dim(object_field, odd * last, margin, 1)
    rows_second = paired(rows_second, "row", 1)
    rows_first = paired(rows_first, "row", 0)
    inner_first, inner_second = call(
        functools.partial(pack_kernel, margin), (inner, inner), scalars=1, operands=1
    )(place, object_field)
    above, below, columns = call(
        functools.partial(corner_kernel, counts),
        (edge_rows, edge_rows, shape(2 * planes, reach // per, LANES)),
        scalars=1,
        operands=4,
    )(place, rows_first, rows_second, inner_first, inner_second)
    columns = paired(columns, "col", 0)
    relay = relayed(columns[planes:], "col")

    ordered, total, powers = call(
        functools.partial(prepare_kernel, margin),
        (
            shape(frames, 2 * length, length // 2),
            shape(SUBLANES, LANES),
            shape(side // LANES + 2, reach + SUBLANES, LANES),
        ),
        scalars=1,
        operands=2,
        scratch=(pltpu.VMEM((frames, 2, length, length // 2), f32),),
        cost=pl.CostEstimate(flops=10**9, bytes_accessed=2 * measured.size * 4, transcendentals=0),
    )(positions[0, 0], measured, probe)
    matrices, row_turn, column_turn = tables(length)
    half_rows = blocks // 2 * 3 * tiles * rows
    depth = 3 * reach // per
    work, kept, sent = call(
        functools.partial(frames_kernel, counts, blocks),
        (
            shape(2, side // LANES + 2, reach + SUBLANES, LANES),
            shape(half_rows + SUBLANES, LANES),
            shape(half_rows + SUBLANES + 2 * depth, LANES),
        ),
        scalars=2,
        operands=12,
        scratch=(
            pltpu.VMEM((2, side // LANES + 2, reach + SUBLANES, LANES), f32),
            pltpu.VMEM((3, length, length), f32),
        ),
    )(
        place,
        positions[0, 0],
        object_field,
        above,
        below,
        columns,
        relay,
        probe,
        ordered,
        total,
        powers,
        jnp.asarray(matrices),
        jnp.asarray(row_turn),
        jnp.asarray(column_turn),
    )

    arrived = paired(sent, "col", 0)
    current = kept + arrived[: half_rows + SUBLANES]
    first = arrived[half_rows + SUBLANES : half_rows + SUBLANES + depth]
    second = relayed(arrived[half_rows + SUBLANES + depth :], "col")
    block = 3 * tiles * rows
    total = current[-SUBLANES:]
    quarters = [
        jnp.concatenate([current[d * block : (d + 1) * block], total], 0) for d in range(blocks // 2)
    ]
    terms = [exchanged(quarters[d], orders, d) for d in range(2, blocks // 2)]
    near_quarter, second = lax.optimization_barrier((quarters[1], second))
    terms = [quarters[0], exchanged(near_quarter, orders, 1)] + terms
    while len(terms) > 1:
        terms = [terms[k] + terms[k + 1] for k in range(0, len(terms), 2)]
    current = terms[0]
    count = 3 * tiles * margin
    edges = call(
        functools.partial(row_edge_kernel, counts, margin),
        shape(2 * count, LANES),
        scalars=1,
        operands=4,
    )(place, work, powers, first, second)
    edges = paired(edges, "row", 0)
    for step in range(halvings, len(orders[0])):
        if step == halvings + 1:
            current, edges = lax.optimization_barrier((current, edges))
            row_first = edges[:count]
            row_second = relayed(edges[count:], "row")
        current = current + exchanged(current, orders, 1 << step)
    size = tiles * rows
    weight = current[2 * size : 3 * size]
    stepped = current[: 2 * size] / jnp.concatenate([weight, weight], 0)
    stepped = jnp.concatenate(
        [stepped] + [exchanged(stepped, orders, d) for d in range(1, blocks // 2)], 0
    )
    object_next = call(
        functools.partial(object_kernel, counts, margin),
        shape(*object_field.shape),
        scalars=1,
        operands=7,
    )(place, object_field, work, powers, first, second, row_first, row_second)
    stepped = jnp.concatenate([stepped, paired(stepped, "col", 0)], 0)
    frame_count = frames * counts[0] * counts[1]
    probe_next = call(
        functools.partial(probe_kernel, frame_count, blocks),
        shape(*probe.shape),
        scalars=1,
        operands=2,
    )(place, stepped, current[3 * size :])
    return (object_next, probe_next)


def solution(mesh):
    return jax.shard_map(
        per_device,
        mesh=mesh,
        in_specs=(
            P(None, "row", "col"),
            P(),
            P("row", "col", None, None, None),
            P("row", "col", None, None),
        ),
        out_specs=(P(None, "row", "col"), P()),
        check_vma=False,
    )
```
